32 devices in a mesh: macro: 8 (over z, y), pool: 4 (over x, core).
Axes of the slice: x: 2, y: 2, z: 4, core: 2. Of those that a mesh axis runs over, the one named last changes fastest.
Arguments:
- history: float32 [729, 16384], P(None, ('macro', 'pool')), may hold values from -6 to 6
- yield_flags: int32 [729, 16384], P(None, ('macro', 'pool')), may hold values 0 or 1
- strain: float32 [6, 16384], P(None, ('macro', 'pool')), may hold values from -6 to 6
- qp_to_rve: int32 [32, 512], P(('macro', 'pool')), may hold values from 0 to 511, each once within a row
- new_owner: int32 [16384, 1], P(('macro', 'pool')), may hold values from 0 to 31; in each aligned block of 512 rows (0 to 511, 512 to 1023, ...) at most 32 rows name the same one
- stiffness: float32 [9, 9, 81, 81], replicated, as said below
- pattern: int32 [9, 9], replicated, may hold values from 0 to 1, as said below
- coupling: float32 [3, 6, 729], replicated, as said below
- plastic_dir: float32 [3, 729], replicated, may hold values from -6 to 6
Outputs:
- new_history: float32 [729, 32768], P(None, ('macro', 'pool'))
- stress: float32 [6, 16384], P(None, ('macro', 'pool'))
The draws below stay inside these ranges and needn't reach their ends.
Inputs may be any that keep to these rules, and one draw needn't show every extreme that they name: `new_owner`: among the rows of one device no owner is named more than 32 times, a bound that some block reaches. `qp_to_rve`: each row is a permutation of 0 to 511. `pattern`: Symmetric, with ones on the diagonal. stiffness[a, b] is the transpose of stiffness[b, a]; diagonal entries of diagonal blocks lie in 0.5 to 1.5, all others in 0 to 0.032. `coupling`: entries lie in -5.7 to 6.3.
All inputs are finite; a program needn't handle non-finite values. No bound on the sum of `yield_flags` on one device may be relied on, other than what follows from the above.
Results may differ from the reference program's by a relative error of at most 0.0003.
Values sent between devices are 32-bit elements; how exact they have to be, the bound alone decides.
No kernel may reach another device: no remote copies, remote signals or barrier semaphores. Data moves between devices by JAX's collectives and lax.ppermute only.
A program may use at most 128 MiB of HBM per device.

```python
import math
import jax
import jax.numpy as jnp
import numpy as np
from jax import lax

NB = 9
BLK = 81
COMP = 3
VOIGT = 6
ITERS = 3
R_DEV = 512
NODES = 729
RVES = 16384
CAP = 32
N_MACRO = 8
N_POOL = 4


def draw_stiffness(key, part):
    key_off = jax.random.fold_in(key, 11)
    key_diag = jax.random.fold_in(key, 12)
    raw = jax.random.uniform(key_off, (NB, NB, BLK, BLK), jnp.float32, 0.0, 0.032)
    sym = 0.5 * (raw + jnp.transpose(raw, (1, 0, 3, 2)))
    diag_vals = jax.random.uniform(key_diag, (NB, BLK), jnp.float32, 0.5, 1.5)
    eye_blocks = (jnp.arange(NB)[:, None] == jnp.arange(NB)[None, :]).astype(jnp.float32)
    eye_nodes = (jnp.arange(BLK)[:, None] == jnp.arange(BLK)[None, :]).astype(jnp.float32)
    on_diag = eye_blocks[:, :, None, None] * eye_nodes[None, None, :, :]
    return sym * (1.0 - on_diag) + diag_vals[:, None, :, None] * on_diag


def draw_pattern(key, part):
    groups = jax.random.randint(jax.random.fold_in(key, 21), (NB,), 0, 3).astype(jnp.int32)
    return (groups[:, None] == groups[None, :]).astype(jnp.int32)


def draw_coupling(key, part):
    key_noise = jax.random.fold_in(key, 31)
    noise = jnp.clip(jax.random.normal(key_noise, (COMP, VOIGT, NODES), jnp.float32), -6.0, 6.0)
    offset = 0.3
    return noise + offset


def set_ends(values, own_key, smallest, high):
    extent = values.shape
    place = [jax.random.randint(jax.random.fold_in(own_key, axis), (), 0, extent[axis]) for axis in range(len(extent))]
    values = values.at[tuple(place)].set(smallest)
    longest = extent.index(max(extent))
    place[longest] = (place[longest] + 1) % extent[longest]
    return values.at[tuple(place)].set(high)


def block_levels(rng, shape, shards, low, high):
    def one(dim, parts):
        heights = jax.random.uniform(jax.random.fold_in(jax.random.fold_in(rng, 6), dim), (parts,), jnp.float32, low / len(shards), high / len(shards))
        return jnp.repeat(jnp.exp(heights), shape[dim] // parts).reshape((-1,) + (1,) * (len(shape) - dim - 1))

    loudness = one(*shards[0])
    for cut in shards[1:]:
        loudness = loudness * one(*cut)
    return loudness


def routed_block(stream_key, own, number, rows, amount, top, bound, lean):
    sequence = jax.random.permutation(stream_key, amount)
    packed, common = shares(amount, rows * top, bound, lean, True), shares(amount, rows * top, bound, lean, False)
    places = jnp.arange(amount)

    def named(tallies, rotation):
        used = int((tallies > 0).sum())
        fixed = max(1, used // 4)
        passed = fixed + (places - fixed + rotation * (used - fixed)) % max(1, amount - fixed)
        return jnp.zeros((amount,), jnp.int32).at[sequence[jnp.where(places < fixed, places, passed)]].set(jnp.asarray(tallies, jnp.int32))

    tallies = jnp.where(number % 4 == 0, named(packed, number // 4), named(common, number - number // 4 - 1))
    mixed = jax.random.permutation(jax.random.fold_in(own, 3), amount)
    giver, receiver = mixed[0:amount // 2 * 2:2], mixed[1:amount // 2 * 2:2]
    room = jnp.minimum(tallies[giver] - 1, bound - tallies[receiver]) // 2
    room = jnp.where((giver == sequence[0]) | (receiver == sequence[0]) | (tallies[receiver] == 0), 0, jnp.maximum(room, 0))
    passed = jax.random.randint(jax.random.fold_in(own, 4), (amount // 2,), 0, 1 << 20) % (room + 1)
    tallies = tallies.at[giver].add(-passed).at[receiver].add(passed)
    items = jnp.searchsorted(jnp.cumsum(tallies), jnp.arange(rows * top), side="right").astype(jnp.int32)
    grid = items.reshape(top, rows).T
    grid = grid[jax.random.permutation(jax.random.fold_in(own, 1), rows)]
    rotation = jax.random.randint(jax.random.fold_in(own, 2), (rows, 1), 0, top)
    return jnp.take_along_axis(grid, (jnp.arange(top)[None, :] + rotation) % top, axis=1)


def shares(number_of, total, limit, skew, full):
    portions = [(1 << 20) // math.isqrt(rank ** skew) + 1 for rank in range(1, number_of + 1)]
    largest = limit if full else min(limit, max(-(-total // number_of), total * portions[0] // sum(portions)))
    least = 1 if total - largest >= number_of - 1 else 0
    holding, rest = [largest] + [least] * (number_of - 1), total - largest - least * (number_of - 1)
    while rest > 0:
        free = [i for i in range(1, number_of) if holding[i] < largest] or [i for i in range(1, number_of) if holding[i] < limit]
        whole, budget = sum([portions[i] for i in free]), rest
        for i in free:
            extra = min(limit - holding[i], max(1, budget * portions[i] // whole), rest)
            holding[i] = holding[i] + extra
            rest = rest - extra
    return np.array(holding)


def bell_draw(own_key, extent, deviation, limit, cuts=(), kind=jnp.bfloat16):
    values = jax.random.normal(own_key, extent, jnp.float32) * deviation
    if len(cuts) > 0:
        values = block_levels(own_key, extent, cuts, -0.22, 0.18) * values
    return jnp.clip(values, min=-limit, max=limit).astype(kind)


def setup_inputs(seed: int = 0) -> dict:
    seeds = jax.random.split(jax.random.key(seed), 10)
    history = bell_draw(seeds[0], (NODES, RVES), 1.0, 6.0, ((1, 32),), jnp.float32)
    yield_flags = set_ends((jax.random.randint(seeds[1], (NODES, RVES), 0, 3) < 1).astype(jnp.int32), jax.random.fold_in(seeds[1], 1), 0, 1)
    strain = bell_draw(seeds[2], (VOIGT, RVES), 1.0, 6.0, ((1, 32),), jnp.float32)
    qp_to_rve = jax.vmap(lambda own: jax.random.permutation(own, R_DEV))(jax.random.split(seeds[3], (N_MACRO * N_POOL))).reshape((N_MACRO * N_POOL, R_DEV)).astype(jnp.int32)
    new_owner_keys = jax.random.split(jax.random.fold_in(seeds[4], 1), RVES // R_DEV)
    new_owner_turns = jax.random.permutation(jax.random.fold_in(seeds[4], 3), RVES // R_DEV)
    new_owner = jax.vmap(lambda own, number: routed_block(jax.random.fold_in(seeds[4], 2), own, number, R_DEV, N_MACRO * N_POOL, 1, CAP, 2))(new_owner_keys, new_owner_turns).reshape((RVES, 1))
    stiffness = draw_stiffness(jax.random.fold_in(seeds[9], 71), 0)
    pattern = draw_pattern(jax.random.fold_in(seeds[9], 71), 0)
    coupling = draw_coupling(jax.random.fold_in(seeds[9], 71), 0)
    plastic_dir = bell_draw(seeds[8], (COMP, NODES), 1.0, 6.0, (), jnp.float32)
    return {"history": history, "yield_flags": yield_flags, "strain": strain, "qp_to_rve": qp_to_rve, "new_owner": new_owner, "stiffness": stiffness, "pattern": pattern, "coupling": coupling, "plastic_dir": plastic_dir}


exact_setting = lax.Precision.HIGHEST

def dense_stiffness(stiffness, pattern):
    block_rows = stiffness.shape[0]
    block_size = stiffness.shape[2]
    masked = stiffness * pattern.astype(jnp.float32)[:, :, None, None]
    return jnp.transpose(masked, (0, 2, 1, 3)).reshape(block_rows * block_size, block_rows * block_size)

def micro_solve(dense_k, coupling, plastic_dir, hist, weight, strain_columns):
    node_total = hist.shape[0]
    component_total = coupling.shape[0]
    columns = hist.shape[1]
    tangent_matrix = 1.5 - weight
    driving = jnp.einsum('ckn,ks->ncs', coupling, strain_columns, precision=exact_setting)
    source = driving - (weight * hist)[:, None, :] * jnp.transpose(plastic_dir)[:, :, None]

    def apply_op(vector_in):
        product = jnp.dot(dense_k, vector_in.reshape(node_total, component_total * columns), precision=exact_setting, preferred_element_type=jnp.float32)
        return product.reshape(node_total, component_total, columns) + tangent_matrix[:, None, :] * vector_in
    solved_field = jnp.zeros_like(source)
    residual = source
    direction = source
    norm_now = lax.optimization_barrier(jnp.sum(residual * residual, axis=(0, 1)))
    for iteration in range(ITERS):
        applied = apply_op(direction)
        step_size = norm_now / jnp.maximum(lax.optimization_barrier(jnp.sum(direction * applied, axis=(0, 1))), 1.0)
        solved_field = solved_field + step_size * direction
        residual = residual - step_size * applied
        norm_next = lax.optimization_barrier(jnp.sum(residual * residual, axis=(0, 1)))
        direction = residual + norm_next / jnp.maximum(norm_now, 1.0) * direction
        norm_now = norm_next
    homogenizing_scale = 1.0 / math.sqrt(component_total * node_total)
    stress_columns = strain_columns + homogenizing_scale * jnp.einsum('dlj,jdf->lf', coupling, tangent_matrix[:, None, :] * solved_field, precision=exact_setting)
    updated = hist + weight * jnp.einsum('cn,ncs->ns', plastic_dir, solved_field, precision=exact_setting)
    return (updated, stress_columns)

def reference(history, yield_flags, strain, qp_to_rve, new_owner, stiffness, pattern, coupling, plastic_dir):
    devices = N_MACRO * N_POOL
    dense_k = dense_stiffness(stiffness, pattern)
    hist_blocks = history.reshape(NODES, devices, R_DEV).transpose(1, 0, 2)
    flag_blocks = yield_flags.reshape(NODES, devices, R_DEV).transpose(1, 0, 2)
    strain_blocks = strain.reshape(VOIGT, devices, R_DEV).transpose(1, 0, 2)
    owner_blocks = new_owner.reshape(devices, R_DEV).astype(jnp.int32)

    def one_block(pieces):
        hist, flags, strain_part, qmap, owner = pieces
        weight = flags.astype(jnp.float32) * hist * hist / (1.0 + hist * hist)
        rve_strain = jnp.zeros_like(strain_part).at[:, qmap.astype(jnp.int32)].set(strain_part)
        updated, stress_rve = micro_solve(dense_k, coupling, plastic_dir, hist, weight, rve_strain)
        stress_qp = stress_rve[:, qmap.astype(jnp.int32)]
        onehot = (owner[:, None] == jnp.arange(devices, dtype=jnp.int32)[None, :]).astype(jnp.int32)
        rank = lax.optimization_barrier(jnp.sum((jnp.cumsum(onehot, axis=0) - onehot) * onehot, axis=1)).astype(jnp.int32)
        return (updated, stress_qp, rank)
    updated, stress_qp, rank = lax.map(one_block, (hist_blocks, flag_blocks, strain_blocks, qp_to_rve, owner_blocks))
    sources = jnp.arange(devices, dtype=jnp.int32)[:, None]
    column = (owner_blocks * (devices * CAP) + sources * CAP + rank).astype(jnp.int32)
    values = updated.transpose(1, 0, 2).reshape(NODES, devices * R_DEV)
    new_history = jnp.zeros((NODES, devices * devices * CAP), jnp.float32).at[:, column.reshape(-1)].set(values)
    stress_out = stress_qp.transpose(1, 0, 2).reshape(VOIGT, devices * R_DEV)
    return (new_history, stress_out)
```

```python
import functools
import math

import jax
import jax.numpy as jnp
from jax import lax
from jax.experimental import pallas as pl
from jax.experimental.pallas import tpu as pltpu
from jax.sharding import PartitionSpec as P

ITERS = 3
LANES = 128

NN = (((1,), (0,)), ((), ()))
NT = (((1,), (1,)), ((), ()))
TN = (((0,), (0,)), ((), ()))


def up(value, unit):
    return -(-value // unit) * unit


def dot(a, b, dims=NN):
    return lax.dot_general(a, b, dims, preferred_element_type=jnp.float32)


def halves(x):
    hi = x.astype(jnp.bfloat16)
    lo = (x - hi.astype(jnp.float32)).astype(jnp.bfloat16)
    return hi, lo


def hot(row, count):
    rows = lax.broadcasted_iota(jnp.int32, (count, row.shape[1]), 0)
    return jnp.where(rows == row, 1.0, 0.0).astype(jnp.bfloat16)


def prep_kernel(devices, owner, qp, hist, flag, strain, stiff, pattern, coupling, plastic,
                khi, klo, hist_s, weight_s, strain_s, place_s, qp_s, cstack, pdir, kfull, pad):
    nodes, columns = hist.shape
    rows = hist_s.shape[0]
    nb, blk = stiff.shape[0], stiff.shape[2]
    comps, voigt = coupling.shape[0], coupling.shape[1]

    kfull[...] = jnp.zeros_like(kfull)
    for a in range(nb):
        for b in range(nb):
            kfull[a * blk:(a + 1) * blk, b * blk:(b + 1) * blk] = (
                stiff[a, b] * pattern[a, b].astype(jnp.float32)
            )
    k = kfull[...]
    kh = k.astype(jnp.bfloat16)
    khi[...] = kh
    klo[...] = (k - kh.astype(jnp.float32)).astype(jnp.bfloat16)

    own = owner[...]
    owner_ids = lax.broadcasted_iota(jnp.int32, (devices, columns), 0)
    mine = jnp.where(owner_ids == own, 1.0, 0.0)
    earlier = jnp.where(
        lax.broadcasted_iota(jnp.int32, (columns, columns), 0)
        < lax.broadcasted_iota(jnp.int32, (columns, columns), 1), 1.0, 0.0
    ).astype(jnp.bfloat16)
    before = dot(mine.astype(jnp.bfloat16), earlier)
    rank = jnp.sum(before * mine, axis=0, keepdims=True)
    tally = jnp.sum(mine, axis=1, keepdims=True)
    ahead = rank + jnp.where(owner_ids < own, 1.0, 0.0)
    position = jnp.sum(jnp.minimum(tally, ahead), axis=0, keepdims=True).astype(jnp.int32)

    order = hot(position, columns)
    for source, target in ((hist, hist_s),):
        hi, lo = halves(source[...])
        target[...] = jnp.zeros_like(target)
        target[0:nodes, :] = dot(hi, order, NT) + dot(lo, order, NT)
    h = hist_s[...]
    weight_s[...] = jnp.zeros_like(weight_s)
    weight_s[0:nodes, :] = dot(flag[...].astype(jnp.float32).astype(jnp.bfloat16), order, NT)
    weight_s[...] = weight_s[...] * h * h / (1.0 + h * h)

    pad[...] = jnp.zeros_like(pad)
    pad[0:1, :] = own.astype(jnp.float32)
    pad[1:2, :] = rank
    place_s[...] = dot(pad[...].astype(jnp.bfloat16), order, NT).astype(jnp.int32)

    pad[0:1, :] = (position // 256).astype(jnp.float32)
    pad[1:2, :] = (position % 256).astype(jnp.float32)
    found = dot(pad[...].astype(jnp.bfloat16), hot(qp[...], columns))
    at = (found[0:1, :] * 256.0 + found[1:2, :]).astype(jnp.int32)
    qp_s[...] = jnp.broadcast_to(at, qp_s.shape)
    pad[...] = jnp.zeros_like(pad)
    pad[0:voigt, :] = strain[...]
    hi, lo = halves(pad[...])
    serves = hot(at, columns)
    strain_s[...] = dot(hi, serves, NT) + dot(lo, serves, NT)

    cstack[...] = jnp.zeros_like(cstack)
    for c in range(comps):
        cpl = coupling[c]
        hi = cpl.astype(jnp.bfloat16).astype(jnp.float32)
        cstack[c, 0:voigt, 0:nodes] = hi
        cstack[c, 8:8 + voigt, 0:nodes] = hi
        cstack[c, 16:16 + voigt, 0:nodes] = cpl - hi
    pdir[...] = jnp.zeros_like(pdir)
    for c in range(comps):
        spread = jnp.broadcast_to(plastic[c:c + 1, :], (LANES, nodes))
        pdir[c, 0:nodes, :] = jnp.transpose(spread)


def sweep(rows, comps):
    cuts = [rows // 16 * i // 4 * 16 for i in range(5)]
    for top, end in zip(cuts, cuts[1:]):
        for c in range(comps):
            yield slice(top, end), slice(c * LANES, (c + 1) * LANES), c


def fold(x):
    return jnp.sum(x.reshape(x.shape[0] // 8, 8, x.shape[1]), axis=0)


def total(parts):
    return jnp.sum(parts, axis=0, keepdims=True)


def solve_kernel(scale, nodes, khi, klo, hist, weight, strain, cstack, pdir,
                 updated, stress, field, resid, image, solved, vhi, vlo):
    rows = hist.shape[0]
    comps = pdir.shape[0]
    zero = jnp.zeros((8, LANES), jnp.float32)
    s = strain[...]
    s_hi = s.astype(jnp.bfloat16).astype(jnp.float32)
    s3 = jnp.concatenate([s_hi, s - s_hi, s_hi, jnp.zeros_like(s)], axis=0).astype(jnp.bfloat16)
    vhi[rows:, :] = jnp.zeros((vhi.shape[0] - rows, vhi.shape[1]), jnp.bfloat16)
    vlo[rows:, :] = jnp.zeros((vlo.shape[0] - rows, vlo.shape[1]), jnp.bfloat16)
    for c in range(comps):
        image[:, c * LANES:(c + 1) * LANES] = dot(cstack[c].astype(jnp.bfloat16), s3, TN)
    parts = zero
    for r, l, c in sweep(rows, comps):
        d = image[r, l] - weight[r, :] * hist[r, :] * pdir[c, r, :]
        resid[r, l] = d
        field[r, l] = d
        vhi[r, l], vlo[r, l] = halves(d)
        parts = parts + fold(d * d)
    norm = total(parts)
    for step in range(ITERS):
        high = vhi[...]
        image[...] = dot(khi[...], high) + dot(khi[...], vlo[...]) + dot(klo[...], high)
        parts = zero
        for r, l, c in sweep(rows, comps):
            d = field[r, l]
            q = image[r, l] + (1.5 - weight[r, :]) * d
            image[r, l] = q
            parts = parts + fold(d * q)
        alpha = norm / jnp.maximum(total(parts), 1.0)
        if step == ITERS - 1:
            break
        parts = zero
        for r, l, c in sweep(rows, comps):
            gain = alpha * field[r, l]
            solved[r, l] = gain if step == 0 else solved[r, l] + gain
            left = resid[r, l] - alpha * image[r, l]
            resid[r, l] = left
            parts = parts + fold(left * left)
        following = total(parts)
        beta = following / jnp.maximum(norm, 1.0)
        norm = following
        for r, l, c in sweep(rows, comps):
            d = resid[r, l] + beta * field[r, l]
            field[r, l] = d
            vhi[r, l], vlo[r, l] = halves(d)
    for r, l, c in sweep(rows, comps):
        x = solved[r, l] + alpha * field[r, l]
        flow = pdir[c, r, :] * x
        image[r, 0:LANES] = flow if c == 0 else image[r, 0:LANES] + flow
        vhi[r, l], vlo[r, l] = halves((1.5 - weight[r, :]) * x)
    updated[...] = hist[...] + weight[...] * image[:, 0:LANES]
    out = s
    for c in range(comps):
        l = slice(c * LANES, (c + 1) * LANES)
        cpl = cstack[c].astype(jnp.bfloat16)
        main = dot(cpl, vhi[0:rows, l])
        minor = dot(cpl, vlo[0:rows, l])
        out = out + scale * (main[0:8] + main[16:24] + minor[0:8])
    stress[...] = out


def ship_kernel(low, high, place, updated, out):
    nodes = out.shape[1]
    count = high - low
    own = place[0:1, :]
    rank = place[1:2, :]
    slot = jnp.where((rank >= low) & (rank < high), own * count + rank - low, -1)
    placing = hot(slot, out.shape[0])
    hi, lo = halves(updated[...])
    out[...] = (dot(placing, hi, NT) + dot(placing, lo, NT))[:, 0:nodes]


def back_kernel(at, stress, out):
    serves = hot(at[0:1, :], stress.shape[1])
    hi, lo = halves(stress[...])
    out[...] = (dot(hi, serves) + dot(lo, serves))[0:out.shape[0], :]


def params():
    return pltpu.CompilerParams(vmem_limit_bytes=56 * 2**20)


def shards(
    history, yield_flags, strain, qp_to_rve, new_owner, stiffness, pattern, coupling, plastic_dir
):
    devices = lax.axis_size(("macro", "pool"))
    nodes, columns = history.shape
    comps, voigt = coupling.shape[0], coupling.shape[1]
    per_peer = 2 * columns // devices
    rows = up(nodes, 32)
    deep = up(nodes, 256)
    f32, bf16, i32 = jnp.float32, jnp.bfloat16, jnp.int32
    vmem = pl.BlockSpec(memory_space=pltpu.VMEM)
    smem = pl.BlockSpec(memory_space=pltpu.SMEM)
    khi, klo, hist_s, weight_s, strain_s, place_s, qp_s, cstack, pdir = pl.pallas_call(
        functools.partial(prep_kernel, devices),
        out_shape=(
            jax.ShapeDtypeStruct((rows, deep), bf16),
            jax.ShapeDtypeStruct((rows, deep), bf16),
            jax.ShapeDtypeStruct((rows, columns), f32),
            jax.ShapeDtypeStruct((rows, columns), f32),
            jax.ShapeDtypeStruct((8, columns), f32),
            jax.ShapeDtypeStruct((8, columns), i32),
            jax.ShapeDtypeStruct((8, columns), i32),
            jax.ShapeDtypeStruct((comps, 32, rows), f32),
            jax.ShapeDtypeStruct((comps, rows, LANES), f32),
        ),
        in_specs=[vmem] * 6 + [smem] + [vmem] * 2,
        out_specs=[vmem] * 9,
        scratch_shapes=[pltpu.VMEM((rows, deep), f32), pltpu.VMEM((8, columns), f32)],
        compiler_params=params(),
    )(new_owner.reshape(1, columns), qp_to_rve, history, yield_flags, strain, stiffness, pattern,
      coupling, plastic_dir)

    whole = lambda shape: pl.BlockSpec(shape, lambda i: (0,) * len(shape))
    part = lambda height: pl.BlockSpec((height, LANES), lambda i: (0, i))
    wide = comps * LANES
    updated, stress_s = pl.pallas_call(
        functools.partial(solve_kernel, 1.0 / math.sqrt(comps * nodes), nodes),
        grid=(columns // LANES,),
        out_shape=(
            jax.ShapeDtypeStruct((rows, columns), f32),
            jax.ShapeDtypeStruct((8, columns), f32),
        ),
        in_specs=[whole((rows, deep)), whole((rows, deep)), part(rows), part(rows), part(8),
                  whole((comps, 32, rows)), whole((comps, rows, LANES))],
        out_specs=[part(rows), part(8)],
        scratch_shapes=[pltpu.VMEM((rows, wide), f32) for _ in range(4)]
        + [pltpu.VMEM((deep, wide), bf16) for _ in range(2)],
        compiler_params=params(),
    )(khi, klo, hist_s, weight_s, strain_s, cstack, pdir)

    shipped = pl.pallas_call(
        functools.partial(ship_kernel, 0, per_peer),
        out_shape=jax.ShapeDtypeStruct((devices * per_peer, nodes), f32),
        in_specs=[vmem, vmem],
        out_specs=vmem,
        compiler_params=params(),
    )(place_s, updated)
    arrived = lax.all_to_all(
        shipped.reshape(devices, per_peer, nodes), ("macro", "pool"), split_axis=0, concat_axis=0,
        tiled=True,
    )
    new_history = jnp.transpose(arrived.reshape(devices * per_peer, nodes))
    stress_out = pl.pallas_call(
        back_kernel,
        out_shape=jax.ShapeDtypeStruct((voigt, columns), f32),
        in_specs=[vmem, vmem],
        out_specs=vmem,
        compiler_params=params(),
    )(qp_s, stress_s)
    return (new_history, stress_out)


def solution(mesh):
    return jax.shard_map(
        shards,
        mesh=mesh,
        in_specs=(
            P(None, ("macro", "pool")),
            P(None, ("macro", "pool")),
            P(None, ("macro", "pool")),
            P(("macro", "pool"), None),
            P(("macro", "pool"), None),
            P(),
            P(),
            P(),
            P(),
        ),
        out_specs=(P(None, ("macro", "pool")), P(None, ("macro", "pool"))),
        check_vma=False,
    )
```

```python
import functools
import math

import jax
import jax.numpy as jnp
from jax import lax
from jax.experimental import pallas as pl
from jax.experimental.pallas import tpu as pltpu
from jax.sharding import PartitionSpec as P

ITERS = 3
LANES = 128

NN = (((1,), (0,)), ((), ()))
NT = (((1,), (1,)), ((), ()))
TN = (((0,), (0,)), ((), ()))


def up(value, unit):
    return -(-value // unit) * unit


def dot(a, b, dims=NN):
    return lax.dot_general(a, b, dims, preferred_element_type=jnp.float32)


def halves(x):
    hi = x.astype(jnp.bfloat16)
    lo = (x - hi.astype(jnp.float32)).astype(jnp.bfloat16)
    return hi, lo


def hot(row, count):
    rows = lax.broadcasted_iota(jnp.int32, (count, row.shape[1]), 0)
    return jnp.where(rows == row, 1.0, 0.0).astype(jnp.bfloat16)


def prep_kernel(devices, per_peer, owner, qp, hist, flag, strain, stiff, pattern, coupling, plastic,
                khi, klo, hist_s, weight_s, strain_s, place_s, qp_s, cstack, pdir, kfull, pad):
    nodes, columns = hist.shape
    rows = hist_s.shape[0]
    nb, blk = stiff.shape[0], stiff.shape[2]
    comps, voigt = coupling.shape[0], coupling.shape[1]

    kfull[...] = jnp.zeros_like(kfull)
    for a in range(nb):
        for b in range(nb):
            kfull[a * blk:(a + 1) * blk, b * blk:(b + 1) * blk] = (
                stiff[a, b] * pattern[a, b].astype(jnp.float32)
            )
    k = kfull[...]
    kh = k.astype(jnp.bfloat16)
    khi[...] = kh
    klo[...] = (k - kh.astype(jnp.float32)).astype(jnp.bfloat16)

    me = lax.axis_index("macro") * lax.axis_size("pool") + lax.axis_index("pool")
    key = owner[...] ^ (me ^ (devices // 2))
    key_ids = lax.broadcasted_iota(jnp.int32, (devices, columns), 0)
    mine = jnp.where(key_ids == key, 1.0, 0.0)
    earlier = jnp.where(
        lax.broadcasted_iota(jnp.int32, (columns, columns), 0)
        < lax.broadcasted_iota(jnp.int32, (columns, columns), 1), 1.0, 0.0
    ).astype(jnp.bfloat16)
    before = dot(mine.astype(jnp.bfloat16), earlier)
    rank = jnp.sum(before * mine, axis=0, keepdims=True)
    tally = jnp.sum(mine, axis=1, keepdims=True)
    ahead = jnp.where(key_ids < key, tally, 0.0)
    position = (rank + jnp.sum(ahead, axis=0, keepdims=True)).astype(jnp.int32)

    order = hot(position, columns)
    for source, target in ((hist, hist_s),):
        hi, lo = halves(source[...])
        target[...] = jnp.zeros_like(target)
        target[0:nodes, :] = dot(hi, order, NT) + dot(lo, order, NT)
    h = hist_s[...]
    weight_s[...] = jnp.zeros_like(weight_s)
    weight_s[0:nodes, :] = dot(flag[...].astype(jnp.float32).astype(jnp.bfloat16), order, NT)
    weight_s[...] = weight_s[...] * h * h / (1.0 + h * h)

    pad[...] = jnp.zeros_like(pad)
    pad[0:1, :] = key.astype(jnp.float32)
    pad[1:2, :] = rank
    placed = dot(pad[...].astype(jnp.bfloat16), order, NT)
    place_s[...] = jnp.broadcast_to(
        (placed[0:1, :] * per_peer + placed[1:2, :]).astype(jnp.int32), place_s.shape
    )

    pad[0:1, :] = (position // 256).astype(jnp.float32)
    pad[1:2, :] = (position % 256).astype(jnp.float32)
    found = dot(pad[...].astype(jnp.bfloat16), hot(qp[...], columns))
    at = (found[0:1, :] * 256.0 + found[1:2, :]).astype(jnp.int32)
    qp_s[...] = jnp.broadcast_to(at, qp_s.shape)
    pad[...] = jnp.zeros_like(pad)
    pad[0:voigt, :] = strain[...]
    hi, lo = halves(pad[...])
    serves = hot(at, columns)
    strain_s[...] = dot(hi, serves, NT) + dot(lo, serves, NT)

    cstack[...] = jnp.zeros_like(cstack)
    for c in range(comps):
        cpl = coupling[c]
        hi = cpl.astype(jnp.bfloat16).astype(jnp.float32)
        cstack[c, 0:voigt, 0:nodes] = hi
        cstack[c, 8:8 + voigt, 0:nodes] = hi
        cstack[c, 16:16 + voigt, 0:nodes] = cpl - hi
    pdir[...] = jnp.zeros_like(pdir)
    for c in range(comps):
        spread = jnp.broadcast_to(plastic[c:c + 1, :], (LANES, nodes))
        pdir[c, 0:nodes, :] = jnp.transpose(spread)


def sweep(rows, comps):
    cuts = [rows // 16 * i // 4 * 16 for i in range(5)]
    for top, end in zip(cuts, cuts[1:]):
        for c in range(comps):
            yield slice(top, end), slice(c * LANES, (c + 1) * LANES), c


def fold(x):
    return jnp.sum(x.reshape(x.shape[0] // 8, 8, x.shape[1]), axis=0)


def total(parts):
    return jnp.sum(parts, axis=0, keepdims=True)


def solve_kernel(scale, first, cap, earlier, khi, klo, hist, weight, strain, cstack, pdir, place,
                 *refs):
    earlier_updated, refs = refs[:earlier], refs[earlier:]
    updated, stress, blocks = refs[0], refs[1], refs[2:-5]
    field, resid, image, solved, split = refs[-5:]
    rows = hist.shape[0]
    comps = pdir.shape[0]
    zero = jnp.zeros((8, LANES), jnp.float32)
    s = strain[...]
    s_hi = s.astype(jnp.bfloat16).astype(jnp.float32)
    s3 = jnp.concatenate([s_hi, s - s_hi, s_hi, jnp.zeros_like(s)], axis=0).astype(jnp.bfloat16)
    wide = comps * LANES
    split[rows:, :] = jnp.zeros((split.shape[0] - rows, 2 * wide), jnp.bfloat16)
    for c in range(comps):
        image[:, c * LANES:(c + 1) * LANES] = dot(cstack[c].astype(jnp.bfloat16), s3, TN)
    parts = zero
    for r, l, c in sweep(rows, comps):
        d = image[r, l] - weight[r, :] * hist[r, :] * pdir[c, r, :]
        resid[r, l] = d
        field[r, l] = d
        split[r, l], split[r, wide + c * LANES:wide + (c + 1) * LANES] = halves(d)
        parts = parts + fold(d * d)
    norm = total(parts)
    for step in range(ITERS):
        both = dot(khi[...], split[...])
        image[...] = both[:, 0:wide] + both[:, wide:] + dot(klo[...], split[:, 0:wide])
        parts = zero
        for r, l, c in sweep(rows, comps):
            d = field[r, l]
            q = image[r, l] + (1.5 - weight[r, :]) * d
            image[r, l] = q
            parts = parts + fold(d * q)
        alpha = norm / jnp.maximum(total(parts), 1.0)
        if step == ITERS - 1:
            break
        parts = zero
        for r, l, c in sweep(rows, comps):
            gain = alpha * field[r, l]
            solved[r, l] = gain if step == 0 else solved[r, l] + gain
            left = resid[r, l] - alpha * image[r, l]
            resid[r, l] = left
            parts = parts + fold(left * left)
        following = total(parts)
        beta = following / jnp.maximum(norm, 1.0)
        norm = following
        for r, l, c in sweep(rows, comps):
            d = resid[r, l] + beta * field[r, l]
            field[r, l] = d
            split[r, l], split[r, wide + c * LANES:wide + (c + 1) * LANES] = halves(d)
    for r, l, c in sweep(rows, comps):
        x = solved[r, l] + alpha * field[r, l]
        flow = pdir[c, r, :] * x
        image[r, 0:LANES] = flow if c == 0 else image[r, 0:LANES] + flow
        split[r, l], split[r, wide + c * LANES:wide + (c + 1) * LANES] = halves((1.5 - weight[r, :]) * x)
    updated[...] = hist[...] + weight[...] * image[:, 0:LANES]
    place_blocks(first, cap, place, [*earlier_updated, updated], blocks)
    out = s
    for c in range(comps):
        l = slice(c * LANES, (c + 1) * LANES)
        cpl = cstack[c].astype(jnp.bfloat16)
        main = dot(cpl, split[0:rows, l])
        minor = dot(cpl, split[0:rows, wide + c * LANES:wide + (c + 1) * LANES])
        out = out + scale * (main[0:8] + main[16:24] + minor[0:8])
    stress[...] = out


def place_blocks(first, cap, place, sources, blocks):
    nodes = blocks[0].shape[1]
    count = cap * len(blocks)
    width = LANES * len(sources)
    placing = hot(place[0:1, 0:width] - first, count)
    sums = 0.0
    for i, source in enumerate(sources):
        hi, lo = halves(source[...])
        cut = placing[:, i * LANES:(i + 1) * LANES]
        sums = sums + (dot(cut, hi, NT) + dot(cut, lo, NT))
    for i, block in enumerate(blocks):
        block[...] = sums[i * cap:(i + 1) * cap, 0:nodes]


def ship_kernel(first, cap, chunks, place, *refs):
    place_blocks(first, cap, place, refs[:chunks], refs[chunks:])


def land_kernel(devices, cap, *refs):
    blocks, out, stage = refs[:devices], refs[-2], refs[-1]
    nodes = out.shape[0]
    me = lax.axis_index("macro") * lax.axis_size("pool") + lax.axis_index("pool")
    group = LANES // cap
    for q in range(devices // group):
        for i in range(group):
            at = pl.multiple_of(((me % group) ^ i) * cap, cap)
            stage[pl.ds(at, cap), 0:nodes] = blocks[q * group + i][...]
        lanes = pl.multiple_of(((me // group) ^ q) * LANES, LANES)
        out[:, pl.ds(lanes, LANES)] = jnp.transpose(stage[...])[0:nodes, :]


def back_kernel(at, *refs):
    out = refs[-1]
    stress = jnp.concatenate([ref[...] for ref in refs[:-1]], axis=1)
    serves = hot(at[0:1, :], stress.shape[1])
    hi, lo = halves(stress)
    out[...] = (dot(hi, serves) + dot(lo, serves))[0:out.shape[0], :]


def params():
    return pltpu.CompilerParams(vmem_limit_bytes=56 * 2**20)


def shards(
    history, yield_flags, strain, qp_to_rve, new_owner, stiffness, pattern, coupling, plastic_dir
):
    devices = lax.axis_size(("macro", "pool"))
    nodes, columns = history.shape
    comps, voigt = coupling.shape[0], coupling.shape[1]
    per_peer = 2 * columns // devices
    rows = up(nodes, 32)
    deep = up(nodes, 256)
    f32, bf16, i32 = jnp.float32, jnp.bfloat16, jnp.int32
    vmem = pl.BlockSpec(memory_space=pltpu.VMEM)
    smem = pl.BlockSpec(memory_space=pltpu.SMEM)
    khi, klo, hist_s, weight_s, strain_s, place_s, qp_s, cstack, pdir = pl.pallas_call(
        functools.partial(prep_kernel, devices, per_peer),
        out_shape=(
            jax.ShapeDtypeStruct((rows, deep), bf16),
            jax.ShapeDtypeStruct((rows, deep), bf16),
            jax.ShapeDtypeStruct((rows, columns), f32),
            jax.ShapeDtypeStruct((rows, columns), f32),
            jax.ShapeDtypeStruct((8, columns), f32),
            jax.ShapeDtypeStruct((8, columns), i32),
            jax.ShapeDtypeStruct((8, columns), i32),
            jax.ShapeDtypeStruct((comps, 32, rows), f32),
            jax.ShapeDtypeStruct((comps, rows, LANES), f32),
        ),
        in_specs=[vmem] * 6 + [smem] + [vmem] * 2,
        out_specs=[vmem] * 9,
        scratch_shapes=[pltpu.VMEM((rows, deep), f32), pltpu.VMEM((8, columns), f32)],
        compiler_params=params(),
    )(new_owner.reshape(1, columns), qp_to_rve, history, yield_flags, strain, stiffness, pattern,
      coupling, plastic_dir)

    chunks = columns // LANES
    group = LANES // per_peer
    wide = comps * LANES
    block = jax.ShapeDtypeStruct((per_peer, nodes), f32)
    whole = lambda shape: pl.BlockSpec(shape, lambda i: (0,) * len(shape))
    updated, stress_s, blocks = [], [], []
    for k in range(chunks):
        part = lambda height: pl.BlockSpec((height, LANES), lambda i, k=k: (0, k))
        done = pl.pallas_call(
            functools.partial(
                solve_kernel, 1.0 / math.sqrt(comps * nodes), k * LANES, per_peer, k
            ),
            grid=(1,),
            out_shape=(
                jax.ShapeDtypeStruct((rows, LANES), f32),
                jax.ShapeDtypeStruct((8, LANES), f32),
            ) + (block,) * group,
            in_specs=[whole((rows, deep)), whole((rows, deep)), part(rows), part(rows), part(8),
                      whole((comps, 32, rows)), whole((comps, rows, LANES)), whole((8, columns))]
            + [whole((rows, LANES))] * k,
            out_specs=[whole((rows, LANES)), whole((8, LANES))]
            + [whole((per_peer, nodes))] * group,
            scratch_shapes=[pltpu.VMEM((rows, wide), f32) for _ in range(4)]
            + [pltpu.VMEM((deep, 2 * wide), bf16)],
            compiler_params=params(),
            cost_estimate=pl.CostEstimate(
                flops=18 * rows * deep * wide, bytes_accessed=8 * 2**20, transcendentals=0
            ),
        )(khi, klo, hist_s, weight_s, strain_s, cstack, pdir, place_s, *updated)
        updated.append(done[0])
        stress_s.append(done[1])
        blocks.extend(done[2:])
    rest = devices - len(blocks)
    blocks.extend(pl.pallas_call(
        functools.partial(ship_kernel, chunks * LANES, per_peer, chunks),
        out_shape=(block,) * rest,
        in_specs=[vmem] * (1 + chunks),
        out_specs=[vmem] * rest,
        compiler_params=params(),
        cost_estimate=pl.CostEstimate(
            flops=4 * rows * columns * columns, bytes_accessed=4 * 2**20, transcendentals=0
        ),
    )(place_s, *updated))
    arrived = [None] * devices
    for place, sent in enumerate(blocks):
        mask = place ^ (devices // 2)
        pairs = [(s, s ^ mask) for s in range(devices)]
        arrived[mask] = lax.ppermute(sent, ("macro", "pool"), pairs) if mask else sent
    new_history = pl.pallas_call(
        functools.partial(land_kernel, devices, per_peer),
        out_shape=jax.ShapeDtypeStruct((nodes, devices * per_peer), f32),
        in_specs=[vmem] * devices,
        out_specs=vmem,
        scratch_shapes=[pltpu.VMEM((LANES, deep), f32)],
        compiler_params=params(),
    )(*arrived)
    stress_out = pl.pallas_call(
        back_kernel,
        out_shape=jax.ShapeDtypeStruct((voigt, columns), f32),
        in_specs=[vmem] * (1 + chunks),
        out_specs=vmem,
        compiler_params=params(),
    )(qp_s, *stress_s)
    return (new_history, stress_out)


def solution(mesh):
    return jax.shard_map(
        shards,
        mesh=mesh,
        in_specs=(
            P(None, ("macro", "pool")),
            P(None, ("macro", "pool")),
            P(None, ("macro", "pool")),
            P(("macro", "pool"), None),
            P(("macro", "pool"), None),
            P(),
            P(),
            P(),
            P(),
        ),
        out_specs=(P(None, ("macro", "pool")), P(None, ("macro", "pool"))),
        check_vma=False,
    )
```

```python
import functools
import math

import jax
import jax.numpy as jnp
from jax import lax
from jax.experimental import pallas as pl
from jax.experimental.pallas import tpu as pltpu
from jax.sharding import PartitionSpec as P

ITERS = 3
LANES = 128
PLANES = 4

NN = (((1,), (0,)), ((), ()))
NT = (((1,), (1,)), ((), ()))
TN = (((0,), (0,)), ((), ()))


def up(value, unit):
    return -(-value // unit) * unit


def dot(a, b, dims=NN):
    return lax.dot_general(a, b, dims, preferred_element_type=jnp.float32)


def halves(x):
    hi = x.astype(jnp.bfloat16)
    lo = (x - hi.astype(jnp.float32)).astype(jnp.bfloat16)
    return hi, lo


def whereabouts(devices):
    me = lax.axis_index("macro") * lax.axis_size("pool") + lax.axis_index("pool")
    lanes = devices // PLANES
    return me, me // lanes, me % lanes, lanes


def hot(row, count):
    rows = lax.broadcasted_iota(jnp.int32, (count, row.shape[1]), 0)
    return jnp.where(rows == row, 1.0, 0.0).astype(jnp.bfloat16)


def prep_kernel(devices, per_peer, owner, qp, hist, flag, strain, stiff, pattern, coupling, plastic,
                khi, klo, hist_s, weight_s, strain_s, place_s, qp_s, cstack, pdir, kfull, pad):
    nodes, columns = hist.shape
    rows = hist_s.shape[0]
    nb, blk = stiff.shape[0], stiff.shape[2]
    comps, voigt = coupling.shape[0], coupling.shape[1]

    kfull[...] = jnp.zeros_like(kfull)
    for a in range(nb):
        for b in range(nb):
            kfull[a * blk:(a + 1) * blk, b * blk:(b + 1) * blk] = (
                stiff[a, b] * pattern[a, b].astype(jnp.float32)
            )
    k = kfull[...]
    kh = k.astype(jnp.bfloat16)
    khi[...] = kh
    klo[...] = (k - kh.astype(jnp.float32)).astype(jnp.bfloat16)

    me, plane, lane, lanes = whereabouts(devices)
    half = lanes // 2
    apart = owner[...] // lanes ^ plane
    target = owner[...] % lanes
    across = (target ^ lane) % lanes // half
    there = across * half + jnp.where(across == 0, target % half, (target ^ lane) % half)
    turn = jnp.where(apart == 2, 0, jnp.where(apart == 3, 1, jnp.where(apart == 1, 2, 3)))
    key = turn * lanes + jnp.where(apart == 3, there, target)
    key_ids = lax.broadcasted_iota(jnp.int32, (devices, columns), 0)
    mine = jnp.where(key_ids == key, 1.0, 0.0)
    earlier = jnp.where(
        lax.broadcasted_iota(jnp.int32, (columns, columns), 0)
        < lax.broadcasted_iota(jnp.int32, (columns, columns), 1), 1.0, 0.0
    ).astype(jnp.bfloat16)
    before = dot(mine.astype(jnp.bfloat16), earlier)
    rank = jnp.sum(before * mine, axis=0, keepdims=True)
    tally = jnp.sum(mine, axis=1, keepdims=True)
    ahead = jnp.where(key_ids < key, tally, 0.0)
    position = (rank + jnp.sum(ahead, axis=0, keepdims=True)).astype(jnp.int32)

    order = hot(position, columns)
    for source, target in ((hist, hist_s),):
        hi, lo = halves(source[...])
        target[...] = jnp.zeros_like(target)
        target[0:nodes, :] = dot(hi, order, NT) + dot(lo, order, NT)
    h = hist_s[...]
    weight_s[...] = jnp.zeros_like(weight_s)
    weight_s[0:nodes, :] = dot(flag[...].astype(jnp.float32).astype(jnp.bfloat16), order, NT)
    weight_s[...] = weight_s[...] * h * h / (1.0 + h * h)

    pad[...] = jnp.zeros_like(pad)
    pad[0:1, :] = key.astype(jnp.float32)
    pad[1:2, :] = rank
    placed = dot(pad[...].astype(jnp.bfloat16), order, NT)
    place_s[...] = jnp.broadcast_to(
        (placed[0:1, :] * per_peer + placed[1:2, :]).astype(jnp.int32), place_s.shape
    )

    pad[0:1, :] = (position // 256).astype(jnp.float32)
    pad[1:2, :] = (position % 256).astype(jnp.float32)
    found = dot(pad[...].astype(jnp.bfloat16), hot(qp[...], columns))
    at = (found[0:1, :] * 256.0 + found[1:2, :]).astype(jnp.int32)
    qp_s[...] = jnp.broadcast_to(at, qp_s.shape)
    pad[...] = jnp.zeros_like(pad)
    pad[0:voigt, :] = strain[...]
    hi, lo = halves(pad[...])
    serves = hot(at, columns)
    strain_s[...] = dot(hi, serves, NT) + dot(lo, serves, NT)

    cstack[...] = jnp.zeros_like(cstack)
    for c in range(comps):
        cpl = coupling[c]
        hi = cpl.astype(jnp.bfloat16).astype(jnp.float32)
        cstack[c, 0:voigt, 0:nodes] = hi
        cstack[c, 8:8 + voigt, 0:nodes] = hi
        cstack[c, 16:16 + voigt, 0:nodes] = cpl - hi
    pdir[...] = jnp.zeros_like(pdir)
    for c in range(comps):
        spread = jnp.broadcast_to(plastic[c:c + 1, :], (LANES, nodes))
        pdir[c, 0:nodes, :] = jnp.transpose(spread)


def sweep(rows, comps):
    cuts = [rows // 16 * i // 4 * 16 for i in range(5)]
    for top, end in zip(cuts, cuts[1:]):
        for c in range(comps):
            yield slice(top, end), slice(c * LANES, (c + 1) * LANES), c


def fold(x):
    return jnp.sum(x.reshape(x.shape[0] // 8, 8, x.shape[1]), axis=0)


def total(parts):
    return jnp.sum(parts, axis=0, keepdims=True)


def solve_kernel(scale, first, earlier, khi, klo, hist, weight, strain, cstack, pdir, place,
                 *refs):
    earlier_updated, refs = refs[:earlier], refs[earlier:]
    updated, stress, blocks = refs[0], refs[1], refs[2:-5]
    field, resid, image, solved, split = refs[-5:]
    rows = hist.shape[0]
    comps = pdir.shape[0]
    zero = jnp.zeros((8, LANES), jnp.float32)
    s = strain[...]
    s_hi = s.astype(jnp.bfloat16).astype(jnp.float32)
    s3 = jnp.concatenate([s_hi, s - s_hi, s_hi, jnp.zeros_like(s)], axis=0).astype(jnp.bfloat16)
    wide = comps * LANES
    split[rows:, :] = jnp.zeros((split.shape[0] - rows, 2 * wide), jnp.bfloat16)
    for c in range(comps):
        image[:, c * LANES:(c + 1) * LANES] = dot(cstack[c].astype(jnp.bfloat16), s3, TN)
    parts = zero
    for r, l, c in sweep(rows, comps):
        d = image[r, l] - weight[r, :] * hist[r, :] * pdir[c, r, :]
        resid[r, l] = d
        field[r, l] = d
        split[r, l], split[r, wide + c * LANES:wide + (c + 1) * LANES] = halves(d)
        parts = parts + fold(d * d)
    norm = total(parts)
    for step in range(ITERS):
        both = dot(khi[...], split[...])
        image[...] = both[:, 0:wide] + both[:, wide:] + dot(klo[...], split[:, 0:wide])
        parts = zero
        for r, l, c in sweep(rows, comps):
            d = field[r, l]
            q = image[r, l] + (1.5 - weight[r, :]) * d
            image[r, l] = q
            parts = parts + fold(d * q)
        alpha = norm / jnp.maximum(total(parts), 1.0)
        if step == ITERS - 1:
            break
        parts = zero
        for r, l, c in sweep(rows, comps):
            gain = alpha * field[r, l]
            solved[r, l] = gain if step == 0 else solved[r, l] + gain
            left = resid[r, l] - alpha * image[r, l]
            resid[r, l] = left
            parts = parts + fold(left * left)
        following = total(parts)
        beta = following / jnp.maximum(norm, 1.0)
        norm = following
        for r, l, c in sweep(rows, comps):
            d = resid[r, l] + beta * field[r, l]
            field[r, l] = d
            split[r, l], split[r, wide + c * LANES:wide + (c + 1) * LANES] = halves(d)
    for r, l, c in sweep(rows, comps):
        x = solved[r, l] + alpha * field[r, l]
        flow = pdir[c, r, :] * x
        image[r, 0:LANES] = flow if c == 0 else image[r, 0:LANES] + flow
        split[r, l], split[r, wide + c * LANES:wide + (c + 1) * LANES] = halves((1.5 - weight[r, :]) * x)
    updated[...] = hist[...] + weight[...] * image[:, 0:LANES]
    place_blocks(first, place, [*earlier_updated, updated], blocks)
    out = s
    for c in range(comps):
        l = slice(c * LANES, (c + 1) * LANES)
        cpl = cstack[c].astype(jnp.bfloat16)
        main = dot(cpl, split[0:rows, l])
        minor = dot(cpl, split[0:rows, wide + c * LANES:wide + (c + 1) * LANES])
        out = out + scale * (main[0:8] + main[16:24] + minor[0:8])
    stress[...] = out


def place_blocks(first, place, sources, blocks):
    rows = sources[0].shape[0]
    count = sum(block.shape[0] for block in blocks)
    width = LANES * len(sources)
    placing = hot(place[0:1, 0:width] - first, count)
    sums = 0.0
    for i, source in enumerate(sources):
        hi, lo = halves(source[...])
        cut = placing[:, i * LANES:(i + 1) * LANES]
        sums = sums + (dot(cut, hi, NT) + dot(cut, lo, NT))
    top = 0
    for block in blocks:
        block[:, 0:rows] = sums[top:top + block.shape[0], :]
        block[:, rows:] = jnp.zeros((block.shape[0], block.shape[1] - rows), jnp.float32)
        top += block.shape[0]


def ship_kernel(first, chunks, place, *refs):
    place_blocks(first, place, refs[:chunks], refs[chunks:])


def land_kernel(devices, cap, two, near, one, own, *refs):
    direct, out, stage = refs[:-2], refs[-2], refs[-1]
    nodes = out.shape[0]
    me, plane, lane, lanes = whereabouts(devices)
    half = lanes // 2
    span = half * cap

    def land(tile, at):
        columns = pl.multiple_of(at * span, LANES)
        out[:, pl.ds(columns, span)] = jnp.transpose(tile)[0:nodes, :]

    for arrived, apart in ((own, 0), (two, 2), (one, 1)):
        for part in range(2):
            land(arrived[part * span:(part + 1) * span, :], (plane ^ apart) * 2 + part)
    side = lane // half
    land(near[...], (plane ^ 3) * 2 + side)
    for i, block in enumerate(direct):
        at = pl.multiple_of(((lane % half) ^ i) * cap, cap)
        stage[pl.ds(at, cap), :] = block[...]
    columns = pl.multiple_of(((plane ^ 3) * 2 + 1 - side) * span, LANES)
    out[:, pl.ds(columns, span)] = jnp.transpose(stage[...])[0:nodes, :]


def back_kernel(at, *refs):
    out = refs[-1]
    stress = jnp.concatenate([ref[...] for ref in refs[:-1]], axis=1)
    serves = hot(at[0:1, :], stress.shape[1])
    hi, lo = halves(stress)
    out[...] = (dot(hi, serves) + dot(lo, serves))[0:out.shape[0], :]


def params():
    return pltpu.CompilerParams(vmem_limit_bytes=56 * 2**20)


def shards(
    history, yield_flags, strain, qp_to_rve, new_owner, stiffness, pattern, coupling, plastic_dir
):
    devices = lax.axis_size(("macro", "pool"))
    nodes, columns = history.shape
    comps, voigt = coupling.shape[0], coupling.shape[1]
    per_peer = 2 * columns // devices
    rows = up(nodes, 32)
    deep = up(nodes, 256)
    f32, bf16, i32 = jnp.float32, jnp.bfloat16, jnp.int32
    vmem = pl.BlockSpec(memory_space=pltpu.VMEM)
    smem = pl.BlockSpec(memory_space=pltpu.SMEM)
    khi, klo, hist_s, weight_s, strain_s, place_s, qp_s, cstack, pdir = pl.pallas_call(
        functools.partial(prep_kernel, devices, per_peer),
        out_shape=(
            jax.ShapeDtypeStruct((rows, deep), bf16),
            jax.ShapeDtypeStruct((rows, deep), bf16),
            jax.ShapeDtypeStruct((rows, columns), f32),
            jax.ShapeDtypeStruct((rows, columns), f32),
            jax.ShapeDtypeStruct((8, columns), f32),
            jax.ShapeDtypeStruct((8, columns), i32),
            jax.ShapeDtypeStruct((8, columns), i32),
            jax.ShapeDtypeStruct((comps, 32, rows), f32),
            jax.ShapeDtypeStruct((comps, rows, LANES), f32),
        ),
        in_specs=[vmem] * 6 + [smem] + [vmem] * 2,
        out_specs=[vmem] * 9,
        scratch_shapes=[pltpu.VMEM((rows, deep), f32), pltpu.VMEM((8, columns), f32)],
        compiler_params=params(),
    )(new_owner.reshape(1, columns), qp_to_rve, history, yield_flags, strain, stiffness, pattern,
      coupling, plastic_dir)

    chunks = columns // LANES
    lanes = devices // PLANES
    half = lanes // 2
    wide = comps * LANES
    block = lambda height: jax.ShapeDtypeStruct((height, deep), f32)
    whole = lambda shape: pl.BlockSpec(shape, lambda i: (0,) * len(shape))
    updated, stress_s, ready = [], [], []
    for k in range(chunks):
        part = lambda height: pl.BlockSpec((height, LANES), lambda i, k=k: (0, k))
        outs = [block(half * per_peer)] if k < 3 else [block(per_peer)] * half
        done = pl.pallas_call(
            functools.partial(solve_kernel, 1.0 / math.sqrt(comps * nodes), k * LANES, k),
            grid=(1,),
            out_shape=(
                jax.ShapeDtypeStruct((rows, LANES), f32),
                jax.ShapeDtypeStruct((8, LANES), f32),
                *outs,
            ),
            in_specs=[whole((rows, deep)), whole((rows, deep)), part(rows), part(rows), part(8),
                      whole((comps, 32, rows)), whole((comps, rows, LANES)), whole((8, columns))]
            + [whole((rows, LANES))] * k,
            out_specs=[whole((rows, LANES)), whole((8, LANES))] + [whole(o.shape) for o in outs],
            scratch_shapes=[pltpu.VMEM((rows, wide), f32) for _ in range(4)]
            + [pltpu.VMEM((deep, 2 * wide), bf16)],
            compiler_params=params(),
            cost_estimate=pl.CostEstimate(
                flops=18 * rows * deep * wide, bytes_accessed=8 * 2**20, transcendentals=0
            ),
        )(khi, klo, hist_s, weight_s, strain_s, cstack, pdir, place_s, *updated)
        updated.append(done[0])
        stress_s.append(done[1])
        ready.append(done[2:])
    last = pl.pallas_call(
        functools.partial(ship_kernel, chunks * LANES, chunks),
        out_shape=(block(lanes * per_peer),) * 2,
        in_specs=[vmem] * (1 + chunks),
        out_specs=[vmem] * 2,
        compiler_params=params(),
        cost_estimate=pl.CostEstimate(
            flops=4 * rows * columns * columns, bytes_accessed=4 * 2**20, transcendentals=0
        ),
    )(place_s, *updated)

    axes = ("macro", "pool")

    def hop(sent, mask):
        return lax.ppermute(sent, axes, [(s, s ^ mask) for s in range(devices)])

    def spread(sent, size):
        groups = [list(range(first, first + size)) for first in range(0, devices, size)]
        shape = sent.shape
        return lax.all_to_all(
            sent.reshape(size, per_peer, deep), axes, split_axis=0, concat_axis=0,
            axis_index_groups=groups, tiled=True,
        ).reshape(shape)

    two_a, two_b = hop(ready[0][0], 2 * lanes), hop(ready[1][0], 2 * lanes)
    near = hop(ready[2][0], 3 * lanes)
    direct = [hop(sent, 3 * lanes + half + i) for i, sent in enumerate(ready[3])]
    one = hop(last[0], lanes)
    two_a, two_b, own = lax.optimization_barrier((two_a, two_b, last[1]))
    own = spread(own, lanes)
    two = spread(jnp.concatenate([two_a, two_b], axis=0), lanes)
    near, two, own = lax.optimization_barrier((near, two, own))
    near = spread(near, half)
    one = spread(one, lanes)
    new_history = pl.pallas_call(
        functools.partial(land_kernel, devices, per_peer),
        out_shape=jax.ShapeDtypeStruct((nodes, devices * per_peer), f32),
        in_specs=[vmem] * (4 + half),
        out_specs=vmem,
        scratch_shapes=[pltpu.VMEM((LANES, deep), f32)],
        compiler_params=params(),
    )(two, near, one, own, *direct)
    stress_out = pl.pallas_call(
        back_kernel,
        out_shape=jax.ShapeDtypeStruct((voigt, columns), f32),
        in_specs=[vmem] * (1 + chunks),
        out_specs=vmem,
        compiler_params=params(),
    )(qp_s, *stress_s)
    return (new_history, stress_out)


def solution(mesh):
    return jax.shard_map(
        shards,
        mesh=mesh,
        in_specs=(
            P(None, ("macro", "pool")),
            P(None, ("macro", "pool")),
            P(None, ("macro", "pool")),
            P(("macro", "pool"), None),
            P(("macro", "pool"), None),
            P(),
            P(),
            P(),
            P(),
        ),
        out_specs=(P(None, ("macro", "pool")), P(None, ("macro", "pool"))),
        check_vma=False,
    )
```

```python
import functools
import math

import jax
import jax.numpy as jnp
from jax import lax
from jax.experimental import pallas as pl
from jax.experimental.pallas import tpu as pltpu
from jax.sharding import PartitionSpec as P

ITERS = 3
LANES = 128
PLANES = 4

NN = (((1,), (0,)), ((), ()))
NT = (((1,), (1,)), ((), ()))
TN = (((0,), (0,)), ((), ()))


def up(value, unit):
    return -(-value // unit) * unit


def dot(a, b, dims=NN):
    return lax.dot_general(a, b, dims, preferred_element_type=jnp.float32)


def halves(x):
    hi = x.astype(jnp.bfloat16)
    lo = (x - hi.astype(jnp.float32)).astype(jnp.bfloat16)
    return hi, lo


def whereabouts(devices):
    me = lax.axis_index("macro") * lax.axis_size("pool") + lax.axis_index("pool")
    lanes = devices // PLANES
    return me, me // lanes, me % lanes, lanes


def hot(row, count):
    rows = lax.broadcasted_iota(jnp.int32, (count, row.shape[1]), 0)
    return jnp.where(rows == row, 1.0, 0.0).astype(jnp.bfloat16)


def prep_kernel(devices, per_peer, owner, qp, hist, flag, strain, stiff, pattern, coupling, plastic,
                khi, klo, hist_s, weight_s, strain_s, place_s, qp_s, cstack, pdir, kfull, pad):
    nodes, columns = hist.shape
    rows = hist_s.shape[0]
    nb, blk = stiff.shape[0], stiff.shape[2]
    comps, voigt = coupling.shape[0], coupling.shape[1]

    kfull[...] = jnp.zeros_like(kfull)
    for a in range(nb):
        for b in range(nb):
            kfull[a * blk:(a + 1) * blk, b * blk:(b + 1) * blk] = (
                stiff[a, b] * pattern[a, b].astype(jnp.float32)
            )
    k = kfull[...]
    kh = k.astype(jnp.bfloat16)
    khi[...] = kh
    klo[...] = (k - kh.astype(jnp.float32)).astype(jnp.bfloat16)

    me, plane, lane, lanes = whereabouts(devices)
    half = lanes // 2
    apart = owner[...] // lanes ^ plane
    target = owner[...] % lanes
    across = (target ^ lane) % lanes // half
    there = across * half + target % half
    turn = jnp.where(apart == 2, 0, jnp.where(apart == 1, 1, jnp.where(apart == 3, 2, 3)))
    key = turn * lanes + jnp.where(apart == 3, there, target)
    key_ids = lax.broadcasted_iota(jnp.int32, (devices, columns), 0)
    mine = jnp.where(key_ids == key, 1.0, 0.0)
    earlier = jnp.where(
        lax.broadcasted_iota(jnp.int32, (columns, columns), 0)
        < lax.broadcasted_iota(jnp.int32, (columns, columns), 1), 1.0, 0.0
    ).astype(jnp.bfloat16)
    before = dot(mine.astype(jnp.bfloat16), earlier)
    rank = jnp.sum(before * mine, axis=0, keepdims=True)
    tally = jnp.sum(mine, axis=1, keepdims=True)
    ahead = jnp.where(key_ids < key, tally, 0.0)
    position = (rank + jnp.sum(ahead, axis=0, keepdims=True)).astype(jnp.int32)

    order = hot(position, columns)
    for source, target in ((hist, hist_s),):
        hi, lo = halves(source[...])
        target[...] = jnp.zeros_like(target)
        target[0:nodes, :] = dot(hi, order, NT) + dot(lo, order, NT)
    h = hist_s[...]
    weight_s[...] = jnp.zeros_like(weight_s)
    weight_s[0:nodes, :] = dot(flag[...].astype(jnp.float32).astype(jnp.bfloat16), order, NT)
    weight_s[...] = weight_s[...] * h * h / (1.0 + h * h)

    pad[...] = jnp.zeros_like(pad)
    pad[0:1, :] = key.astype(jnp.float32)
    pad[1:2, :] = rank
    placed = dot(pad[...].astype(jnp.bfloat16), order, NT)
    place_s[...] = jnp.broadcast_to(
        (placed[0:1, :] * per_peer + placed[1:2, :]).astype(jnp.int32), place_s.shape
    )

    pad[0:1, :] = (position // 256).astype(jnp.float32)
    pad[1:2, :] = (position % 256).astype(jnp.float32)
    found = dot(pad[...].astype(jnp.bfloat16), hot(qp[...], columns))
    at = (found[0:1, :] * 256.0 + found[1:2, :]).astype(jnp.int32)
    qp_s[...] = jnp.broadcast_to(at, qp_s.shape)
    pad[...] = jnp.zeros_like(pad)
    pad[0:voigt, :] = strain[...]
    hi, lo = halves(pad[...])
    serves = hot(at, columns)
    strain_s[...] = dot(hi, serves, NT) + dot(lo, serves, NT)

    cstack[...] = jnp.zeros_like(cstack)
    for c in range(comps):
        cpl = coupling[c]
        hi = cpl.astype(jnp.bfloat16).astype(jnp.float32)
        cstack[c, 0:voigt, 0:nodes] = hi
        cstack[c, 8:8 + voigt, 0:nodes] = hi
        cstack[c, 16:16 + voigt, 0:nodes] = cpl - hi
    pdir[...] = jnp.zeros_like(pdir)
    for c in range(comps):
        spread = jnp.broadcast_to(plastic[c:c + 1, :], (LANES, nodes))
        pdir[c, 0:nodes, :] = jnp.transpose(spread)


def sweep(rows, comps):
    cuts = [rows // 16 * i // 4 * 16 for i in range(5)]
    for top, end in zip(cuts, cuts[1:]):
        for c in range(comps):
            yield slice(top, end), slice(c * LANES, (c + 1) * LANES), c


def fold(x):
    return jnp.sum(x.reshape(x.shape[0] // 8, 8, x.shape[1]), axis=0)


def total(parts):
    return jnp.sum(parts, axis=0, keepdims=True)


def solve_kernel(scale, first, earlier, khi, klo, hist, weight, strain, cstack, pdir, place,
                 *refs):
    earlier_updated, refs = refs[:earlier], refs[earlier:]
    updated, stress, blocks = refs[0], refs[1], refs[2:-5]
    field, resid, image, solved, split = refs[-5:]
    rows = hist.shape[0]
    comps = pdir.shape[0]
    zero = jnp.zeros((8, LANES), jnp.float32)
    s = strain[...]
    s_hi = s.astype(jnp.bfloat16).astype(jnp.float32)
    s3 = jnp.concatenate([s_hi, s - s_hi, s_hi, jnp.zeros_like(s)], axis=0).astype(jnp.bfloat16)
    wide = comps * LANES
    split[rows:, :] = jnp.zeros((split.shape[0] - rows, 2 * wide), jnp.bfloat16)
    for c in range(comps):
        image[:, c * LANES:(c + 1) * LANES] = dot(cstack[c].astype(jnp.bfloat16), s3, TN)
    parts = zero
    for r, l, c in sweep(rows, comps):
        d = image[r, l] - weight[r, :] * hist[r, :] * pdir[c, r, :]
        resid[r, l] = d
        field[r, l] = d
        split[r, l], split[r, wide + c * LANES:wide + (c + 1) * LANES] = halves(d)
        parts = parts + fold(d * d)
    norm = total(parts)
    for step in range(ITERS):
        both = dot(khi[...], split[...])
        image[...] = both[:, 0:wide] + both[:, wide:] + dot(klo[...], split[:, 0:wide])
        parts = zero
        for r, l, c in sweep(rows, comps):
            d = field[r, l]
            q = image[r, l] + (1.5 - weight[r, :]) * d
            image[r, l] = q
            parts = parts + fold(d * q)
        alpha = norm / jnp.maximum(total(parts), 1.0)
        if step == ITERS - 1:
            break
        parts = zero
        for r, l, c in sweep(rows, comps):
            gain = alpha * field[r, l]
            solved[r, l] = gain if step == 0 else solved[r, l] + gain
            left = resid[r, l] - alpha * image[r, l]
            resid[r, l] = left
            parts = parts + fold(left * left)
        following = total(parts)
        beta = following / jnp.maximum(norm, 1.0)
        norm = following
        for r, l, c in sweep(rows, comps):
            d = resid[r, l] + beta * field[r, l]
            field[r, l] = d
            split[r, l], split[r, wide + c * LANES:wide + (c + 1) * LANES] = halves(d)
    for r, l, c in sweep(rows, comps):
        x = solved[r, l] + alpha * field[r, l]
        flow = pdir[c, r, :] * x
        image[r, 0:LANES] = flow if c == 0 else image[r, 0:LANES] + flow
        split[r, l], split[r, wide + c * LANES:wide + (c + 1) * LANES] = halves((1.5 - weight[r, :]) * x)
    updated[...] = hist[...] + weight[...] * image[:, 0:LANES]
    place_blocks(first, place, [*earlier_updated, updated], blocks)
    out = s
    for c in range(comps):
        l = slice(c * LANES, (c + 1) * LANES)
        cpl = cstack[c].astype(jnp.bfloat16)
        main = dot(cpl, split[0:rows, l])
        minor = dot(cpl, split[0:rows, wide + c * LANES:wide + (c + 1) * LANES])
        out = out + scale * (main[0:8] + main[16:24] + minor[0:8])
    stress[...] = out


def place_blocks(first, place, sources, blocks):
    rows = sources[0].shape[0]
    count = sum(block.shape[0] for block in blocks)
    width = LANES * len(sources)
    placing = hot(place[0:1, 0:width] - first, count)
    sums = 0.0
    for i, source in enumerate(sources):
        hi, lo = halves(source[...])
        cut = placing[:, i * LANES:(i + 1) * LANES]
        sums = sums + (dot(cut, hi, NT) + dot(cut, lo, NT))
    top = 0
    for block in blocks:
        block[:, 0:rows] = sums[top:top + block.shape[0], :]
        block[:, rows:] = jnp.zeros((block.shape[0], block.shape[1] - rows), jnp.float32)
        top += block.shape[0]


def ship_kernel(first, chunks, place, *refs):
    place_blocks(first, place, refs[:chunks], refs[chunks:])


def land(tile, out, stage, sem, slot, at):
    nodes = out.shape[0]
    stage[slot] = jnp.transpose(tile)[0:nodes, :]
    columns = pl.multiple_of(at * LANES, LANES)
    copy = pltpu.make_async_copy(stage.at[slot], out.at[:, pl.ds(columns, LANES)], sem.at[slot])
    copy.start()
    return copy


def land_kernel(devices, two, one, own, out, stage, sem):
    me, plane, lane, lanes = whereabouts(devices)
    copies = []
    for arrived, apart in ((own, 0), (two, 2), (one, 1)):
        for part in range(arrived.shape[0] // LANES):
            at = (plane ^ apart) * (arrived.shape[0] // LANES) + part
            tile = arrived[part * LANES:(part + 1) * LANES, :]
            copies.append(land(tile, out, stage, sem, len(copies), at))
    for copy in copies:
        copy.wait()


def last_kernel(devices, near, far, history, out, stage, sem):
    me, plane, lane, lanes = whereabouts(devices)
    side = lane // (lanes // 2)
    first = land(near[...], out, stage, sem, 0, (plane ^ 3) * 2 + side)
    second = land(far[...], out, stage, sem, 1, (plane ^ 3) * 2 + 1 - side)
    first.wait()
    second.wait()


def back_kernel(at, *refs):
    out = refs[-1]
    stress = jnp.concatenate([ref[...] for ref in refs[:-1]], axis=1)
    serves = hot(at[0:1, :], stress.shape[1])
    hi, lo = halves(stress)
    out[...] = (dot(hi, serves) + dot(lo, serves))[0:out.shape[0], :]


def params(mib=24):
    return pltpu.CompilerParams(vmem_limit_bytes=mib * 2**20)


def shards(
    history, yield_flags, strain, qp_to_rve, new_owner, stiffness, pattern, coupling, plastic_dir
):
    devices = lax.axis_size(("macro", "pool"))
    nodes, columns = history.shape
    comps, voigt = coupling.shape[0], coupling.shape[1]
    per_peer = 2 * columns // devices
    rows = up(nodes, 32)
    deep = up(nodes, 256)
    f32, bf16, i32 = jnp.float32, jnp.bfloat16, jnp.int32
    vmem = pl.BlockSpec(memory_space=pltpu.VMEM)
    smem = pl.BlockSpec(memory_space=pltpu.SMEM)
    khi, klo, hist_s, weight_s, strain_s, place_s, qp_s, cstack, pdir = pl.pallas_call(
        functools.partial(prep_kernel, devices, per_peer),
        out_shape=(
            jax.ShapeDtypeStruct((rows, deep), bf16),
            jax.ShapeDtypeStruct((rows, deep), bf16),
            jax.ShapeDtypeStruct((rows, columns), f32),
            jax.ShapeDtypeStruct((rows, columns), f32),
            jax.ShapeDtypeStruct((8, columns), f32),
            jax.ShapeDtypeStruct((8, columns), i32),
            jax.ShapeDtypeStruct((8, columns), i32),
            jax.ShapeDtypeStruct((comps, 32, rows), f32),
            jax.ShapeDtypeStruct((comps, rows, LANES), f32),
        ),
        in_specs=[vmem] * 6 + [smem] + [vmem] * 2,
        out_specs=[vmem] * 9,
        scratch_shapes=[pltpu.VMEM((rows, deep), f32), pltpu.VMEM((8, columns), f32)],
        compiler_params=params(40),
    )(new_owner.reshape(1, columns), qp_to_rve, history, yield_flags, strain, stiffness, pattern,
      coupling, plastic_dir)

    chunks = columns // LANES
    small = pl.CostEstimate(flops=2**10, bytes_accessed=2**10, transcendentals=0)
    lanes = devices // PLANES
    half = lanes // 2
    wide = comps * LANES
    block = lambda height: jax.ShapeDtypeStruct((height, deep), f32)
    whole = lambda shape: pl.BlockSpec(shape, lambda i: (0,) * len(shape))
    updated, stress_s, ready = [], [], []
    for k in range(chunks):
        part = lambda height: pl.BlockSpec((height, LANES), lambda i, k=k: (0, k))
        outs = [block(LANES)]
        if k == chunks - 1:
            outs = [block(LANES)] * 3
        done = pl.pallas_call(
            functools.partial(solve_kernel, 1.0 / math.sqrt(comps * nodes), k * LANES, k),
            grid=(1,),
            out_shape=(
                jax.ShapeDtypeStruct((rows, LANES), f32),
                jax.ShapeDtypeStruct((8, LANES), f32),
                *outs,
            ),
            in_specs=[whole((rows, deep)), whole((rows, deep)), part(rows), part(rows), part(8),
                      whole((comps, 32, rows)), whole((comps, rows, LANES)), whole((8, columns))]
            + [whole((rows, LANES))] * k,
            out_specs=[whole((rows, LANES)), whole((8, LANES))] + [whole(o.shape) for o in outs],
            scratch_shapes=[pltpu.VMEM((rows, wide), f32) for _ in range(4)]
            + [pltpu.VMEM((deep, 2 * wide), bf16)],
            compiler_params=params(),
            cost_estimate=small,
        )(khi, klo, hist_s, weight_s, strain_s, cstack, pdir, place_s, *updated)
        updated.append(done[0])
        stress_s.append(done[1])
        ready.append(done[2:])
    own_sent = pl.pallas_call(
        functools.partial(ship_kernel, 6 * LANES, chunks),
        out_shape=block(2 * LANES),
        in_specs=[vmem] * (1 + chunks),
        out_specs=vmem,
        compiler_params=params(),
        cost_estimate=small,
    )(place_s, *updated)

    axes = ("macro", "pool")

    def hop(sent, mask):
        return lax.ppermute(sent, axes, [(s, s ^ mask) for s in range(devices)])

    def spread(sent, size):
        groups = [list(range(first, first + size)) for first in range(0, devices, size)]
        shape = sent.shape
        return lax.all_to_all(
            sent.reshape(size, per_peer, deep), axes, split_axis=0, concat_axis=0,
            axis_index_groups=groups, tiled=True,
        ).reshape(shape)

    two_a, two_b = hop(ready[0][0], 2 * lanes), hop(ready[1][0], 2 * lanes)
    one_a, one_b = hop(ready[2][0], lanes), hop(ready[3][0], lanes)
    near = hop(ready[3][1], 3 * lanes)
    far = hop(ready[3][2], 3 * lanes + half)
    two_a, two_b, _ = lax.optimization_barrier((two_a, two_b, updated[3]))
    two = spread(jnp.concatenate([two_a, two_b], axis=0), lanes)
    own = spread(own_sent, lanes)
    one_a, one_b, near, _ = lax.optimization_barrier((one_a, one_b, near, own_sent))
    one = spread(jnp.concatenate([one_a, one_b], axis=0), lanes)
    near = spread(near, half)
    far, _, _ = lax.optimization_barrier((far, near, one))
    far = spread(far, half)
    hbm = pl.BlockSpec(memory_space=pl.ANY)
    history_shape = jax.ShapeDtypeStruct((nodes, devices * per_peer), f32)
    new_history = pl.pallas_call(
        functools.partial(land_kernel, devices),
        out_shape=history_shape,
        in_specs=[vmem] * 3,
        out_specs=hbm,
        scratch_shapes=[pltpu.VMEM((6, nodes, LANES), f32), pltpu.SemaphoreType.DMA((6,))],
        compiler_params=params(),
        cost_estimate=small,
    )(two, one, own)
    new_history = pl.pallas_call(
        functools.partial(last_kernel, devices),
        out_shape=history_shape,
        in_specs=[vmem, vmem, hbm],
        out_specs=hbm,
        scratch_shapes=[pltpu.VMEM((2, nodes, LANES), f32), pltpu.SemaphoreType.DMA((2,))],
        input_output_aliases={2: 0},
        compiler_params=params(),
        cost_estimate=small,
    )(near, far, new_history)
    stress_out = pl.pallas_call(
        back_kernel,
        out_shape=jax.ShapeDtypeStruct((voigt, columns), f32),
        in_specs=[vmem] * (1 + chunks),
        out_specs=vmem,
        compiler_params=params(),
    )(qp_s, *stress_s)
    return (new_history, stress_out)


def solution(mesh):
    return jax.shard_map(
        shards,
        mesh=mesh,
        in_specs=(
            P(None, ("macro", "pool")),
            P(None, ("macro", "pool")),
            P(None, ("macro", "pool")),
            P(("macro", "pool"), None),
            P(("macro", "pool"), None),
            P(),
            P(),
            P(),
            P(),
        ),
        out_specs=(P(None, ("macro", "pool")), P(None, ("macro", "pool"))),
        check_vma=False,
    )
```

```python
import functools
import math

import jax
import jax.numpy as jnp
from jax import lax
from jax.experimental import pallas as pl
from jax.experimental.pallas import tpu as pltpu
from jax.sharding import PartitionSpec as P

ITERS = 3
LANES = 128
PLANES = 4

NN = (((1,), (0,)), ((), ()))
NT = (((1,), (1,)), ((), ()))
TN = (((0,), (0,)), ((), ()))


def up(value, unit):
    return -(-value // unit) * unit


def dot(a, b, dims=NN):
    return lax.dot_general(a, b, dims, preferred_element_type=jnp.float32)


def halves(x):
    hi = x.astype(jnp.bfloat16)
    lo = (x - hi.astype(jnp.float32)).astype(jnp.bfloat16)
    return hi, lo


def whereabouts(devices):
    me = lax.axis_index("macro") * lax.axis_size("pool") + lax.axis_index("pool")
    lanes = devices // PLANES
    return me, me // lanes, me % lanes, lanes


def hot(row, count):
    rows = lax.broadcasted_iota(jnp.int32, (count, row.shape[1]), 0)
    return jnp.where(rows == row, 1.0, 0.0).astype(jnp.bfloat16)


def prep_kernel(devices, per_peer, *refs):
    sources, outs, (kfull, pad), local, sem = refs[:9], refs[9:18], refs[18:20], refs[20:29], refs[29]
    khi, klo, hist_s, weight_s, strain_s, place_s, qp_s, cstack, pdir = outs
    owner, qp, strain, stiff, pattern, hist, flag, coupling, plastic = local
    copies = [
        pltpu.make_async_copy(source, target, sem.at[i])
        for i, (source, target) in enumerate(zip(sources, local))
    ]
    for copy in copies:
        copy.start()
    nodes, columns = hist.shape
    nb, blk = stiff.shape[0], stiff.shape[2]
    comps, voigt = coupling.shape[0], coupling.shape[1]

    me, plane, lane, lanes = whereabouts(devices)
    for copy in copies[:3]:
        copy.wait()
    apart = owner[...] // lanes ^ plane
    target = owner[...] % lanes
    turn = jnp.where(apart == 2, 0, jnp.where(apart == 3, 1, jnp.where(apart == 1, 2, 3)))
    key = turn * lanes + jnp.where(apart >= 2, target, target ^ lane)
    key_ids = lax.broadcasted_iota(jnp.int32, (devices, columns), 0)
    mine = jnp.where(key_ids == key, 1.0, 0.0)
    earlier = jnp.where(
        lax.broadcasted_iota(jnp.int32, (columns, columns), 0)
        < lax.broadcasted_iota(jnp.int32, (columns, columns), 1), 1.0, 0.0
    ).astype(jnp.bfloat16)
    before = dot(mine.astype(jnp.bfloat16), earlier)
    rank = jnp.sum(before * mine, axis=0, keepdims=True)
    tally = jnp.sum(mine, axis=1, keepdims=True)
    ahead = jnp.where(key_ids < key, tally, 0.0)
    position = (rank + jnp.sum(ahead, axis=0, keepdims=True)).astype(jnp.int32)

    order = hot(position, columns)
    pad[...] = jnp.zeros_like(pad)
    pad[0:1, :] = key.astype(jnp.float32)
    pad[1:2, :] = rank
    placed = dot(pad[...].astype(jnp.bfloat16), order, NT)
    place_s[...] = jnp.broadcast_to(
        (placed[0:1, :] * per_peer + placed[1:2, :]).astype(jnp.int32), place_s.shape
    )

    pad[0:1, :] = (position // 256).astype(jnp.float32)
    pad[1:2, :] = (position % 256).astype(jnp.float32)
    found = dot(pad[...].astype(jnp.bfloat16), hot(qp[...], columns))
    at = (found[0:1, :] * 256.0 + found[1:2, :]).astype(jnp.int32)
    qp_s[...] = jnp.broadcast_to(at, qp_s.shape)
    pad[...] = jnp.zeros_like(pad)
    pad[0:voigt, :] = strain[...]
    hi, lo = halves(pad[...])
    serves = hot(at, columns)
    strain_s[...] = dot(hi, serves, NT) + dot(lo, serves, NT)

    kfull[...] = jnp.zeros_like(kfull)
    copies[3].wait()
    copies[4].wait()
    for a in range(nb):
        for b in range(nb):
            kfull[a * blk:(a + 1) * blk, b * blk:(b + 1) * blk] = (
                stiff[a, b] * pattern[a, b].astype(jnp.float32)
            )
    k = kfull[...]
    kh = k.astype(jnp.bfloat16)
    khi[...] = kh
    klo[...] = (k - kh.astype(jnp.float32)).astype(jnp.bfloat16)

    copies[5].wait()
    copies[6].wait()
    hi, lo = halves(hist[...])
    hist_s[...] = jnp.zeros_like(hist_s)
    hist_s[0:nodes, :] = dot(hi, order, NT) + dot(lo, order, NT)
    h = hist_s[...]
    weight_s[...] = jnp.zeros_like(weight_s)
    weight_s[0:nodes, :] = dot(flag[...].astype(jnp.float32).astype(jnp.bfloat16), order, NT)
    weight_s[...] = weight_s[...] * h * h / (1.0 + h * h)

    copies[7].wait()
    copies[8].wait()
    cstack[...] = jnp.zeros_like(cstack)
    for c in range(comps):
        cpl = coupling[c]
        hi = cpl.astype(jnp.bfloat16).astype(jnp.float32)
        cstack[c, 0:voigt, 0:nodes] = hi
        cstack[c, 8:8 + voigt, 0:nodes] = hi
        cstack[c, 16:16 + voigt, 0:nodes] = cpl - hi
    pdir[...] = jnp.zeros_like(pdir)
    for c in range(comps):
        spread = jnp.broadcast_to(plastic[c:c + 1, :], (LANES, nodes))
        pdir[c, 0:nodes, :] = jnp.transpose(spread)


def sweep(rows, comps, span):
    pieces = 4 * span // LANES
    cuts = [rows // 16 * i // pieces * 16 for i in range(pieces + 1)]
    for top, end in zip(cuts, cuts[1:]):
        for c in range(comps):
            yield slice(top, end), slice(c * span, (c + 1) * span), c


def fold(x):
    return jnp.sum(x.reshape(x.shape[0] // 8, 8, x.shape[1]), axis=0)


def total(parts):
    return jnp.sum(parts, axis=0, keepdims=True)


def solve_kernel(scale, first, earlier, khi, klo, hist, weight, strain, cstack, pdir, place, *refs):
    earlier_updated, refs = refs[:earlier], refs[earlier:]
    updated, stress, blocks = refs[0], refs[1], refs[2:-5]
    field, resid, image, solved, split = refs[-5:]
    rows, span = hist.shape
    comps = pdir.shape[0]
    wide = comps * span
    zero = jnp.zeros((8, span), jnp.float32)

    def flow(c, r):
        return jnp.concatenate([pdir[c, r, :]] * (span // LANES), axis=1)

    def keep(r, c, x):
        split[r, c * span:(c + 1) * span], split[r, wide + c * span:wide + (c + 1) * span] = (
            halves(x)
        )

    s = strain[...]
    s_hi = s.astype(jnp.bfloat16).astype(jnp.float32)
    s3 = jnp.concatenate([s_hi, s - s_hi, s_hi, jnp.zeros_like(s)], axis=0).astype(jnp.bfloat16)
    split[rows:, :] = jnp.zeros((split.shape[0] - rows, 2 * wide), jnp.bfloat16)
    for c in range(comps):
        image[:, c * span:(c + 1) * span] = dot(cstack[c].astype(jnp.bfloat16), s3, TN)
    parts = zero
    for r, l, c in sweep(rows, comps, span):
        d = image[r, l] - weight[r, :] * hist[r, :] * flow(c, r)
        resid[r, l] = d
        field[r, l] = d
        keep(r, c, d)
        parts = parts + fold(d * d)
    norm = total(parts)
    for step in range(ITERS):
        both = dot(khi[...], split[...])
        image[...] = both[:, 0:wide] + both[:, wide:] + dot(klo[...], split[:, 0:wide])
        parts = zero
        for r, l, c in sweep(rows, comps, span):
            d = field[r, l]
            q = image[r, l] + (1.5 - weight[r, :]) * d
            image[r, l] = q
            parts = parts + fold(d * q)
        alpha = norm / jnp.maximum(total(parts), 1.0)
        if step == ITERS - 1:
            break
        parts = zero
        for r, l, c in sweep(rows, comps, span):
            gain = alpha * field[r, l]
            solved[r, l] = gain if step == 0 else solved[r, l] + gain
            left = resid[r, l] - alpha * image[r, l]
            resid[r, l] = left
            parts = parts + fold(left * left)
        following = total(parts)
        beta = following / jnp.maximum(norm, 1.0)
        norm = following
        for r, l, c in sweep(rows, comps, span):
            d = resid[r, l] + beta * field[r, l]
            field[r, l] = d
            keep(r, c, d)
    for r, l, c in sweep(rows, comps, span):
        x = solved[r, l] + alpha * field[r, l]
        pushed = flow(c, r) * x
        image[r, 0:span] = pushed if c == 0 else image[r, 0:span] + pushed
        keep(r, c, (1.5 - weight[r, :]) * x)
    updated[...] = hist[...] + weight[...] * image[:, 0:span]
    if blocks:
        place_blocks(first, place, [*earlier_updated, updated], blocks)
    out = s
    for c in range(comps):
        cpl = cstack[c].astype(jnp.bfloat16)
        main = dot(cpl, split[0:rows, c * span:(c + 1) * span])
        minor = dot(cpl, split[0:rows, wide + c * span:wide + (c + 1) * span])
        out = out + scale * (main[0:8] + main[16:24] + minor[0:8])
    stress[...] = out


def place_blocks(first, place, sources, blocks):
    rows = sources[0].shape[0]
    count = sum(block.shape[0] for block in blocks)
    width = sum(source.shape[1] for source in sources)
    placing = hot(place[0:1, 0:width] - first, count)
    sums, left = 0.0, 0
    for source in sources:
        hi, lo = halves(source[...])
        cut = placing[:, left:left + source.shape[1]]
        sums = sums + (dot(cut, hi, NT) + dot(cut, lo, NT))
        left += source.shape[1]
    top = 0
    for block in blocks:
        block[:, 0:rows] = sums[top:top + block.shape[0], :]
        block[:, rows:] = jnp.zeros((block.shape[0], block.shape[1] - rows), jnp.float32)
        top += block.shape[0]


def ship_kernel(first, chunks, place, *refs):
    place_blocks(first, place, refs[:chunks], refs[chunks:])


def land(tile, out, stage, sem, slot, at):
    nodes = out.shape[0]
    stage[slot] = jnp.transpose(tile)[0:nodes, :]
    columns = pl.multiple_of(at * LANES, LANES)
    copy = pltpu.make_async_copy(stage.at[slot], out.at[:, pl.ds(columns, LANES)], sem.at[slot])
    copy.start()
    return copy


def land_group(block, count, plane, out, stage, sem, slot):
    height = block.shape[0] // count
    copies = []
    for part in range(count):
        tile = block[part * height:(part + 1) * height, :]
        copies.append(land(tile, out, stage, sem, slot + part, plane * count + part))
    return copies


def land_kernel(devices, cap, *refs):
    blocks, (out, stage, sem, gather) = refs[:-4], refs[-4:]
    me, plane, lane, lanes = whereabouts(devices)
    copies = []
    for apart in range(2):
        for i in range(lanes):
            at = pl.multiple_of((lane ^ i) * cap, cap)
            gather[apart, pl.ds(at, cap), :] = blocks[apart * lanes + i][...]
        copies += land_group(gather.at[apart], 2, plane ^ apart, out, stage, sem, 2 * apart)
    for copy in copies:
        copy.wait()


def last_kernel(devices, pair, history, out, stage, sem):
    me, plane, lane, lanes = whereabouts(devices)
    group = pair.shape[0] // 2
    copies = []
    for part in range(2):
        mine = (plane // 2) == part
        source = jnp.where(mine, plane ^ 2, plane ^ 3)
        block = pair.at[part * group:(part + 1) * group, :]
        copies += land_group(block, 2, source, out, stage, sem, 2 * part)
    for copy in copies:
        copy.wait()


def back_kernel(at, *refs):
    out = refs[-1]
    stress = jnp.concatenate([ref[...] for ref in refs[:-1]], axis=1)
    serves = hot(at[0:1, :], stress.shape[1])
    hi, lo = halves(stress)
    out[...] = (dot(hi, serves) + dot(lo, serves))[0:out.shape[0], :]


def params(mib=24):
    return pltpu.CompilerParams(vmem_limit_bytes=mib * 2**20)


def shards(
    history, yield_flags, strain, qp_to_rve, new_owner, stiffness, pattern, coupling, plastic_dir
):
    devices = lax.axis_size(("macro", "pool"))
    nodes, columns = history.shape
    comps, voigt = coupling.shape[0], coupling.shape[1]
    per_peer = 2 * columns // devices
    rows = up(nodes, 32)
    deep = up(nodes, 256)
    f32, bf16, i32 = jnp.float32, jnp.bfloat16, jnp.int32
    vmem = pl.BlockSpec(memory_space=pltpu.VMEM)
    inputs = (new_owner.reshape(1, columns), qp_to_rve, strain, stiffness, pattern, history,
              yield_flags, coupling, plastic_dir)
    khi, klo, hist_s, weight_s, strain_s, place_s, qp_s, cstack, pdir = pl.pallas_call(
        functools.partial(prep_kernel, devices, per_peer),
        out_shape=(
            jax.ShapeDtypeStruct((rows, deep), bf16),
            jax.ShapeDtypeStruct((rows, deep), bf16),
            jax.ShapeDtypeStruct((rows, columns), f32),
            jax.ShapeDtypeStruct((rows, columns), f32),
            jax.ShapeDtypeStruct((8, columns), f32),
            jax.ShapeDtypeStruct((8, columns), i32),
            jax.ShapeDtypeStruct((8, columns), i32),
            jax.ShapeDtypeStruct((comps, 32, rows), f32),
            jax.ShapeDtypeStruct((comps, rows, LANES), f32),
        ),
        in_specs=[pl.BlockSpec(memory_space=pltpu.HBM)] * 9,
        out_specs=[vmem] * 9,
        scratch_shapes=[pltpu.VMEM((rows, deep), f32), pltpu.VMEM((8, columns), f32)]
        + [(pltpu.SMEM if x is pattern else pltpu.VMEM)(x.shape, x.dtype) for x in inputs]
        + [pltpu.SemaphoreType.DMA((9,))],
        compiler_params=params(46),
    )(*inputs)

    lanes = devices // PLANES
    group = lanes * per_peer
    block = lambda height: jax.ShapeDtypeStruct((height, deep), f32)
    whole = lambda shape: pl.BlockSpec(shape, lambda i: (0,) * len(shape))
    updated, stress_s, ready = [], [], []
    left = 0
    for span in (LANES, LANES, columns - 2 * LANES):
        part = lambda height: pl.BlockSpec((height, span), lambda i, at=left // span: (0, at))
        wide = comps * span
        outs = [block(LANES)] if len(updated) < 2 else []
        done = pl.pallas_call(
            functools.partial(solve_kernel, 1.0 / math.sqrt(comps * nodes), left, len(updated)),
            grid=(1,),
            out_shape=(
                jax.ShapeDtypeStruct((rows, span), f32),
                jax.ShapeDtypeStruct((8, span), f32),
                *outs,
            ),
            in_specs=[whole((rows, deep)), whole((rows, deep)), part(rows), part(rows), part(8),
                      whole((comps, 32, rows)), whole((comps, rows, LANES)), whole((8, columns))]
            + [whole(u.shape) for u in updated],
            out_specs=[whole((rows, span)), whole((8, span))] + [whole(o.shape) for o in outs],
            scratch_shapes=[pltpu.VMEM((rows, wide), f32) for _ in range(4)]
            + [pltpu.VMEM((deep, 2 * wide), bf16)],
            compiler_params=params(28),
            cost_estimate=pl.CostEstimate(
                flops=2 * rows * deep * wide, bytes_accessed=2**20, transcendentals=0
            ),
        )(khi, klo, hist_s, weight_s, strain_s, cstack, pdir, place_s, *updated)
        updated.append(done[0])
        stress_s.append(done[1])
        ready.extend(done[2:])
        left += span
    three, *singles = pl.pallas_call(
        functools.partial(ship_kernel, group, len(updated)),
        out_shape=(block(group),) + (block(per_peer),) * (2 * lanes),
        in_specs=[vmem] * (1 + len(updated)),
        out_specs=[vmem] * (1 + 2 * lanes),
        compiler_params=params(28),
        cost_estimate=pl.CostEstimate(
            flops=2**20, bytes_accessed=2**20, transcendentals=0
        ),
    )(place_s, *updated)

    axes = ("macro", "pool")

    def hop(sent, mask):
        if mask == 0:
            return sent
        return lax.ppermute(sent, axes, [(s, s ^ mask) for s in range(devices)])

    two = jnp.concatenate([hop(sent, 2 * lanes) for sent in ready], axis=0)
    two, three, *singles = lax.optimization_barrier((two, three, *singles))
    lower = lax.axis_index(axes) < devices // 2
    pair = jnp.concatenate(
        [jnp.where(lower, two, three), jnp.where(lower, three, two)], axis=0
    ).reshape(2 * lanes, per_peer, deep)
    planes = [list(range(z * lanes, (z + 1) * lanes)) for z in range(PLANES)]
    pair = lax.all_to_all(
        pair, axes, split_axis=0, concat_axis=0, tiled=True,
        axis_index_groups=[planes[0] + planes[3], planes[1] + planes[2]],
    ).reshape(2 * group, deep)
    one = [hop(sent, lanes + i) for i, sent in enumerate(singles[:lanes])]
    own = [hop(sent, i) for i, sent in enumerate(singles[lanes:])]
    hbm = pl.BlockSpec(memory_space=pl.ANY)
    history_shape = jax.ShapeDtypeStruct((nodes, devices * per_peer), f32)
    staging = [pltpu.VMEM((4, nodes, LANES), f32), pltpu.SemaphoreType.DMA((4,))]
    new_history = pl.pallas_call(
        functools.partial(land_kernel, devices, per_peer),
        out_shape=history_shape,
        in_specs=[vmem] * (2 * lanes),
        out_specs=hbm,
        scratch_shapes=staging + [pltpu.VMEM((2, group, deep), f32)],
        compiler_params=params(),
    )(*own, *one)
    new_history = pl.pallas_call(
        functools.partial(last_kernel, devices),
        out_shape=history_shape,
        in_specs=[vmem, hbm],
        out_specs=hbm,
        scratch_shapes=staging,
        input_output_aliases={1: 0},
        compiler_params=params(),
    )(pair, new_history)
    stress_out = pl.pallas_call(
        back_kernel,
        out_shape=jax.ShapeDtypeStruct((voigt, columns), f32),
        in_specs=[vmem] * (1 + len(stress_s)),
        out_specs=vmem,
        compiler_params=params(),
    )(qp_s, *stress_s)
    return (new_history, stress_out)


def solution(mesh):
    return jax.shard_map(
        shards,
        mesh=mesh,
        in_specs=(
            P(None, ("macro", "pool")),
            P(None, ("macro", "pool")),
            P(None, ("macro", "pool")),
            P(("macro", "pool"), None),
            P(("macro", "pool"), None),
            P(),
            P(),
            P(),
            P(),
        ),
        out_specs=(P(None, ("macro", "pool")), P(None, ("macro", "pool"))),
        check_vma=False,
    )
```

```python
import functools
import math

import jax
import jax.numpy as jnp
from jax import lax
from jax.experimental import pallas as pl
from jax.experimental.pallas import tpu as pltpu
from jax.sharding import PartitionSpec as P

ITERS = 3
LANES = 128
PLANES = 4

NN = (((1,), (0,)), ((), ()))
NT = (((1,), (1,)), ((), ()))
TN = (((0,), (0,)), ((), ()))


def up(value, unit):
    return -(-value // unit) * unit


def dot(a, b, dims=NN):
    return lax.dot_general(a, b, dims, preferred_element_type=jnp.float32)


def halves(x):
    hi = x.astype(jnp.bfloat16)
    lo = (x - hi.astype(jnp.float32)).astype(jnp.bfloat16)
    return hi, lo


def whereabouts(devices):
    me = lax.axis_index("macro") * lax.axis_size("pool") + lax.axis_index("pool")
    lanes = devices // PLANES
    return me, me // lanes, me % lanes, lanes


def hot(row, count):
    rows = lax.broadcasted_iota(jnp.int32, (count, row.shape[1]), 0)
    return jnp.where(rows == row, 1.0, 0.0).astype(jnp.bfloat16)


def pack_kernel(coupling, plastic, strain, owner, qp, pattern, small):
    top = 0
    for c in range(coupling.shape[0]):
        small[top:top + coupling.shape[1], :] = coupling[c]
        top += coupling.shape[1]
    for part in (plastic, strain, owner, qp):
        small[top:top + part.shape[0], 0:part.shape[1]] = part[...].astype(jnp.float32)
        top += part.shape[0]
    count = pattern.shape[0]
    for a in range(count):
        small[top:top + 1, a * count:(a + 1) * count] = pattern[a:a + 1, :].astype(jnp.float32)


def prep_kernel(devices, per_peer, comps, voigt, *refs):
    sources, outs, (kfull, pad), local, sem = refs[:4], refs[4:13], refs[13:15], refs[15:19], refs[19]
    khi, klo, hist_s, weight_s, strain_s, place_s, qp_s, cstack, pdir = outs
    small, stiff, hist, flag = local
    copies = [
        pltpu.make_async_copy(source, target, sem.at[i])
        for i, (source, target) in enumerate(zip(sources, local))
    ]
    for copy in copies:
        copy.start()
    nodes, columns = hist.shape
    nb, blk = stiff.shape[0], stiff.shape[2]
    at_plastic = comps * voigt
    at_strain = at_plastic + comps
    at_owner = at_strain + voigt
    copies[0].wait()

    me, plane, lane, lanes = whereabouts(devices)
    owner = small[at_owner:at_owner + 1, 0:columns].astype(jnp.int32)
    apart = owner // lanes ^ plane
    target = owner % lanes
    away = target ^ lane
    near = (away % 2) * lanes + jnp.where(apart == 1, 0, lanes // 2) + away // 2
    key = jnp.where(apart == 2, target, jnp.where(apart == 3, lanes + target, 2 * lanes + near))
    key_ids = lax.broadcasted_iota(jnp.int32, (devices, columns), 0)
    mine = jnp.where(key_ids == key, 1.0, 0.0)
    earlier = jnp.where(
        lax.broadcasted_iota(jnp.int32, (columns, columns), 0)
        < lax.broadcasted_iota(jnp.int32, (columns, columns), 1), 1.0, 0.0
    ).astype(jnp.bfloat16)
    before = dot(mine.astype(jnp.bfloat16), earlier)
    rank = jnp.sum(before * mine, axis=0, keepdims=True)
    tally = jnp.sum(mine, axis=1, keepdims=True)
    ahead = jnp.where(key_ids < key, tally, 0.0)
    position = (rank + jnp.sum(ahead, axis=0, keepdims=True)).astype(jnp.int32)

    order = hot(position, columns)
    pad[...] = jnp.zeros_like(pad)
    pad[0:1, :] = key.astype(jnp.float32)
    pad[1:2, :] = rank
    placed = dot(pad[...].astype(jnp.bfloat16), order, NT)
    place_s[...] = jnp.broadcast_to(
        (placed[0:1, :] * per_peer + placed[1:2, :]).astype(jnp.int32), place_s.shape
    )

    pad[0:1, :] = (position // 256).astype(jnp.float32)
    pad[1:2, :] = (position % 256).astype(jnp.float32)
    found = dot(pad[...].astype(jnp.bfloat16), hot(small[at_owner + 1:at_owner + 2, 0:columns].astype(jnp.int32), columns))
    at = (found[0:1, :] * 256.0 + found[1:2, :]).astype(jnp.int32)
    qp_s[...] = jnp.broadcast_to(at, qp_s.shape)
    pad[...] = jnp.zeros_like(pad)
    pad[0:voigt, :] = small[at_strain:at_owner, 0:columns]
    hi, lo = halves(pad[...])
    serves = hot(at, columns)
    strain_s[...] = dot(hi, serves, NT) + dot(lo, serves, NT)

    kfull[...] = jnp.zeros_like(kfull)
    copies[1].wait()
    for a in range(nb):
        for b in range(nb):
            kfull[a * blk:(a + 1) * blk, b * blk:(b + 1) * blk] = (
                stiff[a, b] * small[at_owner + 2:at_owner + 3, a * nb + b:a * nb + b + 1]
            )
    k = kfull[...]
    kh = k.astype(jnp.bfloat16)
    khi[...] = kh
    klo[...] = (k - kh.astype(jnp.float32)).astype(jnp.bfloat16)

    copies[2].wait()
    copies[3].wait()
    hi, lo = halves(hist[...])
    hist_s[...] = jnp.zeros_like(hist_s)
    hist_s[0:nodes, :] = dot(hi, order, NT) + dot(lo, order, NT)
    h = hist_s[...]
    weight_s[...] = jnp.zeros_like(weight_s)
    weight_s[0:nodes, :] = dot(flag[...].astype(jnp.float32).astype(jnp.bfloat16), order, NT)
    weight_s[...] = weight_s[...] * h * h / (1.0 + h * h)

    cstack[...] = jnp.zeros_like(cstack)
    for c in range(comps):
        cpl = small[c * voigt:(c + 1) * voigt, :]
        hi = cpl.astype(jnp.bfloat16).astype(jnp.float32)
        cstack[c, 0:voigt, 0:nodes] = hi
        cstack[c, 8:8 + voigt, 0:nodes] = hi
        cstack[c, 16:16 + voigt, 0:nodes] = cpl - hi
    pdir[...] = jnp.zeros_like(pdir)
    for c in range(comps):
        spread = jnp.broadcast_to(small[at_plastic + c:at_plastic + c + 1, :], (LANES, nodes))
        pdir[c, 0:nodes, :] = jnp.transpose(spread)


def sweep(rows, comps, span):
    pieces = 4 * span // LANES
    cuts = [rows // 16 * i // pieces * 16 for i in range(pieces + 1)]
    for top, end in zip(cuts, cuts[1:]):
        for c in range(comps):
            yield slice(top, end), slice(c * span, (c + 1) * span), c


def fold(x):
    return jnp.sum(x.reshape(x.shape[0] // 8, 8, x.shape[1]), axis=0)


def total(parts):
    return jnp.sum(parts, axis=0, keepdims=True)


def solve_kernel(scale, first, earlier, khi, klo, hist, weight, strain, cstack, pdir, place, *refs):
    earlier_updated, refs = refs[:earlier], refs[earlier:]
    updated, stress, blocks = refs[0], refs[1], refs[2:-5]
    field, resid, image, solved, split = refs[-5:]
    rows, span = hist.shape
    comps = pdir.shape[0]
    wide = comps * span
    zero = jnp.zeros((8, span), jnp.float32)

    def flow(c, r):
        return jnp.concatenate([pdir[c, r, :]] * (span // LANES), axis=1)

    def keep(r, c, x):
        split[r, c * span:(c + 1) * span], split[r, wide + c * span:wide + (c + 1) * span] = (
            halves(x)
        )

    s = strain[...]
    s_hi = s.astype(jnp.bfloat16).astype(jnp.float32)
    s3 = jnp.concatenate([s_hi, s - s_hi, s_hi, jnp.zeros_like(s)], axis=0).astype(jnp.bfloat16)
    split[rows:, :] = jnp.zeros((split.shape[0] - rows, 2 * wide), jnp.bfloat16)
    for c in range(comps):
        image[:, c * span:(c + 1) * span] = dot(cstack[c].astype(jnp.bfloat16), s3, TN)
    parts = zero
    for r, l, c in sweep(rows, comps, span):
        d = image[r, l] - weight[r, :] * hist[r, :] * flow(c, r)
        resid[r, l] = d
        field[r, l] = d
        keep(r, c, d)
        parts = parts + fold(d * d)
    norm = total(parts)
    for step in range(ITERS):
        both = dot(khi[...], split[...])
        image[...] = both[:, 0:wide] + both[:, wide:] + dot(klo[...], split[:, 0:wide])
        parts = zero
        for r, l, c in sweep(rows, comps, span):
            d = field[r, l]
            q = image[r, l] + (1.5 - weight[r, :]) * d
            image[r, l] = q
            parts = parts + fold(d * q)
        alpha = norm / jnp.maximum(total(parts), 1.0)
        if step == ITERS - 1:
            break
        parts = zero
        for r, l, c in sweep(rows, comps, span):
            gain = alpha * field[r, l]
            solved[r, l] = gain if step == 0 else solved[r, l] + gain
            left = resid[r, l] - alpha * image[r, l]
            resid[r, l] = left
            parts = parts + fold(left * left)
        following = total(parts)
        beta = following / jnp.maximum(norm, 1.0)
        norm = following
        for r, l, c in sweep(rows, comps, span):
            d = resid[r, l] + beta * field[r, l]
            field[r, l] = d
            keep(r, c, d)
    for r, l, c in sweep(rows, comps, span):
        x = solved[r, l] + alpha * field[r, l]
        pushed = flow(c, r) * x
        image[r, 0:span] = pushed if c == 0 else image[r, 0:span] + pushed
        keep(r, c, (1.5 - weight[r, :]) * x)
    updated[...] = hist[...] + weight[...] * image[:, 0:span]
    if blocks:
        place_blocks(first, place, [*earlier_updated, updated], blocks)
    out = s
    for c in range(comps):
        cpl = cstack[c].astype(jnp.bfloat16)
        main = dot(cpl, split[0:rows, c * span:(c + 1) * span])
        minor = dot(cpl, split[0:rows, wide + c * span:wide + (c + 1) * span])
        out = out + scale * (main[0:8] + main[16:24] + minor[0:8])
    stress[...] = out


def place_blocks(first, place, sources, blocks):
    rows = sources[0].shape[0]
    count = sum(block.shape[0] for block in blocks)
    width = sum(source.shape[1] for source in sources)
    placing = hot(place[0:1, 0:width] - first, count)
    sums, left = 0.0, 0
    for source in sources:
        hi, lo = halves(source[...])
        cut = placing[:, left:left + source.shape[1]]
        sums = sums + (dot(cut, hi, NT) + dot(cut, lo, NT))
        left += source.shape[1]
    top = 0
    for block in blocks:
        block[:, 0:rows] = sums[top:top + block.shape[0], :]
        block[:, rows:] = jnp.zeros((block.shape[0], block.shape[1] - rows), jnp.float32)
        top += block.shape[0]


def ship_kernel(first, chunks, place, at, *refs):
    updated, stress, blocks, out = refs[:chunks], refs[chunks:2 * chunks], refs[2 * chunks:-1], refs[-1]
    place_blocks(first, place, updated, blocks)
    hi, lo = halves(jnp.concatenate([ref[...] for ref in stress], axis=1))
    serves = hot(at[0:1, :], hi.shape[1])
    out[...] = (dot(hi, serves) + dot(lo, serves))[0:out.shape[0], :]


def pair_kernel(devices, two_a, two_b, three, pair):
    me, plane, lane, lanes = whereabouts(devices)
    group, part = three.shape[0], two_a.shape[0]
    mine = pl.multiple_of(plane // 2 * group, group)
    other = pl.multiple_of((1 - plane // 2) * group, group)
    pair[pl.ds(mine, part), :] = two_a[...]
    pair[pl.ds(mine + part, part), :] = two_b[...]
    pair[pl.ds(other, group), :] = three[...]


def join_kernel(cap, kept, swapped, *blocks):
    for i, block in enumerate(blocks):
        block[0:cap, :] = kept[i * cap:(i + 1) * cap, :]
        block[cap:, :] = swapped[i * cap:(i + 1) * cap, :]


def land(tile, out, stage, sem, slot, at):
    nodes = out.shape[0]
    stage[slot] = jnp.transpose(tile)[0:nodes, :]
    columns = pl.multiple_of(at * LANES, LANES)
    copy = pltpu.make_async_copy(stage.at[slot], out.at[:, pl.ds(columns, LANES)], sem.at[slot])
    copy.start()
    return copy


def land_group(block, count, plane, out, stage, sem, slot):
    height = block.shape[0] // count
    copies = []
    for part in range(count):
        tile = block[part * height:(part + 1) * height, :]
        copies.append(land(tile, out, stage, sem, slot + part, plane * count + part))
    return copies


def land_kernel(devices, cap, *refs):
    blocks, (out, stage, sem, gather) = refs[:-4], refs[-4:]
    me, plane, lane, lanes = whereabouts(devices)
    half = lanes // 2
    copies = []
    for i, apart in enumerate((1, 0)):
        for k in range(lanes):
            at = pl.multiple_of((lane ^ k) * cap, cap)
            block = blocks[i * half + k // 2]
            gather[i, pl.ds(at, cap), :] = block[k % 2 * cap:(k % 2 + 1) * cap, :]
        copies += land_group(gather.at[i], 2, plane ^ apart, out, stage, sem, 2 * i)
    for copy in copies:
        copy.wait()


def last_kernel(devices, pair, history, out, stage, sem):
    me, plane, lane, lanes = whereabouts(devices)
    group = pair.shape[0] // 2
    copies = []
    for part in range(2):
        mine = (plane // 2) == part
        source = jnp.where(mine, plane ^ 2, plane ^ 3)
        block = pair.at[part * group:(part + 1) * group, :]
        copies += land_group(block, 2, source, out, stage, sem, 2 * part)
    for copy in copies:
        copy.wait()


def params(mib=24):
    return pltpu.CompilerParams(vmem_limit_bytes=mib * 2**20)


def shards(
    history, yield_flags, strain, qp_to_rve, new_owner, stiffness, pattern, coupling, plastic_dir
):
    devices = lax.axis_size(("macro", "pool"))
    nodes, columns = history.shape
    comps, voigt = coupling.shape[0], coupling.shape[1]
    per_peer = 2 * columns // devices
    rows = up(nodes, 32)
    deep = up(nodes, 256)
    f32, bf16, i32 = jnp.float32, jnp.bfloat16, jnp.int32
    vmem = pl.BlockSpec(memory_space=pltpu.VMEM)
    small_inputs = (coupling, plastic_dir, strain, new_owner.reshape(1, columns), qp_to_rve, pattern)
    small = pl.pallas_call(
        pack_kernel,
        out_shape=jax.ShapeDtypeStruct((32, nodes), f32),
        in_specs=[vmem] * len(small_inputs),
        out_specs=vmem,
        compiler_params=params(60),
    )(*small_inputs)
    inputs = (small, stiffness, history, yield_flags)
    khi, klo, hist_s, weight_s, strain_s, place_s, qp_s, cstack, pdir = pl.pallas_call(
        functools.partial(prep_kernel, devices, per_peer, comps, voigt),
        out_shape=(
            jax.ShapeDtypeStruct((rows, deep), bf16),
            jax.ShapeDtypeStruct((rows, deep), bf16),
            jax.ShapeDtypeStruct((rows, columns), f32),
            jax.ShapeDtypeStruct((rows, columns), f32),
            jax.ShapeDtypeStruct((8, columns), f32),
            jax.ShapeDtypeStruct((8, columns), i32),
            jax.ShapeDtypeStruct((8, columns), i32),
            jax.ShapeDtypeStruct((comps, 32, rows), f32),
            jax.ShapeDtypeStruct((comps, rows, LANES), f32),
        ),
        in_specs=[pl.BlockSpec(memory_space=pltpu.HBM)] * 4,
        out_specs=[vmem] * 9,
        scratch_shapes=[pltpu.VMEM((rows, deep), f32), pltpu.VMEM((8, columns), f32)]
        + [pltpu.VMEM(x.shape, x.dtype) for x in inputs]
        + [pltpu.SemaphoreType.DMA((4,))],
        compiler_params=params(46),
    )(*inputs)

    lanes = devices // PLANES
    group = lanes * per_peer
    block = lambda height: jax.ShapeDtypeStruct((height, deep), f32)
    whole = lambda shape: pl.BlockSpec(shape, lambda i: (0,) * len(shape))
    updated, stress_s, ready = [], [], []
    left = 0
    for span in (LANES,) * (columns // LANES):
        part = lambda height: pl.BlockSpec((height, span), lambda i, at=left // span: (0, at))
        wide = comps * span
        outs = [block(LANES)] if len(updated) < 2 else []
        done = pl.pallas_call(
            functools.partial(solve_kernel, 1.0 / math.sqrt(comps * nodes), left, len(updated)),
            grid=(1,),
            out_shape=(
                jax.ShapeDtypeStruct((rows, span), f32),
                jax.ShapeDtypeStruct((8, span), f32),
                *outs,
            ),
            in_specs=[whole((rows, deep)), whole((rows, deep)), part(rows), part(rows), part(8),
                      whole((comps, 32, rows)), whole((comps, rows, LANES)), whole((8, columns))]
            + [whole(u.shape) for u in updated],
            out_specs=[whole((rows, span)), whole((8, span))] + [whole(o.shape) for o in outs],
            scratch_shapes=[pltpu.VMEM((rows, wide), f32) for _ in range(4)]
            + [pltpu.VMEM((deep, 2 * wide), bf16)],
            compiler_params=params(),
            cost_estimate=pl.CostEstimate(
                flops=18 * rows * deep * wide, bytes_accessed=2**20, transcendentals=0
            ),
        )(khi, klo, hist_s, weight_s, strain_s, cstack, pdir, place_s, *updated)
        updated.append(done[0])
        stress_s.append(done[1])
        ready.extend(done[2:])
        left += span
    three, kept, swapped, stress_out = pl.pallas_call(
        functools.partial(ship_kernel, group, len(updated)),
        out_shape=(block(group),) * 3 + (jax.ShapeDtypeStruct((voigt, columns), f32),),
        in_specs=[vmem] * (2 + 2 * len(updated)),
        out_specs=[vmem] * 4,
        compiler_params=params(),
        cost_estimate=pl.CostEstimate(
            flops=4 * rows * columns * columns, bytes_accessed=2**20, transcendentals=0
        ),
    )(place_s, qp_s, *updated, *stress_s)

    axes = ("macro", "pool")

    def hop(sent, mask):
        if mask == 0:
            return sent
        return lax.ppermute(sent, axes, [(s, s ^ mask) for s in range(devices)])

    two_a, two_b = [hop(sent, 2 * lanes) for sent in ready]
    two_a, two_b, three, swapped = lax.optimization_barrier((two_a, two_b, three, swapped))
    swapped = hop(swapped, 1)
    pair = pl.pallas_call(
        functools.partial(pair_kernel, devices),
        out_shape=block(2 * group),
        in_specs=[vmem] * 3,
        out_specs=vmem,
        compiler_params=params(),
    )(two_a, two_b, three).reshape(2 * lanes, per_peer, deep)
    pair, swapped = lax.optimization_barrier((pair, swapped))
    planes = [list(range(z * lanes, (z + 1) * lanes)) for z in range(PLANES)]
    pair = lax.all_to_all(
        pair, axes, split_axis=0, concat_axis=0, tiled=True,
        axis_index_groups=[planes[0] + planes[3], planes[1] + planes[2]],
    ).reshape(2 * group, deep)
    joined = pl.pallas_call(
        functools.partial(join_kernel, per_peer),
        out_shape=(block(2 * per_peer),) * lanes,
        in_specs=[vmem] * 2,
        out_specs=[vmem] * lanes,
        compiler_params=params(),
    )(kept, swapped)
    half = lanes // 2
    joined = [
        hop(sent, (lanes if i < half else 0) + i % half * 2) for i, sent in enumerate(joined)
    ]
    hbm = pl.BlockSpec(memory_space=pl.ANY)
    history_shape = jax.ShapeDtypeStruct((nodes, devices * per_peer), f32)
    staging = [pltpu.VMEM((4, nodes, LANES), f32), pltpu.SemaphoreType.DMA((4,))]
    new_history = pl.pallas_call(
        functools.partial(land_kernel, devices, per_peer),
        out_shape=history_shape,
        in_specs=[vmem] * lanes,
        out_specs=hbm,
        scratch_shapes=staging + [pltpu.VMEM((2, group, deep), f32)],
        compiler_params=params(),
    )(*joined)
    new_history = pl.pallas_call(
        functools.partial(last_kernel, devices),
        out_shape=history_shape,
        in_specs=[vmem, hbm],
        out_specs=hbm,
        scratch_shapes=staging,
        input_output_aliases={1: 0},
        compiler_params=params(),
    )(pair, new_history)
    return (new_history, stress_out)


def solution(mesh):
    return jax.shard_map(
        shards,
        mesh=mesh,
        in_specs=(
            P(None, ("macro", "pool")),
            P(None, ("macro", "pool")),
            P(None, ("macro", "pool")),
            P(("macro", "pool"), None),
            P(("macro", "pool"), None),
            P(),
            P(),
            P(),
            P(),
        ),
        out_specs=(P(None, ("macro", "pool")), P(None, ("macro", "pool"))),
        check_vma=False,
    )
```

```python
import functools
import math

import jax
import jax.numpy as jnp
from jax import lax
from jax.experimental import pallas as pl
from jax.experimental.pallas import tpu as pltpu
from jax.sharding import PartitionSpec as P

ITERS = 3
LANES = 128
PLANES = 4
PATTERN = 32

NN = (((1,), (0,)), ((), ()))
NT = (((1,), (1,)), ((), ()))
TN = (((0,), (0,)), ((), ()))


def up(value, unit):
    return -(-value // unit) * unit


def dot(a, b, dims=NN):
    return lax.dot_general(a, b, dims, preferred_element_type=jnp.float32)


def halves(x):
    hi = x.astype(jnp.bfloat16)
    lo = (x - hi.astype(jnp.float32)).astype(jnp.bfloat16)
    return hi, lo


def whereabouts(devices):
    me = lax.axis_index("macro") * lax.axis_size("pool") + lax.axis_index("pool")
    lanes = devices // PLANES
    return me, me // lanes, me % lanes, lanes


def hot(row, count):
    rows = lax.broadcasted_iota(jnp.int32, (count, row.shape[1]), 0)
    return jnp.where(rows == row, 1.0, 0.0).astype(jnp.bfloat16)


def pack_kernel(coupling, plastic, strain, owner, qp, pattern, small):
    top = 0
    for c in range(coupling.shape[0]):
        small[top:top + coupling.shape[1], :] = coupling[c]
        top += coupling.shape[1]
    for part in (plastic, strain, owner, qp):
        small[top:top + part.shape[0], 0:part.shape[1]] = part[...].astype(jnp.float32)
        top += part.shape[0]
    count = pattern.shape[0]
    for a in range(count):
        for b in range(count):
            couples = jnp.full((1, LANES), pattern[a, b].astype(jnp.float32))
            small[PATTERN + a * count + b:PATTERN + a * count + b + 1, 0:LANES] = couples


def prep_kernel(devices, per_peer, comps, voigt, *refs):
    sources, outs, (kfull, pad), local, sem = refs[:4], refs[4:13], refs[13:15], refs[15:19], refs[19]
    khi, klo, hist_s, weight_s, strain_s, place_s, qp_s, cstack, pdir = outs
    small, stiff, hist, flag = local
    copies = [
        pltpu.make_async_copy(source, target, sem.at[i])
        for i, (source, target) in enumerate(zip(sources, local))
    ]
    for copy in copies:
        copy.start()
    nodes, columns = hist.shape
    nb, blk = stiff.shape[0], stiff.shape[2]
    at_plastic = comps * voigt
    at_strain = at_plastic + comps
    at_owner = at_strain + voigt
    copies[0].wait()

    me, plane, lane, lanes = whereabouts(devices)
    owner = small[at_owner:at_owner + 1, 0:columns].astype(jnp.int32)
    apart = owner // lanes ^ plane
    target = owner % lanes
    away = target ^ lane
    shifted = away % 2 * (lanes // 2) + away // 2
    turn = jnp.where(apart == 2, 0, jnp.where(apart == 1, 1, jnp.where(apart == 3, 2, 3)))
    key = turn * lanes + jnp.where((apart == 2) | (apart == 1), shifted, target)
    key_ids = lax.broadcasted_iota(jnp.int32, (devices, columns), 0)
    mine = jnp.where(key_ids == key, 1.0, 0.0)
    earlier = jnp.where(
        lax.broadcasted_iota(jnp.int32, (columns, columns), 0)
        < lax.broadcasted_iota(jnp.int32, (columns, columns), 1), 1.0, 0.0
    ).astype(jnp.bfloat16)
    before = dot(mine.astype(jnp.bfloat16), earlier)
    rank = jnp.sum(before * mine, axis=0, keepdims=True)
    tally = jnp.sum(mine, axis=1, keepdims=True)
    ahead = jnp.where(key_ids < key, tally, 0.0)
    position = (rank + jnp.sum(ahead, axis=0, keepdims=True)).astype(jnp.int32)

    order = hot(position, columns)
    pad[...] = jnp.zeros_like(pad)
    pad[0:1, :] = key.astype(jnp.float32)
    pad[1:2, :] = rank
    placed = dot(pad[...].astype(jnp.bfloat16), order, NT)
    place_s[...] = jnp.broadcast_to(
        (placed[0:1, :] * per_peer + placed[1:2, :]).astype(jnp.int32), place_s.shape
    )

    pad[0:1, :] = (position // 256).astype(jnp.float32)
    pad[1:2, :] = (position % 256).astype(jnp.float32)
    found = dot(pad[...].astype(jnp.bfloat16), hot(small[at_owner + 1:at_owner + 2, 0:columns].astype(jnp.int32), columns))
    at = (found[0:1, :] * 256.0 + found[1:2, :]).astype(jnp.int32)
    qp_s[...] = jnp.broadcast_to(at, qp_s.shape)
    pad[...] = jnp.zeros_like(pad)
    pad[0:voigt, :] = small[at_strain:at_owner, 0:columns]
    hi, lo = halves(pad[...])
    serves = hot(at, columns)
    strain_s[...] = dot(hi, serves, NT) + dot(lo, serves, NT)

    kfull[...] = jnp.zeros_like(kfull)
    copies[1].wait()
    for a in range(nb):
        for b in range(nb):
            kfull[a * blk:(a + 1) * blk, b * blk:(b + 1) * blk] = (
                stiff[a, b] * small[PATTERN + a * nb + b:PATTERN + a * nb + b + 1, 0:blk]
            )
    k = kfull[...]
    kh = k.astype(jnp.bfloat16)
    khi[...] = kh
    klo[...] = (k - kh.astype(jnp.float32)).astype(jnp.bfloat16)

    copies[2].wait()
    copies[3].wait()
    hi, lo = halves(hist[...])
    hist_s[...] = jnp.zeros_like(hist_s)
    hist_s[0:nodes, :] = dot(hi, order, NT) + dot(lo, order, NT)
    h = hist_s[...]
    weight_s[...] = jnp.zeros_like(weight_s)
    weight_s[0:nodes, :] = dot(flag[...].astype(jnp.float32).astype(jnp.bfloat16), order, NT)
    weight_s[...] = weight_s[...] * h * h / (1.0 + h * h)

    cstack[...] = jnp.zeros_like(cstack)
    for c in range(comps):
        cpl = small[c * voigt:(c + 1) * voigt, :]
        hi = cpl.astype(jnp.bfloat16).astype(jnp.float32)
        cstack[c, 0:voigt, 0:nodes] = hi
        cstack[c, 8:8 + voigt, 0:nodes] = hi
        cstack[c, 16:16 + voigt, 0:nodes] = cpl - hi
    pdir[...] = jnp.zeros_like(pdir)
    for c in range(comps):
        spread = jnp.broadcast_to(small[at_plastic + c:at_plastic + c + 1, :], (LANES, nodes))
        pdir[c, 0:nodes, :] = jnp.transpose(spread)


def sweep(rows, comps, span):
    pieces = 4 * span // LANES
    cuts = [rows // 16 * i // pieces * 16 for i in range(pieces + 1)]
    for top, end in zip(cuts, cuts[1:]):
        for c in range(comps):
            yield slice(top, end), slice(c * span, (c + 1) * span), c


def fold(x):
    return jnp.sum(x.reshape(x.shape[0] // 8, 8, x.shape[1]), axis=0)


def total(parts):
    return jnp.sum(parts, axis=0, keepdims=True)


def solve_kernel(scale, first, earlier, khi, klo, hist, weight, strain, cstack, pdir, place, *refs):
    earlier_updated, refs = refs[:earlier], refs[earlier:]
    updated, stress, blocks = refs[0], refs[1], refs[2:-5]
    field, resid, image, solved, split = refs[-5:]
    rows, span = hist.shape
    comps = pdir.shape[0]
    wide = comps * span
    zero = jnp.zeros((8, span), jnp.float32)

    def flow(c, r):
        return jnp.concatenate([pdir[c, r, :]] * (span // LANES), axis=1)

    def keep(r, c, x):
        split[r, c * span:(c + 1) * span], split[r, wide + c * span:wide + (c + 1) * span] = (
            halves(x)
        )

    s = strain[...]
    s_hi = s.astype(jnp.bfloat16).astype(jnp.float32)
    s3 = jnp.concatenate([s_hi, s - s_hi, s_hi, jnp.zeros_like(s)], axis=0).astype(jnp.bfloat16)
    split[rows:, :] = jnp.zeros((split.shape[0] - rows, 2 * wide), jnp.bfloat16)
    for c in range(comps):
        image[:, c * span:(c + 1) * span] = dot(cstack[c].astype(jnp.bfloat16), s3, TN)
    parts = zero
    for r, l, c in sweep(rows, comps, span):
        d = image[r, l] - weight[r, :] * hist[r, :] * flow(c, r)
        resid[r, l] = d
        field[r, l] = d
        keep(r, c, d)
        parts = parts + fold(d * d)
    norm = total(parts)
    for step in range(ITERS):
        both = dot(khi[...], split[...])
        image[...] = both[:, 0:wide] + both[:, wide:] + dot(klo[...], split[:, 0:wide])
        parts = zero
        for r, l, c in sweep(rows, comps, span):
            d = field[r, l]
            q = image[r, l] + (1.5 - weight[r, :]) * d
            image[r, l] = q
            parts = parts + fold(d * q)
        alpha = norm / jnp.maximum(total(parts), 1.0)
        if step == ITERS - 1:
            break
        parts = zero
        for r, l, c in sweep(rows, comps, span):
            gain = alpha * field[r, l]
            solved[r, l] = gain if step == 0 else solved[r, l] + gain
            left = resid[r, l] - alpha * image[r, l]
            resid[r, l] = left
            parts = parts + fold(left * left)
        following = total(parts)
        beta = following / jnp.maximum(norm, 1.0)
        norm = following
        for r, l, c in sweep(rows, comps, span):
            d = resid[r, l] + beta * field[r, l]
            field[r, l] = d
            keep(r, c, d)
    for r, l, c in sweep(rows, comps, span):
        x = solved[r, l] + alpha * field[r, l]
        pushed = flow(c, r) * x
        image[r, 0:span] = pushed if c == 0 else image[r, 0:span] + pushed
        keep(r, c, (1.5 - weight[r, :]) * x)
    updated[...] = hist[...] + weight[...] * image[:, 0:span]
    sent = blocks[0]
    put(sent, 0, placed_rows(first, sent.shape[0], place, [*earlier_updated, updated]))
    out = s
    for c in range(comps):
        cpl = cstack[c].astype(jnp.bfloat16)
        main = dot(cpl, split[0:rows, c * span:(c + 1) * span])
        minor = dot(cpl, split[0:rows, wide + c * span:wide + (c + 1) * span])
        out = out + scale * (main[0:8] + main[16:24] + minor[0:8])
    stress[...] = out


def placed_rows(first, count, place, sources):
    width = sum(source.shape[1] for source in sources)
    placing = hot(place[0:1, 0:width] - first, count)
    sums, left = 0.0, 0
    for source in sources:
        hi, lo = halves(source[...])
        cut = placing[:, left:left + source.shape[1]]
        sums = sums + (dot(cut, hi, NT) + dot(cut, lo, NT))
        left += source.shape[1]
    return sums


def put(block, top, rows):
    height, filled = rows.shape
    block[pl.ds(top, height), 0:filled] = rows
    rest = jnp.zeros((height, block.shape[1] - filled), jnp.float32)
    block[pl.ds(top, height), filled:] = rest


def ship_kernel(devices, first, chunks, place, at, *refs):
    updated, stress, (pair, out) = refs[:chunks], refs[chunks:2 * chunks], refs[2 * chunks:]
    me, plane, lane, lanes = whereabouts(devices)
    group = pair.shape[0] // 2
    rows = placed_rows(first, 2 * group, place, updated)
    put(pair, pl.multiple_of((1 - plane // 2) * group, group), rows[0:group])
    put(pair, pl.multiple_of(plane // 2 * group, group), rows[group:])
    hi, lo = halves(jnp.concatenate([ref[...] for ref in stress], axis=1))
    serves = hot(at[0:1, :], hi.shape[1])
    out[...] = (dot(hi, serves) + dot(lo, serves))[0:out.shape[0], :]


def hold_kernel(own_core, sibling, held):
    held[0] = own_core[...]
    held[1] = sibling[...]


def join_kernel(cap, held, own_core, sibling, *blocks):
    for i, block in enumerate(blocks):
        rows = slice(i * cap, (i + 1) * cap)
        block[0:cap, :] = held[0, rows, :]
        block[cap:2 * cap, :] = held[1, rows, :]
        block[2 * cap:3 * cap, :] = own_core[rows, :]
        block[3 * cap:, :] = sibling[rows, :]


def land(tile, out, stage, sem, slot, at):
    nodes = out.shape[0]
    stage[slot] = jnp.transpose(tile)[0:nodes, :]
    columns = pl.multiple_of(at * LANES, LANES)
    copy = pltpu.make_async_copy(stage.at[slot], out.at[:, pl.ds(columns, LANES)], sem.at[slot])
    copy.start()
    return copy


def land_group(block, count, plane, out, stage, sem, slot):
    height = block.shape[0] // count
    copies = []
    for part in range(count):
        tile = block[part * height:(part + 1) * height, :]
        copies.append(land(tile, out, stage, sem, slot + part, plane * count + part))
    return copies


def land_kernel(devices, cap, pair, *refs):
    blocks, (out, stage, sem, gather) = refs[:-4], refs[-4:]
    me, plane, lane, lanes = whereabouts(devices)
    group = pair.shape[0] // 2
    copies = []
    for part in range(2):
        source = jnp.where(plane // 2 == part, plane, plane ^ 3)
        block = pair.at[part * group:(part + 1) * group, :]
        copies += land_group(block, 2, source, out, stage, sem, 2 * part)
    for i, apart in enumerate((2, 1)):
        for k in range(lanes):
            at = pl.multiple_of((lane ^ k) * cap, cap)
            top = (2 * i + k % 2) * cap
            gather[i, pl.ds(at, cap), :] = blocks[k // 2][top:top + cap, :]
        copies += land_group(gather.at[i], 2, plane ^ apart, out, stage, sem, 4 + 2 * i)
    for copy in copies:
        copy.wait()


def params(mib=24):
    return pltpu.CompilerParams(vmem_limit_bytes=mib * 2**20)


def shards(
    history, yield_flags, strain, qp_to_rve, new_owner, stiffness, pattern, coupling, plastic_dir
):
    devices = lax.axis_size(("macro", "pool"))
    nodes, columns = history.shape
    comps, voigt = coupling.shape[0], coupling.shape[1]
    per_peer = 2 * columns // devices
    rows = up(nodes, 32)
    deep = up(nodes, 256)
    f32, bf16, i32 = jnp.float32, jnp.bfloat16, jnp.int32
    vmem = pl.BlockSpec(memory_space=pltpu.VMEM)
    small_inputs = (coupling, plastic_dir, strain, new_owner.reshape(1, columns), qp_to_rve, pattern)
    small = pl.pallas_call(
        pack_kernel,
        out_shape=jax.ShapeDtypeStruct((up(PATTERN + pattern.size, 8), nodes), f32),
        in_specs=[vmem] * 5 + [pl.BlockSpec(memory_space=pltpu.SMEM)],
        out_specs=vmem,
        compiler_params=params(60),
    )(*small_inputs)
    inputs = (small, stiffness, history, yield_flags)
    khi, klo, hist_s, weight_s, strain_s, place_s, qp_s, cstack, pdir = pl.pallas_call(
        functools.partial(prep_kernel, devices, per_peer, comps, voigt),
        out_shape=(
            jax.ShapeDtypeStruct((rows, deep), bf16),
            jax.ShapeDtypeStruct((rows, deep), bf16),
            jax.ShapeDtypeStruct((rows, columns), f32),
            jax.ShapeDtypeStruct((rows, columns), f32),
            jax.ShapeDtypeStruct((8, columns), f32),
            jax.ShapeDtypeStruct((8, columns), i32),
            jax.ShapeDtypeStruct((8, columns), i32),
            jax.ShapeDtypeStruct((comps, 32, rows), f32),
            jax.ShapeDtypeStruct((comps, rows, LANES), f32),
        ),
        in_specs=[pl.BlockSpec(memory_space=pltpu.HBM)] * 4,
        out_specs=[vmem] * 9,
        scratch_shapes=[pltpu.VMEM((rows, deep), f32), pltpu.VMEM((8, columns), f32)]
        + [pltpu.VMEM(x.shape, x.dtype) for x in inputs]
        + [pltpu.SemaphoreType.DMA((4,))],
        compiler_params=params(46),
    )(*inputs)

    lanes = devices // PLANES
    group = lanes * per_peer
    block = lambda height: jax.ShapeDtypeStruct((height, deep), f32)
    whole = lambda shape: pl.BlockSpec(shape, lambda i: (0,) * len(shape))
    updated, stress_s, ready = [], [], []
    left = 0
    for span in (LANES,) * (columns // LANES):
        part = lambda height: pl.BlockSpec((height, span), lambda i, at=left // span: (0, at))
        wide = comps * span
        outs = [block(LANES)]
        done = pl.pallas_call(
            functools.partial(solve_kernel, 1.0 / math.sqrt(comps * nodes), left, len(updated)),
            grid=(1,),
            out_shape=(
                jax.ShapeDtypeStruct((rows, span), f32),
                jax.ShapeDtypeStruct((8, span), f32),
                *outs,
            ),
            in_specs=[whole((rows, deep)), whole((rows, deep)), part(rows), part(rows), part(8),
                      whole((comps, 32, rows)), whole((comps, rows, LANES)), whole((8, columns))]
            + [whole(u.shape) for u in updated],
            out_specs=[whole((rows, span)), whole((8, span))] + [whole(o.shape) for o in outs],
            scratch_shapes=[pltpu.VMEM((rows, wide), f32) for _ in range(4)]
            + [pltpu.VMEM((deep, 2 * wide), bf16)],
            compiler_params=params(),
            cost_estimate=pl.CostEstimate(
                flops=18 * rows * deep * wide, bytes_accessed=2**20, transcendentals=0
            ),
        )(khi, klo, hist_s, weight_s, strain_s, cstack, pdir, place_s, *updated)
        updated.append(done[0])
        stress_s.append(done[1])
        ready.extend(done[2:])
        left += span
    pair, stress_out = pl.pallas_call(
        functools.partial(ship_kernel, devices, 2 * group, len(updated)),
        out_shape=(block(2 * group), jax.ShapeDtypeStruct((voigt, columns), f32)),
        in_specs=[vmem] * (2 + 2 * len(updated)),
        out_specs=[vmem] * 2,
        compiler_params=params(),
        cost_estimate=pl.CostEstimate(
            flops=4 * rows * columns * columns, bytes_accessed=2**20, transcendentals=0
        ),
    )(place_s, qp_s, *updated, *stress_s)

    axes = ("macro", "pool")

    def hop(sent, mask):
        return lax.ppermute(sent, axes, [(s, s ^ mask) for s in range(devices)])

    planes = [list(range(z * lanes, (z + 1) * lanes)) for z in range(PLANES)]
    pair = lax.all_to_all(
        pair.reshape(2 * lanes, per_peer, deep), axes, split_axis=0, concat_axis=0, tiled=True,
        axis_index_groups=[planes[0] + planes[3], planes[1] + planes[2]],
    ).reshape(2 * group, deep)
    held = pl.pallas_call(
        hold_kernel,
        out_shape=jax.ShapeDtypeStruct((2, LANES, deep), f32),
        in_specs=[vmem] * 2,
        out_specs=vmem,
        compiler_params=params(),
        cost_estimate=pl.CostEstimate(flops=2**40, bytes_accessed=2**20, transcendentals=0),
    )(hop(ready[0], 2 * lanes), hop(ready[1], 2 * lanes + 1))
    own_core, sibling = hop(ready[2], lanes), hop(ready[3], lanes + 1)
    own_core, sibling, held = lax.optimization_barrier((own_core, sibling, held))
    half = lanes // 2
    joined = pl.pallas_call(
        functools.partial(join_kernel, per_peer),
        out_shape=(block(4 * per_peer),) * half,
        in_specs=[vmem] * 3,
        out_specs=[vmem] * half,
        compiler_params=params(),
    )(held, own_core, sibling)
    joined = [sent if i == 0 else hop(sent, 2 * i) for i, sent in enumerate(joined)]
    new_history = pl.pallas_call(
        functools.partial(land_kernel, devices, per_peer),
        out_shape=jax.ShapeDtypeStruct((nodes, devices * per_peer), f32),
        in_specs=[vmem] * (1 + half),
        out_specs=pl.BlockSpec(memory_space=pl.ANY),
        scratch_shapes=[pltpu.VMEM((8, nodes, LANES), f32), pltpu.SemaphoreType.DMA((8,)),
                        pltpu.VMEM((2, group, deep), f32)],
        compiler_params=params(),
    )(pair, *joined)
    return (new_history, stress_out)


def solution(mesh):
    return jax.shard_map(
        shards,
        mesh=mesh,
        in_specs=(
            P(None, ("macro", "pool")),
            P(None, ("macro", "pool")),
            P(None, ("macro", "pool")),
            P(("macro", "pool"), None),
            P(("macro", "pool"), None),
            P(),
            P(),
            P(),
            P(),
        ),
        out_specs=(P(None, ("macro", "pool")), P(None, ("macro", "pool"))),
        check_vma=False,
    )
```

```python
import functools
import math

import jax
import jax.numpy as jnp
from jax import lax
from jax.experimental import pallas as pl
from jax.experimental.pallas import tpu as pltpu
from jax.sharding import PartitionSpec as P

ITERS = 3
LANES = 128
PLANES = 4
PATTERN = 32

NN = (((1,), (0,)), ((), ()))
NT = (((1,), (1,)), ((), ()))
TN = (((0,), (0,)), ((), ()))


def up(value, unit):
    return -(-value // unit) * unit


def dot(a, b, dims=NN):
    return lax.dot_general(a, b, dims, preferred_element_type=jnp.float32)


def halves(x):
    hi = x.astype(jnp.bfloat16)
    lo = (x - hi.astype(jnp.float32)).astype(jnp.bfloat16)
    return hi, lo


def whereabouts(devices):
    me = lax.axis_index("macro") * lax.axis_size("pool") + lax.axis_index("pool")
    lanes = devices // PLANES
    return me, me // lanes, me % lanes, lanes


def hot(row, count):
    rows = lax.broadcasted_iota(jnp.int32, (count, row.shape[1]), 0)
    return jnp.where(rows == row, 1.0, 0.0).astype(jnp.bfloat16)


def pack_kernel(coupling, plastic, strain, owner, qp, pattern, small):
    top = 0
    for c in range(coupling.shape[0]):
        small[top:top + coupling.shape[1], :] = coupling[c]
        top += coupling.shape[1]
    for part in (plastic, strain, owner, qp):
        small[top:top + part.shape[0], 0:part.shape[1]] = part[...].astype(jnp.float32)
        top += part.shape[0]
    count = pattern.shape[0]
    for a in range(count):
        for b in range(count):
            couples = jnp.full((1, LANES), pattern[a, b].astype(jnp.float32))
            small[PATTERN + a * count + b:PATTERN + a * count + b + 1, 0:LANES] = couples


def prep_kernel(devices, per_peer, comps, voigt, *refs):
    sources, outs, (kfull, pad), local, sem = refs[:4], refs[4:13], refs[13:15], refs[15:19], refs[19]
    khi, klo, hist_s, weight_s, strain_s, place_s, qp_s, cstack, pdir = outs
    small, stiff, hist, flag = local
    copies = [
        pltpu.make_async_copy(source, target, sem.at[i])
        for i, (source, target) in enumerate(zip(sources, local))
    ]
    for copy in copies:
        copy.start()
    nodes, columns = hist.shape
    nb, blk = stiff.shape[0], stiff.shape[2]
    at_plastic = comps * voigt
    at_strain = at_plastic + comps
    at_owner = at_strain + voigt
    copies[0].wait()

    me, plane, lane, lanes = whereabouts(devices)
    owner = small[at_owner:at_owner + 1, 0:columns].astype(jnp.int32)
    apart = owner // lanes ^ plane
    target = owner % lanes
    away = target ^ lane
    shifted = away % 2 * (lanes // 2) + away // 2
    turn = jnp.where(apart == 2, 0, jnp.where(apart == 1, 1, jnp.where(apart == 3, 2, 3)))
    key = turn * lanes + jnp.where((apart == 2) | (apart == 1), shifted, target)
    key_ids = lax.broadcasted_iota(jnp.int32, (devices, columns), 0)
    mine = jnp.where(key_ids == key, 1.0, 0.0)
    earlier = jnp.where(
        lax.broadcasted_iota(jnp.int32, (columns, columns), 0)
        < lax.broadcasted_iota(jnp.int32, (columns, columns), 1), 1.0, 0.0
    ).astype(jnp.bfloat16)
    before = dot(mine.astype(jnp.bfloat16), earlier)
    rank = jnp.sum(before * mine, axis=0, keepdims=True)
    tally = jnp.sum(mine, axis=1, keepdims=True)
    ahead = jnp.where(key_ids < key, tally, 0.0)
    position = (rank + jnp.sum(ahead, axis=0, keepdims=True)).astype(jnp.int32)

    order = hot(position, columns)
    pad[...] = jnp.zeros_like(pad)
    pad[0:1, :] = key.astype(jnp.float32)
    pad[1:2, :] = rank
    placed = dot(pad[...].astype(jnp.bfloat16), order, NT)
    place_s[...] = jnp.broadcast_to(
        (placed[0:1, :] * per_peer + placed[1:2, :]).astype(jnp.int32), place_s.shape
    )

    pad[0:1, :] = (position // 256).astype(jnp.float32)
    pad[1:2, :] = (position % 256).astype(jnp.float32)
    found = dot(pad[...].astype(jnp.bfloat16), hot(small[at_owner + 1:at_owner + 2, 0:columns].astype(jnp.int32), columns))
    at = (found[0:1, :] * 256.0 + found[1:2, :]).astype(jnp.int32)
    qp_s[...] = jnp.broadcast_to(at, qp_s.shape)
    pad[...] = jnp.zeros_like(pad)
    pad[0:voigt, :] = small[at_strain:at_owner, 0:columns]
    hi, lo = halves(pad[...])
    serves = hot(at, columns)
    strain_s[...] = dot(hi, serves, NT) + dot(lo, serves, NT)

    kfull[...] = jnp.zeros_like(kfull)
    copies[1].wait()
    for a in range(nb):
        for b in range(nb):
            kfull[a * blk:(a + 1) * blk, b * blk:(b + 1) * blk] = (
                stiff[a, b] * small[PATTERN + a * nb + b:PATTERN + a * nb + b + 1, 0:blk]
            )
    k = kfull[...]
    kh = k.astype(jnp.bfloat16)
    khi[...] = kh
    klo[...] = (k - kh.astype(jnp.float32)).astype(jnp.bfloat16)

    copies[2].wait()
    copies[3].wait()
    hi, lo = halves(hist[...])
    hist_s[...] = jnp.zeros_like(hist_s)
    hist_s[0:nodes, :] = dot(hi, order, NT) + dot(lo, order, NT)
    h = hist_s[...]
    weight_s[...] = jnp.zeros_like(weight_s)
    weight_s[0:nodes, :] = dot(flag[...].astype(jnp.float32).astype(jnp.bfloat16), order, NT)
    weight_s[...] = weight_s[...] * h * h / (1.0 + h * h)

    cstack[...] = jnp.zeros_like(cstack)
    for c in range(comps):
        cpl = small[c * voigt:(c + 1) * voigt, :]
        hi = cpl.astype(jnp.bfloat16).astype(jnp.float32)
        cstack[c, 0:voigt, 0:nodes] = hi
        cstack[c, 8:8 + voigt, 0:nodes] = hi
        cstack[c, 16:16 + voigt, 0:nodes] = cpl - hi
    pdir[...] = jnp.zeros_like(pdir)
    for c in range(comps):
        spread = jnp.broadcast_to(small[at_plastic + c:at_plastic + c + 1, :], (LANES, nodes))
        pdir[c, 0:nodes, :] = jnp.transpose(spread)


def sweep(rows, comps, span):
    pieces = 4 * span // LANES
    cuts = [rows // 16 * i // pieces * 16 for i in range(pieces + 1)]
    for top, end in zip(cuts, cuts[1:]):
        for c in range(comps):
            yield slice(top, end), slice(c * span, (c + 1) * span), c


def fold(x):
    return jnp.sum(x.reshape(x.shape[0] // 8, 8, x.shape[1]), axis=0)


def total(parts):
    return jnp.sum(parts, axis=0, keepdims=True)


def solve_kernel(scale, first, earlier, khi, klo, hist, weight, strain, cstack, pdir, place, *refs):
    earlier_updated, refs = refs[:earlier], refs[earlier:]
    updated, stress, blocks = refs[0], refs[1], refs[2:-5]
    field, resid, image, solved, split = refs[-5:]
    rows, span = hist.shape
    comps = pdir.shape[0]
    wide = comps * span
    zero = jnp.zeros((8, span), jnp.float32)

    def flow(c, r):
        return jnp.concatenate([pdir[c, r, :]] * (span // LANES), axis=1)

    def keep(r, c, x):
        split[r, c * span:(c + 1) * span], split[r, wide + c * span:wide + (c + 1) * span] = (
            halves(x)
        )

    s = strain[...]
    s_hi = s.astype(jnp.bfloat16).astype(jnp.float32)
    s3 = jnp.concatenate([s_hi, s - s_hi, s_hi, jnp.zeros_like(s)], axis=0).astype(jnp.bfloat16)
    split[rows:, :] = jnp.zeros((split.shape[0] - rows, 2 * wide), jnp.bfloat16)
    for c in range(comps):
        image[:, c * span:(c + 1) * span] = dot(cstack[c].astype(jnp.bfloat16), s3, TN)
    parts = zero
    for r, l, c in sweep(rows, comps, span):
        d = image[r, l] - weight[r, :] * hist[r, :] * flow(c, r)
        resid[r, l] = d
        field[r, l] = d
        keep(r, c, d)
        parts = parts + fold(d * d)
    norm = total(parts)
    for step in range(ITERS):
        both = dot(khi[...], split[...])
        image[...] = both[:, 0:wide] + both[:, wide:] + dot(klo[...], split[:, 0:wide])
        parts = zero
        for r, l, c in sweep(rows, comps, span):
            d = field[r, l]
            q = image[r, l] + (1.5 - weight[r, :]) * d
            image[r, l] = q
            parts = parts + fold(d * q)
        alpha = norm / jnp.maximum(total(parts), 1.0)
        if step == ITERS - 1:
            break
        parts = zero
        for r, l, c in sweep(rows, comps, span):
            gain = alpha * field[r, l]
            solved[r, l] = gain if step == 0 else solved[r, l] + gain
            left = resid[r, l] - alpha * image[r, l]
            resid[r, l] = left
            parts = parts + fold(left * left)
        following = total(parts)
        beta = following / jnp.maximum(norm, 1.0)
        norm = following
        for r, l, c in sweep(rows, comps, span):
            d = resid[r, l] + beta * field[r, l]
            field[r, l] = d
            keep(r, c, d)
    for r, l, c in sweep(rows, comps, span):
        x = solved[r, l] + alpha * field[r, l]
        pushed = flow(c, r) * x
        image[r, 0:span] = pushed if c == 0 else image[r, 0:span] + pushed
        keep(r, c, (1.5 - weight[r, :]) * x)
    updated[...] = hist[...] + weight[...] * image[:, 0:span]
    sent = blocks[0]
    put(sent, 0, placed_rows(first, sent.shape[0], place, [*earlier_updated, updated]))
    out = s
    for c in range(comps):
        cpl = cstack[c].astype(jnp.bfloat16)
        main = dot(cpl, split[0:rows, c * span:(c + 1) * span])
        minor = dot(cpl, split[0:rows, wide + c * span:wide + (c + 1) * span])
        out = out + scale * (main[0:8] + main[16:24] + minor[0:8])
    stress[...] = out


def placed_rows(first, count, place, sources):
    width = sum(source.shape[1] for source in sources)
    placing = hot(place[0:1, 0:width] - first, count)
    sums, left = 0.0, 0
    for source in sources:
        hi, lo = halves(source[...])
        cut = placing[:, left:left + source.shape[1]]
        sums = sums + (dot(cut, hi, NT) + dot(cut, lo, NT))
        left += source.shape[1]
    return sums


def put(block, top, rows):
    height, filled = rows.shape
    block[pl.ds(top, height), 0:filled] = rows
    rest = jnp.zeros((height, block.shape[1] - filled), jnp.float32)
    block[pl.ds(top, height), filled:] = rest


def ship_kernel(devices, first, chunks, place, at, *refs):
    updated, stress, (pair, out) = refs[:chunks], refs[chunks:2 * chunks], refs[2 * chunks:]
    me, plane, lane, lanes = whereabouts(devices)
    group = pair.shape[0] // 2
    rows = placed_rows(first, 2 * group, place, updated)
    put(pair, pl.multiple_of((1 - plane // 2) * group, group), rows[0:group])
    put(pair, pl.multiple_of(plane // 2 * group, group), rows[group:])
    hi, lo = halves(jnp.concatenate([ref[...] for ref in stress], axis=1))
    serves = hot(at[0:1, :], hi.shape[1])
    out[...] = (dot(hi, serves) + dot(lo, serves))[0:out.shape[0], :]


def join_kernel(cap, *refs):
    landed, blocks = refs[:4], refs[4:]
    for i, block in enumerate(blocks):
        for k, rows in enumerate(landed):
            block[k * cap:(k + 1) * cap, :] = rows[i * cap:(i + 1) * cap, :]


def land(tile, out, stage, sem, slot, at):
    nodes = out.shape[0]
    stage[slot] = jnp.transpose(tile)[0:nodes, :]
    columns = pl.multiple_of(at * LANES, LANES)
    copy = pltpu.make_async_copy(stage.at[slot], out.at[:, pl.ds(columns, LANES)], sem.at[slot])
    copy.start()
    return copy


def land_group(block, count, plane, out, stage, sem, slot):
    height = block.shape[0] // count
    copies = []
    for part in range(count):
        tile = block[part * height:(part + 1) * height, :]
        copies.append(land(tile, out, stage, sem, slot + part, plane * count + part))
    return copies


def land_kernel(devices, cap, pair, *refs):
    blocks, (out, stage, sem, gather) = refs[:-4], refs[-4:]
    me, plane, lane, lanes = whereabouts(devices)
    group = pair.shape[0] // 2
    copies = []
    for part in range(2):
        source = jnp.where(plane // 2 == part, plane, plane ^ 3)
        block = pair.at[part * group:(part + 1) * group, :]
        copies += land_group(block, 2, source, out, stage, sem, 2 * part)
    for i, apart in enumerate((2, 1)):
        for k in range(lanes):
            at = pl.multiple_of((lane ^ k) * cap, cap)
            top = (2 * i + k % 2) * cap
            gather[i, pl.ds(at, cap), :] = blocks[k // 2][top:top + cap, :]
        copies += land_group(gather.at[i], 2, plane ^ apart, out, stage, sem, 4 + 2 * i)
    for copy in copies:
        copy.wait()


def params(mib=24):
    return pltpu.CompilerParams(vmem_limit_bytes=mib * 2**20)


def shards(
    history, yield_flags, strain, qp_to_rve, new_owner, stiffness, pattern, coupling, plastic_dir
):
    devices = lax.axis_size(("macro", "pool"))
    nodes, columns = history.shape
    comps, voigt = coupling.shape[0], coupling.shape[1]
    per_peer = 2 * columns // devices
    rows = up(nodes, 32)
    deep = up(nodes, 256)
    f32, bf16, i32 = jnp.float32, jnp.bfloat16, jnp.int32
    vmem = pl.BlockSpec(memory_space=pltpu.VMEM)
    small_inputs = (coupling, plastic_dir, strain, new_owner.reshape(1, columns), qp_to_rve, pattern)
    small = pl.pallas_call(
        pack_kernel,
        out_shape=jax.ShapeDtypeStruct((up(PATTERN + pattern.size, 8), nodes), f32),
        in_specs=[vmem] * 5 + [pl.BlockSpec(memory_space=pltpu.SMEM)],
        out_specs=vmem,
        compiler_params=params(60),
    )(*small_inputs)
    inputs = (small, stiffness, history, yield_flags)
    khi, klo, hist_s, weight_s, strain_s, place_s, qp_s, cstack, pdir = pl.pallas_call(
        functools.partial(prep_kernel, devices, per_peer, comps, voigt),
        out_shape=(
            jax.ShapeDtypeStruct((rows, deep), bf16),
            jax.ShapeDtypeStruct((rows, deep), bf16),
            jax.ShapeDtypeStruct((rows, columns), f32),
            jax.ShapeDtypeStruct((rows, columns), f32),
            jax.ShapeDtypeStruct((8, columns), f32),
            jax.ShapeDtypeStruct((8, columns), i32),
            jax.ShapeDtypeStruct((8, columns), i32),
            jax.ShapeDtypeStruct((comps, 32, rows), f32),
            jax.ShapeDtypeStruct((comps, rows, LANES), f32),
        ),
        in_specs=[pl.BlockSpec(memory_space=pltpu.HBM)] * 4,
        out_specs=[vmem] * 9,
        scratch_shapes=[pltpu.VMEM((rows, deep), f32), pltpu.VMEM((8, columns), f32)]
        + [pltpu.VMEM(x.shape, x.dtype) for x in inputs]
        + [pltpu.SemaphoreType.DMA((4,))],
        compiler_params=params(46),
    )(*inputs)

    lanes = devices // PLANES
    group = lanes * per_peer
    block = lambda height: jax.ShapeDtypeStruct((height, deep), f32)
    whole = lambda shape: pl.BlockSpec(shape, lambda i: (0,) * len(shape))
    updated, stress_s, ready = [], [], []
    left = 0
    for span in (LANES,) * (columns // LANES):
        part = lambda height: pl.BlockSpec((height, span), lambda i, at=left // span: (0, at))
        wide = comps * span
        outs = [block(LANES)]
        done = pl.pallas_call(
            functools.partial(solve_kernel, 1.0 / math.sqrt(comps * nodes), left, len(updated)),
            grid=(1,),
            out_shape=(
                jax.ShapeDtypeStruct((rows, span), f32),
                jax.ShapeDtypeStruct((8, span), f32),
                *outs,
            ),
            in_specs=[whole((rows, deep)), whole((rows, deep)), part(rows), part(rows), part(8),
                      whole((comps, 32, rows)), whole((comps, rows, LANES)), whole((8, columns))]
            + [whole(u.shape) for u in updated],
            out_specs=[whole((rows, span)), whole((8, span))] + [whole(o.shape) for o in outs],
            scratch_shapes=[pltpu.VMEM((rows, wide), f32) for _ in range(4)]
            + [pltpu.VMEM((deep, 2 * wide), bf16)],
            compiler_params=params(),
            cost_estimate=pl.CostEstimate(
                flops=18 * rows * deep * wide, bytes_accessed=2**20, transcendentals=0
            ),
        )(khi, klo, hist_s, weight_s, strain_s, cstack, pdir, place_s, *updated)
        updated.append(done[0])
        stress_s.append(done[1])
        ready.extend(done[2:])
        left += span
    pair, stress_out = pl.pallas_call(
        functools.partial(ship_kernel, devices, 2 * group, len(updated)),
        out_shape=(block(2 * group), jax.ShapeDtypeStruct((voigt, columns), f32)),
        in_specs=[vmem] * (2 + 2 * len(updated)),
        out_specs=[vmem] * 2,
        compiler_params=params(),
        cost_estimate=pl.CostEstimate(
            flops=4 * rows * columns * columns, bytes_accessed=2**20, transcendentals=0
        ),
    )(place_s, qp_s, *updated, *stress_s)

    axes = ("macro", "pool")

    def hop(sent, mask):
        return lax.ppermute(sent, axes, [(s, s ^ mask) for s in range(devices)])

    planes = [list(range(z * lanes, (z + 1) * lanes)) for z in range(PLANES)]
    pair = lax.all_to_all(
        pair.reshape(2 * lanes, per_peer, deep), axes, split_axis=0, concat_axis=0, tiled=True,
        axis_index_groups=[planes[0] + planes[3], planes[1] + planes[2]],
    ).reshape(2 * group, deep)
    hops = (2 * lanes, 2 * lanes + 1, lanes, lanes + 1)
    landed = []
    for sent, mask in zip(ready, hops):
        landed.append(hop(sent, mask))
        landed[-2:] = lax.optimization_barrier(tuple(landed[-2:]))
    half = lanes // 2
    joined = pl.pallas_call(
        functools.partial(join_kernel, per_peer),
        out_shape=(block(4 * per_peer),) * half,
        in_specs=[vmem] * 4,
        out_specs=[vmem] * half,
        compiler_params=params(),
        cost_estimate=pl.CostEstimate(flops=2**40, bytes_accessed=2**20, transcendentals=0),
    )(*landed)
    joined = [sent if i == 0 else hop(sent, 2 * i) for i, sent in enumerate(joined)]
    new_history = pl.pallas_call(
        functools.partial(land_kernel, devices, per_peer),
        out_shape=jax.ShapeDtypeStruct((nodes, devices * per_peer), f32),
        in_specs=[vmem] * (1 + half),
        out_specs=pl.BlockSpec(memory_space=pl.ANY),
        scratch_shapes=[pltpu.VMEM((8, nodes, LANES), f32), pltpu.SemaphoreType.DMA((8,)),
                        pltpu.VMEM((2, group, deep), f32)],
        compiler_params=params(),
    )(pair, *joined)
    return (new_history, stress_out)


def solution(mesh):
    return jax.shard_map(
        shards,
        mesh=mesh,
        in_specs=(
            P(None, ("macro", "pool")),
            P(None, ("macro", "pool")),
            P(None, ("macro", "pool")),
            P(("macro", "pool"), None),
            P(("macro", "pool"), None),
            P(),
            P(),
            P(),
            P(),
        ),
        out_specs=(P(None, ("macro", "pool")), P(None, ("macro", "pool"))),
        check_vma=False,
    )
```

```python
import functools
import math

import jax
import jax.numpy as jnp
from jax import lax
from jax.experimental import pallas as pl
from jax.experimental.pallas import tpu as pltpu
from jax.sharding import PartitionSpec as P

ITERS = 3
LANES = 128
PLANES = 4
PATTERN = 32

NN = (((1,), (0,)), ((), ()))
NT = (((1,), (1,)), ((), ()))
TN = (((0,), (0,)), ((), ()))


def up(value, unit):
    return -(-value // unit) * unit


def dot(a, b, dims=NN):
    return lax.dot_general(a, b, dims, preferred_element_type=jnp.float32)


def halves(x):
    hi = x.astype(jnp.bfloat16)
    lo = (x - hi.astype(jnp.float32)).astype(jnp.bfloat16)
    return hi, lo


def whereabouts(devices):
    me = lax.axis_index("macro") * lax.axis_size("pool") + lax.axis_index("pool")
    lanes = devices // PLANES
    return me, me // lanes, me % lanes, lanes


def hot(row, count):
    rows = lax.broadcasted_iota(jnp.int32, (count, row.shape[1]), 0)
    return jnp.where(rows == row, 1.0, 0.0).astype(jnp.bfloat16)


def pack_kernel(coupling, plastic, strain, owner, qp, pattern, small):
    top = 0
    for c in range(coupling.shape[0]):
        small[top:top + coupling.shape[1], :] = coupling[c]
        top += coupling.shape[1]
    for part in (plastic, strain, owner, qp):
        small[top:top + part.shape[0], 0:part.shape[1]] = part[...].astype(jnp.float32)
        top += part.shape[0]
    count = pattern.shape[0]
    for a in range(count):
        for b in range(count):
            couples = jnp.full((1, LANES), pattern[a, b].astype(jnp.float32))
            small[PATTERN + a * count + b:PATTERN + a * count + b + 1, 0:LANES] = couples


def prep_kernel(devices, per_peer, comps, voigt, *refs):
    sources, outs, (kfull, pad), local, sem = refs[:4], refs[4:13], refs[13:15], refs[15:19], refs[19]
    khi, klo, hist_s, weight_s, strain_s, place_s, qp_s, cstack, pdir = outs
    small, stiff, hist, flag = local
    copies = [
        pltpu.make_async_copy(source, target, sem.at[i])
        for i, (source, target) in enumerate(zip(sources, local))
    ]
    for copy in copies:
        copy.start()
    nodes, columns = hist.shape
    nb, blk = stiff.shape[0], stiff.shape[2]
    at_plastic = comps * voigt
    at_strain = at_plastic + comps
    at_owner = at_strain + voigt
    copies[0].wait()

    me, plane, lane, lanes = whereabouts(devices)
    owner = small[at_owner:at_owner + 1, 0:columns].astype(jnp.int32)
    apart = owner // lanes ^ plane
    target = owner % lanes
    away = target ^ lane
    hopping = (away % 2 * 2 + jnp.where(apart == 2, 0, 1)) * (lanes // 2) + away // 2
    staying = jnp.where(apart == 3, 2, 3) * lanes + target
    key = jnp.where((apart == 2) | (apart == 1), hopping, staying)
    key_ids = lax.broadcasted_iota(jnp.int32, (devices, columns), 0)
    mine = jnp.where(key_ids == key, 1.0, 0.0)
    earlier = jnp.where(
        lax.broadcasted_iota(jnp.int32, (columns, columns), 0)
        < lax.broadcasted_iota(jnp.int32, (columns, columns), 1), 1.0, 0.0
    ).astype(jnp.bfloat16)
    before = dot(mine.astype(jnp.bfloat16), earlier)
    rank = jnp.sum(before * mine, axis=0, keepdims=True)
    tally = jnp.sum(mine, axis=1, keepdims=True)
    ahead = jnp.where(key_ids < key, tally, 0.0)
    position = (rank + jnp.sum(ahead, axis=0, keepdims=True)).astype(jnp.int32)

    order = hot(position, columns)
    pad[...] = jnp.zeros_like(pad)
    pad[0:1, :] = key.astype(jnp.float32)
    pad[1:2, :] = rank
    placed = dot(pad[...].astype(jnp.bfloat16), order, NT)
    place_s[...] = jnp.broadcast_to(
        (placed[0:1, :] * per_peer + placed[1:2, :]).astype(jnp.int32), place_s.shape
    )

    pad[0:1, :] = (position // 256).astype(jnp.float32)
    pad[1:2, :] = (position % 256).astype(jnp.float32)
    found = dot(pad[...].astype(jnp.bfloat16), hot(small[at_owner + 1:at_owner + 2, 0:columns].astype(jnp.int32), columns))
    at = (found[0:1, :] * 256.0 + found[1:2, :]).astype(jnp.int32)
    qp_s[...] = jnp.broadcast_to(at, qp_s.shape)
    pad[...] = jnp.zeros_like(pad)
    pad[0:voigt, :] = small[at_strain:at_owner, 0:columns]
    hi, lo = halves(pad[...])
    serves = hot(at, columns)
    strain_s[...] = dot(hi, serves, NT) + dot(lo, serves, NT)

    kfull[...] = jnp.zeros_like(kfull)
    copies[1].wait()
    for a in range(nb):
        for b in range(nb):
            kfull[a * blk:(a + 1) * blk, b * blk:(b + 1) * blk] = (
                stiff[a, b] * small[PATTERN + a * nb + b:PATTERN + a * nb + b + 1, 0:blk]
            )
    k = kfull[...]
    kh = k.astype(jnp.bfloat16)
    khi[...] = kh
    klo[...] = (k - kh.astype(jnp.float32)).astype(jnp.bfloat16)

    copies[2].wait()
    copies[3].wait()
    hi, lo = halves(hist[...])
    hist_s[...] = jnp.zeros_like(hist_s)
    hist_s[0:nodes, :] = dot(hi, order, NT) + dot(lo, order, NT)
    h = hist_s[...]
    weight_s[...] = jnp.zeros_like(weight_s)
    weight_s[0:nodes, :] = dot(flag[...].astype(jnp.float32).astype(jnp.bfloat16), order, NT)
    weight_s[...] = weight_s[...] * h * h / (1.0 + h * h)

    cstack[...] = jnp.zeros_like(cstack)
    for c in range(comps):
        cpl = small[c * voigt:(c + 1) * voigt, :]
        hi = cpl.astype(jnp.bfloat16).astype(jnp.float32)
        cstack[c, 0:voigt, 0:nodes] = hi
        cstack[c, 8:8 + voigt, 0:nodes] = hi
        cstack[c, 16:16 + voigt, 0:nodes] = cpl - hi
    pdir[...] = jnp.zeros_like(pdir)
    for c in range(comps):
        spread = jnp.broadcast_to(small[at_plastic + c:at_plastic + c + 1, :], (LANES, nodes))
        pdir[c, 0:nodes, :] = jnp.transpose(spread)


def sweep(rows, comps, span):
    pieces = 4 * span // LANES
    cuts = [rows // 16 * i // pieces * 16 for i in range(pieces + 1)]
    for top, end in zip(cuts, cuts[1:]):
        for c in range(comps):
            yield slice(top, end), slice(c * span, (c + 1) * span), c


def fold(x):
    return jnp.sum(x.reshape(x.shape[0] // 8, 8, x.shape[1]), axis=0)


def total(parts):
    return jnp.sum(parts, axis=0, keepdims=True)


def solve_kernel(scale, first, earlier, khi, klo, hist, weight, strain, cstack, pdir, place, *refs):
    earlier_updated, refs = refs[:earlier], refs[earlier:]
    updated, stress, blocks = refs[0], refs[1], refs[2:-5]
    field, resid, image, solved, split = refs[-5:]
    rows, span = hist.shape
    comps = pdir.shape[0]
    wide = comps * span
    zero = jnp.zeros((8, span), jnp.float32)

    def flow(c, r):
        return jnp.concatenate([pdir[c, r, :]] * (span // LANES), axis=1)

    def keep(r, c, x):
        split[r, c * span:(c + 1) * span], split[r, wide + c * span:wide + (c + 1) * span] = (
            halves(x)
        )

    s = strain[...]
    s_hi = s.astype(jnp.bfloat16).astype(jnp.float32)
    s3 = jnp.concatenate([s_hi, s - s_hi, s_hi, jnp.zeros_like(s)], axis=0).astype(jnp.bfloat16)
    split[rows:, :] = jnp.zeros((split.shape[0] - rows, 2 * wide), jnp.bfloat16)
    for c in range(comps):
        image[:, c * span:(c + 1) * span] = dot(cstack[c].astype(jnp.bfloat16), s3, TN)
    parts = zero
    for r, l, c in sweep(rows, comps, span):
        d = image[r, l] - weight[r, :] * hist[r, :] * flow(c, r)
        resid[r, l] = d
        field[r, l] = d
        keep(r, c, d)
        parts = parts + fold(d * d)
    norm = total(parts)
    for step in range(ITERS):
        both = dot(khi[...], split[...])
        image[...] = both[:, 0:wide] + both[:, wide:] + dot(klo[...], split[:, 0:wide])
        parts = zero
        for r, l, c in sweep(rows, comps, span):
            d = field[r, l]
            q = image[r, l] + (1.5 - weight[r, :]) * d
            image[r, l] = q
            parts = parts + fold(d * q)
        alpha = norm / jnp.maximum(total(parts), 1.0)
        if step == ITERS - 1:
            break
        parts = zero
        for r, l, c in sweep(rows, comps, span):
            gain = alpha * field[r, l]
            solved[r, l] = gain if step == 0 else solved[r, l] + gain
            left = resid[r, l] - alpha * image[r, l]
            resid[r, l] = left
            parts = parts + fold(left * left)
        following = total(parts)
        beta = following / jnp.maximum(norm, 1.0)
        norm = following
        for r, l, c in sweep(rows, comps, span):
            d = resid[r, l] + beta * field[r, l]
            field[r, l] = d
            keep(r, c, d)
    for r, l, c in sweep(rows, comps, span):
        x = solved[r, l] + alpha * field[r, l]
        pushed = flow(c, r) * x
        image[r, 0:span] = pushed if c == 0 else image[r, 0:span] + pushed
        keep(r, c, (1.5 - weight[r, :]) * x)
    updated[...] = hist[...] + weight[...] * image[:, 0:span]
    sent = blocks[0]
    put(sent, 0, placed_rows(first, sent.shape[0], place, [*earlier_updated, updated]))
    out = s
    for c in range(comps):
        cpl = cstack[c].astype(jnp.bfloat16)
        main = dot(cpl, split[0:rows, c * span:(c + 1) * span])
        minor = dot(cpl, split[0:rows, wide + c * span:wide + (c + 1) * span])
        out = out + scale * (main[0:8] + main[16:24] + minor[0:8])
    stress[...] = out


def placed_rows(first, count, place, sources):
    width = sum(source.shape[1] for source in sources)
    placing = hot(place[0:1, 0:width] - first, count)
    sums, left = 0.0, 0
    for source in sources:
        hi, lo = halves(source[...])
        cut = placing[:, left:left + source.shape[1]]
        sums = sums + (dot(cut, hi, NT) + dot(cut, lo, NT))
        left += source.shape[1]
    return sums


def put(block, top, rows):
    height, filled = rows.shape
    block[pl.ds(top, height), 0:filled] = rows
    rest = jnp.zeros((height, block.shape[1] - filled), jnp.float32)
    block[pl.ds(top, height), filled:] = rest


def ship_kernel(devices, first, chunks, place, at, *refs):
    updated, stress, (pair, out) = refs[:chunks], refs[chunks:2 * chunks], refs[2 * chunks:]
    me, plane, lane, lanes = whereabouts(devices)
    group = pair.shape[0] // 2
    rows = placed_rows(first, 2 * group, place, updated)
    put(pair, pl.multiple_of((1 - plane // 2) * group, group), rows[0:group])
    put(pair, pl.multiple_of(plane // 2 * group, group), rows[group:])
    hi, lo = halves(jnp.concatenate([ref[...] for ref in stress], axis=1))
    serves = hot(at[0:1, :], hi.shape[1])
    out[...] = (dot(hi, serves) + dot(lo, serves))[0:out.shape[0], :]


def join_kernel(cap, *refs):
    landed, blocks = refs[:4], refs[4:]
    for i, block in enumerate(blocks):
        for k, rows in enumerate(landed):
            block[k * cap:(k + 1) * cap, :] = rows[i * cap:(i + 1) * cap, :]


def land(tile, out, stage, sem, slot, at):
    nodes = out.shape[0]
    stage[slot] = jnp.transpose(tile)[0:nodes, :]
    columns = pl.multiple_of(at * LANES, LANES)
    copy = pltpu.make_async_copy(stage.at[slot], out.at[:, pl.ds(columns, LANES)], sem.at[slot])
    copy.start()
    return copy


def land_group(block, count, plane, out, stage, sem, slot):
    height = block.shape[0] // count
    copies = []
    for part in range(count):
        tile = block[part * height:(part + 1) * height, :]
        copies.append(land(tile, out, stage, sem, slot + part, plane * count + part))
    return copies


def land_kernel(devices, cap, pair, *refs):
    blocks, (out, stage, sem, gather) = refs[:-4], refs[-4:]
    me, plane, lane, lanes = whereabouts(devices)
    group = pair.shape[0] // 2
    copies = []
    for part in range(2):
        source = jnp.where(plane // 2 == part, plane, plane ^ 3)
        block = pair.at[part * group:(part + 1) * group, :]
        copies += land_group(block, 2, source, out, stage, sem, 2 * part)
    for i, apart in enumerate((2, 1)):
        for k in range(lanes):
            at = pl.multiple_of((lane ^ k) * cap, cap)
            top = (2 * (k % 2) + i) * cap
            gather[i, pl.ds(at, cap), :] = blocks[k // 2][top:top + cap, :]
        copies += land_group(gather.at[i], 2, plane ^ apart, out, stage, sem, 4 + 2 * i)
    for copy in copies:
        copy.wait()


def params(mib=24):
    return pltpu.CompilerParams(vmem_limit_bytes=mib * 2**20)


def shards(
    history, yield_flags, strain, qp_to_rve, new_owner, stiffness, pattern, coupling, plastic_dir
):
    devices = lax.axis_size(("macro", "pool"))
    nodes, columns = history.shape
    comps, voigt = coupling.shape[0], coupling.shape[1]
    per_peer = 2 * columns // devices
    rows = up(nodes, 32)
    deep = up(nodes, 256)
    f32, bf16, i32 = jnp.float32, jnp.bfloat16, jnp.int32
    vmem = pl.BlockSpec(memory_space=pltpu.VMEM)
    small_inputs = (coupling, plastic_dir, strain, new_owner.reshape(1, columns), qp_to_rve, pattern)
    small = pl.pallas_call(
        pack_kernel,
        out_shape=jax.ShapeDtypeStruct((up(PATTERN + pattern.size, 8), nodes), f32),
        in_specs=[vmem] * 5 + [pl.BlockSpec(memory_space=pltpu.SMEM)],
        out_specs=vmem,
        compiler_params=params(60),
    )(*small_inputs)
    inputs = (small, stiffness, history, yield_flags)
    khi, klo, hist_s, weight_s, strain_s, place_s, qp_s, cstack, pdir = pl.pallas_call(
        functools.partial(prep_kernel, devices, per_peer, comps, voigt),
        out_shape=(
            jax.ShapeDtypeStruct((rows, deep), bf16),
            jax.ShapeDtypeStruct((rows, deep), bf16),
            jax.ShapeDtypeStruct((rows, columns), f32),
            jax.ShapeDtypeStruct((rows, columns), f32),
            jax.ShapeDtypeStruct((8, columns), f32),
            jax.ShapeDtypeStruct((8, columns), i32),
            jax.ShapeDtypeStruct((8, columns), i32),
            jax.ShapeDtypeStruct((comps, 32, rows), f32),
            jax.ShapeDtypeStruct((comps, rows, LANES), f32),
        ),
        in_specs=[pl.BlockSpec(memory_space=pltpu.HBM)] * 4,
        out_specs=[vmem] * 9,
        scratch_shapes=[pltpu.VMEM((rows, deep), f32), pltpu.VMEM((8, columns), f32)]
        + [pltpu.VMEM(x.shape, x.dtype) for x in inputs]
        + [pltpu.SemaphoreType.DMA((4,))],
        compiler_params=params(46),
    )(*inputs)

    lanes = devices // PLANES
    group = lanes * per_peer
    block = lambda height: jax.ShapeDtypeStruct((height, deep), f32)
    whole = lambda shape: pl.BlockSpec(shape, lambda i: (0,) * len(shape))
    updated, stress_s, ready = [], [], []
    left = 0
    for span in (LANES,) * (columns // LANES):
        part = lambda height: pl.BlockSpec((height, span), lambda i, at=left // span: (0, at))
        wide = comps * span
        outs = [block(LANES)]
        done = pl.pallas_call(
            functools.partial(solve_kernel, 1.0 / math.sqrt(comps * nodes), left, len(updated)),
            grid=(1,),
            out_shape=(
                jax.ShapeDtypeStruct((rows, span), f32),
                jax.ShapeDtypeStruct((8, span), f32),
                *outs,
            ),
            in_specs=[whole((rows, deep)), whole((rows, deep)), part(rows), part(rows), part(8),
                      whole((comps, 32, rows)), whole((comps, rows, LANES)), whole((8, columns))]
            + [whole(u.shape) for u in updated],
            out_specs=[whole((rows, span)), whole((8, span))] + [whole(o.shape) for o in outs],
            scratch_shapes=[pltpu.VMEM((rows, wide), f32) for _ in range(4)]
            + [pltpu.VMEM((deep, 2 * wide), bf16)],
            compiler_params=params(),
            cost_estimate=pl.CostEstimate(
                flops=18 * rows * deep * wide, bytes_accessed=2**20, transcendentals=0
            ),
        )(khi, klo, hist_s, weight_s, strain_s, cstack, pdir, place_s, *updated)
        updated.append(done[0])
        stress_s.append(done[1])
        ready.extend(done[2:])
        left += span
    pair, stress_out = pl.pallas_call(
        functools.partial(ship_kernel, devices, 2 * group, len(updated)),
        out_shape=(block(2 * group), jax.ShapeDtypeStruct((voigt, columns), f32)),
        in_specs=[vmem] * (2 + 2 * len(updated)),
        out_specs=[vmem] * 2,
        compiler_params=params(),
        cost_estimate=pl.CostEstimate(
            flops=4 * rows * columns * columns, bytes_accessed=2**20, transcendentals=0
        ),
    )(place_s, qp_s, *updated, *stress_s)

    axes = ("macro", "pool")

    def hop(sent, mask):
        return lax.ppermute(sent, axes, [(s, s ^ mask) for s in range(devices)])

    planes = [list(range(z * lanes, (z + 1) * lanes)) for z in range(PLANES)]
    pair = lax.all_to_all(
        pair.reshape(2 * lanes, per_peer, deep), axes, split_axis=0, concat_axis=0, tiled=True,
        axis_index_groups=[planes[0] + planes[3], planes[1] + planes[2]],
    ).reshape(2 * group, deep)
    hops = (2 * lanes, lanes, 2 * lanes + 1, lanes + 1)
    landed = []
    for sent, mask in zip(ready, hops):
        landed.append(hop(sent, mask))
        landed[-2:] = lax.optimization_barrier(tuple(landed[-2:]))
    half = lanes // 2
    joined = pl.pallas_call(
        functools.partial(join_kernel, per_peer),
        out_shape=(block(4 * per_peer),) * half,
        in_specs=[vmem] * 4,
        out_specs=[vmem] * half,
        compiler_params=params(),
        cost_estimate=pl.CostEstimate(flops=2**40, bytes_accessed=2**20, transcendentals=0),
    )(*landed)
    joined = [sent if i == 0 else hop(sent, 2 * i) for i, sent in enumerate(joined)]
    new_history = pl.pallas_call(
        functools.partial(land_kernel, devices, per_peer),
        out_shape=jax.ShapeDtypeStruct((nodes, devices * per_peer), f32),
        in_specs=[vmem] * (1 + half),
        out_specs=pl.BlockSpec(memory_space=pl.ANY),
        scratch_shapes=[pltpu.VMEM((8, nodes, LANES), f32), pltpu.SemaphoreType.DMA((8,)),
                        pltpu.VMEM((2, group, deep), f32)],
        compiler_params=params(),
    )(pair, *joined)
    return (new_history, stress_out)


def solution(mesh):
    return jax.shard_map(
        shards,
        mesh=mesh,
        in_specs=(
            P(None, ("macro", "pool")),
            P(None, ("macro", "pool")),
            P(None, ("macro", "pool")),
            P(("macro", "pool"), None),
            P(("macro", "pool"), None),
            P(),
            P(),
            P(),
            P(),
        ),
        out_specs=(P(None, ("macro", "pool")), P(None, ("macro", "pool"))),
        check_vma=False,
    )
```

```python
import functools
import math

import jax
import jax.numpy as jnp
from jax import lax
from jax.experimental import pallas as pl
from jax.experimental.pallas import tpu as pltpu
from jax.sharding import PartitionSpec as P

ITERS = 3
LANES = 128
PLANES = 4
PATTERN = 32

NN = (((1,), (0,)), ((), ()))
NT = (((1,), (1,)), ((), ()))
TN = (((0,), (0,)), ((), ()))


def up(value, unit):
    return -(-value // unit) * unit


def dot(a, b, dims=NN):
    return lax.dot_general(a, b, dims, preferred_element_type=jnp.float32)


def halves(x):
    hi = x.astype(jnp.bfloat16)
    lo = (x - hi.astype(jnp.float32)).astype(jnp.bfloat16)
    return hi, lo


def whereabouts(devices):
    me = lax.axis_index("macro") * lax.axis_size("pool") + lax.axis_index("pool")
    lanes = devices // PLANES
    return me, me // lanes, me % lanes, lanes


def hot(row, count):
    rows = lax.broadcasted_iota(jnp.int32, (count, row.shape[1]), 0)
    return jnp.where(rows == row, 1.0, 0.0).astype(jnp.bfloat16)


def pack_kernel(coupling, plastic, strain, owner, qp, pattern, small):
    top = 0
    for c in range(coupling.shape[0]):
        small[top:top + coupling.shape[1], :] = coupling[c]
        top += coupling.shape[1]
    for part in (plastic, strain, owner, qp):
        small[top:top + part.shape[0], 0:part.shape[1]] = part[...].astype(jnp.float32)
        top += part.shape[0]
    count = pattern.shape[0]
    for a in range(count):
        for b in range(count):
            couples = jnp.full((1, LANES), pattern[a, b].astype(jnp.float32))
            small[PATTERN + a * count + b:PATTERN + a * count + b + 1, 0:LANES] = couples


def prep_kernel(devices, per_peer, comps, voigt, *refs):
    sources, outs, (kfull, pad), local, sem = refs[:4], refs[4:13], refs[13:15], refs[15:19], refs[19]
    khi, klo, hist_s, weight_s, strain_s, place_s, qp_s, cstack, pdir = outs
    small, stiff, hist, flag = local
    copies = [
        pltpu.make_async_copy(source, target, sem.at[i])
        for i, (source, target) in enumerate(zip(sources, local))
    ]
    for copy in copies:
        copy.start()
    nodes, columns = hist.shape
    nb, blk = stiff.shape[0], stiff.shape[2]
    at_plastic = comps * voigt
    at_strain = at_plastic + comps
    at_owner = at_strain + voigt
    copies[0].wait()

    me, plane, lane, lanes = whereabouts(devices)
    owner = small[at_owner:at_owner + 1, 0:columns].astype(jnp.int32)
    apart = owner // lanes ^ plane
    target = owner % lanes
    away = target ^ lane
    hopping = (away % 2 * 2 + jnp.where(apart == 2, 0, 1)) * (lanes // 2) + away // 2
    staying = jnp.where(apart == 3, 2, 3) * lanes + target
    key = jnp.where((apart == 2) | (apart == 1), hopping, staying)
    key_ids = lax.broadcasted_iota(jnp.int32, (devices, columns), 0)
    mine = jnp.where(key_ids == key, 1.0, 0.0)
    earlier = jnp.where(
        lax.broadcasted_iota(jnp.int32, (columns, columns), 0)
        < lax.broadcasted_iota(jnp.int32, (columns, columns), 1), 1.0, 0.0
    ).astype(jnp.bfloat16)
    before = dot(mine.astype(jnp.bfloat16), earlier)
    rank = jnp.sum(before * mine, axis=0, keepdims=True)
    tally = jnp.sum(mine, axis=1, keepdims=True)
    ahead = jnp.where(key_ids < key, tally, 0.0)
    position = (rank + jnp.sum(ahead, axis=0, keepdims=True)).astype(jnp.int32)

    order = hot(position, columns)
    pad[...] = jnp.zeros_like(pad)
    pad[0:1, :] = key.astype(jnp.float32)
    pad[1:2, :] = rank
    placed = dot(pad[...].astype(jnp.bfloat16), order, NT)
    place_s[...] = jnp.broadcast_to(
        (placed[0:1, :] * per_peer + placed[1:2, :]).astype(jnp.int32), place_s.shape
    )

    pad[0:1, :] = (position // 256).astype(jnp.float32)
    pad[1:2, :] = (position % 256).astype(jnp.float32)
    found = dot(pad[...].astype(jnp.bfloat16), hot(small[at_owner + 1:at_owner + 2, 0:columns].astype(jnp.int32), columns))
    at = (found[0:1, :] * 256.0 + found[1:2, :]).astype(jnp.int32)
    qp_s[...] = jnp.broadcast_to(at, qp_s.shape)
    pad[...] = jnp.zeros_like(pad)
    pad[0:voigt, :] = small[at_strain:at_owner, 0:columns]
    hi, lo = halves(pad[...])
    serves = hot(at, columns)
    strain_s[...] = dot(hi, serves, NT) + dot(lo, serves, NT)

    kfull[...] = jnp.zeros_like(kfull)
    copies[1].wait()
    for a in range(nb):
        for b in range(nb):
            kfull[a * blk:(a + 1) * blk, b * blk:(b + 1) * blk] = (
                stiff[a, b] * small[PATTERN + a * nb + b:PATTERN + a * nb + b + 1, 0:blk]
            )
    k = kfull[...]
    kh = k.astype(jnp.bfloat16)
    khi[...] = kh
    klo[...] = (k - kh.astype(jnp.float32)).astype(jnp.bfloat16)

    copies[2].wait()
    copies[3].wait()
    hi, lo = halves(hist[...])
    hist_s[...] = jnp.zeros_like(hist_s)
    hist_s[0:nodes, :] = dot(hi, order, NT) + dot(lo, order, NT)
    h = hist_s[...]
    weight_s[...] = jnp.zeros_like(weight_s)
    weight_s[0:nodes, :] = dot(flag[...].astype(jnp.float32).astype(jnp.bfloat16), order, NT)
    weight_s[...] = weight_s[...] * h * h / (1.0 + h * h)

    cstack[...] = jnp.zeros_like(cstack)
    for c in range(comps):
        cpl = small[c * voigt:(c + 1) * voigt, :]
        hi = cpl.astype(jnp.bfloat16).astype(jnp.float32)
        cstack[c, 0:voigt, 0:nodes] = hi
        cstack[c, 8:8 + voigt, 0:nodes] = hi
        cstack[c, 16:16 + voigt, 0:nodes] = cpl - hi
    pdir[...] = jnp.zeros_like(pdir)
    for c in range(comps):
        spread = jnp.broadcast_to(small[at_plastic + c:at_plastic + c + 1, :], (LANES, nodes))
        pdir[c, 0:nodes, :] = jnp.transpose(spread)


def sweep(rows, comps, span):
    pieces = 4 * span // LANES
    cuts = [rows // 16 * i // pieces * 16 for i in range(pieces + 1)]
    for top, end in zip(cuts, cuts[1:]):
        for c in range(comps):
            yield slice(top, end), slice(c * span, (c + 1) * span), c


def fold(x):
    return jnp.sum(x.reshape(x.shape[0] // 8, 8, x.shape[1]), axis=0)


def total(parts):
    return jnp.sum(parts, axis=0, keepdims=True)


def solve_kernel(scale, first, earlier, khi, klo, hist, weight, strain, cstack, pdir, place, *refs):
    earlier_updated, refs = refs[:earlier], refs[earlier:]
    updated, stress, blocks = refs[0], refs[1], refs[2:-5]
    field, resid, image, solved, split = refs[-5:]
    rows, span = hist.shape
    comps = pdir.shape[0]
    wide = comps * span
    zero = jnp.zeros((8, span), jnp.float32)

    def flow(c, r):
        return jnp.concatenate([pdir[c, r, :]] * (span // LANES), axis=1)

    def keep(r, c, x):
        split[r, c * span:(c + 1) * span], split[r, wide + c * span:wide + (c + 1) * span] = (
            halves(x)
        )

    s = strain[...]
    s_hi = s.astype(jnp.bfloat16).astype(jnp.float32)
    s3 = jnp.concatenate([s_hi, s - s_hi, s_hi, jnp.zeros_like(s)], axis=0).astype(jnp.bfloat16)
    split[rows:, :] = jnp.zeros((split.shape[0] - rows, 2 * wide), jnp.bfloat16)
    for c in range(comps):
        image[:, c * span:(c + 1) * span] = dot(cstack[c].astype(jnp.bfloat16), s3, TN)
    parts = zero
    for r, l, c in sweep(rows, comps, span):
        d = image[r, l] - weight[r, :] * hist[r, :] * flow(c, r)
        resid[r, l] = d
        field[r, l] = d
        keep(r, c, d)
        parts = parts + fold(d * d)
    norm = total(parts)
    for step in range(ITERS):
        both = dot(khi[...], split[...])
        image[...] = both[:, 0:wide] + both[:, wide:] + dot(klo[...], split[:, 0:wide])
        parts = zero
        for r, l, c in sweep(rows, comps, span):
            d = field[r, l]
            q = image[r, l] + (1.5 - weight[r, :]) * d
            image[r, l] = q
            parts = parts + fold(d * q)
        alpha = norm / jnp.maximum(total(parts), 1.0)
        if step == ITERS - 1:
            break
        parts = zero
        for r, l, c in sweep(rows, comps, span):
            gain = alpha * field[r, l]
            solved[r, l] = gain if step == 0 else solved[r, l] + gain
            left = resid[r, l] - alpha * image[r, l]
            resid[r, l] = left
            parts = parts + fold(left * left)
        following = total(parts)
        beta = following / jnp.maximum(norm, 1.0)
        norm = following
        for r, l, c in sweep(rows, comps, span):
            d = resid[r, l] + beta * field[r, l]
            field[r, l] = d
            keep(r, c, d)
    for r, l, c in sweep(rows, comps, span):
        x = solved[r, l] + alpha * field[r, l]
        pushed = flow(c, r) * x
        image[r, 0:span] = pushed if c == 0 else image[r, 0:span] + pushed
        keep(r, c, (1.5 - weight[r, :]) * x)
    updated[...] = hist[...] + weight[...] * image[:, 0:span]
    top, count = 0, sum(block.shape[0] for block in blocks)
    sent = placed_rows(first, count, place, [*earlier_updated, updated])
    for block in blocks:
        put(block, 0, sent[top:top + block.shape[0]])
        top += block.shape[0]
    out = s
    for c in range(comps):
        cpl = cstack[c].astype(jnp.bfloat16)
        main = dot(cpl, split[0:rows, c * span:(c + 1) * span])
        minor = dot(cpl, split[0:rows, wide + c * span:wide + (c + 1) * span])
        out = out + scale * (main[0:8] + main[16:24] + minor[0:8])
    stress[...] = out


def placed_rows(first, count, place, sources):
    width = sum(source.shape[1] for source in sources)
    placing = hot(place[0:1, 0:width] - first, count)
    sums, left = 0.0, 0
    for source in sources:
        hi, lo = halves(source[...])
        cut = placing[:, left:left + source.shape[1]]
        sums = sums + (dot(cut, hi, NT) + dot(cut, lo, NT))
        left += source.shape[1]
    return sums


def put(block, top, rows):
    height, filled = rows.shape
    block[pl.ds(top, height), 0:filled] = rows
    rest = jnp.zeros((height, block.shape[1] - filled), jnp.float32)
    block[pl.ds(top, height), filled:] = rest


def ship_kernel(devices, first, chunks, place, at, *refs):
    updated, stress, (pair, out) = refs[:chunks], refs[chunks:2 * chunks], refs[2 * chunks:]
    me, plane, lane, lanes = whereabouts(devices)
    group = pair.shape[0] // 2
    rows = placed_rows(first, 2 * group, place, updated)
    put(pair, pl.multiple_of((1 - plane // 2) * group, group), rows[0:group])
    put(pair, pl.multiple_of(plane // 2 * group, group), rows[group:])
    hi, lo = halves(jnp.concatenate([ref[...] for ref in stress], axis=1))
    serves = hot(at[0:1, :], hi.shape[1])
    out[...] = (dot(hi, serves) + dot(lo, serves))[0:out.shape[0], :]


def join_kernel(cap, *refs):
    landed, blocks = refs[:3], refs[3:]
    for i, block in enumerate(blocks):
        for k, rows in enumerate(landed):
            block[k * cap:(k + 1) * cap, :] = rows[i * cap:(i + 1) * cap, :]


def land(tile, out, stage, sem, slot, at):
    nodes = out.shape[0]
    stage[slot] = jnp.transpose(tile)[0:nodes, :]
    columns = pl.multiple_of(at * LANES, LANES)
    copy = pltpu.make_async_copy(stage.at[slot], out.at[:, pl.ds(columns, LANES)], sem.at[slot])
    copy.start()
    return copy


def land_group(block, count, plane, out, stage, sem, slot):
    height = block.shape[0] // count
    copies = []
    for part in range(count):
        tile = block[part * height:(part + 1) * height, :]
        copies.append(land(tile, out, stage, sem, slot + part, plane * count + part))
    return copies


def land_kernel(devices, cap, pair, *refs):
    blocks, (out, stage, sem, gather) = refs[:-4], refs[-4:]
    me, plane, lane, lanes = whereabouts(devices)
    group = pair.shape[0] // 2
    copies = []
    for part in range(2):
        source = jnp.where(plane // 2 == part, plane, plane ^ 3)
        block = pair.at[part * group:(part + 1) * group, :]
        copies += land_group(block, 2, source, out, stage, sem, 2 * part)
    for i, apart in enumerate((2, 1)):
        for k in range(lanes):
            at = pl.multiple_of((lane ^ k) * cap, cap)
            if i == 1 and k % 2 == 1:
                gather[i, pl.ds(at, cap), :] = blocks[lanes // 2 + k // 2][...]
            else:
                top = (2 * (k % 2) + i) * cap
                gather[i, pl.ds(at, cap), :] = blocks[k // 2][top:top + cap, :]
        copies += land_group(gather.at[i], 2, plane ^ apart, out, stage, sem, 4 + 2 * i)
    for copy in copies:
        copy.wait()


def params(mib=24):
    return pltpu.CompilerParams(vmem_limit_bytes=mib * 2**20)


def shards(
    history, yield_flags, strain, qp_to_rve, new_owner, stiffness, pattern, coupling, plastic_dir
):
    devices = lax.axis_size(("macro", "pool"))
    nodes, columns = history.shape
    comps, voigt = coupling.shape[0], coupling.shape[1]
    per_peer = 2 * columns // devices
    rows = up(nodes, 32)
    deep = up(nodes, 256)
    f32, bf16, i32 = jnp.float32, jnp.bfloat16, jnp.int32
    vmem = pl.BlockSpec(memory_space=pltpu.VMEM)
    small_inputs = (coupling, plastic_dir, strain, new_owner.reshape(1, columns), qp_to_rve, pattern)
    small = pl.pallas_call(
        pack_kernel,
        out_shape=jax.ShapeDtypeStruct((up(PATTERN + pattern.size, 8), nodes), f32),
        in_specs=[vmem] * 5 + [pl.BlockSpec(memory_space=pltpu.SMEM)],
        out_specs=vmem,
        compiler_params=params(60),
    )(*small_inputs)
    inputs = (small, stiffness, history, yield_flags)
    khi, klo, hist_s, weight_s, strain_s, place_s, qp_s, cstack, pdir = pl.pallas_call(
        functools.partial(prep_kernel, devices, per_peer, comps, voigt),
        out_shape=(
            jax.ShapeDtypeStruct((rows, deep), bf16),
            jax.ShapeDtypeStruct((rows, deep), bf16),
            jax.ShapeDtypeStruct((rows, columns), f32),
            jax.ShapeDtypeStruct((rows, columns), f32),
            jax.ShapeDtypeStruct((8, columns), f32),
            jax.ShapeDtypeStruct((8, columns), i32),
            jax.ShapeDtypeStruct((8, columns), i32),
            jax.ShapeDtypeStruct((comps, 32, rows), f32),
            jax.ShapeDtypeStruct((comps, rows, LANES), f32),
        ),
        in_specs=[pl.BlockSpec(memory_space=pltpu.HBM)] * 4,
        out_specs=[vmem] * 9,
        scratch_shapes=[pltpu.VMEM((rows, deep), f32), pltpu.VMEM((8, columns), f32)]
        + [pltpu.VMEM(x.shape, x.dtype) for x in inputs]
        + [pltpu.SemaphoreType.DMA((4,))],
        compiler_params=params(46),
    )(*inputs)

    lanes = devices // PLANES
    half = lanes // 2
    group = lanes * per_peer
    block = lambda height: jax.ShapeDtypeStruct((height, deep), f32)
    whole = lambda shape: pl.BlockSpec(shape, lambda i: (0,) * len(shape))
    updated, stress_s, ready = [], [], []
    left = 0
    for span in (LANES,) * (columns // LANES):
        part = lambda height: pl.BlockSpec((height, span), lambda i, at=left // span: (0, at))
        wide = comps * span
        outs = [block(LANES)] if len(updated) < 3 else [block(per_peer)] * half
        done = pl.pallas_call(
            functools.partial(solve_kernel, 1.0 / math.sqrt(comps * nodes), left, len(updated)),
            grid=(1,),
            out_shape=(
                jax.ShapeDtypeStruct((rows, span), f32),
                jax.ShapeDtypeStruct((8, span), f32),
                *outs,
            ),
            in_specs=[whole((rows, deep)), whole((rows, deep)), part(rows), part(rows), part(8),
                      whole((comps, 32, rows)), whole((comps, rows, LANES)), whole((8, columns))]
            + [whole(u.shape) for u in updated],
            out_specs=[whole((rows, span)), whole((8, span))] + [whole(o.shape) for o in outs],
            scratch_shapes=[pltpu.VMEM((rows, wide), f32) for _ in range(4)]
            + [pltpu.VMEM((deep, 2 * wide), bf16)],
            compiler_params=params(),
            cost_estimate=pl.CostEstimate(
                flops=18 * rows * deep * wide, bytes_accessed=2**20, transcendentals=0
            ),
        )(khi, klo, hist_s, weight_s, strain_s, cstack, pdir, place_s, *updated)
        updated.append(done[0])
        stress_s.append(done[1])
        ready.append(done[2:])
        left += span
    pair, stress_out = pl.pallas_call(
        functools.partial(ship_kernel, devices, 2 * group, len(updated)),
        out_shape=(block(2 * group), jax.ShapeDtypeStruct((voigt, columns), f32)),
        in_specs=[vmem] * (2 + 2 * len(updated)),
        out_specs=[vmem] * 2,
        compiler_params=params(),
        cost_estimate=pl.CostEstimate(
            flops=4 * rows * columns * columns, bytes_accessed=2**20, transcendentals=0
        ),
    )(place_s, qp_s, *updated, *stress_s)

    axes = ("macro", "pool")

    def hop(sent, mask):
        return lax.ppermute(sent, axes, [(s, s ^ mask) for s in range(devices)])

    pair, *straight = lax.optimization_barrier((pair, *ready[-1]))
    planes = [list(range(z * lanes, (z + 1) * lanes)) for z in range(PLANES)]
    pair = lax.all_to_all(
        pair.reshape(2 * lanes, per_peer, deep), axes, split_axis=0, concat_axis=0, tiled=True,
        axis_index_groups=[planes[0] + planes[3], planes[1] + planes[2]],
    ).reshape(2 * group, deep)
    hops = (2 * lanes, lanes, 2 * lanes + 1)
    landed = []
    for (sent,), mask in zip(ready, hops):
        landed.append(hop(sent, mask))
        landed[-2:] = lax.optimization_barrier(tuple(landed[-2:]))
    joined = pl.pallas_call(
        functools.partial(join_kernel, per_peer),
        out_shape=(block(3 * per_peer),) * half,
        in_specs=[vmem] * 3,
        out_specs=[vmem] * half,
        compiler_params=params(),
        cost_estimate=pl.CostEstimate(flops=2**40, bytes_accessed=2**20, transcendentals=0),
    )(*landed)
    joined = [sent if i == 0 else hop(sent, 2 * i) for i, sent in enumerate(joined)]
    direct = [hop(sent, lanes + 2 * i + 1) for i, sent in enumerate(straight)]
    new_history = pl.pallas_call(
        functools.partial(land_kernel, devices, per_peer),
        out_shape=jax.ShapeDtypeStruct((nodes, devices * per_peer), f32),
        in_specs=[vmem] * (1 + 2 * half),
        out_specs=pl.BlockSpec(memory_space=pl.ANY),
        scratch_shapes=[pltpu.VMEM((8, nodes, LANES), f32), pltpu.SemaphoreType.DMA((8,)),
                        pltpu.VMEM((2, group, deep), f32)],
        compiler_params=params(),
    )(pair, *joined, *direct)
    return (new_history, stress_out)


def solution(mesh):
    return jax.shard_map(
        shards,
        mesh=mesh,
        in_specs=(
            P(None, ("macro", "pool")),
            P(None, ("macro", "pool")),
            P(None, ("macro", "pool")),
            P(("macro", "pool"), None),
            P(("macro", "pool"), None),
            P(),
            P(),
            P(),
            P(),
        ),
        out_specs=(P(None, ("macro", "pool")), P(None, ("macro", "pool"))),
        check_vma=False,
    )
```

```python
import functools
import math

import jax
import jax.numpy as jnp
from jax import lax
from jax.experimental import pallas as pl
from jax.experimental.pallas import tpu as pltpu
from jax.sharding import PartitionSpec as P

ITERS = 3
LANES = 128
PLANES = 4
PATTERN = 32

NN = (((1,), (0,)), ((), ()))
NT = (((1,), (1,)), ((), ()))
TN = (((0,), (0,)), ((), ()))


def up(value, unit):
    return -(-value // unit) * unit


def dot(a, b, dims=NN):
    return lax.dot_general(a, b, dims, preferred_element_type=jnp.float32)


def halves(x):
    hi = x.astype(jnp.bfloat16)
    lo = (x - hi.astype(jnp.float32)).astype(jnp.bfloat16)
    return hi, lo


def whereabouts(devices):
    me = lax.axis_index("macro") * lax.axis_size("pool") + lax.axis_index("pool")
    lanes = devices // PLANES
    return me, me // lanes, me % lanes, lanes


def hot(row, count):
    rows = lax.broadcasted_iota(jnp.int32, (count, row.shape[1]), 0)
    return jnp.where(rows == row, 1.0, 0.0).astype(jnp.bfloat16)


def pack_kernel(coupling, plastic, strain, owner, qp, pattern, small):
    top = 0
    for c in range(coupling.shape[0]):
        small[top:top + coupling.shape[1], :] = coupling[c]
        top += coupling.shape[1]
    for part in (plastic, strain, owner, qp):
        small[top:top + part.shape[0], 0:part.shape[1]] = part[...].astype(jnp.float32)
        top += part.shape[0]
    count = pattern.shape[0]
    for a in range(count):
        for b in range(count):
            couples = jnp.full((1, LANES), pattern[a, b].astype(jnp.float32))
            small[PATTERN + a * count + b:PATTERN + a * count + b + 1, 0:LANES] = couples


def prep_kernel(devices, per_peer, comps, voigt, *refs):
    sources, outs, (kfull, pad), local, sem = refs[:4], refs[4:13], refs[13:15], refs[15:19], refs[19]
    khi, klo, hist_s, weight_s, strain_s, place_s, qp_s, cstack, pdir = outs
    small, stiff, hist, flag = local
    copies = [
        pltpu.make_async_copy(source, target, sem.at[i])
        for i, (source, target) in enumerate(zip(sources, local))
    ]
    for copy in copies:
        copy.start()
    nodes, columns = hist.shape
    nb, blk = stiff.shape[0], stiff.shape[2]
    at_plastic = comps * voigt
    at_strain = at_plastic + comps
    at_owner = at_strain + voigt
    copies[0].wait()

    me, plane, lane, lanes = whereabouts(devices)
    owner = small[at_owner:at_owner + 1, 0:columns].astype(jnp.int32)
    apart = owner // lanes ^ plane
    target = owner % lanes
    away = target ^ lane
    hopping = (away % 2 * 2 + jnp.where(apart == 2, 0, 1)) * (lanes // 2) + away // 2
    staying = jnp.where(apart == 3, 2, 3) * lanes + target
    key = jnp.where((apart == 2) | (apart == 1), hopping, staying)
    key_ids = lax.broadcasted_iota(jnp.int32, (devices, columns), 0)
    mine = jnp.where(key_ids == key, 1.0, 0.0)
    earlier = jnp.where(
        lax.broadcasted_iota(jnp.int32, (columns, columns), 0)
        < lax.broadcasted_iota(jnp.int32, (columns, columns), 1), 1.0, 0.0
    ).astype(jnp.bfloat16)
    before = dot(mine.astype(jnp.bfloat16), earlier)
    rank = jnp.sum(before * mine, axis=0, keepdims=True)
    tally = jnp.sum(mine, axis=1, keepdims=True)
    ahead = jnp.where(key_ids < key, tally, 0.0)
    position = (rank + jnp.sum(ahead, axis=0, keepdims=True)).astype(jnp.int32)

    order = hot(position, columns)
    pad[...] = jnp.zeros_like(pad)
    pad[0:1, :] = key.astype(jnp.float32)
    pad[1:2, :] = rank
    placed = dot(pad[...].astype(jnp.bfloat16), order, NT)
    place_s[...] = jnp.broadcast_to(
        (placed[0:1, :] * per_peer + placed[1:2, :]).astype(jnp.int32), place_s.shape
    )

    pad[0:1, :] = (position // 256).astype(jnp.float32)
    pad[1:2, :] = (position % 256).astype(jnp.float32)
    found = dot(pad[...].astype(jnp.bfloat16), hot(small[at_owner + 1:at_owner + 2, 0:columns].astype(jnp.int32), columns))
    at = (found[0:1, :] * 256.0 + found[1:2, :]).astype(jnp.int32)
    qp_s[...] = jnp.broadcast_to(at, qp_s.shape)
    pad[...] = jnp.zeros_like(pad)
    pad[0:voigt, :] = small[at_strain:at_owner, 0:columns]
    hi, lo = halves(pad[...])
    serves = hot(at, columns)
    strain_s[...] = dot(hi, serves, NT) + dot(lo, serves, NT)

    kfull[...] = jnp.zeros_like(kfull)
    copies[1].wait()
    for a in range(nb):
        for b in range(nb):
            kfull[a * blk:(a + 1) * blk, b * blk:(b + 1) * blk] = (
                stiff[a, b] * small[PATTERN + a * nb + b:PATTERN + a * nb + b + 1, 0:blk]
            )
    k = kfull[...]
    kh = k.astype(jnp.bfloat16)
    khi[...] = kh
    klo[...] = (k - kh.astype(jnp.float32)).astype(jnp.bfloat16)

    copies[2].wait()
    copies[3].wait()
    hi, lo = halves(hist[...])
    hist_s[...] = jnp.zeros_like(hist_s)
    hist_s[0:nodes, :] = dot(hi, order, NT) + dot(lo, order, NT)
    h = hist_s[...]
    weight_s[...] = jnp.zeros_like(weight_s)
    weight_s[0:nodes, :] = dot(flag[...].astype(jnp.float32).astype(jnp.bfloat16), order, NT)
    weight_s[...] = weight_s[...] * h * h / (1.0 + h * h)

    cstack[...] = jnp.zeros_like(cstack)
    for c in range(comps):
        cpl = small[c * voigt:(c + 1) * voigt, :]
        hi = cpl.astype(jnp.bfloat16).astype(jnp.float32)
        cstack[c, 0:voigt, 0:nodes] = hi
        cstack[c, 8:8 + voigt, 0:nodes] = hi
        cstack[c, 16:16 + voigt, 0:nodes] = cpl - hi
    pdir[...] = jnp.zeros_like(pdir)
    for c in range(comps):
        spread = jnp.broadcast_to(small[at_plastic + c:at_plastic + c + 1, :], (LANES, nodes))
        pdir[c, 0:nodes, :] = jnp.transpose(spread)


def row_blocks(rows, span):
    pieces = 4 * span // LANES
    cuts = [rows // 16 * i // pieces * 16 for i in range(pieces + 1)]
    return [slice(top, end) for top, end in zip(cuts, cuts[1:])]


def sweep(rows, comps, span):
    for r in row_blocks(rows, span):
        for c in range(comps):
            yield r, slice(c * span, (c + 1) * span), c


def fold(x):
    return jnp.sum(x.reshape(x.shape[0] // 8, 8, x.shape[1]), axis=0)


def total(parts):
    return jnp.sum(parts, axis=0, keepdims=True)


def solve_kernel(scale, first, earlier, khi, klo, hist, weight, strain, cstack, pdir, place, *refs):
    earlier_updated, refs = refs[:earlier], refs[earlier:]
    updated, stress, blocks = refs[0], refs[1], refs[2:-5]
    field, resid, image, solved, split = refs[-5:]
    rows, span = hist.shape
    comps = pdir.shape[0]
    wide = comps * span
    zero = jnp.zeros((8, span), jnp.float32)

    def flow(c, r):
        return jnp.concatenate([pdir[c, r, :]] * (span // LANES), axis=1)

    def keep(r, c, x):
        split[r, c * span:(c + 1) * span], split[r, wide + c * span:wide + (c + 1) * span] = (
            halves(x)
        )

    s = strain[...]
    s_hi = s.astype(jnp.bfloat16).astype(jnp.float32)
    s3 = jnp.concatenate([s_hi, s - s_hi, s_hi, jnp.zeros_like(s)], axis=0).astype(jnp.bfloat16)
    split[rows:, :] = jnp.zeros((split.shape[0] - rows, 2 * wide), jnp.bfloat16)
    for c in range(comps):
        image[:, c * span:(c + 1) * span] = dot(cstack[c].astype(jnp.bfloat16), s3, TN)
    parts = zero
    for r, l, c in sweep(rows, comps, span):
        d = image[r, l] - weight[r, :] * hist[r, :] * flow(c, r)
        resid[r, l] = d
        field[r, l] = d
        keep(r, c, d)
        parts = parts + fold(d * d)
    norm = total(parts)
    for step in range(ITERS):
        parts = zero
        for r in row_blocks(rows, span):
            both = dot(khi[r, :], split[...])
            low = dot(klo[r, :], split[:, 0:wide])
            tangent = 1.5 - weight[r, :]
            for c in range(comps):
                l = slice(c * span, (c + 1) * span)
                d = field[r, l]
                q = both[:, l] + both[:, wide + c * span:wide + (c + 1) * span] + low[:, l]
                q = q + tangent * d
                image[r, l] = q
                parts = parts + fold(d * q)
        alpha = norm / jnp.maximum(total(parts), 1.0)
        if step == ITERS - 1:
            break
        parts = zero
        for r, l, c in sweep(rows, comps, span):
            gain = alpha * field[r, l]
            solved[r, l] = gain if step == 0 else solved[r, l] + gain
            left = resid[r, l] - alpha * image[r, l]
            resid[r, l] = left
            parts = parts + fold(left * left)
        following = total(parts)
        beta = following / jnp.maximum(norm, 1.0)
        norm = following
        for r, l, c in sweep(rows, comps, span):
            d = resid[r, l] + beta * field[r, l]
            field[r, l] = d
            keep(r, c, d)
    for r, l, c in sweep(rows, comps, span):
        x = solved[r, l] + alpha * field[r, l]
        pushed = flow(c, r) * x
        image[r, 0:span] = pushed if c == 0 else image[r, 0:span] + pushed
        keep(r, c, (1.5 - weight[r, :]) * x)
    updated[...] = hist[...] + weight[...] * image[:, 0:span]
    top, count = 0, sum(block.shape[0] for block in blocks)
    sent = placed_rows(first, count, place, [*earlier_updated, updated])
    for block in blocks:
        put(block, 0, sent[top:top + block.shape[0]])
        top += block.shape[0]
    out = s
    for c in range(comps):
        cpl = cstack[c].astype(jnp.bfloat16)
        main = dot(cpl, split[0:rows, c * span:(c + 1) * span])
        minor = dot(cpl, split[0:rows, wide + c * span:wide + (c + 1) * span])
        out = out + scale * (main[0:8] + main[16:24] + minor[0:8])
    stress[...] = out


def placed_rows(first, count, place, sources):
    width = sum(source.shape[1] for source in sources)
    placing = hot(place[0:1, 0:width] - first, count)
    sums, left = 0.0, 0
    for source in sources:
        hi, lo = halves(source[...])
        cut = placing[:, left:left + source.shape[1]]
        sums = sums + (dot(cut, hi, NT) + dot(cut, lo, NT))
        left += source.shape[1]
    return sums


def put(block, top, rows):
    height, filled = rows.shape
    block[pl.ds(top, height), 0:filled] = rows
    rest = jnp.zeros((height, block.shape[1] - filled), jnp.float32)
    block[pl.ds(top, height), filled:] = rest


def ship_kernel(devices, first, chunks, place, at, *refs):
    updated, stress, (pair, out) = refs[:chunks], refs[chunks:2 * chunks], refs[2 * chunks:]
    me, plane, lane, lanes = whereabouts(devices)
    group = pair.shape[0] // 2
    rows = placed_rows(first, 2 * group, place, updated)
    put(pair, pl.multiple_of((1 - plane // 2) * group, group), rows[0:group])
    put(pair, pl.multiple_of(plane // 2 * group, group), rows[group:])
    hi, lo = halves(jnp.concatenate([ref[...] for ref in stress], axis=1))
    serves = hot(at[0:1, :], hi.shape[1])
    out[...] = (dot(hi, serves) + dot(lo, serves))[0:out.shape[0], :]


def join_kernel(cap, *refs):
    landed, blocks = refs[:3], refs[3:]
    for i, block in enumerate(blocks):
        for k, rows in enumerate(landed):
            block[k * cap:(k + 1) * cap, :] = rows[i * cap:(i + 1) * cap, :]


def land(tile, out, stage, sem, slot, at):
    nodes = out.shape[0]
    stage[slot] = jnp.transpose(tile)[0:nodes, :]
    columns = pl.multiple_of(at * LANES, LANES)
    copy = pltpu.make_async_copy(stage.at[slot], out.at[:, pl.ds(columns, LANES)], sem.at[slot])
    copy.start()
    return copy


def land_group(block, count, plane, out, stage, sem, slot):
    height = block.shape[0] // count
    copies = []
    for part in range(count):
        tile = block[part * height:(part + 1) * height, :]
        copies.append(land(tile, out, stage, sem, slot + part, plane * count + part))
    return copies


def land_kernel(devices, cap, pair, *refs):
    blocks, (out, stage, sem, gather) = refs[:-4], refs[-4:]
    me, plane, lane, lanes = whereabouts(devices)
    group = pair.shape[0] // 2
    copies = []
    for part in range(2):
        source = jnp.where(plane // 2 == part, plane, plane ^ 3)
        block = pair.at[part * group:(part + 1) * group, :]
        copies += land_group(block, 2, source, out, stage, sem, 2 * part)
    for i, apart in enumerate((2, 1)):
        for k in range(lanes):
            at = pl.multiple_of((lane ^ k) * cap, cap)
            if i == 1 and k % 2 == 1:
                gather[i, pl.ds(at, cap), :] = blocks[lanes // 2 + k // 2][...]
            else:
                top = (2 * (k % 2) + i) * cap
                gather[i, pl.ds(at, cap), :] = blocks[k // 2][top:top + cap, :]
        copies += land_group(gather.at[i], 2, plane ^ apart, out, stage, sem, 4 + 2 * i)
    for copy in copies:
        copy.wait()


def params(mib=24):
    return pltpu.CompilerParams(vmem_limit_bytes=mib * 2**20)


def shards(
    history, yield_flags, strain, qp_to_rve, new_owner, stiffness, pattern, coupling, plastic_dir
):
    devices = lax.axis_size(("macro", "pool"))
    nodes, columns = history.shape
    comps, voigt = coupling.shape[0], coupling.shape[1]
    per_peer = 2 * columns // devices
    rows = up(nodes, 32)
    deep = up(nodes, 256)
    f32, bf16, i32 = jnp.float32, jnp.bfloat16, jnp.int32
    vmem = pl.BlockSpec(memory_space=pltpu.VMEM)
    small_inputs = (coupling, plastic_dir, strain, new_owner.reshape(1, columns), qp_to_rve, pattern)
    small = pl.pallas_call(
        pack_kernel,
        out_shape=jax.ShapeDtypeStruct((up(PATTERN + pattern.size, 8), nodes), f32),
        in_specs=[vmem] * 5 + [pl.BlockSpec(memory_space=pltpu.SMEM)],
        out_specs=vmem,
        compiler_params=params(60),
    )(*small_inputs)
    inputs = (small, stiffness, history, yield_flags)
    khi, klo, hist_s, weight_s, strain_s, place_s, qp_s, cstack, pdir = pl.pallas_call(
        functools.partial(prep_kernel, devices, per_peer, comps, voigt),
        out_shape=(
            jax.ShapeDtypeStruct((rows, deep), bf16),
            jax.ShapeDtypeStruct((rows, deep), bf16),
            jax.ShapeDtypeStruct((rows, columns), f32),
            jax.ShapeDtypeStruct((rows, columns), f32),
            jax.ShapeDtypeStruct((8, columns), f32),
            jax.ShapeDtypeStruct((8, columns), i32),
            jax.ShapeDtypeStruct((8, columns), i32),
            jax.ShapeDtypeStruct((comps, 32, rows), f32),
            jax.ShapeDtypeStruct((comps, rows, LANES), f32),
        ),
        in_specs=[pl.BlockSpec(memory_space=pltpu.HBM)] * 4,
        out_specs=[vmem] * 9,
        scratch_shapes=[pltpu.VMEM((rows, deep), f32), pltpu.VMEM((8, columns), f32)]
        + [pltpu.VMEM(x.shape, x.dtype) for x in inputs]
        + [pltpu.SemaphoreType.DMA((4,))],
        compiler_params=params(46),
    )(*inputs)

    lanes = devices // PLANES
    half = lanes // 2
    group = lanes * per_peer
    block = lambda height: jax.ShapeDtypeStruct((height, deep), f32)
    whole = lambda shape: pl.BlockSpec(shape, lambda i: (0,) * len(shape))
    updated, stress_s, ready = [], [], []
    left = 0
    for span in (LANES,) * (columns // LANES):
        part = lambda height: pl.BlockSpec((height, span), lambda i, at=left // span: (0, at))
        wide = comps * span
        outs = [block(LANES)] if len(updated) < 3 else [block(per_peer)] * half
        done = pl.pallas_call(
            functools.partial(solve_kernel, 1.0 / math.sqrt(comps * nodes), left, len(updated)),
            grid=(1,),
            out_shape=(
                jax.ShapeDtypeStruct((rows, span), f32),
                jax.ShapeDtypeStruct((8, span), f32),
                *outs,
            ),
            in_specs=[whole((rows, deep)), whole((rows, deep)), part(rows), part(rows), part(8),
                      whole((comps, 32, rows)), whole((comps, rows, LANES)), whole((8, columns))]
            + [whole(u.shape) for u in updated],
            out_specs=[whole((rows, span)), whole((8, span))] + [whole(o.shape) for o in outs],
            scratch_shapes=[pltpu.VMEM((rows, wide), f32) for _ in range(4)]
            + [pltpu.VMEM((deep, 2 * wide), bf16)],
            compiler_params=params(),
            cost_estimate=pl.CostEstimate(
                flops=18 * rows * deep * wide, bytes_accessed=2**20, transcendentals=0
            ),
        )(khi, klo, hist_s, weight_s, strain_s, cstack, pdir, place_s, *updated)
        updated.append(done[0])
        stress_s.append(done[1])
        ready.append(done[2:])
        left += span
    pair, stress_out = pl.pallas_call(
        functools.partial(ship_kernel, devices, 2 * group, len(updated)),
        out_shape=(block(2 * group), jax.ShapeDtypeStruct((voigt, columns), f32)),
        in_specs=[vmem] * (2 + 2 * len(updated)),
        out_specs=[vmem] * 2,
        compiler_params=params(),
        cost_estimate=pl.CostEstimate(
            flops=4 * rows * columns * columns, bytes_accessed=2**20, transcendentals=0
        ),
    )(place_s, qp_s, *updated, *stress_s)

    axes = ("macro", "pool")

    def hop(sent, mask):
        return lax.ppermute(sent, axes, [(s, s ^ mask) for s in range(devices)])

    pair, *straight = lax.optimization_barrier((pair, *ready[-1]))
    planes = [list(range(z * lanes, (z + 1) * lanes)) for z in range(PLANES)]
    pair = lax.all_to_all(
        pair.reshape(2 * lanes, per_peer, deep), axes, split_axis=0, concat_axis=0, tiled=True,
        axis_index_groups=[planes[0] + planes[3], planes[1] + planes[2]],
    ).reshape(2 * group, deep)
    hops = (2 * lanes, lanes, 2 * lanes + 1)
    landed = []
    for (sent,), mask in zip(ready, hops):
        landed.append(hop(sent, mask))
        landed[-2:] = lax.optimization_barrier(tuple(landed[-2:]))
    joined = pl.pallas_call(
        functools.partial(join_kernel, per_peer),
        out_shape=(block(3 * per_peer),) * half,
        in_specs=[vmem] * 3,
        out_specs=[vmem] * half,
        compiler_params=params(),
        cost_estimate=pl.CostEstimate(flops=2**40, bytes_accessed=2**20, transcendentals=0),
    )(*landed)
    joined = [sent if i == 0 else hop(sent, 2 * i) for i, sent in enumerate(joined)]
    direct = [hop(sent, lanes + 2 * i + 1) for i, sent in enumerate(straight)]
    new_history = pl.pallas_call(
        functools.partial(land_kernel, devices, per_peer),
        out_shape=jax.ShapeDtypeStruct((nodes, devices * per_peer), f32),
        in_specs=[vmem] * (1 + 2 * half),
        out_specs=pl.BlockSpec(memory_space=pl.ANY),
        scratch_shapes=[pltpu.VMEM((8, nodes, LANES), f32), pltpu.SemaphoreType.DMA((8,)),
                        pltpu.VMEM((2, group, deep), f32)],
        compiler_params=params(),
    )(pair, *joined, *direct)
    return (new_history, stress_out)


def solution(mesh):
    return jax.shard_map(
        shards,
        mesh=mesh,
        in_specs=(
            P(None, ("macro", "pool")),
            P(None, ("macro", "pool")),
            P(None, ("macro", "pool")),
            P(("macro", "pool"), None),
            P(("macro", "pool"), None),
            P(),
            P(),
            P(),
            P(),
        ),
        out_specs=(P(None, ("macro", "pool")), P(None, ("macro", "pool"))),
        check_vma=False,
    )
```

```python
import functools
import math

import jax
import jax.numpy as jnp
from jax import lax
from jax.experimental import pallas as pl
from jax.experimental.pallas import tpu as pltpu
from jax.sharding import PartitionSpec as P

ITERS = 3
LANES = 128
PLANES = 4
PATTERN = 32

NN = (((1,), (0,)), ((), ()))
NT = (((1,), (1,)), ((), ()))
TN = (((0,), (0,)), ((), ()))


def up(value, unit):
    return -(-value // unit) * unit


def dot(a, b, dims=NN):
    return lax.dot_general(a, b, dims, preferred_element_type=jnp.float32)


def halves(x):
    hi = x.astype(jnp.bfloat16)
    lo = (x - hi.astype(jnp.float32)).astype(jnp.bfloat16)
    return hi, lo


def whereabouts(devices):
    me = lax.axis_index("macro") * lax.axis_size("pool") + lax.axis_index("pool")
    lanes = devices // PLANES
    return me, me // lanes, me % lanes, lanes


def hot(row, count):
    rows = lax.broadcasted_iota(jnp.int32, (count, row.shape[1]), 0)
    return jnp.where(rows == row, 1.0, 0.0).astype(jnp.bfloat16)


def pack_kernel(coupling, plastic, strain, owner, qp, pattern, small):
    top = 0
    for c in range(coupling.shape[0]):
        small[top:top + coupling.shape[1], :] = coupling[c]
        top += coupling.shape[1]
    for part in (plastic, strain, owner, qp):
        small[top:top + part.shape[0], 0:part.shape[1]] = part[...].astype(jnp.float32)
        top += part.shape[0]
    count = pattern.shape[0]
    for a in range(count):
        for b in range(count):
            couples = jnp.full((1, LANES), pattern[a, b].astype(jnp.float32))
            small[PATTERN + a * count + b:PATTERN + a * count + b + 1, 0:LANES] = couples


def prep_kernel(devices, per_peer, comps, voigt, *refs):
    sources, outs, (kfull, pad), local, sem = refs[:4], refs[4:13], refs[13:15], refs[15:19], refs[19]
    khi, klo, hist_s, weight_s, strain_s, place_s, qp_s, cstack, pdir = outs
    small, stiff, hist, flag = local
    copies = [
        pltpu.make_async_copy(source, target, sem.at[i])
        for i, (source, target) in enumerate(zip(sources, local))
    ]
    for copy in copies:
        copy.start()
    nodes, columns = hist.shape
    nb, blk = stiff.shape[0], stiff.shape[2]
    at_plastic = comps * voigt
    at_strain = at_plastic + comps
    at_owner = at_strain + voigt
    copies[0].wait()

    me, plane, lane, lanes = whereabouts(devices)
    owner = small[at_owner:at_owner + 1, 0:columns].astype(jnp.int32)
    apart = owner // lanes ^ plane
    target = owner % lanes
    away = target ^ lane
    hopping = (away % 2 * 2 + jnp.where(apart == 2, 0, 1)) * (lanes // 2) + away // 2
    staying = jnp.where(apart == 3, 2, 3) * lanes + target
    key = jnp.where((apart == 2) | (apart == 1), hopping, staying)
    key_ids = lax.broadcasted_iota(jnp.int32, (devices, columns), 0)
    mine = jnp.where(key_ids == key, 1.0, 0.0)
    earlier = jnp.where(
        lax.broadcasted_iota(jnp.int32, (columns, columns), 0)
        < lax.broadcasted_iota(jnp.int32, (columns, columns), 1), 1.0, 0.0
    ).astype(jnp.bfloat16)
    before = dot(mine.astype(jnp.bfloat16), earlier)
    rank = jnp.sum(before * mine, axis=0, keepdims=True)
    tally = jnp.sum(mine, axis=1, keepdims=True)
    ahead = jnp.where(key_ids < key, tally, 0.0)
    position = (rank + jnp.sum(ahead, axis=0, keepdims=True)).astype(jnp.int32)

    order = hot(position, columns)
    pad[...] = jnp.zeros_like(pad)
    pad[0:1, :] = key.astype(jnp.float32)
    pad[1:2, :] = rank
    placed = dot(pad[...].astype(jnp.bfloat16), order, NT)
    place_s[...] = jnp.broadcast_to(
        (placed[0:1, :] * per_peer + placed[1:2, :]).astype(jnp.int32), place_s.shape
    )

    pad[0:1, :] = (position // 256).astype(jnp.float32)
    pad[1:2, :] = (position % 256).astype(jnp.float32)
    found = dot(pad[...].astype(jnp.bfloat16), hot(small[at_owner + 1:at_owner + 2, 0:columns].astype(jnp.int32), columns))
    at = (found[0:1, :] * 256.0 + found[1:2, :]).astype(jnp.int32)
    qp_s[...] = jnp.broadcast_to(at, qp_s.shape)
    pad[...] = jnp.zeros_like(pad)
    pad[0:voigt, :] = small[at_strain:at_owner, 0:columns]
    hi, lo = halves(pad[...])
    serves = hot(at, columns)
    strain_s[...] = dot(hi, serves, NT) + dot(lo, serves, NT)

    kfull[...] = jnp.zeros_like(kfull)
    copies[1].wait()
    for a in range(nb):
        for b in range(nb):
            kfull[a * blk:(a + 1) * blk, b * blk:(b + 1) * blk] = (
                stiff[a, b] * small[PATTERN + a * nb + b:PATTERN + a * nb + b + 1, 0:blk]
            )
    k = kfull[...]
    kh = k.astype(jnp.bfloat16)
    khi[...] = kh
    klo[...] = (k - kh.astype(jnp.float32)).astype(jnp.bfloat16)

    copies[2].wait()
    copies[3].wait()
    hi, lo = halves(hist[...])
    hist_s[...] = jnp.zeros_like(hist_s)
    hist_s[0:nodes, :] = dot(hi, order, NT) + dot(lo, order, NT)
    h = hist_s[...]
    weight_s[...] = jnp.zeros_like(weight_s)
    weight_s[0:nodes, :] = dot(flag[...].astype(jnp.float32).astype(jnp.bfloat16), order, NT)
    weight_s[...] = weight_s[...] * h * h / (1.0 + h * h)

    cstack[...] = jnp.zeros_like(cstack)
    for c in range(comps):
        cpl = small[c * voigt:(c + 1) * voigt, :]
        hi = cpl.astype(jnp.bfloat16).astype(jnp.float32)
        cstack[c, 0:voigt, 0:nodes] = hi
        cstack[c, 8:8 + voigt, 0:nodes] = hi
        cstack[c, 16:16 + voigt, 0:nodes] = cpl - hi
    pdir[...] = jnp.zeros_like(pdir)
    for c in range(comps):
        spread = jnp.broadcast_to(small[at_plastic + c:at_plastic + c + 1, :], (LANES, nodes))
        pdir[c, 0:nodes, :] = jnp.transpose(spread)


def row_blocks(rows, span):
    pieces = 4 * span // LANES
    cuts = [rows // 16 * i // pieces * 16 for i in range(pieces + 1)]
    return [slice(top, end) for top, end in zip(cuts, cuts[1:])]


def sweep(rows, comps, span):
    for r in row_blocks(rows, span):
        for c in range(comps):
            yield r, slice(c * span, (c + 1) * span), c


def fold(x):
    return jnp.sum(x.reshape(x.shape[0] // 8, 8, x.shape[1]), axis=0)


def total(parts):
    return jnp.sum(parts, axis=0, keepdims=True)


def solve_kernel(scale, first, earlier, khi, klo, hist, weight, strain, cstack, pdir, place, *refs):
    earlier_updated, refs = refs[:earlier], refs[earlier:]
    updated, stress, blocks = refs[0], refs[1], refs[2:-5]
    field, resid, image, solved, split = refs[-5:]
    rows, span = hist.shape
    comps = pdir.shape[0]
    wide = comps * span
    zero = jnp.zeros((8, span), jnp.float32)

    def flow(c, r):
        return jnp.concatenate([pdir[c, r, :]] * (span // LANES), axis=1)

    def keep(r, c, x):
        split[r, c * span:(c + 1) * span], split[r, wide + c * span:wide + (c + 1) * span] = (
            halves(x)
        )

    s = strain[...]
    s_hi = s.astype(jnp.bfloat16).astype(jnp.float32)
    s3 = jnp.concatenate([s_hi, s - s_hi, s_hi, jnp.zeros_like(s)], axis=0).astype(jnp.bfloat16)
    split[rows:, :] = jnp.zeros((split.shape[0] - rows, 2 * wide), jnp.bfloat16)
    for c in range(comps):
        image[:, c * span:(c + 1) * span] = dot(cstack[c].astype(jnp.bfloat16), s3, TN)
    parts = zero
    for r, l, c in sweep(rows, comps, span):
        d = image[r, l] - weight[r, :] * hist[r, :] * flow(c, r)
        resid[r, l] = d
        field[r, l] = d
        keep(r, c, d)
        parts = parts + fold(d * d)
    norm = total(parts)
    solved[...] = jnp.zeros_like(solved)

    def step_length(norm):
        parts = zero
        for r in row_blocks(rows, span):
            both = dot(khi[r, :], split[...])
            low = dot(klo[r, :], split[:, 0:wide])
            tangent = 1.5 - weight[r, :]
            for c in range(comps):
                l = slice(c * span, (c + 1) * span)
                d = field[r, l]
                q = both[:, l] + both[:, wide + c * span:wide + (c + 1) * span] + low[:, l]
                q = q + tangent * d
                image[r, l] = q
                parts = parts + fold(d * q)
        return norm / jnp.maximum(total(parts), 1.0)

    def step(_, norm):
        alpha = step_length(norm)
        parts = zero
        for r, l, c in sweep(rows, comps, span):
            solved[r, l] = solved[r, l] + alpha * field[r, l]
            left = resid[r, l] - alpha * image[r, l]
            resid[r, l] = left
            parts = parts + fold(left * left)
        following = total(parts)
        beta = following / jnp.maximum(norm, 1.0)
        for r, l, c in sweep(rows, comps, span):
            d = resid[r, l] + beta * field[r, l]
            field[r, l] = d
            keep(r, c, d)
        return following

    alpha = step_length(lax.fori_loop(0, ITERS - 1, step, norm))
    for r, l, c in sweep(rows, comps, span):
        x = solved[r, l] + alpha * field[r, l]
        pushed = flow(c, r) * x
        image[r, 0:span] = pushed if c == 0 else image[r, 0:span] + pushed
        keep(r, c, (1.5 - weight[r, :]) * x)
    updated[...] = hist[...] + weight[...] * image[:, 0:span]
    top, count = 0, sum(block.shape[0] for block in blocks)
    sent = placed_rows(first, count, place, [*earlier_updated, updated])
    for block in blocks:
        put(block, 0, sent[top:top + block.shape[0]])
        top += block.shape[0]
    out = s
    for c in range(comps):
        cpl = cstack[c].astype(jnp.bfloat16)
        main = dot(cpl, split[0:rows, c * span:(c + 1) * span])
        minor = dot(cpl, split[0:rows, wide + c * span:wide + (c + 1) * span])
        out = out + scale * (main[0:8] + main[16:24] + minor[0:8])
    stress[...] = out


def placed_rows(first, count, place, sources):
    width = sum(source.shape[1] for source in sources)
    placing = hot(place[0:1, 0:width] - first, count)
    sums, left = 0.0, 0
    for source in sources:
        hi, lo = halves(source[...])
        cut = placing[:, left:left + source.shape[1]]
        sums = sums + (dot(cut, hi, NT) + dot(cut, lo, NT))
        left += source.shape[1]
    return sums


def put(block, top, rows):
    height, filled = rows.shape
    block[pl.ds(top, height), 0:filled] = rows
    rest = jnp.zeros((height, block.shape[1] - filled), jnp.float32)
    block[pl.ds(top, height), filled:] = rest


def ship_kernel(devices, first, chunks, place, at, *refs):
    updated, stress, (pair, out) = refs[:chunks], refs[chunks:2 * chunks], refs[2 * chunks:]
    me, plane, lane, lanes = whereabouts(devices)
    group = pair.shape[0] // 2
    rows = placed_rows(first, 2 * group, place, updated)
    put(pair, pl.multiple_of((1 - plane // 2) * group, group), rows[0:group])
    put(pair, pl.multiple_of(plane // 2 * group, group), rows[group:])
    hi, lo = halves(jnp.concatenate([ref[...] for ref in stress], axis=1))
    serves = hot(at[0:1, :], hi.shape[1])
    out[...] = (dot(hi, serves) + dot(lo, serves))[0:out.shape[0], :]


def join_kernel(cap, *refs):
    landed, blocks = refs[:3], refs[3:]
    for i, block in enumerate(blocks):
        for k, rows in enumerate(landed):
            block[k * cap:(k + 1) * cap, :] = rows[i * cap:(i + 1) * cap, :]


def land(tile, out, stage, sem, slot, at):
    nodes = out.shape[0]
    stage[slot] = jnp.transpose(tile)[0:nodes, :]
    columns = pl.multiple_of(at * LANES, LANES)
    copy = pltpu.make_async_copy(stage.at[slot], out.at[:, pl.ds(columns, LANES)], sem.at[slot])
    copy.start()
    return copy


def land_group(block, count, plane, out, stage, sem, slot):
    height = block.shape[0] // count
    copies = []
    for part in range(count):
        tile = block[part * height:(part + 1) * height, :]
        copies.append(land(tile, out, stage, sem, slot + part, plane * count + part))
    return copies


def land_kernel(devices, cap, pair, *refs):
    blocks, (out, stage, sem, gather) = refs[:-4], refs[-4:]
    me, plane, lane, lanes = whereabouts(devices)
    group = pair.shape[0] // 2
    copies = []
    for part in range(2):
        source = jnp.where(plane // 2 == part, plane, plane ^ 3)
        block = pair.at[part * group:(part + 1) * group, :]
        copies += land_group(block, 2, source, out, stage, sem, 2 * part)
    for i, apart in enumerate((2, 1)):
        for k in range(lanes):
            at = pl.multiple_of((lane ^ k) * cap, cap)
            if i == 1 and k % 2 == 1:
                gather[i, pl.ds(at, cap), :] = blocks[lanes // 2 + k // 2][...]
            else:
                top = (2 * (k % 2) + i) * cap
                gather[i, pl.ds(at, cap), :] = blocks[k // 2][top:top + cap, :]
        copies += land_group(gather.at[i], 2, plane ^ apart, out, stage, sem, 4 + 2 * i)
    for copy in copies:
        copy.wait()


def params(mib=24):
    return pltpu.CompilerParams(vmem_limit_bytes=mib * 2**20)


def shards(
    history, yield_flags, strain, qp_to_rve, new_owner, stiffness, pattern, coupling, plastic_dir
):
    devices = lax.axis_size(("macro", "pool"))
    nodes, columns = history.shape
    comps, voigt = coupling.shape[0], coupling.shape[1]
    per_peer = 2 * columns // devices
    rows = up(nodes, 32)
    deep = up(nodes, 256)
    f32, bf16, i32 = jnp.float32, jnp.bfloat16, jnp.int32
    vmem = pl.BlockSpec(memory_space=pltpu.VMEM)
    small_inputs = (coupling, plastic_dir, strain, new_owner.reshape(1, columns), qp_to_rve, pattern)
    small = pl.pallas_call(
        pack_kernel,
        out_shape=jax.ShapeDtypeStruct((up(PATTERN + pattern.size, 8), nodes), f32),
        in_specs=[vmem] * 5 + [pl.BlockSpec(memory_space=pltpu.SMEM)],
        out_specs=vmem,
        compiler_params=params(60),
    )(*small_inputs)
    inputs = (small, stiffness, history, yield_flags)
    khi, klo, hist_s, weight_s, strain_s, place_s, qp_s, cstack, pdir = pl.pallas_call(
        functools.partial(prep_kernel, devices, per_peer, comps, voigt),
        out_shape=(
            jax.ShapeDtypeStruct((rows, deep), bf16),
            jax.ShapeDtypeStruct((rows, deep), bf16),
            jax.ShapeDtypeStruct((rows, columns), f32),
            jax.ShapeDtypeStruct((rows, columns), f32),
            jax.ShapeDtypeStruct((8, columns), f32),
            jax.ShapeDtypeStruct((8, columns), i32),
            jax.ShapeDtypeStruct((8, columns), i32),
            jax.ShapeDtypeStruct((comps, 32, rows), f32),
            jax.ShapeDtypeStruct((comps, rows, LANES), f32),
        ),
        in_specs=[pl.BlockSpec(memory_space=pltpu.HBM)] * 4,
        out_specs=[vmem] * 9,
        scratch_shapes=[pltpu.VMEM((rows, deep), f32), pltpu.VMEM((8, columns), f32)]
        + [pltpu.VMEM(x.shape, x.dtype) for x in inputs]
        + [pltpu.SemaphoreType.DMA((4,))],
        compiler_params=params(46),
    )(*inputs)

    lanes = devices // PLANES
    half = lanes // 2
    group = lanes * per_peer
    block = lambda height: jax.ShapeDtypeStruct((height, deep), f32)
    whole = lambda shape: pl.BlockSpec(shape, lambda i: (0,) * len(shape))
    updated, stress_s, ready = [], [], []
    left = 0
    for span in (LANES,) * (columns // LANES):
        part = lambda height: pl.BlockSpec((height, span), lambda i, at=left // span: (0, at))
        wide = comps * span
        outs = [block(LANES)] if len(updated) < 3 else [block(per_peer)] * half
        done = pl.pallas_call(
            functools.partial(solve_kernel, 1.0 / math.sqrt(comps * nodes), left, len(updated)),
            grid=(1,),
            out_shape=(
                jax.ShapeDtypeStruct((rows, span), f32),
                jax.ShapeDtypeStruct((8, span), f32),
                *outs,
            ),
            in_specs=[whole((rows, deep)), whole((rows, deep)), part(rows), part(rows), part(8),
                      whole((comps, 32, rows)), whole((comps, rows, LANES)), whole((8, columns))]
            + [whole(u.shape) for u in updated],
            out_specs=[whole((rows, span)), whole((8, span))] + [whole(o.shape) for o in outs],
            scratch_shapes=[pltpu.VMEM((rows, wide), f32) for _ in range(4)]
            + [pltpu.VMEM((deep, 2 * wide), bf16)],
            compiler_params=params(),
            cost_estimate=pl.CostEstimate(
                flops=18 * rows * deep * wide, bytes_accessed=2**20, transcendentals=0
            ),
        )(khi, klo, hist_s, weight_s, strain_s, cstack, pdir, place_s, *updated)
        updated.append(done[0])
        stress_s.append(done[1])
        ready.append(done[2:])
        left += span
    pair, stress_out = pl.pallas_call(
        functools.partial(ship_kernel, devices, 2 * group, len(updated)),
        out_shape=(block(2 * group), jax.ShapeDtypeStruct((voigt, columns), f32)),
        in_specs=[vmem] * (2 + 2 * len(updated)),
        out_specs=[vmem] * 2,
        compiler_params=params(),
        cost_estimate=pl.CostEstimate(
            flops=4 * rows * columns * columns, bytes_accessed=2**20, transcendentals=0
        ),
    )(place_s, qp_s, *updated, *stress_s)

    axes = ("macro", "pool")

    def hop(sent, mask):
        return lax.ppermute(sent, axes, [(s, s ^ mask) for s in range(devices)])

    pair, *straight = lax.optimization_barrier((pair, *ready[-1]))
    planes = [list(range(z * lanes, (z + 1) * lanes)) for z in range(PLANES)]
    pair = lax.all_to_all(
        pair.reshape(2 * lanes, per_peer, deep), axes, split_axis=0, concat_axis=0, tiled=True,
        axis_index_groups=[planes[0] + planes[3], planes[1] + planes[2]],
    ).reshape(2 * group, deep)
    hops = (2 * lanes, lanes, 2 * lanes + 1)
    landed = []
    for (sent,), mask in zip(ready, hops):
        landed.append(hop(sent, mask))
        landed[-2:] = lax.optimization_barrier(tuple(landed[-2:]))
    joined = pl.pallas_call(
        functools.partial(join_kernel, per_peer),
        out_shape=(block(3 * per_peer),) * half,
        in_specs=[vmem] * 3,
        out_specs=[vmem] * half,
        compiler_params=params(),
        cost_estimate=pl.CostEstimate(flops=2**40, bytes_accessed=2**20, transcendentals=0),
    )(*landed)
    joined = [sent if i == 0 else hop(sent, 2 * i) for i, sent in enumerate(joined)]
    direct = [hop(sent, lanes + 2 * i + 1) for i, sent in enumerate(straight)]
    new_history = pl.pallas_call(
        functools.partial(land_kernel, devices, per_peer),
        out_shape=jax.ShapeDtypeStruct((nodes, devices * per_peer), f32),
        in_specs=[vmem] * (1 + 2 * half),
        out_specs=pl.BlockSpec(memory_space=pl.ANY),
        scratch_shapes=[pltpu.VMEM((8, nodes, LANES), f32), pltpu.SemaphoreType.DMA((8,)),
                        pltpu.VMEM((2, group, deep), f32)],
        compiler_params=params(),
    )(pair, *joined, *direct)
    return (new_history, stress_out)


def solution(mesh):
    return jax.shard_map(
        shards,
        mesh=mesh,
        in_specs=(
            P(None, ("macro", "pool")),
            P(None, ("macro", "pool")),
            P(None, ("macro", "pool")),
            P(("macro", "pool"), None),
            P(("macro", "pool"), None),
            P(),
            P(),
            P(),
            P(),
        ),
        out_specs=(P(None, ("macro", "pool")), P(None, ("macro", "pool"))),
        check_vma=False,
    )
```

```python
import functools
import math

import jax
import jax.numpy as jnp
from jax import lax
from jax.experimental import pallas as pl
from jax.experimental.pallas import tpu as pltpu
from jax.sharding import PartitionSpec as P

ITERS = 3
LANES = 128
PLANES = 4
PATTERN = 32
ROOM = 8192

NN = (((1,), (0,)), ((), ()))
NT = (((1,), (1,)), ((), ()))


def up(value, unit):
    return -(-value // unit) * unit


def dot(a, b, dims=NN):
    return lax.dot_general(a, b, dims, preferred_element_type=jnp.float32)


def halves(x):
    hi = x.astype(jnp.bfloat16)
    lo = (x - hi.astype(jnp.float32)).astype(jnp.bfloat16)
    return hi, lo


def whereabouts(devices):
    me = lax.axis_index("macro") * lax.axis_size("pool") + lax.axis_index("pool")
    lanes = devices // PLANES
    return me, me // lanes, me % lanes, lanes


def hot(row, count):
    rows = lax.broadcasted_iota(jnp.int32, (count, row.shape[1]), 0)
    return jnp.where(rows == row, 1.0, 0.0).astype(jnp.bfloat16)


def pack_kernel(coupling, plastic, strain, owner, qp, pattern, packed, small, sem):
    top = 0
    for c in range(coupling.shape[0]):
        small[top:top + coupling.shape[1], :] = coupling[c]
        top += coupling.shape[1]
    for part in (plastic, strain, owner, qp):
        small[top:top + part.shape[0], 0:part.shape[1]] = part[...].astype(jnp.float32)
        top += part.shape[0]
    count = pattern.shape[0]
    for a in range(count):
        for b in range(count):
            couples = jnp.full((1, LANES), pattern[a, b].astype(jnp.float32))
            small[PATTERN + a * count + b:PATTERN + a * count + b + 1, 0:LANES] = couples
    copy = pltpu.make_async_copy(small, packed.at[pl.ds(0, small.shape[0]), :], sem)
    copy.start()
    copy.wait()


def prep_kernel(devices, per_peer, comps, voigt, *refs):
    sources, outs, local = refs[:4], refs[4:14], refs[14:18]
    kfull, pad, stack, sem = refs[18:]
    khi, klo, hist_s, weight_s, strain_s, place_s, qp_s, cstack, loads, pdir = outs
    small, stiff, hist, flag = local
    copies = [
        pltpu.make_async_copy(source, target, sem.at[i])
        for i, (source, target) in enumerate(
            zip((sources[0].at[pl.ds(0, local[0].shape[0]), :], *sources[1:]), local)
        )
    ]
    for copy in copies:
        copy.start()
    nodes, columns = hist.shape
    nb, blk = stiff.shape[0], stiff.shape[2]
    at_plastic = comps * voigt
    at_strain = at_plastic + comps
    at_owner = at_strain + voigt
    copies[0].wait()

    me, plane, lane, lanes = whereabouts(devices)
    owner = small[at_owner:at_owner + 1, 0:columns].astype(jnp.int32)
    apart = owner // lanes ^ plane
    target = owner % lanes
    away = target ^ lane
    hopping = (away % 2 * 2 + jnp.where(apart == 2, 0, 1)) * (lanes // 2) + away // 2
    staying = jnp.where(apart == 3, 2, 3) * lanes + target
    key = jnp.where((apart == 2) | (apart == 1), hopping, staying)
    key_ids = lax.broadcasted_iota(jnp.int32, (devices, columns), 0)
    mine = jnp.where(key_ids == key, 1.0, 0.0)
    earlier = jnp.where(
        lax.broadcasted_iota(jnp.int32, (columns, columns), 0)
        < lax.broadcasted_iota(jnp.int32, (columns, columns), 1), 1.0, 0.0
    ).astype(jnp.bfloat16)
    before = dot(mine.astype(jnp.bfloat16), earlier)
    rank = jnp.sum(before * mine, axis=0, keepdims=True)
    tally = jnp.sum(mine, axis=1, keepdims=True)
    ahead = jnp.where(key_ids < key, tally, 0.0)
    position = (rank + jnp.sum(ahead, axis=0, keepdims=True)).astype(jnp.int32)

    order = hot(position, columns)
    pad[...] = jnp.zeros_like(pad)
    pad[0:1, :] = key.astype(jnp.float32)
    pad[1:2, :] = rank
    placed = dot(pad[...].astype(jnp.bfloat16), order, NT)
    place_s[...] = jnp.broadcast_to(
        (placed[0:1, :] * per_peer + placed[1:2, :]).astype(jnp.int32), place_s.shape
    )

    pad[0:1, :] = (position // 256).astype(jnp.float32)
    pad[1:2, :] = (position % 256).astype(jnp.float32)
    found = dot(pad[...].astype(jnp.bfloat16), hot(small[at_owner + 1:at_owner + 2, 0:columns].astype(jnp.int32), columns))
    at = (found[0:1, :] * 256.0 + found[1:2, :]).astype(jnp.int32)
    qp_s[...] = jnp.broadcast_to(at, qp_s.shape)
    pad[...] = jnp.zeros_like(pad)
    pad[0:voigt, :] = small[at_strain:at_owner, 0:columns]
    hi, lo = halves(pad[...])
    serves = hot(at, columns)
    strain_s[...] = dot(hi, serves, NT) + dot(lo, serves, NT)

    kfull[...] = jnp.zeros_like(kfull)
    copies[1].wait()
    for a in range(nb):
        for b in range(nb):
            kfull[a * blk:(a + 1) * blk, b * blk:(b + 1) * blk] = (
                stiff[a, b] * small[PATTERN + a * nb + b:PATTERN + a * nb + b + 1, 0:blk]
            )
    k = kfull[...]
    kh = k.astype(jnp.bfloat16)
    khi[...] = kh
    klo[...] = (k - kh.astype(jnp.float32)).astype(jnp.bfloat16)

    copies[2].wait()
    copies[3].wait()
    hi, lo = halves(hist[...])
    hist_s[...] = jnp.zeros_like(hist_s)
    hist_s[0:nodes, :] = dot(hi, order, NT) + dot(lo, order, NT)
    h = hist_s[...]
    weight_s[...] = jnp.zeros_like(weight_s)
    weight_s[0:nodes, :] = dot(flag[...].astype(jnp.float32).astype(jnp.bfloat16), order, NT)
    weight_s[...] = weight_s[...] * h * h / (1.0 + h * h)

    for c in range(comps):
        cpl = small[c * voigt:(c + 1) * voigt, :]
        hi = cpl.astype(jnp.bfloat16).astype(jnp.float32)
        stack[...] = jnp.zeros_like(stack)
        stack[0:voigt, 0:nodes] = hi
        stack[8:8 + voigt, 0:nodes] = hi
        stack[16:16 + voigt, 0:nodes] = cpl - hi
        cstack[c] = stack[...].astype(jnp.bfloat16)
        loads[c] = jnp.transpose(stack[...]).astype(jnp.bfloat16)
    pdir[...] = jnp.zeros_like(pdir)
    for c in range(comps):
        spread = jnp.broadcast_to(small[at_plastic + c:at_plastic + c + 1, :], (LANES, nodes))
        pdir[c, 0:nodes, :] = jnp.transpose(spread)


def row_blocks(rows, span):
    pieces = 4 * span // LANES
    cuts = [rows // 16 * i // pieces * 16 for i in range(pieces + 1)]
    return [slice(top, end) for top, end in zip(cuts, cuts[1:])]


def sweep(rows, comps, span):
    for r in row_blocks(rows, span):
        for c in range(comps):
            yield r, slice(c * span, (c + 1) * span), c


def fold(x):
    return jnp.sum(x.reshape(x.shape[0] // 8, 8, x.shape[1]), axis=0)


def total(parts):
    return jnp.sum(parts, axis=0, keepdims=True)


def solve_kernel(scale, first, earlier, khi, klo, hist, weight, strain, cstack, loads, pdir, place,
                 *refs):
    earlier_updated, refs = refs[:earlier], refs[earlier:]
    updated, stress, blocks = refs[0], refs[1], refs[2:-5]
    field, resid, image, steps, split = refs[-5:]
    rows, span = hist.shape
    comps = pdir.shape[0]
    wide = comps * span
    zero = jnp.zeros((8, span), jnp.float32)

    def flow(c, r):
        return jnp.concatenate([pdir[c, r, :]] * (span // LANES), axis=1)

    def keep(r, c, x):
        split[r, c * span:(c + 1) * span], split[r, wide + c * span:wide + (c + 1) * span] = (
            halves(x)
        )

    s = strain[...]
    s_hi = s.astype(jnp.bfloat16).astype(jnp.float32)
    s3 = jnp.concatenate([s_hi, s - s_hi, s_hi, jnp.zeros_like(s)], axis=0).astype(jnp.bfloat16)
    split[rows:, :] = jnp.zeros((split.shape[0] - rows, 2 * wide), jnp.bfloat16)
    for c in range(comps):
        image[:, c * span:(c + 1) * span] = dot(loads[c], s3)
    parts = zero
    for r, l, c in sweep(rows, comps, span):
        d = image[r, l] - weight[r, :] * hist[r, :] * flow(c, r)
        resid[r, l] = d
        field[0, r, l] = d
        keep(r, c, d)
        parts = parts + fold(d * d)
    norm = total(parts)

    def step_length(turn, norm):
        parts = zero
        for r in row_blocks(rows, span):
            both = dot(khi[r, :], split[...])
            low = dot(klo[r, :], split[:, 0:wide])
            tangent = 1.5 - weight[r, :]
            for c in range(comps):
                l = slice(c * span, (c + 1) * span)
                d = field[turn, r, l]
                q = both[:, l] + both[:, wide + c * span:wide + (c + 1) * span] + low[:, l]
                q = q + tangent * d
                image[r, l] = q
                parts = parts + fold(d * q)
        return norm / jnp.maximum(total(parts), 1.0)

    def step(turn, norm):
        alpha = step_length(turn, norm)
        steps[turn] = jnp.broadcast_to(alpha, steps.shape[1:])
        parts = zero
        for r, l, c in sweep(rows, comps, span):
            left = resid[r, l] - alpha * image[r, l]
            resid[r, l] = left
            parts = parts + fold(left * left)
        following = total(parts)
        beta = following / jnp.maximum(norm, 1.0)
        for r, l, c in sweep(rows, comps, span):
            d = resid[r, l] + beta * field[turn, r, l]
            field[turn + 1, r, l] = d
            keep(r, c, d)
        return following

    last = ITERS - 1
    alpha = step_length(last, lax.fori_loop(0, last, step, norm))
    alphas = [steps[turn, 0:1, :] for turn in range(last)]
    for r, l, c in sweep(rows, comps, span):
        x = alphas[0] * field[0, r, l]
        for turn in range(1, last):
            x = x + alphas[turn] * field[turn, r, l]
        x = x + alpha * field[last, r, l]
        pushed = flow(c, r) * x
        image[r, 0:span] = pushed if c == 0 else image[r, 0:span] + pushed
        keep(r, c, (1.5 - weight[r, :]) * x)
    updated[...] = hist[...] + weight[...] * image[:, 0:span]
    top, count = 0, sum(block.shape[0] for block in blocks)
    sent = placed_rows(first, count, place, [*earlier_updated, updated])
    for block in blocks:
        put(block, 0, sent[top:top + block.shape[0]])
        top += block.shape[0]
    out = s
    for c in range(comps):
        cpl = cstack[c]
        main = dot(cpl, split[0:rows, c * span:(c + 1) * span])
        minor = dot(cpl, split[0:rows, wide + c * span:wide + (c + 1) * span])
        out = out + scale * (main[0:8] + main[16:24] + minor[0:8])
    stress[...] = out


def placed_rows(first, count, place, sources):
    width = sum(source.shape[1] for source in sources)
    placing = hot(place[0:1, 0:width] - first, count)
    sums, left = 0.0, 0
    for source in sources:
        hi, lo = halves(source[...])
        cut = placing[:, left:left + source.shape[1]]
        sums = sums + (dot(cut, hi, NT) + dot(cut, lo, NT))
        left += source.shape[1]
    return sums


def put(block, top, rows):
    height, filled = rows.shape
    block[pl.ds(top, height), 0:filled] = rows
    rest = jnp.zeros((height, block.shape[1] - filled), jnp.float32)
    block[pl.ds(top, height), filled:] = rest


def ship_kernel(devices, first, chunks, place, at, *refs):
    updated, stress, (pair, out) = refs[:chunks], refs[chunks:2 * chunks], refs[2 * chunks:]
    me, plane, lane, lanes = whereabouts(devices)
    group = pair.shape[0] // 2
    rows = placed_rows(first, 2 * group, place, updated)
    put(pair, pl.multiple_of((1 - plane // 2) * group, group), rows[0:group])
    put(pair, pl.multiple_of(plane // 2 * group, group), rows[group:])
    hi, lo = halves(jnp.concatenate([ref[...] for ref in stress], axis=1))
    serves = hot(at[0:1, :], hi.shape[1])
    out[...] = (dot(hi, serves) + dot(lo, serves))[0:out.shape[0], :]


def join_kernel(cap, *refs):
    landed, blocks = refs[:3], refs[3:]
    for i, block in enumerate(blocks):
        for k, rows in enumerate(landed):
            block[k * cap:(k + 1) * cap, :] = rows[i * cap:(i + 1) * cap, :]


def land(tile, out, stage, sem, slot, at):
    nodes = out.shape[0]
    stage[slot] = jnp.transpose(tile)[0:nodes, :]
    columns = pl.multiple_of(at * LANES, LANES)
    copy = pltpu.make_async_copy(stage.at[slot], out.at[:, pl.ds(columns, LANES)], sem.at[slot])
    copy.start()
    return copy


def land_group(block, count, plane, out, stage, sem, slot):
    height = block.shape[0] // count
    copies = []
    for part in range(count):
        tile = block[part * height:(part + 1) * height, :]
        copies.append(land(tile, out, stage, sem, slot + part, plane * count + part))
    return copies


def land_kernel(devices, cap, pair, *refs):
    blocks, (out, stage, sem, gather) = refs[:-4], refs[-4:]
    me, plane, lane, lanes = whereabouts(devices)
    group = pair.shape[0] // 2
    copies = []
    for part in range(2):
        source = jnp.where(plane // 2 == part, plane, plane ^ 3)
        block = pair.at[part * group:(part + 1) * group, :]
        copies += land_group(block, 2, source, out, stage, sem, 2 * part)
    for i, apart in enumerate((2, 1)):
        for k in range(lanes):
            at = pl.multiple_of((lane ^ k) * cap, cap)
            if i == 1 and k % 2 == 1:
                gather[i, pl.ds(at, cap), :] = blocks[lanes // 2 + k // 2][...]
            else:
                top = (2 * (k % 2) + i) * cap
                gather[i, pl.ds(at, cap), :] = blocks[k // 2][top:top + cap, :]
        copies += land_group(gather.at[i], 2, plane ^ apart, out, stage, sem, 4 + 2 * i)
    for copy in copies:
        copy.wait()


def params(mib=24):
    return pltpu.CompilerParams(vmem_limit_bytes=mib * 2**20)


def shards(
    history, yield_flags, strain, qp_to_rve, new_owner, stiffness, pattern, coupling, plastic_dir
):
    devices = lax.axis_size(("macro", "pool"))
    nodes, columns = history.shape
    comps, voigt = coupling.shape[0], coupling.shape[1]
    per_peer = 2 * columns // devices
    rows = up(nodes, 32)
    deep = up(nodes, 256)
    f32, bf16, i32 = jnp.float32, jnp.bfloat16, jnp.int32
    vmem = pl.BlockSpec(memory_space=pltpu.VMEM)
    small_inputs = (coupling, plastic_dir, strain, new_owner.reshape(1, columns), qp_to_rve, pattern)
    small_rows = up(PATTERN + pattern.size, 8)
    small = pl.pallas_call(
        pack_kernel,
        out_shape=jax.ShapeDtypeStruct((ROOM, nodes), f32),
        in_specs=[vmem] * 5 + [pl.BlockSpec(memory_space=pltpu.SMEM)],
        out_specs=pl.BlockSpec(memory_space=pltpu.HBM),
        scratch_shapes=[pltpu.VMEM((small_rows, nodes), f32), pltpu.SemaphoreType.DMA],
        compiler_params=params(60),
    )(*small_inputs)
    inputs = (small, stiffness, history, yield_flags)
    khi, klo, hist_s, weight_s, strain_s, place_s, qp_s, cstack, loads, pdir = pl.pallas_call(
        functools.partial(prep_kernel, devices, per_peer, comps, voigt),
        out_shape=(
            jax.ShapeDtypeStruct((rows, deep), bf16),
            jax.ShapeDtypeStruct((rows, deep), bf16),
            jax.ShapeDtypeStruct((rows, columns), f32),
            jax.ShapeDtypeStruct((rows, columns), f32),
            jax.ShapeDtypeStruct((8, columns), f32),
            jax.ShapeDtypeStruct((8, columns), i32),
            jax.ShapeDtypeStruct((8, columns), i32),
            jax.ShapeDtypeStruct((comps, 32, rows), bf16),
            jax.ShapeDtypeStruct((comps, rows, 32), bf16),
            jax.ShapeDtypeStruct((comps, rows, LANES), f32),
        ),
        in_specs=[pl.BlockSpec(memory_space=pltpu.HBM)] * 4,
        out_specs=[vmem] * 10,
        scratch_shapes=[pltpu.VMEM((small_rows, nodes), f32)]
        + [pltpu.VMEM(x.shape, x.dtype) for x in inputs[1:]]
        + [pltpu.VMEM((rows, deep), f32), pltpu.VMEM((8, columns), f32),
           pltpu.VMEM((32, rows), f32), pltpu.SemaphoreType.DMA((4,))],
        compiler_params=params(46),
    )(*inputs)

    lanes = devices // PLANES
    half = lanes // 2
    group = lanes * per_peer
    block = lambda height: jax.ShapeDtypeStruct((height, deep), f32)
    whole = lambda shape: pl.BlockSpec(shape, lambda i: (0,) * len(shape))
    updated, stress_s, ready = [], [], []
    left = 0
    for span in (LANES,) * (columns // LANES):
        part = lambda height: pl.BlockSpec((height, span), lambda i, at=left // span: (0, at))
        wide = comps * span
        outs = [block(LANES)] if len(updated) < 3 else [block(per_peer)] * half
        done = pl.pallas_call(
            functools.partial(solve_kernel, 1.0 / math.sqrt(comps * nodes), left, len(updated)),
            grid=(1,),
            out_shape=(
                jax.ShapeDtypeStruct((rows, span), f32),
                jax.ShapeDtypeStruct((8, span), f32),
                *outs,
            ),
            in_specs=[whole((rows, deep)), whole((rows, deep)), part(rows), part(rows), part(8),
                      whole((comps, 32, rows)), whole((comps, rows, 32)), whole((comps, rows, LANES)),
                      whole((8, columns))]
            + [whole(u.shape) for u in updated],
            out_specs=[whole((rows, span)), whole((8, span))] + [whole(o.shape) for o in outs],
            scratch_shapes=[pltpu.VMEM((ITERS, rows, wide), f32), pltpu.VMEM((rows, wide), f32),
                            pltpu.VMEM((rows, wide), f32), pltpu.VMEM((ITERS, 8, span), f32),
                            pltpu.VMEM((deep, 2 * wide), bf16)],
            compiler_params=params(),
            cost_estimate=pl.CostEstimate(
                flops=18 * rows * deep * wide, bytes_accessed=2**20, transcendentals=0
            ),
        )(khi, klo, hist_s, weight_s, strain_s, cstack, loads, pdir, place_s, *updated)
        updated.append(done[0])
        stress_s.append(done[1])
        ready.append(done[2:])
        left += span
    pair, stress_out = pl.pallas_call(
        functools.partial(ship_kernel, devices, 2 * group, len(updated)),
        out_shape=(block(2 * group), jax.ShapeDtypeStruct((voigt, columns), f32)),
        in_specs=[vmem] * (2 + 2 * len(updated)),
        out_specs=[vmem] * 2,
        compiler_params=params(),
        cost_estimate=pl.CostEstimate(
            flops=4 * rows * columns * columns, bytes_accessed=2**20, transcendentals=0
        ),
    )(place_s, qp_s, *updated, *stress_s)

    axes = ("macro", "pool")

    def hop(sent, mask):
        return lax.ppermute(sent, axes, [(s, s ^ mask) for s in range(devices)])

    pair, *straight = lax.optimization_barrier((pair, *ready[-1]))
    planes = [list(range(z * lanes, (z + 1) * lanes)) for z in range(PLANES)]
    pair = lax.all_to_all(
        pair.reshape(2 * lanes, per_peer, deep), axes, split_axis=0, concat_axis=0, tiled=True,
        axis_index_groups=[planes[0] + planes[3], planes[1] + planes[2]],
    ).reshape(2 * group, deep)
    hops = (2 * lanes, lanes, 2 * lanes + 1)
    landed = []
    for (sent,), mask in zip(ready, hops):
        landed.append(hop(sent, mask))
        landed[-2:] = lax.optimization_barrier(tuple(landed[-2:]))
    joined = pl.pallas_call(
        functools.partial(join_kernel, per_peer),
        out_shape=(block(3 * per_peer),) * half,
        in_specs=[vmem] * 3,
        out_specs=[vmem] * half,
        compiler_params=params(),
        cost_estimate=pl.CostEstimate(flops=2**40, bytes_accessed=2**20, transcendentals=0),
    )(*landed)
    joined = [sent if i == 0 else hop(sent, 2 * i) for i, sent in enumerate(joined)]
    direct = [hop(sent, lanes + 2 * i + 1) for i, sent in enumerate(straight)]
    new_history = pl.pallas_call(
        functools.partial(land_kernel, devices, per_peer),
        out_shape=jax.ShapeDtypeStruct((nodes, devices * per_peer), f32),
        in_specs=[vmem] * (1 + 2 * half),
        out_specs=pl.BlockSpec(memory_space=pl.ANY),
        scratch_shapes=[pltpu.VMEM((8, nodes, LANES), f32), pltpu.SemaphoreType.DMA((8,)),
                        pltpu.VMEM((2, group, deep), f32)],
        compiler_params=params(),
    )(pair, *joined, *direct)
    return (new_history, stress_out)


def solution(mesh):
    return jax.shard_map(
        shards,
        mesh=mesh,
        in_specs=(
            P(None, ("macro", "pool")),
            P(None, ("macro", "pool")),
            P(None, ("macro", "pool")),
            P(("macro", "pool"), None),
            P(("macro", "pool"), None),
            P(),
            P(),
            P(),
            P(),
        ),
        out_specs=(P(None, ("macro", "pool")), P(None, ("macro", "pool"))),
        check_vma=False,
    )
```

```python
import functools
import math

import jax
import jax.numpy as jnp
from jax import lax
from jax.experimental import pallas as pl
from jax.experimental.pallas import tpu as pltpu
from jax.sharding import PartitionSpec as P

ITERS = 3
LANES = 128
PLANES = 4
PATTERN = 32
ROOM = 8192

NN = (((1,), (0,)), ((), ()))
NT = (((1,), (1,)), ((), ()))


def up(value, unit):
    return -(-value // unit) * unit


def dot(a, b, dims=NN):
    return lax.dot_general(a, b, dims, preferred_element_type=jnp.float32)


def halves(x):
    hi = x.astype(jnp.bfloat16)
    lo = (x - hi.astype(jnp.float32)).astype(jnp.bfloat16)
    return hi, lo


def whereabouts(devices):
    me = lax.axis_index("macro") * lax.axis_size("pool") + lax.axis_index("pool")
    lanes = devices // PLANES
    return me, me // lanes, me % lanes, lanes


def hot(row, count):
    rows = lax.broadcasted_iota(jnp.int32, (count, row.shape[1]), 0)
    return jnp.where(rows == row, 1.0, 0.0).astype(jnp.bfloat16)


def pack_kernel(coupling, plastic, strain, owner, qp, pattern, packed, small, sem):
    top = 0
    for c in range(coupling.shape[0]):
        small[top:top + coupling.shape[1], :] = coupling[c]
        top += coupling.shape[1]
    for part in (plastic, strain, owner, qp):
        small[top:top + part.shape[0], 0:part.shape[1]] = part[...].astype(jnp.float32)
        top += part.shape[0]
    count = pattern.shape[0]
    for a in range(count):
        for b in range(count):
            couples = jnp.full((1, LANES), pattern[a, b].astype(jnp.float32))
            small[PATTERN + a * count + b:PATTERN + a * count + b + 1, 0:LANES] = couples
    copy = pltpu.make_async_copy(small, packed.at[pl.ds(0, small.shape[0]), :], sem)
    copy.start()
    copy.wait()


def prep_kernel(devices, per_peer, comps, voigt, *refs):
    sources, outs, local = refs[:4], refs[4:14], refs[14:18]
    kfull, pad, stack, sem = refs[18:]
    khi, klo, hist_s, weight_s, strain_s, place_s, qp_s, cstack, loads, pdir = outs
    small, stiff, hist, flag = local
    copies = [
        pltpu.make_async_copy(source, target, sem.at[i])
        for i, (source, target) in enumerate(
            zip((sources[0].at[pl.ds(0, local[0].shape[0]), :], *sources[1:]), local)
        )
    ]
    for copy in copies:
        copy.start()
    nodes, columns = hist.shape
    nb, blk = stiff.shape[0], stiff.shape[2]
    at_plastic = comps * voigt
    at_strain = at_plastic + comps
    at_owner = at_strain + voigt
    copies[0].wait()

    me, plane, lane, lanes = whereabouts(devices)
    owner = small[at_owner:at_owner + 1, 0:columns].astype(jnp.int32)
    apart = owner // lanes ^ plane
    target = owner % lanes
    away = target ^ lane
    hopping = (away % 2 * 2 + jnp.where(apart == 2, 0, 1)) * (lanes // 2) + away // 2
    staying = jnp.where(apart == 3, 2, 3) * lanes + target
    key = jnp.where((apart == 2) | (apart == 1), hopping, staying)
    key_ids = lax.broadcasted_iota(jnp.int32, (devices, columns), 0)
    mine = jnp.where(key_ids == key, 1.0, 0.0)
    earlier = jnp.where(
        lax.broadcasted_iota(jnp.int32, (columns, columns), 0)
        < lax.broadcasted_iota(jnp.int32, (columns, columns), 1), 1.0, 0.0
    ).astype(jnp.bfloat16)
    before = dot(mine.astype(jnp.bfloat16), earlier)
    rank = jnp.sum(before * mine, axis=0, keepdims=True)
    tally = jnp.sum(mine, axis=1, keepdims=True)
    ahead = jnp.where(key_ids < key, tally, 0.0)
    position = (rank + jnp.sum(ahead, axis=0, keepdims=True)).astype(jnp.int32)

    order = hot(position, columns)
    pad[...] = jnp.zeros_like(pad)
    pad[0:1, :] = key.astype(jnp.float32)
    pad[1:2, :] = rank
    placed = dot(pad[...].astype(jnp.bfloat16), order, NT)
    place_s[...] = jnp.broadcast_to(
        (placed[0:1, :] * per_peer + placed[1:2, :]).astype(jnp.int32), place_s.shape
    )

    pad[0:1, :] = (position // 256).astype(jnp.float32)
    pad[1:2, :] = (position % 256).astype(jnp.float32)
    found = dot(pad[...].astype(jnp.bfloat16), hot(small[at_owner + 1:at_owner + 2, 0:columns].astype(jnp.int32), columns))
    at = (found[0:1, :] * 256.0 + found[1:2, :]).astype(jnp.int32)
    qp_s[...] = jnp.broadcast_to(at, qp_s.shape)
    pad[...] = jnp.zeros_like(pad)
    pad[0:voigt, :] = small[at_strain:at_owner, 0:columns]
    hi, lo = halves(pad[...])
    serves = hot(at, columns)
    strain_s[...] = dot(hi, serves, NT) + dot(lo, serves, NT)

    kfull[...] = jnp.zeros_like(kfull)
    copies[1].wait()
    for a in range(nb):
        for b in range(nb):
            kfull[a * blk:(a + 1) * blk, b * blk:(b + 1) * blk] = (
                stiff[a, b] * small[PATTERN + a * nb + b:PATTERN + a * nb + b + 1, 0:blk]
            )
    k = kfull[...]
    kh = k.astype(jnp.bfloat16)
    khi[...] = kh
    klo[...] = (k - kh.astype(jnp.float32)).astype(jnp.bfloat16)

    copies[2].wait()
    copies[3].wait()
    hi, lo = halves(hist[...])
    hist_s[...] = jnp.zeros_like(hist_s)
    hist_s[0:nodes, :] = dot(hi, order, NT) + dot(lo, order, NT)
    h = hist_s[...]
    weight_s[...] = jnp.zeros_like(weight_s)
    weight_s[0:nodes, :] = dot(flag[...].astype(jnp.float32).astype(jnp.bfloat16), order, NT)
    weight_s[...] = weight_s[...] * h * h / (1.0 + h * h)

    for c in range(comps):
        cpl = small[c * voigt:(c + 1) * voigt, :]
        hi = cpl.astype(jnp.bfloat16).astype(jnp.float32)
        stack[...] = jnp.zeros_like(stack)
        stack[0:voigt, 0:nodes] = hi
        stack[8:8 + voigt, 0:nodes] = hi
        stack[16:16 + voigt, 0:nodes] = cpl - hi
        cstack[c] = stack[...].astype(jnp.bfloat16)
        loads[c] = jnp.transpose(stack[...]).astype(jnp.bfloat16)
    pdir[...] = jnp.zeros_like(pdir)
    for c in range(comps):
        spread = jnp.broadcast_to(small[at_plastic + c:at_plastic + c + 1, :], (LANES, nodes))
        pdir[c, 0:nodes, :] = jnp.transpose(spread)


def row_blocks(rows, span):
    pieces = 4 * span // LANES
    cuts = [rows // 16 * i // pieces * 16 for i in range(pieces + 1)]
    return [slice(top, end) for top, end in zip(cuts, cuts[1:])]


def sweep(rows, comps, span):
    for r in row_blocks(rows, span):
        for c in range(comps):
            yield r, slice(c * span, (c + 1) * span), c


def fold(x):
    return jnp.sum(x.reshape(x.shape[0] // 8, 8, x.shape[1]), axis=0)


def total(parts):
    return jnp.sum(parts, axis=0, keepdims=True)


def solve_kernel(scale, cap, nodes, first, earlier, khi, klo, hist, weight, strain, cstack, loads, pdir, place,
                 *refs):
    earlier_updated, refs = refs[:earlier], refs[earlier:]
    updated, stress, blocks = refs[0], refs[1], refs[2:-5]
    field, resid, image, steps, split = refs[-5:]
    rows, span = hist.shape
    comps = pdir.shape[0]
    wide = comps * span
    zero = jnp.zeros((8, span), jnp.float32)

    def flow(c, r):
        return jnp.concatenate([pdir[c, r, :]] * (span // LANES), axis=1)

    def keep(r, c, x):
        split[r, c * span:(c + 1) * span], split[r, wide + c * span:wide + (c + 1) * span] = (
            halves(x)
        )

    s = strain[...]
    s_hi = s.astype(jnp.bfloat16).astype(jnp.float32)
    s3 = jnp.concatenate([s_hi, s - s_hi, s_hi, jnp.zeros_like(s)], axis=0).astype(jnp.bfloat16)
    split[rows:, :] = jnp.zeros((split.shape[0] - rows, 2 * wide), jnp.bfloat16)
    for c in range(comps):
        image[:, c * span:(c + 1) * span] = dot(loads[c], s3)
    parts = zero
    for r, l, c in sweep(rows, comps, span):
        d = image[r, l] - weight[r, :] * hist[r, :] * flow(c, r)
        resid[r, l] = d
        field[0, r, l] = d
        keep(r, c, d)
        parts = parts + fold(d * d)
    norm = total(parts)

    def step_length(turn, norm):
        parts = zero
        for r in row_blocks(rows, span):
            both = dot(khi[r, :], split[...])
            low = dot(klo[r, :], split[:, 0:wide])
            tangent = 1.5 - weight[r, :]
            for c in range(comps):
                l = slice(c * span, (c + 1) * span)
                d = field[turn, r, l]
                q = both[:, l] + both[:, wide + c * span:wide + (c + 1) * span] + low[:, l]
                q = q + tangent * d
                image[r, l] = q
                parts = parts + fold(d * q)
        return norm / jnp.maximum(total(parts), 1.0)

    def step(turn, norm):
        alpha = step_length(turn, norm)
        steps[turn] = jnp.broadcast_to(alpha, steps.shape[1:])
        parts = zero
        for r, l, c in sweep(rows, comps, span):
            left = resid[r, l] - alpha * image[r, l]
            resid[r, l] = left
            parts = parts + fold(left * left)
        following = total(parts)
        beta = following / jnp.maximum(norm, 1.0)
        for r, l, c in sweep(rows, comps, span):
            d = resid[r, l] + beta * field[turn, r, l]
            field[turn + 1, r, l] = d
            keep(r, c, d)
        return following

    last = ITERS - 1
    alpha = step_length(last, lax.fori_loop(0, last, step, norm))
    alphas = [steps[turn, 0:1, :] for turn in range(last)]
    for r, l, c in sweep(rows, comps, span):
        x = alphas[0] * field[0, r, l]
        for turn in range(1, last):
            x = x + alphas[turn] * field[turn, r, l]
        x = x + alpha * field[last, r, l]
        pushed = flow(c, r) * x
        image[r, 0:span] = pushed if c == 0 else image[r, 0:span] + pushed
        keep(r, c, (1.5 - weight[r, :]) * x)
    updated[...] = hist[...] + weight[...] * image[:, 0:span]
    sent = placed_rows(first, LANES, place, [*earlier_updated, updated], split.shape[0])
    part = LANES // len(blocks)
    for i, block in enumerate(blocks):
        put(block, 0, sent[i * part:(i + 1) * part], cap, nodes)
    out = s
    for c in range(comps):
        cpl = cstack[c]
        main = dot(cpl, split[0:rows, c * span:(c + 1) * span])
        minor = dot(cpl, split[0:rows, wide + c * span:wide + (c + 1) * span])
        out = out + scale * (main[0:8] + main[16:24] + minor[0:8])
    stress[...] = out


def placed_rows(first, count, place, sources, deep):
    width = sum(source.shape[1] for source in sources)
    placing = hot(place[0:1, 0:width] - first, count)
    sums, left = 0.0, 0
    for source in sources:
        rest = jnp.zeros((deep - source.shape[0], source.shape[1]), jnp.float32)
        hi, lo = halves(jnp.concatenate([source[...], rest], axis=0))
        cut = placing[:, left:left + source.shape[1]]
        sums = sums + (dot(cut, hi, NT) + dot(cut, lo, NT))
        left += source.shape[1]
    return sums


def tight(cap, nodes):
    return cap % 32 == 0 and LANES // 2 < nodes % LANES <= LANES * 3 // 4


def height(cap, nodes):
    return cap * (nodes // LANES) + (cap // 2 + cap // 4 if tight(cap, nodes) else cap)


def put(block, top, rows, cap, nodes):
    full, half, quarter = nodes // LANES, cap // 2, cap // 4

    def store(at, piece):
        block[pl.ds(at, piece.shape[0]), :] = piece
        return at + piece.shape[0]

    for first in range(0, rows.shape[0], cap):
        for t in range(full):
            top = store(top, rows[first:first + cap, t * LANES:(t + 1) * LANES])
        tail = rows[first:first + cap, full * LANES:]
        if not tight(cap, nodes):
            top = store(top, tail)
            continue
        lane = lax.broadcasted_iota(jnp.int32, (half, LANES), 1)
        top = store(top, jnp.where(lane < LANES // 2, tail[0:half],
                                   pltpu.roll(tail[half:], LANES // 2, 1)))
        lane = lax.broadcasted_iota(jnp.int32, (quarter, LANES), 1) // (LANES // 4)
        mixed = tail[0:quarter]
        for g in range(4):
            moved = pltpu.roll(tail[g * quarter:(g + 1) * quarter], (g + 2) % 4 * (LANES // 4), 1)
            mixed = jnp.where(lane == g, moved, mixed)
        top = store(top, mixed)


def take(block, top, target, at, cap, nodes):
    full, half, quarter = nodes // LANES, cap // 2, cap // 4
    for t in range(full):
        target[pl.ds(at, cap), t * LANES:(t + 1) * LANES] = block[top + t * cap:top + (t + 1) * cap, :]
    top = top + full * cap
    if not tight(cap, nodes):
        target[pl.ds(at, cap), full * LANES:] = block[top:top + cap, :]
        return
    lane = lax.broadcasted_iota(jnp.int32, (quarter, LANES), 1)
    mixed = block[top + half:top + half + quarter, :]
    for g in range(4):
        left = block[top + g % 2 * quarter:top + (g % 2 + 1) * quarter, :]
        if g >= 2:
            left = pltpu.roll(left, LANES // 2, 1)
        right = mixed if g == 2 else pltpu.roll(mixed, (6 - g) % 4 * (LANES // 4), 1)
        row = pl.multiple_of(at + g * quarter, quarter)
        target[pl.ds(row, quarter), full * LANES:] = jnp.where(lane < LANES // 2, left, right)


def ship_kernel(devices, cap, nodes, first, chunks, place, at, *refs):
    updated, stress, (pair, out) = refs[:chunks], refs[chunks:2 * chunks], refs[2 * chunks:]
    me, plane, lane, lanes = whereabouts(devices)
    group, span = lanes * cap, lanes * height(cap, nodes)
    rows = placed_rows(first, 2 * group, place, updated, up(nodes, 256))
    put(pair, pl.multiple_of((1 - plane // 2) * span, 8), rows[0:group], cap, nodes)
    put(pair, pl.multiple_of(plane // 2 * span, 8), rows[group:], cap, nodes)
    hi, lo = halves(jnp.concatenate([ref[...] for ref in stress], axis=1))
    serves = hot(at[0:1, :], hi.shape[1])
    out[...] = (dot(hi, serves) + dot(lo, serves))[0:out.shape[0], :]


def join_kernel(tall, *refs):
    landed, blocks = refs[:3], refs[3:]
    for i, block in enumerate(blocks):
        for k, rows in enumerate(landed):
            block[k * tall:(k + 1) * tall, :] = rows[i * tall:(i + 1) * tall, :]


def land(tile, out, stage, sem, slot, at):
    nodes = out.shape[0]
    stage[slot] = jnp.transpose(tile)[0:nodes, :]
    columns = pl.multiple_of(at * LANES, LANES)
    copy = pltpu.make_async_copy(stage.at[slot], out.at[:, pl.ds(columns, LANES)], sem.at[slot])
    copy.start()
    return copy


def land_kernel(devices, cap, pair, *refs):
    blocks, (out, stage, sem, gather) = refs[:-4], refs[-4:]
    me, plane, lane, lanes = whereabouts(devices)
    nodes, tall = out.shape[0], height(cap, out.shape[0])
    tiles = lanes * cap // LANES
    copies = []
    for i in range(4):
        target = gather.at[i]
        for k in range(lanes):
            if i < 2:
                take(pair, (i * lanes + k) * tall, target, k * cap, cap, nodes)
                continue
            at = pl.multiple_of((lane ^ k) * cap, cap)
            if i == 3 and k % 2 == 1:
                take(blocks[lanes // 2 + k // 2], 0, target, at, cap, nodes)
            else:
                take(blocks[k // 2], (2 * (k % 2) + i - 2) * tall, target, at, cap, nodes)
        if i < 2:
            source = jnp.where(plane // 2 == i, plane, plane ^ 3)
        else:
            source = plane ^ (4 - i)
        for part in range(tiles):
            tile = gather[i, part * LANES:(part + 1) * LANES, :]
            copies.append(land(tile, out, stage, sem, i * tiles + part, source * tiles + part))
    for copy in copies:
        copy.wait()


def params(mib=24):
    return pltpu.CompilerParams(vmem_limit_bytes=mib * 2**20)


def shards(
    history, yield_flags, strain, qp_to_rve, new_owner, stiffness, pattern, coupling, plastic_dir
):
    devices = lax.axis_size(("macro", "pool"))
    nodes, columns = history.shape
    comps, voigt = coupling.shape[0], coupling.shape[1]
    per_peer = 2 * columns // devices
    rows = up(nodes, 32)
    deep = up(nodes, 256)
    f32, bf16, i32 = jnp.float32, jnp.bfloat16, jnp.int32
    vmem = pl.BlockSpec(memory_space=pltpu.VMEM)
    small_inputs = (coupling, plastic_dir, strain, new_owner.reshape(1, columns), qp_to_rve, pattern)
    small_rows = up(PATTERN + pattern.size, 8)
    small = pl.pallas_call(
        pack_kernel,
        out_shape=jax.ShapeDtypeStruct((ROOM, nodes), f32),
        in_specs=[vmem] * 5 + [pl.BlockSpec(memory_space=pltpu.SMEM)],
        out_specs=pl.BlockSpec(memory_space=pltpu.HBM),
        scratch_shapes=[pltpu.VMEM((small_rows, nodes), f32), pltpu.SemaphoreType.DMA],
        compiler_params=params(60),
    )(*small_inputs)
    inputs = (small, stiffness, history, yield_flags)
    khi, klo, hist_s, weight_s, strain_s, place_s, qp_s, cstack, loads, pdir = pl.pallas_call(
        functools.partial(prep_kernel, devices, per_peer, comps, voigt),
        out_shape=(
            jax.ShapeDtypeStruct((rows, deep), bf16),
            jax.ShapeDtypeStruct((rows, deep), bf16),
            jax.ShapeDtypeStruct((rows, columns), f32),
            jax.ShapeDtypeStruct((rows, columns), f32),
            jax.ShapeDtypeStruct((8, columns), f32),
            jax.ShapeDtypeStruct((8, columns), i32),
            jax.ShapeDtypeStruct((8, columns), i32),
            jax.ShapeDtypeStruct((comps, 32, rows), bf16),
            jax.ShapeDtypeStruct((comps, rows, 32), bf16),
            jax.ShapeDtypeStruct((comps, rows, LANES), f32),
        ),
        in_specs=[pl.BlockSpec(memory_space=pltpu.HBM)] * 4,
        out_specs=[vmem] * 10,
        scratch_shapes=[pltpu.VMEM((small_rows, nodes), f32)]
        + [pltpu.VMEM(x.shape, x.dtype) for x in inputs[1:]]
        + [pltpu.VMEM((rows, deep), f32), pltpu.VMEM((8, columns), f32),
           pltpu.VMEM((32, rows), f32), pltpu.SemaphoreType.DMA((4,))],
        compiler_params=params(46),
    )(*inputs)

    lanes = devices // PLANES
    half = lanes // 2
    group = lanes * per_peer
    tall = height(per_peer, nodes)
    block = lambda count: jax.ShapeDtypeStruct((count * tall, LANES), f32)
    whole = lambda shape: pl.BlockSpec(shape, lambda i: (0,) * len(shape))
    updated, stress_s, ready = [], [], []
    left = 0
    for span in (LANES,) * (columns // LANES):
        part = lambda height: pl.BlockSpec((height, span), lambda i, at=left // span: (0, at))
        wide = comps * span
        outs = [block(half)] if len(updated) < 3 else [block(1)] * half
        done = pl.pallas_call(
            functools.partial(
                solve_kernel, 1.0 / math.sqrt(comps * nodes), per_peer, nodes, left, len(updated)
            ),
            grid=(1,),
            out_shape=(
                jax.ShapeDtypeStruct((rows, span), f32),
                jax.ShapeDtypeStruct((8, span), f32),
                *outs,
            ),
            in_specs=[whole((rows, deep)), whole((rows, deep)), part(rows), part(rows), part(8),
                      whole((comps, 32, rows)), whole((comps, rows, 32)), whole((comps, rows, LANES)),
                      whole((8, columns))]
            + [whole(u.shape) for u in updated],
            out_specs=[whole((rows, span)), whole((8, span))] + [whole(o.shape) for o in outs],
            scratch_shapes=[pltpu.VMEM((ITERS, rows, wide), f32), pltpu.VMEM((rows, wide), f32),
                            pltpu.VMEM((rows, wide), f32), pltpu.VMEM((ITERS, 8, span), f32),
                            pltpu.VMEM((deep, 2 * wide), bf16)],
            compiler_params=params(),
            cost_estimate=pl.CostEstimate(
                flops=18 * rows * deep * wide, bytes_accessed=2**20, transcendentals=0
            ),
        )(khi, klo, hist_s, weight_s, strain_s, cstack, loads, pdir, place_s, *updated)
        updated.append(done[0])
        stress_s.append(done[1])
        ready.append(done[2:])
        left += span
    pair, stress_out = pl.pallas_call(
        functools.partial(ship_kernel, devices, per_peer, nodes, 2 * group, len(updated)),
        out_shape=(block(2 * lanes), jax.ShapeDtypeStruct((voigt, columns), f32)),
        in_specs=[vmem] * (2 + 2 * len(updated)),
        out_specs=[vmem] * 2,
        compiler_params=params(),
        cost_estimate=pl.CostEstimate(
            flops=4 * rows * columns * columns, bytes_accessed=2**20, transcendentals=0
        ),
    )(place_s, qp_s, *updated, *stress_s)

    axes = ("macro", "pool")

    def hop(sent, mask):
        return lax.ppermute(sent, axes, [(s, s ^ mask) for s in range(devices)])

    pair, *straight = lax.optimization_barrier((pair, *ready[-1]))
    planes = [list(range(z * lanes, (z + 1) * lanes)) for z in range(PLANES)]
    pair = lax.all_to_all(
        pair.reshape(2 * lanes, tall, LANES), axes, split_axis=0, concat_axis=0, tiled=True,
        axis_index_groups=[planes[0] + planes[3], planes[1] + planes[2]],
    ).reshape(2 * lanes * tall, LANES)
    hops = (2 * lanes, lanes, 2 * lanes + 1)
    landed = []
    for (sent,), mask in zip(ready, hops):
        landed.append(hop(sent, mask))
        landed[-2:] = lax.optimization_barrier(tuple(landed[-2:]))
    joined = pl.pallas_call(
        functools.partial(join_kernel, tall),
        out_shape=(block(3),) * half,
        in_specs=[vmem] * 3,
        out_specs=[vmem] * half,
        compiler_params=params(),
        cost_estimate=pl.CostEstimate(flops=2**40, bytes_accessed=2**20, transcendentals=0),
    )(*landed)
    joined = [sent if i == 0 else hop(sent, 2 * i) for i, sent in enumerate(joined)]
    direct = [hop(sent, lanes + 2 * i + 1) for i, sent in enumerate(straight)]
    new_history = pl.pallas_call(
        functools.partial(land_kernel, devices, per_peer),
        out_shape=jax.ShapeDtypeStruct((nodes, devices * per_peer), f32),
        in_specs=[vmem] * (1 + 2 * half),
        out_specs=pl.BlockSpec(memory_space=pl.ANY),
        scratch_shapes=[pltpu.VMEM((8, nodes, LANES), f32), pltpu.SemaphoreType.DMA((8,)),
                        pltpu.VMEM((4, group, deep), f32)],
        compiler_params=params(),
    )(pair, *joined, *direct)
    return (new_history, stress_out)


def solution(mesh):
    return jax.shard_map(
        shards,
        mesh=mesh,
        in_specs=(
            P(None, ("macro", "pool")),
            P(None, ("macro", "pool")),
            P(None, ("macro", "pool")),
            P(("macro", "pool"), None),
            P(("macro", "pool"), None),
            P(),
            P(),
            P(),
            P(),
        ),
        out_specs=(P(None, ("macro", "pool")), P(None, ("macro", "pool"))),
        check_vma=False,
    )
```

```python
import functools
import math

import jax
import jax.numpy as jnp
from jax import lax
from jax.experimental import pallas as pl
from jax.experimental.pallas import tpu as pltpu
from jax.sharding import PartitionSpec as P

ITERS = 3
LANES = 128
PLANES = 4
PATTERN = 32
ROOM = 8192

NN = (((1,), (0,)), ((), ()))
NT = (((1,), (1,)), ((), ()))


def up(value, unit):
    return -(-value // unit) * unit


def dot(a, b, dims=NN):
    return lax.dot_general(a, b, dims, preferred_element_type=jnp.float32)


def halves(x):
    hi = x.astype(jnp.bfloat16)
    lo = (x - hi.astype(jnp.float32)).astype(jnp.bfloat16)
    return hi, lo


def whereabouts(devices):
    me = lax.axis_index("macro") * lax.axis_size("pool") + lax.axis_index("pool")
    lanes = devices // PLANES
    return me, me // lanes, me % lanes, lanes


def hot(row, count):
    rows = lax.broadcasted_iota(jnp.int32, (count, row.shape[1]), 0)
    return jnp.where(rows == row, 1.0, 0.0).astype(jnp.bfloat16)


def pack_kernel(coupling, plastic, strain, owner, qp, pattern, packed, small, sem):
    top = 0
    for c in range(coupling.shape[0]):
        small[top:top + coupling.shape[1], :] = coupling[c]
        top += coupling.shape[1]
    for part in (plastic, strain, owner, qp):
        small[top:top + part.shape[0], 0:part.shape[1]] = part[...].astype(jnp.float32)
        top += part.shape[0]
    count = pattern.shape[0]
    for a in range(count):
        for b in range(count):
            couples = jnp.full((1, LANES), pattern[a, b].astype(jnp.float32))
            small[PATTERN + a * count + b:PATTERN + a * count + b + 1, 0:LANES] = couples
    copy = pltpu.make_async_copy(small, packed.at[pl.ds(0, small.shape[0]), :], sem)
    copy.start()
    copy.wait()


def prep_kernel(devices, per_peer, comps, voigt, *refs):
    sources, outs, local = refs[:4], refs[4:14], refs[14:18]
    kfull, pad, stack, sem = refs[18:]
    khi, klo, hist_s, weight_s, strain_s, place_s, qp_s, cstack, loads, pdir = outs
    small, stiff, hist, flag = local
    pairs = [(sources[0].at[pl.ds(0, small.shape[0]), :], small), (sources[2], hist), (sources[3], flag)]
    pairs += [(sources[1].at[a], stiff.at[a]) for a in range(stiff.shape[0])]
    copies = [
        pltpu.make_async_copy(source, target, sem.at[i])
        for i, (source, target) in enumerate(pairs)
    ]
    for copy in copies[:1] + copies[3:] + copies[1:3]:
        copy.start()
    nodes, columns = hist.shape
    nb, blk = stiff.shape[0], stiff.shape[2]
    at_plastic = comps * voigt
    at_strain = at_plastic + comps
    at_owner = at_strain + voigt
    copies[0].wait()

    me, plane, lane, lanes = whereabouts(devices)
    owner = small[at_owner:at_owner + 1, 0:columns].astype(jnp.int32)
    apart = owner // lanes ^ plane
    target = owner % lanes
    away = target ^ lane
    hopping = (away % 2 * 2 + jnp.where(apart == 2, 0, 1)) * (lanes // 2) + away // 2
    staying = jnp.where(apart == 3, 2, 3) * lanes + target
    key = jnp.where((apart == 2) | (apart == 1), hopping, staying)
    key_ids = lax.broadcasted_iota(jnp.int32, (devices, columns), 0)
    mine = jnp.where(key_ids == key, 1.0, 0.0)
    earlier = jnp.where(
        lax.broadcasted_iota(jnp.int32, (columns, columns), 0)
        < lax.broadcasted_iota(jnp.int32, (columns, columns), 1), 1.0, 0.0
    ).astype(jnp.bfloat16)
    before = dot(mine.astype(jnp.bfloat16), earlier)
    rank = jnp.sum(before * mine, axis=0, keepdims=True)
    tally = jnp.sum(mine, axis=1, keepdims=True)
    ahead = jnp.where(key_ids < key, tally, 0.0)
    position = (rank + jnp.sum(ahead, axis=0, keepdims=True)).astype(jnp.int32)

    order = hot(position, columns)
    pad[...] = jnp.zeros_like(pad)
    pad[0:1, :] = key.astype(jnp.float32)
    pad[1:2, :] = rank
    placed = dot(pad[...].astype(jnp.bfloat16), order, NT)
    place_s[...] = jnp.broadcast_to(
        (placed[0:1, :] * per_peer + placed[1:2, :]).astype(jnp.int32), place_s.shape
    )

    pad[0:1, :] = (position // 256).astype(jnp.float32)
    pad[1:2, :] = (position % 256).astype(jnp.float32)
    found = dot(pad[...].astype(jnp.bfloat16), hot(small[at_owner + 1:at_owner + 2, 0:columns].astype(jnp.int32), columns))
    at = (found[0:1, :] * 256.0 + found[1:2, :]).astype(jnp.int32)
    qp_s[...] = jnp.broadcast_to(at, qp_s.shape)
    pad[...] = jnp.zeros_like(pad)
    pad[0:voigt, :] = small[at_strain:at_owner, 0:columns]
    hi, lo = halves(pad[...])
    serves = hot(at, columns)
    strain_s[...] = dot(hi, serves, NT) + dot(lo, serves, NT)

    kfull[...] = jnp.zeros_like(kfull)
    for a in range(nb):
        copies[3 + a].wait()
        for b in range(nb):
            kfull[a * blk:(a + 1) * blk, b * blk:(b + 1) * blk] = (
                stiff[a, b] * small[PATTERN + a * nb + b:PATTERN + a * nb + b + 1, 0:blk]
            )
    k = kfull[...]
    kh = k.astype(jnp.bfloat16)
    khi[...] = kh
    klo[...] = (k - kh.astype(jnp.float32)).astype(jnp.bfloat16)

    copies[1].wait()
    copies[2].wait()
    hi, lo = halves(hist[...])
    hist_s[...] = jnp.zeros_like(hist_s)
    hist_s[0:nodes, :] = dot(hi, order, NT) + dot(lo, order, NT)
    h = hist_s[...]
    weight_s[...] = jnp.zeros_like(weight_s)
    weight_s[0:nodes, :] = dot(flag[...].astype(jnp.float32).astype(jnp.bfloat16), order, NT)
    weight_s[...] = weight_s[...] * h * h / (1.0 + h * h)

    for c in range(comps):
        cpl = small[c * voigt:(c + 1) * voigt, :]
        hi = cpl.astype(jnp.bfloat16).astype(jnp.float32)
        stack[...] = jnp.zeros_like(stack)
        stack[0:voigt, 0:nodes] = hi
        stack[8:8 + voigt, 0:nodes] = hi
        stack[16:16 + voigt, 0:nodes] = cpl - hi
        cstack[c] = stack[...].astype(jnp.bfloat16)
        loads[c] = jnp.transpose(stack[...]).astype(jnp.bfloat16)
    pdir[...] = jnp.zeros_like(pdir)
    for c in range(comps):
        spread = jnp.broadcast_to(small[at_plastic + c:at_plastic + c + 1, :], (LANES, nodes))
        pdir[c, 0:nodes, :] = jnp.transpose(spread)


def row_blocks(rows, span):
    pieces = 4 * span // LANES
    cuts = [rows // 16 * i // pieces * 16 for i in range(pieces + 1)]
    return [slice(top, end) for top, end in zip(cuts, cuts[1:])]


def sweep(rows, comps, span):
    for r in row_blocks(rows, span):
        for c in range(comps):
            yield r, slice(c * span, (c + 1) * span), c


def fold(x):
    return jnp.sum(x.reshape(x.shape[0] // 8, 8, x.shape[1]), axis=0)


def total(parts):
    return jnp.sum(parts, axis=0, keepdims=True)


def solve_kernel(scale, cap, nodes, first, earlier, khi, klo, hist, weight, strain, cstack, loads, pdir, place,
                 *refs):
    earlier_updated, refs = refs[:earlier], refs[earlier:]
    updated, stress, blocks = refs[0], refs[1], refs[2:-5]
    field, resid, image, steps, split = refs[-5:]
    rows, span = hist.shape
    comps = pdir.shape[0]
    wide = comps * span
    zero = jnp.zeros((8, span), jnp.float32)

    def flow(c, r):
        return jnp.concatenate([pdir[c, r, :]] * (span // LANES), axis=1)

    def keep(r, c, x):
        split[r, c * span:(c + 1) * span], split[r, wide + c * span:wide + (c + 1) * span] = (
            halves(x)
        )

    s = strain[...]
    s_hi = s.astype(jnp.bfloat16).astype(jnp.float32)
    s3 = jnp.concatenate([s_hi, s - s_hi, s_hi, jnp.zeros_like(s)], axis=0).astype(jnp.bfloat16)
    split[rows:, :] = jnp.zeros((split.shape[0] - rows, 2 * wide), jnp.bfloat16)
    for c in range(comps):
        image[:, c * span:(c + 1) * span] = dot(loads[c], s3)
    parts = zero
    for r, l, c in sweep(rows, comps, span):
        d = image[r, l] - weight[r, :] * hist[r, :] * flow(c, r)
        resid[r, l] = d
        field[0, r, l] = d
        keep(r, c, d)
        parts = parts + fold(d * d)
    norm = total(parts)

    def step_length(turn, norm):
        parts = zero
        for r in row_blocks(rows, span):
            both = dot(khi[r, :], split[...])
            low = dot(klo[r, :], split[:, 0:wide])
            tangent = 1.5 - weight[r, :]
            for c in range(comps):
                l = slice(c * span, (c + 1) * span)
                d = field[turn, r, l]
                q = both[:, l] + both[:, wide + c * span:wide + (c + 1) * span] + low[:, l]
                q = q + tangent * d
                image[r, l] = q
                parts = parts + fold(d * q)
        return norm / jnp.maximum(total(parts), 1.0)

    def step(turn, norm):
        alpha = step_length(turn, norm)
        steps[turn] = jnp.broadcast_to(alpha, steps.shape[1:])
        parts = zero
        for r, l, c in sweep(rows, comps, span):
            left = resid[r, l] - alpha * image[r, l]
            resid[r, l] = left
            parts = parts + fold(left * left)
        following = total(parts)
        beta = following / jnp.maximum(norm, 1.0)
        for r, l, c in sweep(rows, comps, span):
            d = resid[r, l] + beta * field[turn, r, l]
            field[turn + 1, r, l] = d
            keep(r, c, d)
        return following

    last = ITERS - 1
    alpha = step_length(last, lax.fori_loop(0, last, step, norm))
    alphas = [steps[turn, 0:1, :] for turn in range(last)]
    for r, l, c in sweep(rows, comps, span):
        x = alphas[0] * field[0, r, l]
        for turn in range(1, last):
            x = x + alphas[turn] * field[turn, r, l]
        x = x + alpha * field[last, r, l]
        pushed = flow(c, r) * x
        image[r, 0:span] = pushed if c == 0 else image[r, 0:span] + pushed
        lead = 2 * c * span
        split[r, lead:lead + span], split[r, lead + span:lead + 2 * span] = halves(
            (1.5 - weight[r, :]) * x
        )
    updated[...] = hist[...] + weight[...] * image[:, 0:span]
    sent = placed_rows(first, LANES, place, [*earlier_updated, updated], split.shape[0])
    part = LANES // len(blocks)
    for i, block in enumerate(blocks):
        put(block, 0, sent[i * part:(i + 1) * part], cap, nodes)
    out = s
    for c in range(comps):
        cpl = cstack[c]
        both = dot(cpl, split[0:rows, 2 * c * span:2 * (c + 1) * span])
        out = out + scale * (both[0:8, 0:span] + both[16:24, 0:span] + both[0:8, span:])
    stress[...] = out


def placed_rows(first, count, place, sources, deep):
    width = sum(source.shape[1] for source in sources)
    placing = hot(place[0:1, 0:width] - first, count)
    sums, left = 0.0, 0
    for source in sources:
        rest = jnp.zeros((deep - source.shape[0], source.shape[1]), jnp.float32)
        hi, lo = halves(jnp.concatenate([source[...], rest], axis=0))
        cut = placing[:, left:left + source.shape[1]]
        sums = sums + (dot(cut, hi, NT) + dot(cut, lo, NT))
        left += source.shape[1]
    return sums


def tight(cap, nodes):
    return cap % 32 == 0 and LANES // 2 < nodes % LANES <= LANES * 3 // 4


def height(cap, nodes):
    return cap * (nodes // LANES) + (cap // 2 + cap // 4 if tight(cap, nodes) else cap)


def put(block, top, rows, cap, nodes):
    full, half, quarter = nodes // LANES, cap // 2, cap // 4

    def store(at, piece):
        block[pl.ds(at, piece.shape[0]), :] = piece
        return at + piece.shape[0]

    for first in range(0, rows.shape[0], cap):
        for t in range(full):
            top = store(top, rows[first:first + cap, t * LANES:(t + 1) * LANES])
        tail = rows[first:first + cap, full * LANES:]
        if not tight(cap, nodes):
            top = store(top, tail)
            continue
        lane = lax.broadcasted_iota(jnp.int32, (half, LANES), 1)
        top = store(top, jnp.where(lane < LANES // 2, tail[0:half],
                                   pltpu.roll(tail[half:], LANES // 2, 1)))
        lane = lax.broadcasted_iota(jnp.int32, (quarter, LANES), 1) // (LANES // 4)
        mixed = tail[0:quarter]
        for g in range(4):
            moved = pltpu.roll(tail[g * quarter:(g + 1) * quarter], (g + 2) % 4 * (LANES // 4), 1)
            mixed = jnp.where(lane == g, moved, mixed)
        top = store(top, mixed)


def take(block, top, target, at, cap, nodes):
    full, half, quarter = nodes // LANES, cap // 2, cap // 4
    for t in range(full):
        target[pl.ds(at, cap), t * LANES:(t + 1) * LANES] = block[top + t * cap:top + (t + 1) * cap, :]
    top = top + full * cap
    if not tight(cap, nodes):
        target[pl.ds(at, cap), full * LANES:] = block[top:top + cap, :]
        return
    lane = lax.broadcasted_iota(jnp.int32, (quarter, LANES), 1)
    mixed = block[top + half:top + half + quarter, :]
    for g in range(4):
        left = block[top + g % 2 * quarter:top + (g % 2 + 1) * quarter, :]
        if g >= 2:
            left = pltpu.roll(left, LANES // 2, 1)
        right = mixed if g == 2 else pltpu.roll(mixed, (6 - g) % 4 * (LANES // 4), 1)
        row = pl.multiple_of(at + g * quarter, quarter)
        target[pl.ds(row, quarter), full * LANES:] = jnp.where(lane < LANES // 2, left, right)


def ship_kernel(devices, cap, nodes, first, place, *refs):
    updated, pair = refs[:-1], refs[-1]
    me, plane, lane, lanes = whereabouts(devices)
    group, span = lanes * cap, lanes * height(cap, nodes)
    rows = placed_rows(first, 2 * group, place, updated, up(nodes, 256))
    put(pair, pl.multiple_of((1 - plane // 2) * span, 8), rows[0:group], cap, nodes)
    put(pair, pl.multiple_of(plane // 2 * span, 8), rows[group:], cap, nodes)


def back_kernel(at, *refs):
    out = refs[-1]
    hi, lo = halves(jnp.concatenate([ref[...] for ref in refs[:-1]], axis=1))
    serves = hot(at[0:1, :], hi.shape[1])
    out[...] = (dot(hi, serves) + dot(lo, serves))[0:out.shape[0], :]


def join_kernel(tall, *refs):
    landed, blocks = refs[:3], refs[3:]
    for i, block in enumerate(blocks):
        for k, rows in enumerate(landed):
            block[k * tall:(k + 1) * tall, :] = rows[i * tall:(i + 1) * tall, :]


def land(tile, out, stage, sem, slot, at):
    nodes = out.shape[0]
    stage[slot] = jnp.transpose(tile)[0:nodes, :]
    columns = pl.multiple_of(at * LANES, LANES)
    copy = pltpu.make_async_copy(stage.at[slot], out.at[:, pl.ds(columns, LANES)], sem.at[slot])
    copy.start()
    return copy


def land_kernel(devices, cap, pair, *refs):
    blocks, (out, stage, sem, gather) = refs[:-4], refs[-4:]
    me, plane, lane, lanes = whereabouts(devices)
    nodes, tall = out.shape[0], height(cap, out.shape[0])
    tiles = lanes * cap // LANES
    copies = []
    for i in range(4):
        target = gather.at[i]
        for k in range(lanes):
            if i < 2:
                take(pair, (i * lanes + k) * tall, target, k * cap, cap, nodes)
                continue
            at = pl.multiple_of((lane ^ k) * cap, cap)
            if i == 3 and k % 2 == 1:
                take(blocks[lanes // 2 + k // 2], 0, target, at, cap, nodes)
            else:
                take(blocks[k // 2], (2 * (k % 2) + i - 2) * tall, target, at, cap, nodes)
        if i < 2:
            source = jnp.where(plane // 2 == i, plane, plane ^ 3)
        else:
            source = plane ^ (4 - i)
        for part in range(tiles):
            tile = gather[i, part * LANES:(part + 1) * LANES, :]
            copies.append(land(tile, out, stage, sem, i * tiles + part, source * tiles + part))
    for copy in copies:
        copy.wait()


def params(mib=24):
    return pltpu.CompilerParams(vmem_limit_bytes=mib * 2**20)


def shards(
    history, yield_flags, strain, qp_to_rve, new_owner, stiffness, pattern, coupling, plastic_dir
):
    devices = lax.axis_size(("macro", "pool"))
    nodes, columns = history.shape
    comps, voigt = coupling.shape[0], coupling.shape[1]
    per_peer = 2 * columns // devices
    rows = up(nodes, 32)
    deep = up(nodes, 256)
    f32, bf16, i32 = jnp.float32, jnp.bfloat16, jnp.int32
    vmem = pl.BlockSpec(memory_space=pltpu.VMEM)
    small_inputs = (coupling, plastic_dir, strain, new_owner.reshape(1, columns), qp_to_rve, pattern)
    small_rows = up(PATTERN + pattern.size, 8)
    small = pl.pallas_call(
        pack_kernel,
        out_shape=jax.ShapeDtypeStruct((ROOM, nodes), f32),
        in_specs=[vmem] * 5 + [pl.BlockSpec(memory_space=pltpu.SMEM)],
        out_specs=pl.BlockSpec(memory_space=pltpu.HBM),
        scratch_shapes=[pltpu.VMEM((small_rows, nodes), f32), pltpu.SemaphoreType.DMA],
        compiler_params=params(60),
    )(*small_inputs)
    inputs = (small, stiffness, history, yield_flags)
    khi, klo, hist_s, weight_s, strain_s, place_s, qp_s, cstack, loads, pdir = pl.pallas_call(
        functools.partial(prep_kernel, devices, per_peer, comps, voigt),
        out_shape=(
            jax.ShapeDtypeStruct((rows, deep), bf16),
            jax.ShapeDtypeStruct((rows, deep), bf16),
            jax.ShapeDtypeStruct((rows, columns), f32),
            jax.ShapeDtypeStruct((rows, columns), f32),
            jax.ShapeDtypeStruct((8, columns), f32),
            jax.ShapeDtypeStruct((8, columns), i32),
            jax.ShapeDtypeStruct((8, columns), i32),
            jax.ShapeDtypeStruct((comps, 32, rows), bf16),
            jax.ShapeDtypeStruct((comps, rows, 32), bf16),
            jax.ShapeDtypeStruct((comps, rows, LANES), f32),
        ),
        in_specs=[pl.BlockSpec(memory_space=pltpu.HBM)] * 4,
        out_specs=[vmem] * 10,
        scratch_shapes=[pltpu.VMEM((small_rows, nodes), f32)]
        + [pltpu.VMEM(x.shape, x.dtype) for x in inputs[1:]]
        + [pltpu.VMEM((rows, deep), f32), pltpu.VMEM((8, columns), f32),
           pltpu.VMEM((32, rows), f32), pltpu.SemaphoreType.DMA((3 + stiffness.shape[0],))],
        compiler_params=params(46),
    )(*inputs)

    lanes = devices // PLANES
    half = lanes // 2
    group = lanes * per_peer
    tall = height(per_peer, nodes)
    block = lambda count: jax.ShapeDtypeStruct((count * tall, LANES), f32)
    whole = lambda shape: pl.BlockSpec(shape, lambda i: (0,) * len(shape))
    updated, stress_s, ready = [], [], []
    left = 0
    for span in (LANES,) * (columns // LANES):
        part = lambda height: pl.BlockSpec((height, span), lambda i, at=left // span: (0, at))
        wide = comps * span
        outs = [block(half)] if len(updated) < 3 else [block(1)] * half
        done = pl.pallas_call(
            functools.partial(
                solve_kernel, 1.0 / math.sqrt(comps * nodes), per_peer, nodes, left, len(updated)
            ),
            grid=(1,),
            out_shape=(
                jax.ShapeDtypeStruct((rows, span), f32),
                jax.ShapeDtypeStruct((8, span), f32),
                *outs,
            ),
            in_specs=[whole((rows, deep)), whole((rows, deep)), part(rows), part(rows), part(8),
                      whole((comps, 32, rows)), whole((comps, rows, 32)), whole((comps, rows, LANES)),
                      whole((8, columns))]
            + [whole(u.shape) for u in updated],
            out_specs=[whole((rows, span)), whole((8, span))] + [whole(o.shape) for o in outs],
            scratch_shapes=[pltpu.VMEM((ITERS, rows, wide), f32), pltpu.VMEM((rows, wide), f32),
                            pltpu.VMEM((rows, wide), f32), pltpu.VMEM((ITERS, 8, span), f32),
                            pltpu.VMEM((deep, 2 * wide), bf16)],
            compiler_params=params(),
            cost_estimate=pl.CostEstimate(
                flops=18 * rows * deep * wide, bytes_accessed=2**20, transcendentals=0
            ),
        )(khi, klo, hist_s, weight_s, strain_s, cstack, loads, pdir, place_s, *updated)
        updated.append(done[0])
        stress_s.append(done[1])
        ready.append(done[2:])
        left += span
    pair = pl.pallas_call(
        functools.partial(ship_kernel, devices, per_peer, nodes, 2 * group),
        out_shape=block(2 * lanes),
        in_specs=[vmem] * (1 + len(updated)),
        out_specs=vmem,
        compiler_params=params(),
        cost_estimate=pl.CostEstimate(
            flops=4 * rows * columns * columns, bytes_accessed=2**20, transcendentals=0
        ),
    )(place_s, *updated)

    axes = ("macro", "pool")

    def hop(sent, mask):
        return lax.ppermute(sent, axes, [(s, s ^ mask) for s in range(devices)])

    pair, *straight = lax.optimization_barrier((pair, *ready[-1]))
    planes = [list(range(z * lanes, (z + 1) * lanes)) for z in range(PLANES)]
    pair = lax.all_to_all(
        pair.reshape(2 * lanes, tall, LANES), axes, split_axis=0, concat_axis=0, tiled=True,
        axis_index_groups=[planes[0] + planes[3], planes[1] + planes[2]],
    ).reshape(2 * lanes * tall, LANES)
    hops = (2 * lanes, lanes, 2 * lanes + 1)
    landed = []
    for (sent,), mask in zip(ready, hops):
        landed.append(hop(sent, mask))
        landed[-2:] = lax.optimization_barrier(tuple(landed[-2:]))
    joined = pl.pallas_call(
        functools.partial(join_kernel, tall),
        out_shape=(block(3),) * half,
        in_specs=[vmem] * 3,
        out_specs=[vmem] * half,
        compiler_params=params(),
        cost_estimate=pl.CostEstimate(flops=2**40, bytes_accessed=2**20, transcendentals=0),
    )(*landed)
    joined = [sent if i == 0 else hop(sent, 2 * i) for i, sent in enumerate(joined)]
    direct = [hop(sent, lanes + 2 * i + 1) for i, sent in enumerate(straight)]
    *stress_s, joined[0] = lax.optimization_barrier((*stress_s, joined[0]))
    stress_out = pl.pallas_call(
        back_kernel,
        out_shape=jax.ShapeDtypeStruct((voigt, columns), f32),
        in_specs=[vmem] * (1 + len(stress_s)),
        out_specs=vmem,
        compiler_params=params(),
    )(qp_s, *stress_s)
    joined[0], stress_out = lax.optimization_barrier((joined[0], stress_out))
    new_history = pl.pallas_call(
        functools.partial(land_kernel, devices, per_peer),
        out_shape=jax.ShapeDtypeStruct((nodes, devices * per_peer), f32),
        in_specs=[vmem] * (1 + 2 * half),
        out_specs=pl.BlockSpec(memory_space=pl.ANY),
        scratch_shapes=[pltpu.VMEM((8, nodes, LANES), f32), pltpu.SemaphoreType.DMA((8,)),
                        pltpu.VMEM((4, group, deep), f32)],
        compiler_params=params(),
    )(pair, *joined, *direct)
    return (new_history, stress_out)


def solution(mesh):
    return jax.shard_map(
        shards,
        mesh=mesh,
        in_specs=(
            P(None, ("macro", "pool")),
            P(None, ("macro", "pool")),
            P(None, ("macro", "pool")),
            P(("macro", "pool"), None),
            P(("macro", "pool"), None),
            P(),
            P(),
            P(),
            P(),
        ),
        out_specs=(P(None, ("macro", "pool")), P(None, ("macro", "pool"))),
        check_vma=False,
    )
```

```python
import functools
import math

import jax
import jax.numpy as jnp
from jax import lax
from jax.experimental import pallas as pl
from jax.experimental.pallas import tpu as pltpu
from jax.sharding import PartitionSpec as P

ITERS = 3
LANES = 128
PLANES = 4
PATTERN = 32
ROOM = 8192

NN = (((1,), (0,)), ((), ()))
NT = (((1,), (1,)), ((), ()))


def up(value, unit):
    return -(-value // unit) * unit


def dot(a, b, dims=NN):
    return lax.dot_general(a, b, dims, preferred_element_type=jnp.float32)


def halves(x):
    hi = x.astype(jnp.bfloat16)
    lo = (x - hi.astype(jnp.float32)).astype(jnp.bfloat16)
    return hi, lo


def whereabouts(devices):
    me = lax.axis_index("macro") * lax.axis_size("pool") + lax.axis_index("pool")
    lanes = devices // PLANES
    return me, me // lanes, me % lanes, lanes


def hot(row, count):
    rows = lax.broadcasted_iota(jnp.int32, (count, row.shape[1]), 0)
    return jnp.where(rows == row, 1.0, 0.0).astype(jnp.bfloat16)


def pack_kernel(coupling, plastic, strain, owner, qp, pattern, packed, small, sem):
    top = 0
    for c in range(coupling.shape[0]):
        small[top:top + coupling.shape[1], :] = coupling[c]
        top += coupling.shape[1]
    for part in (plastic, strain, owner, qp):
        small[top:top + part.shape[0], 0:part.shape[1]] = part[...].astype(jnp.float32)
        top += part.shape[0]
    count = pattern.shape[0]
    for a in range(count):
        for b in range(count):
            couples = jnp.full((1, LANES), pattern[a, b].astype(jnp.float32))
            small[PATTERN + a * count + b:PATTERN + a * count + b + 1, 0:LANES] = couples
    copy = pltpu.make_async_copy(small, packed.at[pl.ds(0, small.shape[0]), :], sem)
    copy.start()
    copy.wait()


def prep_kernel(devices, per_peer, comps, voigt, *refs):
    sources, outs, local = refs[:4], refs[4:14], refs[14:18]
    kfull, pad, stack, sem = refs[18:]
    khi, klo, hist_s, weight_s, strain_s, place_s, qp_s, cstack, loads, pdir = outs
    small, stiff, hist, flag = local
    copies = [
        pltpu.make_async_copy(source, target, sem.at[i])
        for i, (source, target) in enumerate(
            zip((sources[0].at[pl.ds(0, local[0].shape[0]), :], *sources[1:]), local)
        )
    ]
    for copy in copies:
        copy.start()
    nodes, columns = hist.shape
    nb, blk = stiff.shape[0], stiff.shape[2]
    at_plastic = comps * voigt
    at_strain = at_plastic + comps
    at_owner = at_strain + voigt
    copies[0].wait()

    me, plane, lane, lanes = whereabouts(devices)
    owner = small[at_owner:at_owner + 1, 0:columns].astype(jnp.int32)
    apart = owner // lanes ^ plane
    target = owner % lanes
    away = target ^ lane
    hopping = (away % 2 * 2 + jnp.where(apart == 2, 0, 1)) * (lanes // 2) + away // 2
    staying = jnp.where(apart == 3, 2, 3) * lanes + target
    key = jnp.where((apart == 2) | (apart == 1), hopping, staying)
    key_ids = lax.broadcasted_iota(jnp.int32, (devices, columns), 0)
    mine = jnp.where(key_ids == key, 1.0, 0.0)
    earlier = jnp.where(
        lax.broadcasted_iota(jnp.int32, (columns, columns), 0)
        < lax.broadcasted_iota(jnp.int32, (columns, columns), 1), 1.0, 0.0
    ).astype(jnp.bfloat16)
    before = dot(mine.astype(jnp.bfloat16), earlier)
    rank = jnp.sum(before * mine, axis=0, keepdims=True)
    tally = jnp.sum(mine, axis=1, keepdims=True)
    ahead = jnp.where(key_ids < key, tally, 0.0)
    position = (rank + jnp.sum(ahead, axis=0, keepdims=True)).astype(jnp.int32)

    order = hot(position, columns)
    pad[...] = jnp.zeros_like(pad)
    pad[0:1, :] = key.astype(jnp.float32)
    pad[1:2, :] = rank
    placed = dot(pad[...].astype(jnp.bfloat16), order, NT)
    place_s[...] = jnp.broadcast_to(
        (placed[0:1, :] * per_peer + placed[1:2, :]).astype(jnp.int32), place_s.shape
    )

    pad[0:1, :] = (position // 256).astype(jnp.float32)
    pad[1:2, :] = (position % 256).astype(jnp.float32)
    found = dot(pad[...].astype(jnp.bfloat16), hot(small[at_owner + 1:at_owner + 2, 0:columns].astype(jnp.int32), columns))
    at = (found[0:1, :] * 256.0 + found[1:2, :]).astype(jnp.int32)
    qp_s[...] = jnp.broadcast_to(at, qp_s.shape)
    pad[...] = jnp.zeros_like(pad)
    pad[0:voigt, :] = small[at_strain:at_owner, 0:columns]
    hi, lo = halves(pad[...])
    serves = hot(at, columns)
    strain_s[...] = dot(hi, serves, NT) + dot(lo, serves, NT)

    kfull[...] = jnp.zeros_like(kfull)
    copies[1].wait()
    for a in range(nb):
        for b in range(nb):
            kfull[a * blk:(a + 1) * blk, b * blk:(b + 1) * blk] = (
                stiff[a, b] * small[PATTERN + a * nb + b:PATTERN + a * nb + b + 1, 0:blk]
            )
    k = kfull[...]
    kh = k.astype(jnp.bfloat16)
    khi[...] = kh
    klo[...] = (k - kh.astype(jnp.float32)).astype(jnp.bfloat16)

    copies[2].wait()
    copies[3].wait()
    hi, lo = halves(hist[...])
    hist_s[...] = jnp.zeros_like(hist_s)
    hist_s[0:nodes, :] = dot(hi, order, NT) + dot(lo, order, NT)
    h = hist_s[...]
    weight_s[...] = jnp.zeros_like(weight_s)
    weight_s[0:nodes, :] = dot(flag[...].astype(jnp.float32).astype(jnp.bfloat16), order, NT)
    weight_s[...] = weight_s[...] * h * h / (1.0 + h * h)

    for c in range(comps):
        cpl = small[c * voigt:(c + 1) * voigt, :]
        hi = cpl.astype(jnp.bfloat16).astype(jnp.float32)
        stack[...] = jnp.zeros_like(stack)
        stack[0:voigt, 0:nodes] = hi
        stack[8:8 + voigt, 0:nodes] = hi
        stack[16:16 + voigt, 0:nodes] = cpl - hi
        cstack[c] = stack[...].astype(jnp.bfloat16)
        loads[c] = jnp.transpose(stack[...]).astype(jnp.bfloat16)
    pdir[...] = jnp.zeros_like(pdir)
    for c in range(comps):
        spread = jnp.broadcast_to(small[at_plastic + c:at_plastic + c + 1, :], (LANES, nodes))
        pdir[c, 0:nodes, :] = jnp.transpose(spread)


def row_blocks(rows, span):
    pieces = 4 * span // LANES
    cuts = [rows // 16 * i // pieces * 16 for i in range(pieces + 1)]
    return [slice(top, end) for top, end in zip(cuts, cuts[1:])]


def sweep(rows, comps, span):
    for r in row_blocks(rows, span):
        for c in range(comps):
            yield r, slice(c * span, (c + 1) * span), c


def fold(x):
    return jnp.sum(x.reshape(x.shape[0] // 8, 8, x.shape[1]), axis=0)


def total(parts):
    return jnp.sum(parts, axis=0, keepdims=True)


def solve_kernel(scale, cap, nodes, first, earlier, khi, klo, hist, weight, strain, cstack, loads, pdir, place,
                 *refs):
    earlier_updated, refs = refs[:earlier], refs[earlier:]
    updated, stress, blocks = refs[0], refs[1], refs[2:-5]
    field, resid, image, steps, split = refs[-5:]
    rows, span = hist.shape
    comps = pdir.shape[0]
    wide = comps * span
    zero = jnp.zeros((8, span), jnp.float32)

    def flow(c, r):
        return jnp.concatenate([pdir[c, r, :]] * (span // LANES), axis=1)

    def keep(r, c, x):
        split[r, c * span:(c + 1) * span], split[r, wide + c * span:wide + (c + 1) * span] = (
            halves(x)
        )

    s = strain[...]
    s_hi = s.astype(jnp.bfloat16).astype(jnp.float32)
    s3 = jnp.concatenate([s_hi, s - s_hi, s_hi, jnp.zeros_like(s)], axis=0).astype(jnp.bfloat16)
    split[rows:, :] = jnp.zeros((split.shape[0] - rows, 2 * wide), jnp.bfloat16)
    for c in range(comps):
        image[:, c * span:(c + 1) * span] = dot(loads[c], s3)
    parts = zero
    for r, l, c in sweep(rows, comps, span):
        d = image[r, l] - weight[r, :] * hist[r, :] * flow(c, r)
        resid[r, l] = d
        field[0, r, l] = d
        keep(r, c, d)
        parts = parts + fold(d * d)
    norm = total(parts)

    def step_length(turn, norm):
        parts = zero
        for r in row_blocks(rows, span):
            both = dot(khi[r, :], split[...])
            low = dot(klo[r, :], split[:, 0:wide])
            tangent = 1.5 - weight[r, :]
            for c in range(comps):
                l = slice(c * span, (c + 1) * span)
                d = field[turn, r, l]
                q = both[:, l] + both[:, wide + c * span:wide + (c + 1) * span] + low[:, l]
                q = q + tangent * d
                image[r, l] = q
                parts = parts + fold(d * q)
        return norm / jnp.maximum(total(parts), 1.0)

    def step(turn, norm):
        alpha = step_length(turn, norm)
        steps[turn] = jnp.broadcast_to(alpha, steps.shape[1:])
        parts = zero
        for r, l, c in sweep(rows, comps, span):
            left = resid[r, l] - alpha * image[r, l]
            resid[r, l] = left
            parts = parts + fold(left * left)
        following = total(parts)
        beta = following / jnp.maximum(norm, 1.0)
        for r, l, c in sweep(rows, comps, span):
            d = resid[r, l] + beta * field[turn, r, l]
            field[turn + 1, r, l] = d
            keep(r, c, d)
        return following

    last = ITERS - 1
    alpha = step_length(last, lax.fori_loop(0, last, step, norm))
    alphas = [steps[turn, 0:1, :] for turn in range(last)]
    for r, l, c in sweep(rows, comps, span):
        x = alphas[0] * field[0, r, l]
        for turn in range(1, last):
            x = x + alphas[turn] * field[turn, r, l]
        x = x + alpha * field[last, r, l]
        pushed = flow(c, r) * x
        image[r, 0:span] = pushed if c == 0 else image[r, 0:span] + pushed
        lead = 2 * c * span
        split[r, lead:lead + span], split[r, lead + span:lead + 2 * span] = halves(
            (1.5 - weight[r, :]) * x
        )
    updated[...] = hist[...] + weight[...] * image[:, 0:span]
    sent = placed_rows(first, LANES, place, [*earlier_updated, updated], split.shape[0])
    part = LANES // len(blocks)
    for i, block in enumerate(blocks):
        put(block, 0, sent[i * part:(i + 1) * part], cap, nodes)
    out = s
    for c in range(comps):
        cpl = cstack[c]
        both = dot(cpl, split[0:rows, 2 * c * span:2 * (c + 1) * span])
        out = out + scale * (both[0:8, 0:span] + both[16:24, 0:span] + both[0:8, span:])
    stress[...] = out


def placed_rows(first, count, place, sources, deep):
    width = sum(source.shape[1] for source in sources)
    placing = hot(place[0:1, 0:width] - first, count)
    sums, left = 0.0, 0
    for source in sources:
        rest = jnp.zeros((deep - source.shape[0], source.shape[1]), jnp.float32)
        hi, lo = halves(jnp.concatenate([source[...], rest], axis=0))
        cut = placing[:, left:left + source.shape[1]]
        sums = sums + (dot(cut, hi, NT) + dot(cut, lo, NT))
        left += source.shape[1]
    return sums


def tight(cap, nodes):
    return cap % 32 == 0 and LANES // 2 < nodes % LANES <= LANES * 3 // 4


def height(cap, nodes):
    return cap * (nodes // LANES) + (cap // 2 + cap // 4 if tight(cap, nodes) else cap)


def put(block, top, rows, cap, nodes):
    full, half, quarter = nodes // LANES, cap // 2, cap // 4

    def store(at, piece):
        block[pl.ds(at, piece.shape[0]), :] = piece
        return at + piece.shape[0]

    for first in range(0, rows.shape[0], cap):
        for t in range(full):
            top = store(top, rows[first:first + cap, t * LANES:(t + 1) * LANES])
        tail = rows[first:first + cap, full * LANES:]
        if not tight(cap, nodes):
            top = store(top, tail)
            continue
        lane = lax.broadcasted_iota(jnp.int32, (half, LANES), 1)
        top = store(top, jnp.where(lane < LANES // 2, tail[0:half],
                                   pltpu.roll(tail[half:], LANES // 2, 1)))
        lane = lax.broadcasted_iota(jnp.int32, (quarter, LANES), 1) // (LANES // 4)
        mixed = tail[0:quarter]
        for g in range(4):
            moved = pltpu.roll(tail[g * quarter:(g + 1) * quarter], (g + 2) % 4 * (LANES // 4), 1)
            mixed = jnp.where(lane == g, moved, mixed)
        top = store(top, mixed)


def take(block, top, target, at, cap, nodes):
    full, half, quarter = nodes // LANES, cap // 2, cap // 4
    for t in range(full):
        target[pl.ds(at, cap), t * LANES:(t + 1) * LANES] = block[top + t * cap:top + (t + 1) * cap, :]
    top = top + full * cap
    if not tight(cap, nodes):
        target[pl.ds(at, cap), full * LANES:] = block[top:top + cap, :]
        return
    lane = lax.broadcasted_iota(jnp.int32, (quarter, LANES), 1)
    mixed = block[top + half:top + half + quarter, :]
    for g in range(4):
        left = block[top + g % 2 * quarter:top + (g % 2 + 1) * quarter, :]
        if g >= 2:
            left = pltpu.roll(left, LANES // 2, 1)
        right = mixed if g == 2 else pltpu.roll(mixed, (6 - g) % 4 * (LANES // 4), 1)
        row = pl.multiple_of(at + g * quarter, quarter)
        target[pl.ds(row, quarter), full * LANES:] = jnp.where(lane < LANES // 2, left, right)


def ship_kernel(devices, cap, nodes, first, place, *refs):
    updated, pair = refs[:-1], refs[-1]
    me, plane, lane, lanes = whereabouts(devices)
    group, span = lanes * cap, lanes * height(cap, nodes)
    rows = placed_rows(first, 2 * group, place, updated, up(nodes, 256))
    put(pair, pl.multiple_of((1 - plane // 2) * span, 8), rows[0:group], cap, nodes)
    put(pair, pl.multiple_of(plane // 2 * span, 8), rows[group:], cap, nodes)


def back_kernel(at, *refs):
    out = refs[-1]
    hi, lo = halves(jnp.concatenate([ref[...] for ref in refs[:-1]], axis=1))
    serves = hot(at[0:1, :], hi.shape[1])
    out[...] = (dot(hi, serves) + dot(lo, serves))[0:out.shape[0], :]


def join_kernel(tall, *refs):
    landed, blocks = refs[:3], refs[3:]
    for i, block in enumerate(blocks):
        for k, rows in enumerate(landed):
            block[k * tall:(k + 1) * tall, :] = rows[i * tall:(i + 1) * tall, :]


def land(tile, out, stage, sem, slot, at):
    nodes = out.shape[0]
    stage[slot] = jnp.transpose(tile)[0:nodes, :]
    columns = pl.multiple_of(at * LANES, LANES)
    copy = pltpu.make_async_copy(stage.at[slot], out.at[:, pl.ds(columns, LANES)], sem.at[slot])
    copy.start()
    return copy


def land_kernel(devices, cap, pair, *refs):
    blocks, (out, stage, sem, gather, fetched, arrival) = refs[:-6], refs[-6:]
    me, plane, lane, lanes = whereabouts(devices)
    nodes, tall = out.shape[0], height(cap, out.shape[0])
    tiles, span = lanes * cap // LANES, lanes * tall
    fetches = [
        pltpu.make_async_copy(pair.at[pl.ds(i * span, span), :], fetched.at[i], arrival.at[i])
        for i in range(2)
    ]
    for fetch in fetches:
        fetch.start()
    copies = []
    for i in (2, 3, 0, 1):
        if i < 2:
            fetches[i].wait()
        target = gather.at[i]
        for k in range(lanes):
            if i < 2:
                take(fetched.at[i], k * tall, target, k * cap, cap, nodes)
                continue
            at = pl.multiple_of((lane ^ k) * cap, cap)
            if i == 3 and k % 2 == 1:
                take(blocks[lanes // 2 + k // 2], 0, target, at, cap, nodes)
            else:
                take(blocks[k // 2], (2 * (k % 2) + i - 2) * tall, target, at, cap, nodes)
        if i < 2:
            source = jnp.where(plane // 2 == i, plane, plane ^ 3)
        else:
            source = plane ^ (4 - i)
        for part in range(tiles):
            tile = gather[i, part * LANES:(part + 1) * LANES, :]
            copies.append(land(tile, out, stage, sem, i * tiles + part, source * tiles + part))
    for copy in copies:
        copy.wait()


def params(mib=24):
    return pltpu.CompilerParams(vmem_limit_bytes=mib * 2**20)


def shards(
    history, yield_flags, strain, qp_to_rve, new_owner, stiffness, pattern, coupling, plastic_dir
):
    devices = lax.axis_size(("macro", "pool"))
    nodes, columns = history.shape
    comps, voigt = coupling.shape[0], coupling.shape[1]
    per_peer = 2 * columns // devices
    rows = up(nodes, 32)
    deep = up(nodes, 256)
    f32, bf16, i32 = jnp.float32, jnp.bfloat16, jnp.int32
    vmem = pl.BlockSpec(memory_space=pltpu.VMEM)
    small_inputs = (coupling, plastic_dir, strain, new_owner.reshape(1, columns), qp_to_rve, pattern)
    small_rows = up(PATTERN + pattern.size, 8)
    small = pl.pallas_call(
        pack_kernel,
        out_shape=jax.ShapeDtypeStruct((ROOM, nodes), f32),
        in_specs=[vmem] * 5 + [pl.BlockSpec(memory_space=pltpu.SMEM)],
        out_specs=pl.BlockSpec(memory_space=pltpu.HBM),
        scratch_shapes=[pltpu.VMEM((small_rows, nodes), f32), pltpu.SemaphoreType.DMA],
        compiler_params=params(60),
    )(*small_inputs)
    inputs = (small, stiffness, history, yield_flags)
    khi, klo, hist_s, weight_s, strain_s, place_s, qp_s, cstack, loads, pdir = pl.pallas_call(
        functools.partial(prep_kernel, devices, per_peer, comps, voigt),
        out_shape=(
            jax.ShapeDtypeStruct((rows, deep), bf16),
            jax.ShapeDtypeStruct((rows, deep), bf16),
            jax.ShapeDtypeStruct((rows, columns), f32),
            jax.ShapeDtypeStruct((rows, columns), f32),
            jax.ShapeDtypeStruct((8, columns), f32),
            jax.ShapeDtypeStruct((8, columns), i32),
            jax.ShapeDtypeStruct((8, columns), i32),
            jax.ShapeDtypeStruct((comps, 32, rows), bf16),
            jax.ShapeDtypeStruct((comps, rows, 32), bf16),
            jax.ShapeDtypeStruct((comps, rows, LANES), f32),
        ),
        in_specs=[pl.BlockSpec(memory_space=pltpu.HBM)] * 4,
        out_specs=[vmem] * 10,
        scratch_shapes=[pltpu.VMEM((small_rows, nodes), f32)]
        + [pltpu.VMEM(x.shape, x.dtype) for x in inputs[1:]]
        + [pltpu.VMEM((rows, deep), f32), pltpu.VMEM((8, columns), f32),
           pltpu.VMEM((32, rows), f32), pltpu.SemaphoreType.DMA((4,))],
        compiler_params=params(46),
    )(*inputs)

    lanes = devices // PLANES
    half = lanes // 2
    group = lanes * per_peer
    tall = height(per_peer, nodes)
    block = lambda count: jax.ShapeDtypeStruct((count * tall, LANES), f32)
    whole = lambda shape: pl.BlockSpec(shape, lambda i: (0,) * len(shape))
    updated, stress_s, ready = [], [], []
    left = 0
    for span in (LANES,) * (columns // LANES):
        part = lambda height: pl.BlockSpec((height, span), lambda i, at=left // span: (0, at))
        wide = comps * span
        outs = [block(half)] if len(updated) < 3 else [block(1)] * half
        done = pl.pallas_call(
            functools.partial(
                solve_kernel, 1.0 / math.sqrt(comps * nodes), per_peer, nodes, left, len(updated)
            ),
            grid=(1,),
            out_shape=(
                jax.ShapeDtypeStruct((rows, span), f32),
                jax.ShapeDtypeStruct((8, span), f32),
                *outs,
            ),
            in_specs=[whole((rows, deep)), whole((rows, deep)), part(rows), part(rows), part(8),
                      whole((comps, 32, rows)), whole((comps, rows, 32)), whole((comps, rows, LANES)),
                      whole((8, columns))]
            + [whole(u.shape) for u in updated],
            out_specs=[whole((rows, span)), whole((8, span))] + [whole(o.shape) for o in outs],
            scratch_shapes=[pltpu.VMEM((ITERS, rows, wide), f32), pltpu.VMEM((rows, wide), f32),
                            pltpu.VMEM((rows, wide), f32), pltpu.VMEM((ITERS, 8, span), f32),
                            pltpu.VMEM((deep, 2 * wide), bf16)],
            compiler_params=params(),
            cost_estimate=pl.CostEstimate(
                flops=18 * rows * deep * wide, bytes_accessed=2**20, transcendentals=0
            ),
        )(khi, klo, hist_s, weight_s, strain_s, cstack, loads, pdir, place_s, *updated)
        updated.append(done[0])
        stress_s.append(done[1])
        ready.append(done[2:])
        left += span
    pair = pl.pallas_call(
        functools.partial(ship_kernel, devices, per_peer, nodes, 2 * group),
        out_shape=block(2 * lanes),
        in_specs=[vmem] * (1 + len(updated)),
        out_specs=vmem,
        compiler_params=params(),
        cost_estimate=pl.CostEstimate(
            flops=4 * rows * columns * columns, bytes_accessed=2**20, transcendentals=0
        ),
    )(place_s, *updated)

    axes = ("macro", "pool")

    def hop(sent, mask):
        return lax.ppermute(sent, axes, [(s, s ^ mask) for s in range(devices)])

    pair, *straight = lax.optimization_barrier((pair, *ready[-1]))
    planes = [list(range(z * lanes, (z + 1) * lanes)) for z in range(PLANES)]
    pair = lax.all_to_all(
        pair.reshape(2 * lanes, tall, LANES), axes, split_axis=0, concat_axis=0, tiled=True,
        axis_index_groups=[planes[0] + planes[3], planes[1] + planes[2]],
    ).reshape(2 * lanes * tall, LANES)
    hops = (2 * lanes, lanes, 2 * lanes + 1)
    landed = []
    for (sent,), mask in zip(ready, hops):
        landed.append(hop(sent, mask))
        landed[-2:] = lax.optimization_barrier(tuple(landed[-2:]))
    joined = pl.pallas_call(
        functools.partial(join_kernel, tall),
        out_shape=(block(3),) * half,
        in_specs=[vmem] * 3,
        out_specs=[vmem] * half,
        compiler_params=params(),
        cost_estimate=pl.CostEstimate(flops=2**40, bytes_accessed=2**20, transcendentals=0),
    )(*landed)
    joined = [sent if i == 0 else hop(sent, 2 * i) for i, sent in enumerate(joined)]
    direct = [hop(sent, lanes + 2 * i + 1) for i, sent in enumerate(straight)]
    *stress_s, joined[0] = lax.optimization_barrier((*stress_s, joined[0]))
    stress_out = pl.pallas_call(
        back_kernel,
        out_shape=jax.ShapeDtypeStruct((voigt, columns), f32),
        in_specs=[vmem] * (1 + len(stress_s)),
        out_specs=vmem,
        compiler_params=params(),
    )(qp_s, *stress_s)
    joined[0], stress_out = lax.optimization_barrier((joined[0], stress_out))
    new_history = pl.pallas_call(
        functools.partial(land_kernel, devices, per_peer),
        out_shape=jax.ShapeDtypeStruct((nodes, devices * per_peer), f32),
        in_specs=[pl.BlockSpec(memory_space=pltpu.HBM)] + [vmem] * (2 * half),
        out_specs=pl.BlockSpec(memory_space=pl.ANY),
        scratch_shapes=[pltpu.VMEM((8, nodes, LANES), f32), pltpu.SemaphoreType.DMA((8,)),
                        pltpu.VMEM((4, group, deep), f32),
                        pltpu.VMEM((2, lanes * tall, LANES), f32), pltpu.SemaphoreType.DMA((2,))],
        compiler_params=params(),
    )(pair, *joined, *direct)
    return (new_history, stress_out)


def solution(mesh):
    return jax.shard_map(
        shards,
        mesh=mesh,
        in_specs=(
            P(None, ("macro", "pool")),
            P(None, ("macro", "pool")),
            P(None, ("macro", "pool")),
            P(("macro", "pool"), None),
            P(("macro", "pool"), None),
            P(),
            P(),
            P(),
            P(),
        ),
        out_specs=(P(None, ("macro", "pool")), P(None, ("macro", "pool"))),
        check_vma=False,
    )
```

```python
import functools
import math

import jax
import jax.numpy as jnp
from jax import lax
from jax.experimental import pallas as pl
from jax.experimental.pallas import tpu as pltpu
from jax.sharding import PartitionSpec as P

ITERS = 3
LANES = 128
PLANES = 4
PATTERN = 32
ROOM = 8192

NN = (((1,), (0,)), ((), ()))
NT = (((1,), (1,)), ((), ()))


def up(value, unit):
    return -(-value // unit) * unit


def dot(a, b, dims=NN):
    return lax.dot_general(a, b, dims, preferred_element_type=jnp.float32)


def halves(x):
    hi = x.astype(jnp.bfloat16)
    lo = (x - hi.astype(jnp.float32)).astype(jnp.bfloat16)
    return hi, lo


def whereabouts(devices):
    me = lax.axis_index("macro") * lax.axis_size("pool") + lax.axis_index("pool")
    lanes = devices // PLANES
    return me, me // lanes, me % lanes, lanes


def hot(row, count):
    rows = lax.broadcasted_iota(jnp.int32, (count, row.shape[1]), 0)
    return jnp.where(rows == row, 1.0, 0.0).astype(jnp.bfloat16)


def pack_kernel(coupling, plastic, strain, owner, qp, pattern, packed, small, sem):
    top = 0
    for c in range(coupling.shape[0]):
        small[top:top + coupling.shape[1], :] = coupling[c]
        top += coupling.shape[1]
    for part in (plastic, strain, owner, qp):
        small[top:top + part.shape[0], 0:part.shape[1]] = part[...].astype(jnp.float32)
        top += part.shape[0]
    count = pattern.shape[0]
    for a in range(count):
        for b in range(count):
            couples = jnp.full((1, LANES), pattern[a, b].astype(jnp.float32))
            small[PATTERN + a * count + b:PATTERN + a * count + b + 1, 0:LANES] = couples
    copy = pltpu.make_async_copy(small, packed.at[pl.ds(0, small.shape[0]), :], sem)
    copy.start()
    copy.wait()


def prep_kernel(devices, per_peer, comps, voigt, *refs):
    sources, outs, local = refs[:4], refs[4:14], refs[14:18]
    kfull, pad, stack, sem = refs[18:]
    khi, klo, hist_s, weight_s, strain_s, place_s, qp_s, cstack, loads, pdir = outs
    small, stiff, hist, flag = local
    copies = [
        pltpu.make_async_copy(source, target, sem.at[i])
        for i, (source, target) in enumerate(
            zip((sources[0].at[pl.ds(0, local[0].shape[0]), :], *sources[1:]), local)
        )
    ]
    for copy in copies:
        copy.start()
    nodes, columns = hist.shape
    nb, blk = stiff.shape[0], stiff.shape[2]
    at_plastic = comps * voigt
    at_strain = at_plastic + comps
    at_owner = at_strain + voigt
    copies[0].wait()

    me, plane, lane, lanes = whereabouts(devices)
    owner = small[at_owner:at_owner + 1, 0:columns].astype(jnp.int32)
    apart = owner // lanes ^ plane
    target = owner % lanes
    away = target ^ lane
    hopping = (away % 2 * 2 + jnp.where(apart == 2, 0, 1)) * (lanes // 2) + away // 2
    staying = jnp.where(apart == 3, 2, 3) * lanes + target
    key = jnp.where((apart == 2) | (apart == 1), hopping, staying)
    key_ids = lax.broadcasted_iota(jnp.int32, (devices, columns), 0)
    mine = jnp.where(key_ids == key, 1.0, 0.0)
    earlier = jnp.where(
        lax.broadcasted_iota(jnp.int32, (columns, columns), 0)
        < lax.broadcasted_iota(jnp.int32, (columns, columns), 1), 1.0, 0.0
    ).astype(jnp.bfloat16)
    before = dot(mine.astype(jnp.bfloat16), earlier)
    rank = jnp.sum(before * mine, axis=0, keepdims=True)
    tally = jnp.sum(mine, axis=1, keepdims=True)
    ahead = jnp.where(key_ids < key, tally, 0.0)
    position = (rank + jnp.sum(ahead, axis=0, keepdims=True)).astype(jnp.int32)

    order = hot(position, columns)
    pad[...] = jnp.zeros_like(pad)
    pad[0:1, :] = key.astype(jnp.float32)
    pad[1:2, :] = rank
    placed = dot(pad[...].astype(jnp.bfloat16), order, NT)
    place_s[...] = jnp.broadcast_to(
        (placed[0:1, :] * per_peer + placed[1:2, :]).astype(jnp.int32), place_s.shape
    )

    pad[0:1, :] = (position // 256).astype(jnp.float32)
    pad[1:2, :] = (position % 256).astype(jnp.float32)
    found = dot(pad[...].astype(jnp.bfloat16), hot(small[at_owner + 1:at_owner + 2, 0:columns].astype(jnp.int32), columns))
    at = (found[0:1, :] * 256.0 + found[1:2, :]).astype(jnp.int32)
    qp_s[...] = jnp.broadcast_to(at, qp_s.shape)
    pad[...] = jnp.zeros_like(pad)
    pad[0:voigt, :] = small[at_strain:at_owner, 0:columns]
    hi, lo = halves(pad[...])
    serves = hot(at, columns)
    strain_s[...] = dot(hi, serves, NT) + dot(lo, serves, NT)

    kfull[...] = jnp.zeros_like(kfull)
    copies[1].wait()
    for a in range(nb):
        for b in range(nb):
            kfull[a * blk:(a + 1) * blk, b * blk:(b + 1) * blk] = (
                stiff[a, b] * small[PATTERN + a * nb + b:PATTERN + a * nb + b + 1, 0:blk]
            )
    k = kfull[...]
    kh = k.astype(jnp.bfloat16)
    khi[...] = kh
    klo[...] = (k - kh.astype(jnp.float32)).astype(jnp.bfloat16)

    copies[2].wait()
    copies[3].wait()
    hi, lo = halves(hist[...])
    hist_s[...] = jnp.zeros_like(hist_s)
    hist_s[0:nodes, :] = dot(hi, order, NT) + dot(lo, order, NT)
    h = hist_s[...]
    weight_s[...] = jnp.zeros_like(weight_s)
    weight_s[0:nodes, :] = dot(flag[...].astype(jnp.float32).astype(jnp.bfloat16), order, NT)
    weight_s[...] = weight_s[...] * h * h / (1.0 + h * h)

    for c in range(comps):
        cpl = small[c * voigt:(c + 1) * voigt, :]
        hi = cpl.astype(jnp.bfloat16).astype(jnp.float32)
        stack[...] = jnp.zeros_like(stack)
        stack[0:voigt, 0:nodes] = hi
        stack[8:8 + voigt, 0:nodes] = hi
        stack[16:16 + voigt, 0:nodes] = cpl - hi
        cstack[c] = stack[...].astype(jnp.bfloat16)
        loads[c] = jnp.transpose(stack[...]).astype(jnp.bfloat16)
    pdir[...] = jnp.zeros_like(pdir)
    for c in range(comps):
        spread = jnp.broadcast_to(small[at_plastic + c:at_plastic + c + 1, :], (LANES, nodes))
        pdir[c, 0:nodes, :] = jnp.transpose(spread)


def row_blocks(rows, span):
    pieces = 4 * span // LANES
    cuts = [rows // 16 * i // pieces * 16 for i in range(pieces + 1)]
    return [slice(top, end) for top, end in zip(cuts, cuts[1:])]


def sweep(rows, comps, span):
    for r in row_blocks(rows, span):
        for c in range(comps):
            yield r, slice(c * span, (c + 1) * span), c


def fold(x):
    return jnp.sum(x.reshape(x.shape[0] // 8, 8, x.shape[1]), axis=0)


def total(parts):
    return jnp.sum(parts, axis=0, keepdims=True)


def solve_kernel(scale, cap, nodes, first, earlier, khi, klo, hist, weight, strain, cstack, loads, pdir, place,
                 *refs):
    earlier_updated, refs = refs[:earlier], refs[earlier:]
    updated, stress, blocks = refs[0], refs[1], refs[2:-5]
    field, resid, image, steps, split = refs[-5:]
    rows, span = hist.shape
    comps = pdir.shape[0]
    wide = comps * span
    zero = jnp.zeros((8, span), jnp.float32)

    def flow(c, r):
        return jnp.concatenate([pdir[c, r, :]] * (span // LANES), axis=1)

    def keep(r, c, x):
        split[r, c * span:(c + 1) * span], split[r, wide + c * span:wide + (c + 1) * span] = (
            halves(x)
        )

    s = strain[...]
    s_hi = s.astype(jnp.bfloat16).astype(jnp.float32)
    s3 = jnp.concatenate([s_hi, s - s_hi, s_hi, jnp.zeros_like(s)], axis=0).astype(jnp.bfloat16)
    split[rows:, :] = jnp.zeros((split.shape[0] - rows, 2 * wide), jnp.bfloat16)
    for c in range(comps):
        image[:, c * span:(c + 1) * span] = dot(loads[c], s3)
    parts = zero
    for r, l, c in sweep(rows, comps, span):
        d = image[r, l] - weight[r, :] * hist[r, :] * flow(c, r)
        resid[r, l] = d
        field[0, r, l] = d
        keep(r, c, d)
        parts = parts + fold(d * d)
    norm = total(parts)

    def step_length(turn, norm):
        parts = zero
        for r in row_blocks(rows, span):
            both = dot(khi[r, :], split[...])
            low = dot(klo[r, :], split[:, 0:wide])
            tangent = 1.5 - weight[r, :]
            for c in range(comps):
                l = slice(c * span, (c + 1) * span)
                d = field[turn, r, l]
                q = both[:, l] + both[:, wide + c * span:wide + (c + 1) * span] + low[:, l]
                q = q + tangent * d
                image[r, l] = q
                parts = parts + fold(d * q)
        return norm / jnp.maximum(total(parts), 1.0)

    def step(turn, norm):
        alpha = step_length(turn, norm)
        steps[turn] = jnp.broadcast_to(alpha, steps.shape[1:])
        parts = zero
        for r, l, c in sweep(rows, comps, span):
            left = resid[r, l] - alpha * image[r, l]
            resid[r, l] = left
            parts = parts + fold(left * left)
        following = total(parts)
        beta = following / jnp.maximum(norm, 1.0)
        for r, l, c in sweep(rows, comps, span):
            d = resid[r, l] + beta * field[turn, r, l]
            field[turn + 1, r, l] = d
            keep(r, c, d)
        return following

    last = ITERS - 1
    alpha = step_length(last, lax.fori_loop(0, last, step, norm))
    alphas = [steps[turn, 0:1, :] for turn in range(last)]
    for r, l, c in sweep(rows, comps, span):
        x = alphas[0] * field[0, r, l]
        for turn in range(1, last):
            x = x + alphas[turn] * field[turn, r, l]
        x = x + alpha * field[last, r, l]
        pushed = flow(c, r) * x
        image[r, 0:span] = pushed if c == 0 else image[r, 0:span] + pushed
        lead = 2 * c * span
        split[r, lead:lead + span], split[r, lead + span:lead + 2 * span] = halves(
            (1.5 - weight[r, :]) * x
        )
    updated[...] = hist[...] + weight[...] * image[:, 0:span]
    sent = placed_rows(first, LANES, place, [*earlier_updated, updated], split.shape[0])
    part = LANES // len(blocks)
    for i, block in enumerate(blocks):
        put(block, 0, sent[i * part:(i + 1) * part], cap, nodes)
    out = s
    for c in range(comps):
        cpl = cstack[c]
        both = dot(cpl, split[0:rows, 2 * c * span:2 * (c + 1) * span])
        out = out + scale * (both[0:8, 0:span] + both[16:24, 0:span] + both[0:8, span:])
    stress[...] = out


def placed_rows(first, count, place, sources, deep):
    width = sum(source.shape[1] for source in sources)
    placing = hot(place[0:1, 0:width] - first, count)
    sums, left = 0.0, 0
    for source in sources:
        rest = jnp.zeros((deep - source.shape[0], source.shape[1]), jnp.float32)
        hi, lo = halves(jnp.concatenate([source[...], rest], axis=0))
        cut = placing[:, left:left + source.shape[1]]
        sums = sums + (dot(cut, hi, NT) + dot(cut, lo, NT))
        left += source.shape[1]
    return sums


def tight(cap, nodes):
    return cap % 32 == 0 and LANES // 2 < nodes % LANES <= LANES * 3 // 4


def height(cap, nodes):
    return cap * (nodes // LANES) + (cap // 2 + cap // 4 if tight(cap, nodes) else cap)


def put(block, top, rows, cap, nodes):
    full, half, quarter = nodes // LANES, cap // 2, cap // 4

    def store(at, piece):
        block[pl.ds(at, piece.shape[0]), :] = piece
        return at + piece.shape[0]

    for first in range(0, rows.shape[0], cap):
        for t in range(full):
            top = store(top, rows[first:first + cap, t * LANES:(t + 1) * LANES])
        tail = rows[first:first + cap, full * LANES:]
        if not tight(cap, nodes):
            top = store(top, tail)
            continue
        lane = lax.broadcasted_iota(jnp.int32, (half, LANES), 1)
        top = store(top, jnp.where(lane < LANES // 2, tail[0:half],
                                   pltpu.roll(tail[half:], LANES // 2, 1)))
        lane = lax.broadcasted_iota(jnp.int32, (quarter, LANES), 1) // (LANES // 4)
        mixed = tail[0:quarter]
        for g in range(4):
            moved = pltpu.roll(tail[g * quarter:(g + 1) * quarter], (g + 2) % 4 * (LANES // 4), 1)
            mixed = jnp.where(lane == g, moved, mixed)
        top = store(top, mixed)


def take(block, top, target, at, cap, nodes):
    full, half, quarter = nodes // LANES, cap // 2, cap // 4
    for t in range(full):
        target[pl.ds(at, cap), t * LANES:(t + 1) * LANES] = block[top + t * cap:top + (t + 1) * cap, :]
    top = top + full * cap
    if not tight(cap, nodes):
        target[pl.ds(at, cap), full * LANES:] = block[top:top + cap, :]
        return
    lane = lax.broadcasted_iota(jnp.int32, (quarter, LANES), 1)
    mixed = block[top + half:top + half + quarter, :]
    for g in range(4):
        left = block[top + g % 2 * quarter:top + (g % 2 + 1) * quarter, :]
        if g >= 2:
            left = pltpu.roll(left, LANES // 2, 1)
        right = mixed if g == 2 else pltpu.roll(mixed, (6 - g) % 4 * (LANES // 4), 1)
        row = pl.multiple_of(at + g * quarter, quarter)
        target[pl.ds(row, quarter), full * LANES:] = jnp.where(lane < LANES // 2, left, right)


def ship_kernel(devices, cap, nodes, first, place, *refs):
    updated, pair = refs[:-1], refs[-1]
    me, plane, lane, lanes = whereabouts(devices)
    group, span = lanes * cap, lanes * height(cap, nodes)
    rows = placed_rows(first, 2 * group, place, updated, up(nodes, 256))
    put(pair, pl.multiple_of((1 - plane // 2) * span, 8), rows[0:group], cap, nodes)
    put(pair, pl.multiple_of(plane // 2 * span, 8), rows[group:], cap, nodes)


def back_kernel(at, *refs):
    out = refs[-1]
    hi, lo = halves(jnp.concatenate([ref[...] for ref in refs[:-1]], axis=1))
    serves = hot(at[0:1, :], hi.shape[1])
    out[...] = (dot(hi, serves) + dot(lo, serves))[0:out.shape[0], :]


def join_kernel(tall, *refs):
    landed, blocks = refs[:3], refs[3:]
    for i, block in enumerate(blocks):
        for k, rows in enumerate(landed):
            block[k * tall:(k + 1) * tall, :] = rows[i * tall:(i + 1) * tall, :]


def land(tile, out, stage, sem, slot, at):
    nodes = out.shape[0]
    stage[slot] = jnp.transpose(tile)[0:nodes, :]
    columns = pl.multiple_of(at * LANES, LANES)
    copy = pltpu.make_async_copy(stage.at[slot], out.at[:, pl.ds(columns, LANES)], sem.at[slot])
    copy.start()
    return copy


def land_pair(devices, cap, pair, out, stage, sem, gather):
    me, plane, lane, lanes = whereabouts(devices)
    nodes, tall = out.shape[0], height(cap, out.shape[0])
    tiles = lanes * cap // LANES
    copies = []
    for i in range(2):
        for k in range(lanes):
            take(pair, (i * lanes + k) * tall, gather.at[i], k * cap, cap, nodes)
        source = jnp.where(plane // 2 == i, plane, plane ^ 3)
        for part in range(tiles):
            tile = gather[i, part * LANES:(part + 1) * LANES, :]
            copies.append(land(tile, out, stage, sem, i * tiles + part, source * tiles + part))
    for copy in copies:
        copy.wait()


def land_hops(devices, cap, *refs):
    blocks, (out, stage, sem, gather) = refs[:-5], refs[-4:]
    me, plane, lane, lanes = whereabouts(devices)
    nodes, tall = out.shape[0], height(cap, out.shape[0])
    tiles = lanes * cap // LANES
    copies = []
    for i in range(2):
        for k in range(lanes):
            at = pl.multiple_of((lane ^ k) * cap, cap)
            if i == 1 and k % 2 == 1:
                take(blocks[lanes // 2 + k // 2], 0, gather.at[i], at, cap, nodes)
            else:
                take(blocks[k // 2], (2 * (k % 2) + i) * tall, gather.at[i], at, cap, nodes)
        source = plane ^ (2 - i)
        for part in range(tiles):
            tile = gather[i, part * LANES:(part + 1) * LANES, :]
            copies.append(land(tile, out, stage, sem, i * tiles + part, source * tiles + part))
    for copy in copies:
        copy.wait()


def params(mib=24):
    return pltpu.CompilerParams(vmem_limit_bytes=mib * 2**20)


def shards(
    history, yield_flags, strain, qp_to_rve, new_owner, stiffness, pattern, coupling, plastic_dir
):
    devices = lax.axis_size(("macro", "pool"))
    nodes, columns = history.shape
    comps, voigt = coupling.shape[0], coupling.shape[1]
    per_peer = 2 * columns // devices
    rows = up(nodes, 32)
    deep = up(nodes, 256)
    f32, bf16, i32 = jnp.float32, jnp.bfloat16, jnp.int32
    vmem = pl.BlockSpec(memory_space=pltpu.VMEM)
    small_inputs = (coupling, plastic_dir, strain, new_owner.reshape(1, columns), qp_to_rve, pattern)
    small_rows = up(PATTERN + pattern.size, 8)
    small = pl.pallas_call(
        pack_kernel,
        out_shape=jax.ShapeDtypeStruct((ROOM, nodes), f32),
        in_specs=[vmem] * 5 + [pl.BlockSpec(memory_space=pltpu.SMEM)],
        out_specs=pl.BlockSpec(memory_space=pltpu.HBM),
        scratch_shapes=[pltpu.VMEM((small_rows, nodes), f32), pltpu.SemaphoreType.DMA],
        compiler_params=params(60),
    )(*small_inputs)
    inputs = (small, stiffness, history, yield_flags)
    khi, klo, hist_s, weight_s, strain_s, place_s, qp_s, cstack, loads, pdir = pl.pallas_call(
        functools.partial(prep_kernel, devices, per_peer, comps, voigt),
        out_shape=(
            jax.ShapeDtypeStruct((rows, deep), bf16),
            jax.ShapeDtypeStruct((rows, deep), bf16),
            jax.ShapeDtypeStruct((rows, columns), f32),
            jax.ShapeDtypeStruct((rows, columns), f32),
            jax.ShapeDtypeStruct((8, columns), f32),
            jax.ShapeDtypeStruct((8, columns), i32),
            jax.ShapeDtypeStruct((8, columns), i32),
            jax.ShapeDtypeStruct((comps, 32, rows), bf16),
            jax.ShapeDtypeStruct((comps, rows, 32), bf16),
            jax.ShapeDtypeStruct((comps, rows, LANES), f32),
        ),
        in_specs=[pl.BlockSpec(memory_space=pltpu.HBM)] * 4,
        out_specs=[vmem] * 10,
        scratch_shapes=[pltpu.VMEM((small_rows, nodes), f32)]
        + [pltpu.VMEM(x.shape, x.dtype) for x in inputs[1:]]
        + [pltpu.VMEM((rows, deep), f32), pltpu.VMEM((8, columns), f32),
           pltpu.VMEM((32, rows), f32), pltpu.SemaphoreType.DMA((4,))],
        compiler_params=params(46),
    )(*inputs)

    lanes = devices // PLANES
    half = lanes // 2
    group = lanes * per_peer
    tall = height(per_peer, nodes)
    block = lambda count: jax.ShapeDtypeStruct((count * tall, LANES), f32)
    whole = lambda shape: pl.BlockSpec(shape, lambda i: (0,) * len(shape))
    updated, stress_s, ready = [], [], []
    left = 0
    for span in (LANES,) * (columns // LANES):
        part = lambda height: pl.BlockSpec((height, span), lambda i, at=left // span: (0, at))
        wide = comps * span
        outs = [block(half)] if len(updated) < 3 else [block(1)] * half
        done = pl.pallas_call(
            functools.partial(
                solve_kernel, 1.0 / math.sqrt(comps * nodes), per_peer, nodes, left, len(updated)
            ),
            grid=(1,),
            out_shape=(
                jax.ShapeDtypeStruct((rows, span), f32),
                jax.ShapeDtypeStruct((8, span), f32),
                *outs,
            ),
            in_specs=[whole((rows, deep)), whole((rows, deep)), part(rows), part(rows), part(8),
                      whole((comps, 32, rows)), whole((comps, rows, 32)), whole((comps, rows, LANES)),
                      whole((8, columns))]
            + [whole(u.shape) for u in updated],
            out_specs=[whole((rows, span)), whole((8, span))] + [whole(o.shape) for o in outs],
            scratch_shapes=[pltpu.VMEM((ITERS, rows, wide), f32), pltpu.VMEM((rows, wide), f32),
                            pltpu.VMEM((rows, wide), f32), pltpu.VMEM((ITERS, 8, span), f32),
                            pltpu.VMEM((deep, 2 * wide), bf16)],
            compiler_params=params(),
            cost_estimate=pl.CostEstimate(
                flops=18 * rows * deep * wide, bytes_accessed=2**20, transcendentals=0
            ),
        )(khi, klo, hist_s, weight_s, strain_s, cstack, loads, pdir, place_s, *updated)
        updated.append(done[0])
        stress_s.append(done[1])
        ready.append(done[2:])
        left += span
    pair = pl.pallas_call(
        functools.partial(ship_kernel, devices, per_peer, nodes, 2 * group),
        out_shape=block(2 * lanes),
        in_specs=[vmem] * (1 + len(updated)),
        out_specs=vmem,
        compiler_params=params(),
        cost_estimate=pl.CostEstimate(
            flops=4 * rows * columns * columns, bytes_accessed=2**20, transcendentals=0
        ),
    )(place_s, *updated)

    axes = ("macro", "pool")

    def hop(sent, mask):
        return lax.ppermute(sent, axes, [(s, s ^ mask) for s in range(devices)])

    pair, *straight = lax.optimization_barrier((pair, *ready[-1]))
    planes = [list(range(z * lanes, (z + 1) * lanes)) for z in range(PLANES)]
    pair = lax.all_to_all(
        pair.reshape(2 * lanes, tall, LANES), axes, split_axis=0, concat_axis=0, tiled=True,
        axis_index_groups=[planes[0] + planes[3], planes[1] + planes[2]],
    ).reshape(2 * lanes * tall, LANES)
    hops = (2 * lanes, lanes, 2 * lanes + 1)
    landed = []
    for (sent,), mask in zip(ready, hops):
        landed.append(hop(sent, mask))
        landed[-2:] = lax.optimization_barrier(tuple(landed[-2:]))
    joined = pl.pallas_call(
        functools.partial(join_kernel, tall),
        out_shape=(block(3),) * half,
        in_specs=[vmem] * 3,
        out_specs=[vmem] * half,
        compiler_params=params(),
        cost_estimate=pl.CostEstimate(flops=2**40, bytes_accessed=2**20, transcendentals=0),
    )(*landed)
    joined = [sent if i == 0 else hop(sent, 2 * i) for i, sent in enumerate(joined)]
    direct = [hop(sent, lanes + 2 * i + 1) for i, sent in enumerate(straight)]
    *stress_s, joined[0] = lax.optimization_barrier((*stress_s, joined[0]))
    stress_out = pl.pallas_call(
        back_kernel,
        out_shape=jax.ShapeDtypeStruct((voigt, columns), f32),
        in_specs=[vmem] * (1 + len(stress_s)),
        out_specs=vmem,
        compiler_params=params(),
    )(qp_s, *stress_s)
    joined[0], stress_out = lax.optimization_barrier((joined[0], stress_out))
    hbm = pl.BlockSpec(memory_space=pl.ANY)
    history_shape = jax.ShapeDtypeStruct((nodes, devices * per_peer), f32)
    staging = [pltpu.VMEM((4, nodes, LANES), f32), pltpu.SemaphoreType.DMA((4,)),
               pltpu.VMEM((2, group, deep), f32)]
    new_history = pl.pallas_call(
        functools.partial(land_pair, devices, per_peer),
        out_shape=history_shape,
        in_specs=[vmem],
        out_specs=hbm,
        scratch_shapes=staging,
        compiler_params=params(),
    )(pair)
    new_history = pl.pallas_call(
        functools.partial(land_hops, devices, per_peer),
        out_shape=history_shape,
        in_specs=[vmem] * (2 * half) + [hbm],
        out_specs=hbm,
        scratch_shapes=staging,
        input_output_aliases={2 * half: 0},
        compiler_params=params(),
    )(*joined, *direct, new_history)
    return (new_history, stress_out)


def solution(mesh):
    return jax.shard_map(
        shards,
        mesh=mesh,
        in_specs=(
            P(None, ("macro", "pool")),
            P(None, ("macro", "pool")),
            P(None, ("macro", "pool")),
            P(("macro", "pool"), None),
            P(("macro", "pool"), None),
            P(),
            P(),
            P(),
            P(),
        ),
        out_specs=(P(None, ("macro", "pool")), P(None, ("macro", "pool"))),
        check_vma=False,
    )
```

```python
import functools
import math

import jax
import jax.numpy as jnp
from jax import lax
from jax.experimental import pallas as pl
from jax.experimental.pallas import tpu as pltpu
from jax.sharding import PartitionSpec as P

ITERS = 3
LANES = 128
PLANES = 4
PATTERN = 32
ROOM = 8192

NN = (((1,), (0,)), ((), ()))
NT = (((1,), (1,)), ((), ()))


def up(value, unit):
    return -(-value // unit) * unit


def dot(a, b, dims=NN):
    return lax.dot_general(a, b, dims, preferred_element_type=jnp.float32)


def halves(x):
    hi = x.astype(jnp.bfloat16)
    lo = (x - hi.astype(jnp.float32)).astype(jnp.bfloat16)
    return hi, lo


def whereabouts(devices):
    me = lax.axis_index("macro") * lax.axis_size("pool") + lax.axis_index("pool")
    lanes = devices // PLANES
    return me, me // lanes, me % lanes, lanes


def hot(row, count):
    rows = lax.broadcasted_iota(jnp.int32, (count, row.shape[1]), 0)
    return jnp.where(rows == row, 1.0, 0.0).astype(jnp.bfloat16)


def pack_kernel(coupling, plastic, strain, owner, qp, pattern, packed, small, sem):
    top = 0
    for c in range(coupling.shape[0]):
        small[top:top + coupling.shape[1], :] = coupling[c]
        top += coupling.shape[1]
    for part in (plastic, strain, owner, qp):
        small[top:top + part.shape[0], 0:part.shape[1]] = part[...].astype(jnp.float32)
        top += part.shape[0]
    count = pattern.shape[0]
    for a in range(count):
        for b in range(count):
            couples = jnp.full((1, LANES), pattern[a, b].astype(jnp.float32))
            small[PATTERN + a * count + b:PATTERN + a * count + b + 1, 0:LANES] = couples
    copy = pltpu.make_async_copy(small, packed.at[pl.ds(0, small.shape[0]), :], sem)
    copy.start()
    copy.wait()


def prep_kernel(devices, per_peer, comps, voigt, *refs):
    sources, outs, local = refs[:4], refs[4:14], refs[14:18]
    kfull, pad, stack, sem = refs[18:]
    khi, klo, hist_s, weight_s, strain_s, place_s, qp_s, cstack, loads, pdir = outs
    small, stiff, hist, flag = local
    copies = [
        pltpu.make_async_copy(source, target, sem.at[i])
        for i, (source, target) in enumerate(
            zip((sources[0].at[pl.ds(0, local[0].shape[0]), :], *sources[1:]), local)
        )
    ]
    for copy in copies:
        copy.start()
    nodes, columns = hist.shape
    nb, blk = stiff.shape[0], stiff.shape[2]
    at_plastic = comps * voigt
    at_strain = at_plastic + comps
    at_owner = at_strain + voigt
    copies[0].wait()

    me, plane, lane, lanes = whereabouts(devices)
    owner = small[at_owner:at_owner + 1, 0:columns].astype(jnp.int32)
    apart = owner // lanes ^ plane
    target = owner % lanes
    away = target ^ lane
    hopping = (away % 2 * 2 + jnp.where(apart == 2, 0, 1)) * (lanes // 2) + away // 2
    staying = jnp.where(apart == 3, 2, 3) * lanes + target
    key = jnp.where((apart == 2) | (apart == 1), hopping, staying)
    key_ids = lax.broadcasted_iota(jnp.int32, (devices, columns), 0)
    mine = jnp.where(key_ids == key, 1.0, 0.0)
    earlier = jnp.where(
        lax.broadcasted_iota(jnp.int32, (columns, columns), 0)
        < lax.broadcasted_iota(jnp.int32, (columns, columns), 1), 1.0, 0.0
    ).astype(jnp.bfloat16)
    before = dot(mine.astype(jnp.bfloat16), earlier)
    rank = jnp.sum(before * mine, axis=0, keepdims=True)
    tally = jnp.sum(mine, axis=1, keepdims=True)
    ahead = jnp.where(key_ids < key, tally, 0.0)
    position = (rank + jnp.sum(ahead, axis=0, keepdims=True)).astype(jnp.int32)

    order = hot(position, columns)
    pad[...] = jnp.zeros_like(pad)
    pad[0:1, :] = key.astype(jnp.float32)
    pad[1:2, :] = rank
    placed = dot(pad[...].astype(jnp.bfloat16), order, NT)
    place_s[...] = jnp.broadcast_to(
        (placed[0:1, :] * per_peer + placed[1:2, :]).astype(jnp.int32), place_s.shape
    )

    pad[0:1, :] = (position // 256).astype(jnp.float32)
    pad[1:2, :] = (position % 256).astype(jnp.float32)
    found = dot(pad[...].astype(jnp.bfloat16), hot(small[at_owner + 1:at_owner + 2, 0:columns].astype(jnp.int32), columns))
    at = (found[0:1, :] * 256.0 + found[1:2, :]).astype(jnp.int32)
    qp_s[...] = jnp.broadcast_to(at, qp_s.shape)
    pad[...] = jnp.zeros_like(pad)
    pad[0:voigt, :] = small[at_strain:at_owner, 0:columns]
    hi, lo = halves(pad[...])
    serves = hot(at, columns)
    strain_s[...] = dot(hi, serves, NT) + dot(lo, serves, NT)

    kfull[...] = jnp.zeros_like(kfull)
    copies[1].wait()
    for a in range(nb):
        for b in range(nb):
            kfull[a * blk:(a + 1) * blk, b * blk:(b + 1) * blk] = (
                stiff[a, b] * small[PATTERN + a * nb + b:PATTERN + a * nb + b + 1, 0:blk]
            )
    k = kfull[...]
    kh = k.astype(jnp.bfloat16)
    khi[...] = kh
    klo[...] = (k - kh.astype(jnp.float32)).astype(jnp.bfloat16)

    copies[2].wait()
    copies[3].wait()
    hi, lo = halves(hist[...])
    hist_s[...] = jnp.zeros_like(hist_s)
    hist_s[0:nodes, :] = dot(hi, order, NT) + dot(lo, order, NT)
    h = hist_s[...]
    weight_s[...] = jnp.zeros_like(weight_s)
    weight_s[0:nodes, :] = dot(flag[...].astype(jnp.float32).astype(jnp.bfloat16), order, NT)
    weight_s[...] = weight_s[...] * h * h / (1.0 + h * h)

    for c in range(comps):
        cpl = small[c * voigt:(c + 1) * voigt, :]
        hi = cpl.astype(jnp.bfloat16).astype(jnp.float32)
        stack[...] = jnp.zeros_like(stack)
        stack[0:voigt, 0:nodes] = hi
        stack[8:8 + voigt, 0:nodes] = hi
        stack[16:16 + voigt, 0:nodes] = cpl - hi
        cstack[c] = stack[...].astype(jnp.bfloat16)
        loads[c] = jnp.transpose(stack[...]).astype(jnp.bfloat16)
    pdir[...] = jnp.zeros_like(pdir)
    for c in range(comps):
        spread = jnp.broadcast_to(small[at_plastic + c:at_plastic + c + 1, :], (LANES, nodes))
        pdir[c, 0:nodes, :] = jnp.transpose(spread)


def row_blocks(rows, span):
    pieces = 4 * span // LANES
    cuts = [rows // 16 * i // pieces * 16 for i in range(pieces + 1)]
    return [slice(top, end) for top, end in zip(cuts, cuts[1:])]


def sweep(rows, comps, span):
    for r in row_blocks(rows, span):
        for c in range(comps):
            yield r, slice(c * span, (c + 1) * span), c


def fold(x):
    return jnp.sum(x.reshape(x.shape[0] // 8, 8, x.shape[1]), axis=0)


def total(parts):
    return jnp.sum(parts, axis=0, keepdims=True)


def solve_kernel(scale, cap, nodes, first, earlier, khi, klo, hist, weight, strain, cstack, loads, pdir, place,
                 *refs):
    earlier_updated, refs = refs[:earlier], refs[earlier:]
    updated, stress, blocks = refs[0], refs[1], refs[2:-5]
    field, resid, image, steps, split = refs[-5:]
    rows, span = hist.shape
    comps = pdir.shape[0]
    wide = comps * span
    zero = jnp.zeros((8, span), jnp.float32)

    def flow(c, r):
        return jnp.concatenate([pdir[c, r, :]] * (span // LANES), axis=1)

    def keep(r, c, x):
        split[r, c * span:(c + 1) * span], split[r, wide + c * span:wide + (c + 1) * span] = (
            halves(x)
        )

    s = strain[...]
    s_hi = s.astype(jnp.bfloat16).astype(jnp.float32)
    s3 = jnp.concatenate([s_hi, s - s_hi, s_hi, jnp.zeros_like(s)], axis=0).astype(jnp.bfloat16)
    split[rows:, :] = jnp.zeros((split.shape[0] - rows, 2 * wide), jnp.bfloat16)
    for c in range(comps):
        image[:, c * span:(c + 1) * span] = dot(loads[c], s3)
    parts = zero
    for r, l, c in sweep(rows, comps, span):
        d = image[r, l] - weight[r, :] * hist[r, :] * flow(c, r)
        resid[r, l] = d
        field[0, r, l] = d
        keep(r, c, d)
        parts = parts + fold(d * d)
    norm = total(parts)

    def step_length(turn, norm):
        parts = zero
        for r in row_blocks(rows, span):
            both = dot(khi[r, :], split[...])
            low = dot(klo[r, :], split[:, 0:wide])
            tangent = 1.5 - weight[r, :]
            for c in range(comps):
                l = slice(c * span, (c + 1) * span)
                d = field[turn, r, l]
                q = both[:, l] + both[:, wide + c * span:wide + (c + 1) * span] + low[:, l]
                q = q + tangent * d
                image[r, l] = q
                parts = parts + fold(d * q)
        return norm / jnp.maximum(total(parts), 1.0)

    def step(turn, norm):
        alpha = step_length(turn, norm)
        steps[turn] = jnp.broadcast_to(alpha, steps.shape[1:])
        parts = zero
        for r, l, c in sweep(rows, comps, span):
            left = resid[r, l] - alpha * image[r, l]
            resid[r, l] = left
            parts = parts + fold(left * left)
        following = total(parts)
        beta = following / jnp.maximum(norm, 1.0)
        for r, l, c in sweep(rows, comps, span):
            d = resid[r, l] + beta * field[turn, r, l]
            field[turn + 1, r, l] = d
            keep(r, c, d)
        return following

    last = ITERS - 1
    alpha = step_length(last, lax.fori_loop(0, last, step, norm))
    alphas = [steps[turn, 0:1, :] for turn in range(last)]
    for r, l, c in sweep(rows, comps, span):
        x = alphas[0] * field[0, r, l]
        for turn in range(1, last):
            x = x + alphas[turn] * field[turn, r, l]
        x = x + alpha * field[last, r, l]
        pushed = flow(c, r) * x
        image[r, 0:span] = pushed if c == 0 else image[r, 0:span] + pushed
        lead = 2 * c * span
        split[r, lead:lead + span], split[r, lead + span:lead + 2 * span] = halves(
            (1.5 - weight[r, :]) * x
        )
    updated[...] = hist[...] + weight[...] * image[:, 0:span]
    sent = placed_rows(first, LANES, place, [*earlier_updated, updated], split.shape[0])
    part = LANES // len(blocks)
    for i, block in enumerate(blocks):
        put(block, 0, sent[i * part:(i + 1) * part], cap, nodes)
    out = s
    for c in range(comps):
        cpl = cstack[c]
        both = dot(cpl, split[0:rows, 2 * c * span:2 * (c + 1) * span])
        out = out + scale * (both[0:8, 0:span] + both[16:24, 0:span] + both[0:8, span:])
    stress[...] = out


def placed_rows(first, count, place, sources, deep):
    width = sum(source.shape[1] for source in sources)
    placing = hot(place[0:1, 0:width] - first, count)
    sums, left = 0.0, 0
    for source in sources:
        rest = jnp.zeros((deep - source.shape[0], source.shape[1]), jnp.float32)
        hi, lo = halves(jnp.concatenate([source[...], rest], axis=0))
        cut = placing[:, left:left + source.shape[1]]
        sums = sums + (dot(cut, hi, NT) + dot(cut, lo, NT))
        left += source.shape[1]
    return sums


def tight(cap, nodes):
    return cap % 32 == 0 and LANES // 2 < nodes % LANES <= LANES * 3 // 4


def height(cap, nodes):
    return cap * (nodes // LANES) + (cap // 2 + cap // 4 if tight(cap, nodes) else cap)


def put(block, top, rows, cap, nodes):
    full, half, quarter = nodes // LANES, cap // 2, cap // 4

    def store(at, piece):
        block[pl.ds(at, piece.shape[0]), :] = piece
        return at + piece.shape[0]

    for first in range(0, rows.shape[0], cap):
        for t in range(full):
            top = store(top, rows[first:first + cap, t * LANES:(t + 1) * LANES])
        tail = rows[first:first + cap, full * LANES:]
        if not tight(cap, nodes):
            top = store(top, tail)
            continue
        lane = lax.broadcasted_iota(jnp.int32, (half, LANES), 1)
        top = store(top, jnp.where(lane < LANES // 2, tail[0:half],
                                   pltpu.roll(tail[half:], LANES // 2, 1)))
        lane = lax.broadcasted_iota(jnp.int32, (quarter, LANES), 1) // (LANES // 4)
        mixed = tail[0:quarter]
        for g in range(4):
            moved = pltpu.roll(tail[g * quarter:(g + 1) * quarter], (g + 2) % 4 * (LANES // 4), 1)
            mixed = jnp.where(lane == g, moved, mixed)
        top = store(top, mixed)


def take(block, top, target, at, cap, nodes):
    full, half, quarter = nodes // LANES, cap // 2, cap // 4
    for t in range(full):
        target[pl.ds(at, cap), t * LANES:(t + 1) * LANES] = block[top + t * cap:top + (t + 1) * cap, :]
    top = top + full * cap
    if not tight(cap, nodes):
        target[pl.ds(at, cap), full * LANES:] = block[top:top + cap, :]
        return
    lane = lax.broadcasted_iota(jnp.int32, (quarter, LANES), 1)
    mixed = block[top + half:top + half + quarter, :]
    for g in range(4):
        left = block[top + g % 2 * quarter:top + (g % 2 + 1) * quarter, :]
        if g >= 2:
            left = pltpu.roll(left, LANES // 2, 1)
        right = mixed if g == 2 else pltpu.roll(mixed, (6 - g) % 4 * (LANES // 4), 1)
        row = pl.multiple_of(at + g * quarter, quarter)
        target[pl.ds(row, quarter), full * LANES:] = jnp.where(lane < LANES // 2, left, right)


def ship_kernel(devices, cap, nodes, first, place, *refs):
    updated, pair = refs[:-1], refs[-1]
    me, plane, lane, lanes = whereabouts(devices)
    group, span = lanes * cap, lanes * height(cap, nodes)
    rows = placed_rows(first, 2 * group, place, updated, up(nodes, 256))
    put(pair, pl.multiple_of((1 - plane // 2) * span, 8), rows[0:group], cap, nodes)
    put(pair, pl.multiple_of(plane // 2 * span, 8), rows[group:], cap, nodes)


def back_kernel(at, *refs):
    out = refs[-1]
    hi, lo = halves(jnp.concatenate([ref[...] for ref in refs[:-1]], axis=1))
    serves = hot(at[0:1, :], hi.shape[1])
    out[...] = (dot(hi, serves) + dot(lo, serves))[0:out.shape[0], :]


def join_kernel(tall, *refs):
    landed, blocks = refs[:3], refs[3:]
    for i, block in enumerate(blocks):
        for k, rows in enumerate(landed):
            block[k * tall:(k + 1) * tall, :] = rows[i * tall:(i + 1) * tall, :]


def land(tile, out, stage, sem, slot, at):
    nodes = out.shape[0]
    stage[slot] = jnp.transpose(tile)[0:nodes, :]
    columns = pl.multiple_of(at * LANES, LANES)
    copy = pltpu.make_async_copy(stage.at[slot], out.at[:, pl.ds(columns, LANES)], sem.at[slot])
    copy.start()
    return copy


def land_pair(devices, cap, pair, history, out, stage, sem, gather):
    me, plane, lane, lanes = whereabouts(devices)
    nodes, tall = out.shape[0], height(cap, out.shape[0])
    tiles = lanes * cap // LANES
    copies = []
    for i in range(2):
        for k in range(lanes):
            take(pair, (i * lanes + k) * tall, gather.at[i], k * cap, cap, nodes)
        source = jnp.where(plane // 2 == i, plane, plane ^ 3)
        for part in range(tiles):
            tile = gather[i, part * LANES:(part + 1) * LANES, :]
            copies.append(land(tile, out, stage, sem, i * tiles + part, source * tiles + part))
    for copy in copies:
        copy.wait()


def land_hops(devices, cap, *refs):
    blocks, (out, stage, sem, gather) = refs[:-4], refs[-4:]
    me, plane, lane, lanes = whereabouts(devices)
    nodes, tall = out.shape[0], height(cap, out.shape[0])
    tiles = lanes * cap // LANES
    copies = []
    for i in range(2):
        for k in range(lanes):
            at = pl.multiple_of((lane ^ k) * cap, cap)
            if i == 1 and k % 2 == 1:
                take(blocks[lanes // 2 + k // 2], 0, gather.at[i], at, cap, nodes)
            else:
                take(blocks[k // 2], (2 * (k % 2) + i) * tall, gather.at[i], at, cap, nodes)
        source = plane ^ (2 - i)
        for part in range(tiles):
            tile = gather[i, part * LANES:(part + 1) * LANES, :]
            copies.append(land(tile, out, stage, sem, i * tiles + part, source * tiles + part))
    for copy in copies:
        copy.wait()


def params(mib=24):
    return pltpu.CompilerParams(vmem_limit_bytes=mib * 2**20)


def shards(
    history, yield_flags, strain, qp_to_rve, new_owner, stiffness, pattern, coupling, plastic_dir
):
    devices = lax.axis_size(("macro", "pool"))
    nodes, columns = history.shape
    comps, voigt = coupling.shape[0], coupling.shape[1]
    per_peer = 2 * columns // devices
    rows = up(nodes, 32)
    deep = up(nodes, 256)
    f32, bf16, i32 = jnp.float32, jnp.bfloat16, jnp.int32
    vmem = pl.BlockSpec(memory_space=pltpu.VMEM)
    small_inputs = (coupling, plastic_dir, strain, new_owner.reshape(1, columns), qp_to_rve, pattern)
    small_rows = up(PATTERN + pattern.size, 8)
    small = pl.pallas_call(
        pack_kernel,
        out_shape=jax.ShapeDtypeStruct((ROOM, nodes), f32),
        in_specs=[vmem] * 5 + [pl.BlockSpec(memory_space=pltpu.SMEM)],
        out_specs=pl.BlockSpec(memory_space=pltpu.HBM),
        scratch_shapes=[pltpu.VMEM((small_rows, nodes), f32), pltpu.SemaphoreType.DMA],
        compiler_params=params(60),
    )(*small_inputs)
    inputs = (small, stiffness, history, yield_flags)
    khi, klo, hist_s, weight_s, strain_s, place_s, qp_s, cstack, loads, pdir = pl.pallas_call(
        functools.partial(prep_kernel, devices, per_peer, comps, voigt),
        out_shape=(
            jax.ShapeDtypeStruct((rows, deep), bf16),
            jax.ShapeDtypeStruct((rows, deep), bf16),
            jax.ShapeDtypeStruct((rows, columns), f32),
            jax.ShapeDtypeStruct((rows, columns), f32),
            jax.ShapeDtypeStruct((8, columns), f32),
            jax.ShapeDtypeStruct((8, columns), i32),
            jax.ShapeDtypeStruct((8, columns), i32),
            jax.ShapeDtypeStruct((comps, 32, rows), bf16),
            jax.ShapeDtypeStruct((comps, rows, 32), bf16),
            jax.ShapeDtypeStruct((comps, rows, LANES), f32),
        ),
        in_specs=[pl.BlockSpec(memory_space=pltpu.HBM)] * 4,
        out_specs=[vmem] * 10,
        scratch_shapes=[pltpu.VMEM((small_rows, nodes), f32)]
        + [pltpu.VMEM(x.shape, x.dtype) for x in inputs[1:]]
        + [pltpu.VMEM((rows, deep), f32), pltpu.VMEM((8, columns), f32),
           pltpu.VMEM((32, rows), f32), pltpu.SemaphoreType.DMA((4,))],
        compiler_params=params(46),
    )(*inputs)

    lanes = devices // PLANES
    half = lanes // 2
    group = lanes * per_peer
    tall = height(per_peer, nodes)
    block = lambda count: jax.ShapeDtypeStruct((count * tall, LANES), f32)
    whole = lambda shape: pl.BlockSpec(shape, lambda i: (0,) * len(shape))
    updated, stress_s, ready = [], [], []
    left = 0
    for span in (LANES,) * (columns // LANES):
        part = lambda height: pl.BlockSpec((height, span), lambda i, at=left // span: (0, at))
        wide = comps * span
        outs = [block(half)] if len(updated) < 3 else [block(1)] * half
        done = pl.pallas_call(
            functools.partial(
                solve_kernel, 1.0 / math.sqrt(comps * nodes), per_peer, nodes, left, len(updated)
            ),
            grid=(1,),
            out_shape=(
                jax.ShapeDtypeStruct((rows, span), f32),
                jax.ShapeDtypeStruct((8, span), f32),
                *outs,
            ),
            in_specs=[whole((rows, deep)), whole((rows, deep)), part(rows), part(rows), part(8),
                      whole((comps, 32, rows)), whole((comps, rows, 32)), whole((comps, rows, LANES)),
                      whole((8, columns))]
            + [whole(u.shape) for u in updated],
            out_specs=[whole((rows, span)), whole((8, span))] + [whole(o.shape) for o in outs],
            scratch_shapes=[pltpu.VMEM((ITERS, rows, wide), f32), pltpu.VMEM((rows, wide), f32),
                            pltpu.VMEM((rows, wide), f32), pltpu.VMEM((ITERS, 8, span), f32),
                            pltpu.VMEM((deep, 2 * wide), bf16)],
            compiler_params=params(),
            cost_estimate=pl.CostEstimate(
                flops=18 * rows * deep * wide, bytes_accessed=2**20, transcendentals=0
            ),
        )(khi, klo, hist_s, weight_s, strain_s, cstack, loads, pdir, place_s, *updated)
        updated.append(done[0])
        stress_s.append(done[1])
        ready.append(done[2:])
        left += span
    pair = pl.pallas_call(
        functools.partial(ship_kernel, devices, per_peer, nodes, 2 * group),
        out_shape=block(2 * lanes),
        in_specs=[vmem] * (1 + len(updated)),
        out_specs=vmem,
        compiler_params=params(),
        cost_estimate=pl.CostEstimate(
            flops=4 * rows * columns * columns, bytes_accessed=2**20, transcendentals=0
        ),
    )(place_s, *updated)

    axes = ("macro", "pool")

    def hop(sent, mask):
        return lax.ppermute(sent, axes, [(s, s ^ mask) for s in range(devices)])

    pair, *straight = lax.optimization_barrier((pair, *ready[-1]))
    planes = [list(range(z * lanes, (z + 1) * lanes)) for z in range(PLANES)]
    pair = lax.all_to_all(
        pair.reshape(2 * lanes, tall, LANES), axes, split_axis=0, concat_axis=0, tiled=True,
        axis_index_groups=[planes[0] + planes[3], planes[1] + planes[2]],
    ).reshape(2 * lanes * tall, LANES)
    hops = (2 * lanes, lanes, 2 * lanes + 1)
    landed = []
    for (sent,), mask in zip(ready, hops):
        landed.append(hop(sent, mask))
        landed[-2:] = lax.optimization_barrier(tuple(landed[-2:]))
    joined = pl.pallas_call(
        functools.partial(join_kernel, tall),
        out_shape=(block(3),) * half,
        in_specs=[vmem] * 3,
        out_specs=[vmem] * half,
        compiler_params=params(),
        cost_estimate=pl.CostEstimate(flops=2**40, bytes_accessed=2**20, transcendentals=0),
    )(*landed)
    joined = [sent if i == 0 else hop(sent, 2 * i) for i, sent in enumerate(joined)]
    direct = [hop(sent, lanes + 2 * i + 1) for i, sent in enumerate(straight)]
    *stress_s, joined[0] = lax.optimization_barrier((*stress_s, joined[0]))
    stress_out = pl.pallas_call(
        back_kernel,
        out_shape=jax.ShapeDtypeStruct((voigt, columns), f32),
        in_specs=[vmem] * (1 + len(stress_s)),
        out_specs=vmem,
        compiler_params=params(),
    )(qp_s, *stress_s)
    joined[0], stress_out = lax.optimization_barrier((joined[0], stress_out))
    hbm = pl.BlockSpec(memory_space=pl.ANY)
    history_shape = jax.ShapeDtypeStruct((nodes, devices * per_peer), f32)
    staging = [pltpu.VMEM((4, nodes, LANES), f32), pltpu.SemaphoreType.DMA((4,)),
               pltpu.VMEM((2, group, deep), f32)]
    new_history = pl.pallas_call(
        functools.partial(land_hops, devices, per_peer),
        out_shape=history_shape,
        in_specs=[vmem] * (2 * half),
        out_specs=hbm,
        scratch_shapes=staging,
        compiler_params=params(),
    )(*joined, *direct)
    new_history = pl.pallas_call(
        functools.partial(land_pair, devices, per_peer),
        out_shape=history_shape,
        in_specs=[vmem, hbm],
        out_specs=hbm,
        scratch_shapes=staging,
        input_output_aliases={1: 0},
        compiler_params=params(),
    )(pair, new_history)
    return (new_history, stress_out)


def solution(mesh):
    return jax.shard_map(
        shards,
        mesh=mesh,
        in_specs=(
            P(None, ("macro", "pool")),
            P(None, ("macro", "pool")),
            P(None, ("macro", "pool")),
            P(("macro", "pool"), None),
            P(("macro", "pool"), None),
            P(),
            P(),
            P(),
            P(),
        ),
        out_specs=(P(None, ("macro", "pool")), P(None, ("macro", "pool"))),
        check_vma=False,
    )
```

```python
import functools
import math

import jax
import jax.numpy as jnp
from jax import lax
from jax.experimental import pallas as pl
from jax.experimental.pallas import tpu as pltpu
from jax.sharding import PartitionSpec as P

ITERS = 3
LANES = 128
PLANES = 4
PATTERN = 32
ROOM = 8192

NN = (((1,), (0,)), ((), ()))
NT = (((1,), (1,)), ((), ()))


def up(value, unit):
    return -(-value // unit) * unit


def dot(a, b, dims=NN):
    return lax.dot_general(a, b, dims, preferred_element_type=jnp.float32)


def halves(x):
    hi = x.astype(jnp.bfloat16)
    lo = (x - hi.astype(jnp.float32)).astype(jnp.bfloat16)
    return hi, lo


def whereabouts(devices):
    me = lax.axis_index("macro") * lax.axis_size("pool") + lax.axis_index("pool")
    lanes = devices // PLANES
    return me, me // lanes, me % lanes, lanes


def hot(row, count):
    rows = lax.broadcasted_iota(jnp.int32, (count, row.shape[1]), 0)
    return jnp.where(rows == row, 1.0, 0.0).astype(jnp.bfloat16)


def pack_kernel(coupling, plastic, strain, owner, qp, pattern, packed, small, sem):
    top = 0
    for c in range(coupling.shape[0]):
        small[top:top + coupling.shape[1], :] = coupling[c]
        top += coupling.shape[1]
    for part in (plastic, strain, owner, qp):
        small[top:top + part.shape[0], 0:part.shape[1]] = part[...].astype(jnp.float32)
        top += part.shape[0]
    count = pattern.shape[0]
    for a in range(count):
        for b in range(count):
            couples = jnp.full((1, LANES), pattern[a, b].astype(jnp.float32))
            small[PATTERN + a * count + b:PATTERN + a * count + b + 1, 0:LANES] = couples
    copy = pltpu.make_async_copy(small, packed.at[pl.ds(0, small.shape[0]), :], sem)
    copy.start()
    copy.wait()


def prep_kernel(devices, per_peer, comps, voigt, *refs):
    sources, outs, local = refs[:4], refs[4:14], refs[14:18]
    kfull, pad, stack, sem = refs[18:]
    khi, klo, hist_s, weight_s, strain_s, place_s, qp_s, cstack, loads, pdir = outs
    small, stiff, hist, flag = local
    copies = [
        pltpu.make_async_copy(source, target, sem.at[i])
        for i, (source, target) in enumerate(
            zip((sources[0].at[pl.ds(0, local[0].shape[0]), :], *sources[1:]), local)
        )
    ]
    for copy in copies:
        copy.start()
    nodes, columns = hist.shape
    nb, blk = stiff.shape[0], stiff.shape[2]
    at_plastic = comps * voigt
    at_strain = at_plastic + comps
    at_owner = at_strain + voigt
    copies[0].wait()

    me, plane, lane, lanes = whereabouts(devices)
    owner = small[at_owner:at_owner + 1, 0:columns].astype(jnp.int32)
    apart = owner // lanes ^ plane
    target = owner % lanes
    away = target ^ lane
    hopping = (away % 2 * 2 + jnp.where(apart == 2, 0, 1)) * (lanes // 2) + away // 2
    staying = jnp.where(apart == 3, 2, 3) * lanes + target
    key = jnp.where((apart == 2) | (apart == 1), hopping, staying)
    key_ids = lax.broadcasted_iota(jnp.int32, (devices, columns), 0)
    mine = jnp.where(key_ids == key, 1.0, 0.0)
    earlier = jnp.where(
        lax.broadcasted_iota(jnp.int32, (columns, columns), 0)
        < lax.broadcasted_iota(jnp.int32, (columns, columns), 1), 1.0, 0.0
    ).astype(jnp.bfloat16)
    before = dot(mine.astype(jnp.bfloat16), earlier)
    rank = jnp.sum(before * mine, axis=0, keepdims=True)
    tally = jnp.sum(mine, axis=1, keepdims=True)
    ahead = jnp.where(key_ids < key, tally, 0.0)
    position = (rank + jnp.sum(ahead, axis=0, keepdims=True)).astype(jnp.int32)

    order = hot(position, columns)
    pad[...] = jnp.zeros_like(pad)
    pad[0:1, :] = key.astype(jnp.float32)
    pad[1:2, :] = rank
    placed = dot(pad[...].astype(jnp.bfloat16), order, NT)
    place_s[...] = jnp.broadcast_to(
        (placed[0:1, :] * per_peer + placed[1:2, :]).astype(jnp.int32), place_s.shape
    )

    pad[0:1, :] = (position // 256).astype(jnp.float32)
    pad[1:2, :] = (position % 256).astype(jnp.float32)
    found = dot(pad[...].astype(jnp.bfloat16), hot(small[at_owner + 1:at_owner + 2, 0:columns].astype(jnp.int32), columns))
    at = (found[0:1, :] * 256.0 + found[1:2, :]).astype(jnp.int32)
    qp_s[...] = jnp.broadcast_to(at, qp_s.shape)
    pad[...] = jnp.zeros_like(pad)
    pad[0:voigt, :] = small[at_strain:at_owner, 0:columns]
    hi, lo = halves(pad[...])
    serves = hot(at, columns)
    strain_s[...] = dot(hi, serves, NT) + dot(lo, serves, NT)

    kfull[...] = jnp.zeros_like(kfull)
    copies[1].wait()
    for a in range(nb):
        for b in range(nb):
            kfull[a * blk:(a + 1) * blk, b * blk:(b + 1) * blk] = (
                stiff[a, b] * small[PATTERN + a * nb + b:PATTERN + a * nb + b + 1, 0:blk]
            )
    k = kfull[...]
    kh = k.astype(jnp.bfloat16)
    khi[...] = kh
    klo[...] = (k - kh.astype(jnp.float32)).astype(jnp.bfloat16)

    copies[2].wait()
    copies[3].wait()
    hi, lo = halves(hist[...])
    hist_s[...] = jnp.zeros_like(hist_s)
    hist_s[0:nodes, :] = dot(hi, order, NT) + dot(lo, order, NT)
    h = hist_s[...]
    weight_s[...] = jnp.zeros_like(weight_s)
    weight_s[0:nodes, :] = dot(flag[...].astype(jnp.float32).astype(jnp.bfloat16), order, NT)
    weight_s[...] = weight_s[...] * h * h / (1.0 + h * h)

    for c in range(comps):
        cpl = small[c * voigt:(c + 1) * voigt, :]
        hi = cpl.astype(jnp.bfloat16).astype(jnp.float32)
        stack[...] = jnp.zeros_like(stack)
        stack[0:voigt, 0:nodes] = hi
        stack[8:8 + voigt, 0:nodes] = hi
        stack[16:16 + voigt, 0:nodes] = cpl - hi
        cstack[c] = stack[...].astype(jnp.bfloat16)
        loads[c] = jnp.transpose(stack[...]).astype(jnp.bfloat16)
    pdir[...] = jnp.zeros_like(pdir)
    for c in range(comps):
        spread = jnp.broadcast_to(small[at_plastic + c:at_plastic + c + 1, :], (LANES, nodes))
        pdir[c, 0:nodes, :] = jnp.transpose(spread)


def row_blocks(rows, span):
    pieces = 2 * span // LANES
    cuts = [rows // 16 * i // pieces * 16 for i in range(pieces + 1)]
    return [slice(top, end) for top, end in zip(cuts, cuts[1:])]


def sweep(rows, comps, span):
    for r in row_blocks(rows, span):
        for c in range(comps):
            yield r, slice(c * span, (c + 1) * span), c


def fold(x):
    return jnp.sum(x.reshape(x.shape[0] // 8, 8, x.shape[1]), axis=0)


def total(parts):
    return jnp.sum(parts, axis=0, keepdims=True)


def solve_kernel(scale, cap, nodes, first, earlier, khi, klo, hist, weight, strain, cstack, loads, pdir, place,
                 *refs):
    earlier_updated, refs = refs[:earlier], refs[earlier:]
    updated, stress, blocks = refs[0], refs[1], refs[2:-5]
    field, resid, image, steps, split = refs[-5:]
    rows, span = hist.shape
    comps = pdir.shape[0]
    wide = comps * span
    zero = jnp.zeros((8, span), jnp.float32)

    def flow(c, r):
        return jnp.concatenate([pdir[c, r, :]] * (span // LANES), axis=1)

    def keep(r, c, x):
        split[r, c * span:(c + 1) * span], split[r, wide + c * span:wide + (c + 1) * span] = (
            halves(x)
        )

    s = strain[...]
    s_hi = s.astype(jnp.bfloat16).astype(jnp.float32)
    s3 = jnp.concatenate([s_hi, s - s_hi, s_hi, jnp.zeros_like(s)], axis=0).astype(jnp.bfloat16)
    split[rows:, :] = jnp.zeros((split.shape[0] - rows, 2 * wide), jnp.bfloat16)
    for c in range(comps):
        image[:, c * span:(c + 1) * span] = dot(loads[c], s3)
    parts = zero
    for r, l, c in sweep(rows, comps, span):
        d = image[r, l] - weight[r, :] * hist[r, :] * flow(c, r)
        resid[r, l] = d
        field[0, r, l] = d
        keep(r, c, d)
        parts = parts + fold(d * d)
    norm = total(parts)

    def step_length(turn, norm):
        parts = zero
        for r in row_blocks(rows, span):
            both = dot(khi[r, :], split[...])
            low = dot(klo[r, :], split[:, 0:wide])
            tangent = 1.5 - weight[r, :]
            for c in range(comps):
                l = slice(c * span, (c + 1) * span)
                d = field[turn, r, l]
                q = both[:, l] + both[:, wide + c * span:wide + (c + 1) * span] + low[:, l]
                q = q + tangent * d
                image[r, l] = q
                parts = parts + fold(d * q)
        return norm / jnp.maximum(total(parts), 1.0)

    def step(turn, norm):
        alpha = step_length(turn, norm)
        steps[turn] = jnp.broadcast_to(alpha, steps.shape[1:])
        parts = zero
        for r, l, c in sweep(rows, comps, span):
            left = resid[r, l] - alpha * image[r, l]
            resid[r, l] = left
            parts = parts + fold(left * left)
        following = total(parts)
        beta = following / jnp.maximum(norm, 1.0)
        for r, l, c in sweep(rows, comps, span):
            d = resid[r, l] + beta * field[turn, r, l]
            field[turn + 1, r, l] = d
            keep(r, c, d)
        return following

    last = ITERS - 1
    alpha = step_length(last, lax.fori_loop(0, last, step, norm))
    alphas = [steps[turn, 0:1, :] for turn in range(last)]
    for r, l, c in sweep(rows, comps, span):
        x = alphas[0] * field[0, r, l]
        for turn in range(1, last):
            x = x + alphas[turn] * field[turn, r, l]
        x = x + alpha * field[last, r, l]
        pushed = flow(c, r) * x
        image[r, 0:span] = pushed if c == 0 else image[r, 0:span] + pushed
        lead = 2 * c * span
        split[r, lead:lead + span], split[r, lead + span:lead + 2 * span] = halves(
            (1.5 - weight[r, :]) * x
        )
    updated[...] = hist[...] + weight[...] * image[:, 0:span]
    sent = placed_rows(first, LANES, place, [*earlier_updated, updated], split.shape[0])
    part = LANES // len(blocks)
    for i, block in enumerate(blocks):
        put(block, 0, sent[i * part:(i + 1) * part], cap, nodes)
    out = s
    for c in range(comps):
        cpl = cstack[c]
        both = dot(cpl, split[0:rows, 2 * c * span:2 * (c + 1) * span])
        out = out + scale * (both[0:8, 0:span] + both[16:24, 0:span] + both[0:8, span:])
    stress[...] = out


def placed_rows(first, count, place, sources, deep):
    width = sum(source.shape[1] for source in sources)
    placing = hot(place[0:1, 0:width] - first, count)
    sums, left = 0.0, 0
    for source in sources:
        rest = jnp.zeros((deep - source.shape[0], source.shape[1]), jnp.float32)
        hi, lo = halves(jnp.concatenate([source[...], rest], axis=0))
        cut = placing[:, left:left + source.shape[1]]
        sums = sums + (dot(cut, hi, NT) + dot(cut, lo, NT))
        left += source.shape[1]
    return sums


def tight(cap, nodes):
    return cap % 32 == 0 and LANES // 2 < nodes % LANES <= LANES * 3 // 4


def height(cap, nodes):
    return cap * (nodes // LANES) + (cap // 2 + cap // 4 if tight(cap, nodes) else cap)


def put(block, top, rows, cap, nodes):
    full, half, quarter = nodes // LANES, cap // 2, cap // 4

    def store(at, piece):
        block[pl.ds(at, piece.shape[0]), :] = piece
        return at + piece.shape[0]

    for first in range(0, rows.shape[0], cap):
        for t in range(full):
            top = store(top, rows[first:first + cap, t * LANES:(t + 1) * LANES])
        tail = rows[first:first + cap, full * LANES:]
        if not tight(cap, nodes):
            top = store(top, tail)
            continue
        lane = lax.broadcasted_iota(jnp.int32, (half, LANES), 1)
        top = store(top, jnp.where(lane < LANES // 2, tail[0:half],
                                   pltpu.roll(tail[half:], LANES // 2, 1)))
        lane = lax.broadcasted_iota(jnp.int32, (quarter, LANES), 1) // (LANES // 4)
        mixed = tail[0:quarter]
        for g in range(4):
            moved = pltpu.roll(tail[g * quarter:(g + 1) * quarter], (g + 2) % 4 * (LANES // 4), 1)
            mixed = jnp.where(lane == g, moved, mixed)
        top = store(top, mixed)


def take(block, top, target, at, cap, nodes):
    full, half, quarter = nodes // LANES, cap // 2, cap // 4
    for t in range(full):
        target[pl.ds(at, cap), t * LANES:(t + 1) * LANES] = block[top + t * cap:top + (t + 1) * cap, :]
    top = top + full * cap
    if not tight(cap, nodes):
        target[pl.ds(at, cap), full * LANES:] = block[top:top + cap, :]
        return
    lane = lax.broadcasted_iota(jnp.int32, (quarter, LANES), 1)
    mixed = block[top + half:top + half + quarter, :]
    for g in range(4):
        left = block[top + g % 2 * quarter:top + (g % 2 + 1) * quarter, :]
        if g >= 2:
            left = pltpu.roll(left, LANES // 2, 1)
        right = mixed if g == 2 else pltpu.roll(mixed, (6 - g) % 4 * (LANES // 4), 1)
        row = pl.multiple_of(at + g * quarter, quarter)
        target[pl.ds(row, quarter), full * LANES:] = jnp.where(lane < LANES // 2, left, right)


def ship_kernel(devices, cap, nodes, first, place, *refs):
    updated, pair = refs[:-1], refs[-1]
    me, plane, lane, lanes = whereabouts(devices)
    group, span = lanes * cap, lanes * height(cap, nodes)
    rows = placed_rows(first, 2 * group, place, updated, up(nodes, 256))
    put(pair, pl.multiple_of((1 - plane // 2) * span, 8), rows[0:group], cap, nodes)
    put(pair, pl.multiple_of(plane // 2 * span, 8), rows[group:], cap, nodes)


def back_kernel(at, *refs):
    out = refs[-1]
    hi, lo = halves(jnp.concatenate([ref[...] for ref in refs[:-1]], axis=1))
    serves = hot(at[0:1, :], hi.shape[1])
    out[...] = (dot(hi, serves) + dot(lo, serves))[0:out.shape[0], :]


def join_kernel(tall, *refs):
    landed, blocks = refs[:3], refs[3:]
    for i, block in enumerate(blocks):
        for k, rows in enumerate(landed):
            block[k * tall:(k + 1) * tall, :] = rows[i * tall:(i + 1) * tall, :]


def land(tile, out, stage, sem, slot, at):
    nodes = out.shape[0]
    stage[slot] = jnp.transpose(tile)[0:nodes, :]
    columns = pl.multiple_of(at * LANES, LANES)
    copy = pltpu.make_async_copy(stage.at[slot], out.at[:, pl.ds(columns, LANES)], sem.at[slot])
    copy.start()
    return copy


def land_pair(devices, cap, pair, out, stage, sem, gather):
    me, plane, lane, lanes = whereabouts(devices)
    nodes, tall = out.shape[0], height(cap, out.shape[0])
    tiles = lanes * cap // LANES
    copies = []
    for i in range(2):
        for k in range(lanes):
            take(pair, (i * lanes + k) * tall, gather.at[i], k * cap, cap, nodes)
        source = jnp.where(plane // 2 == i, plane, plane ^ 3)
        for part in range(tiles):
            tile = gather[i, part * LANES:(part + 1) * LANES, :]
            copies.append(land(tile, out, stage, sem, i * tiles + part, source * tiles + part))
    for copy in copies:
        copy.wait()


def land_hops(devices, cap, *refs):
    blocks, (out, stage, sem, gather) = refs[:-5], refs[-4:]
    me, plane, lane, lanes = whereabouts(devices)
    nodes, tall = out.shape[0], height(cap, out.shape[0])
    tiles = lanes * cap // LANES
    copies = []
    for i in range(2):
        for k in range(lanes):
            at = pl.multiple_of((lane ^ k) * cap, cap)
            if i == 1 and k % 2 == 1:
                take(blocks[lanes // 2 + k // 2], 0, gather.at[i], at, cap, nodes)
            else:
                take(blocks[k // 2], (2 * (k % 2) + i) * tall, gather.at[i], at, cap, nodes)
        source = plane ^ (2 - i)
        for part in range(tiles):
            tile = gather[i, part * LANES:(part + 1) * LANES, :]
            copies.append(land(tile, out, stage, sem, i * tiles + part, source * tiles + part))
    for copy in copies:
        copy.wait()


def params(mib=24):
    return pltpu.CompilerParams(vmem_limit_bytes=mib * 2**20)


def shards(
    history, yield_flags, strain, qp_to_rve, new_owner, stiffness, pattern, coupling, plastic_dir
):
    devices = lax.axis_size(("macro", "pool"))
    nodes, columns = history.shape
    comps, voigt = coupling.shape[0], coupling.shape[1]
    per_peer = 2 * columns // devices
    rows = up(nodes, 32)
    deep = up(nodes, 256)
    f32, bf16, i32 = jnp.float32, jnp.bfloat16, jnp.int32
    vmem = pl.BlockSpec(memory_space=pltpu.VMEM)
    small_inputs = (coupling, plastic_dir, strain, new_owner.reshape(1, columns), qp_to_rve, pattern)
    small_rows = up(PATTERN + pattern.size, 8)
    small = pl.pallas_call(
        pack_kernel,
        out_shape=jax.ShapeDtypeStruct((ROOM, nodes), f32),
        in_specs=[vmem] * 5 + [pl.BlockSpec(memory_space=pltpu.SMEM)],
        out_specs=pl.BlockSpec(memory_space=pltpu.HBM),
        scratch_shapes=[pltpu.VMEM((small_rows, nodes), f32), pltpu.SemaphoreType.DMA],
        compiler_params=params(60),
    )(*small_inputs)
    inputs = (small, stiffness, history, yield_flags)
    khi, klo, hist_s, weight_s, strain_s, place_s, qp_s, cstack, loads, pdir = pl.pallas_call(
        functools.partial(prep_kernel, devices, per_peer, comps, voigt),
        out_shape=(
            jax.ShapeDtypeStruct((rows, deep), bf16),
            jax.ShapeDtypeStruct((rows, deep), bf16),
            jax.ShapeDtypeStruct((rows, columns), f32),
            jax.ShapeDtypeStruct((rows, columns), f32),
            jax.ShapeDtypeStruct((8, columns), f32),
            jax.ShapeDtypeStruct((8, columns), i32),
            jax.ShapeDtypeStruct((8, columns), i32),
            jax.ShapeDtypeStruct((comps, 32, rows), bf16),
            jax.ShapeDtypeStruct((comps, rows, 32), bf16),
            jax.ShapeDtypeStruct((comps, rows, LANES), f32),
        ),
        in_specs=[pl.BlockSpec(memory_space=pltpu.HBM)] * 4,
        out_specs=[vmem] * 10,
        scratch_shapes=[pltpu.VMEM((small_rows, nodes), f32)]
        + [pltpu.VMEM(x.shape, x.dtype) for x in inputs[1:]]
        + [pltpu.VMEM((rows, deep), f32), pltpu.VMEM((8, columns), f32),
           pltpu.VMEM((32, rows), f32), pltpu.SemaphoreType.DMA((4,))],
        compiler_params=params(46),
    )(*inputs)

    lanes = devices // PLANES
    half = lanes // 2
    group = lanes * per_peer
    tall = height(per_peer, nodes)
    block = lambda count: jax.ShapeDtypeStruct((count * tall, LANES), f32)
    whole = lambda shape: pl.BlockSpec(shape, lambda i: (0,) * len(shape))
    updated, stress_s, ready = [], [], []
    left = 0
    for span in (LANES,) * (columns // LANES):
        part = lambda height: pl.BlockSpec((height, span), lambda i, at=left // span: (0, at))
        wide = comps * span
        outs = [block(half)] if len(updated) < 3 else [block(1)] * half
        done = pl.pallas_call(
            functools.partial(
                solve_kernel, 1.0 / math.sqrt(comps * nodes), per_peer, nodes, left, len(updated)
            ),
            grid=(1,),
            out_shape=(
                jax.ShapeDtypeStruct((rows, span), f32),
                jax.ShapeDtypeStruct((8, span), f32),
                *outs,
            ),
            in_specs=[whole((rows, deep)), whole((rows, deep)), part(rows), part(rows), part(8),
                      whole((comps, 32, rows)), whole((comps, rows, 32)), whole((comps, rows, LANES)),
                      whole((8, columns))]
            + [whole(u.shape) for u in updated],
            out_specs=[whole((rows, span)), whole((8, span))] + [whole(o.shape) for o in outs],
            scratch_shapes=[pltpu.VMEM((ITERS, rows, wide), f32), pltpu.VMEM((rows, wide), f32),
                            pltpu.VMEM((rows, wide), f32), pltpu.VMEM((ITERS, 8, span), f32),
                            pltpu.VMEM((deep, 2 * wide), bf16)],
            compiler_params=params(),
            cost_estimate=pl.CostEstimate(
                flops=18 * rows * deep * wide, bytes_accessed=2**20, transcendentals=0
            ),
        )(khi, klo, hist_s, weight_s, strain_s, cstack, loads, pdir, place_s, *updated)
        updated.append(done[0])
        stress_s.append(done[1])
        ready.append(done[2:])
        left += span
    pair = pl.pallas_call(
        functools.partial(ship_kernel, devices, per_peer, nodes, 2 * group),
        out_shape=block(2 * lanes),
        in_specs=[vmem] * (1 + len(updated)),
        out_specs=vmem,
        compiler_params=params(),
        cost_estimate=pl.CostEstimate(
            flops=4 * rows * columns * columns, bytes_accessed=2**20, transcendentals=0
        ),
    )(place_s, *updated)

    axes = ("macro", "pool")

    def hop(sent, mask):
        return lax.ppermute(sent, axes, [(s, s ^ mask) for s in range(devices)])

    pair, *straight = lax.optimization_barrier((pair, *ready[-1]))
    planes = [list(range(z * lanes, (z + 1) * lanes)) for z in range(PLANES)]
    pair = lax.all_to_all(
        pair.reshape(2 * lanes, tall, LANES), axes, split_axis=0, concat_axis=0, tiled=True,
        axis_index_groups=[planes[0] + planes[3], planes[1] + planes[2]],
    ).reshape(2 * lanes * tall, LANES)
    hops = (2 * lanes, lanes, 2 * lanes + 1)
    landed = []
    for (sent,), mask in zip(ready, hops):
        landed.append(hop(sent, mask))
        landed[-2:] = lax.optimization_barrier(tuple(landed[-2:]))
    joined = pl.pallas_call(
        functools.partial(join_kernel, tall),
        out_shape=(block(3),) * half,
        in_specs=[vmem] * 3,
        out_specs=[vmem] * half,
        compiler_params=params(),
        cost_estimate=pl.CostEstimate(flops=2**40, bytes_accessed=2**20, transcendentals=0),
    )(*landed)
    joined = [sent if i == 0 else hop(sent, 2 * i) for i, sent in enumerate(joined)]
    direct = [hop(sent, lanes + 2 * i + 1) for i, sent in enumerate(straight)]
    *stress_s, joined[0] = lax.optimization_barrier((*stress_s, joined[0]))
    stress_out = pl.pallas_call(
        back_kernel,
        out_shape=jax.ShapeDtypeStruct((voigt, columns), f32),
        in_specs=[vmem] * (1 + len(stress_s)),
        out_specs=vmem,
        compiler_params=params(),
    )(qp_s, *stress_s)
    joined[0], stress_out = lax.optimization_barrier((joined[0], stress_out))
    hbm = pl.BlockSpec(memory_space=pl.ANY)
    history_shape = jax.ShapeDtypeStruct((nodes, devices * per_peer), f32)
    staging = [pltpu.VMEM((4, nodes, LANES), f32), pltpu.SemaphoreType.DMA((4,)),
               pltpu.VMEM((2, group, deep), f32)]
    new_history = pl.pallas_call(
        functools.partial(land_pair, devices, per_peer),
        out_shape=history_shape,
        in_specs=[vmem],
        out_specs=hbm,
        scratch_shapes=staging,
        compiler_params=params(),
    )(pair)
    new_history = pl.pallas_call(
        functools.partial(land_hops, devices, per_peer),
        out_shape=history_shape,
        in_specs=[vmem] * (2 * half) + [hbm],
        out_specs=hbm,
        scratch_shapes=staging,
        input_output_aliases={2 * half: 0},
        compiler_params=params(),
    )(*joined, *direct, new_history)
    return (new_history, stress_out)


def solution(mesh):
    return jax.shard_map(
        shards,
        mesh=mesh,
        in_specs=(
            P(None, ("macro", "pool")),
            P(None, ("macro", "pool")),
            P(None, ("macro", "pool")),
            P(("macro", "pool"), None),
            P(("macro", "pool"), None),
            P(),
            P(),
            P(),
            P(),
        ),
        out_specs=(P(None, ("macro", "pool")), P(None, ("macro", "pool"))),
        check_vma=False,
    )
```
